32 devices in a mesh: seq: 8 (over z, core), batch: 4 (over y, x).
Axes of the slice: x: 2, y: 2, z: 4, core: 2. Of those that a mesh axis runs over, the one named last changes fastest.
Arguments:
- x_short: bfloat16 [8, 1024, 768], P('batch', 'seq'), may hold values from -6 to 6
- x_long: bfloat16 [8, 2048, 768], P('batch', 'seq'), may hold values from -6 to 6
- lengths: int32 [2, 8], P(None, 'batch'), may hold values from 256 to 2048, as said below
- cot_short: bfloat16 [8, 1024, 768], P('batch', 'seq'), may hold values from -6 to 6
- cot_long: bfloat16 [8, 2048, 768], P('batch', 'seq'), may hold values from -6 to 6
- w_qkv: bfloat16 [768, 2304], P(('seq', 'batch')), may hold values from -0.21875 to 0.21875
- w_out: bfloat16 [768, 768], P(('seq', 'batch')), may hold values from -1.25 to 1.25
- w_up: bfloat16 [768, 3072], P(('seq', 'batch')), may hold values from -0.21875 to 0.21875
- w_down: bfloat16 [3072, 768], P(('seq', 'batch')), may hold values from -0.109375 to 0.109375
- conv_kernel: bfloat16 [3, 2304], P(None, ('seq', 'batch')), may hold values from -3 to 3
- norm_params: bfloat16 [4, 768], P(None, ('seq', 'batch')), may hold values from -1.2 to 1.4
Outputs:
- y_short: bfloat16 [8, 1024, 768], P('batch', 'seq')
- y_long: bfloat16 [8, 2048, 768], P('batch', 'seq')
- dx_short: float32 [8, 1024, 768], P('batch', 'seq')
- dx_long: float32 [8, 2048, 768], P('batch', 'seq')
- grad_w_qkv: float32 [768, 2304], P(('seq', 'batch'))
- grad_w_out: float32 [768, 768], P(('seq', 'batch'))
- grad_w_up: float32 [768, 3072], P(('seq', 'batch'))
- grad_w_down: float32 [3072, 768], P(('seq', 'batch'))
- grad_conv_kernel: float32 [3, 2304], P(None, ('seq', 'batch'))
- grad_norm_params: float32 [4, 768], P(None, ('seq', 'batch'))
The draws below stay inside these ranges and needn't reach their ends.
Inputs may be any that keep to these rules, and one draw needn't show every extreme that they name: Row 0 holds the lengths of the short sub-batch's sequences, the rest of each 1024-position slot being padding; row 1 those of the long sub-batch, in 2048-position slots. In each row, of the 2 sequences at one index of batch, one fills its whole slot and the other holds a quarter of its slot or more.
All inputs are finite; a program needn't handle non-finite values.
Results may differ from the reference program's by a relative error of at most 0.015.
The reference program's roundings to bfloat16 on the way count: a program that leaves them out, or rounds other values in their place, can miss the bound.
Values may be sent and summed in bfloat16 or wider, within the bound.
A program may use at most 320 MiB of HBM per device.

```python
import jax
import jax.numpy as jnp
from jax import lax

D = 768
HEAD_DIM = 64
FF = 3072
LEN_SHORT = 1024
LEN_LONG = 2048
SEQS = 2
NSEQ = 8


def draw_lengths(key, part):
    key = jax.random.fold_in(key, 7)
    short_key, long_key, slot_key = jax.random.split(key, 3)
    slot_keys = jax.random.split(slot_key, 2)

    def one_row(row_key, pick_key, full_len):
        drawn_lengths = jax.random.randint(row_key, (NSEQ,), full_len // 4, full_len + 1)
        slot_index = jax.random.randint(pick_key, (NSEQ // SEQS, 1), 0, SEQS)
        chosen = (jnp.arange(SEQS, dtype=jnp.int32)[None, :] == slot_index).reshape(NSEQ)
        return jnp.where(chosen, full_len, drawn_lengths)
    return jnp.stack([one_row(short_key, slot_keys[0], LEN_SHORT), one_row(long_key, slot_keys[1], LEN_LONG)]).astype(jnp.int32)


def draw_norm_params(key, part):
    key = jax.random.fold_in(key, 11)
    gain_key, bias_key = jax.random.split(key)
    gains = jax.random.uniform(gain_key, (2, D), jnp.float32, 0.6, 1.4)
    biases = jnp.clip(0.3 * jax.random.normal(bias_key, (2, D), jnp.float32), -1.2, 1.2)
    return jnp.stack([gains[0], biases[0], gains[1], biases[1]]).astype(jnp.bfloat16)


def level_of(stream_key, extent, cuts, low, largest):
    level, own = 1.0, jax.random.fold_in(stream_key, 6)
    for axis_at, parts in cuts:
        steps = jnp.exp(jax.random.uniform(jax.random.fold_in(own, axis_at), (parts,), jnp.float32, low / len(cuts), largest / len(cuts)))
        level = level * jnp.repeat(steps, extent[axis_at] // parts).reshape([-1 if axis == axis_at else 1 for axis in range(len(extent))])
    return level


def normal_values(rng, shape, spread, most, pieces=(), held_as=jnp.bfloat16):
    array = spread * jax.random.normal(rng, shape, jnp.float32)
    if pieces:
        array = array * level_of(rng, shape, pieces, -0.22, 0.18)
    return jnp.clip(array, -most, most).astype(held_as)


def setup_inputs(seed: int = 0) -> dict:
    key_of = jax.random.split(jax.random.key(seed), 12)
    return {
        "x_short": normal_values(key_of[0], (NSEQ, LEN_SHORT, D), 1.0, 6.0, ((0, 4), (1, 8))),
        "x_long": normal_values(key_of[1], (NSEQ, LEN_LONG, D), 1.0, 6.0, ((0, 4), (1, 8))),
        "lengths": draw_lengths(jax.random.fold_in(key_of[11], 71), 0),
        "cot_short": normal_values(key_of[3], (NSEQ, LEN_SHORT, D), 1.0, 6.0, ((0, 4), (1, 8))),
        "cot_long": normal_values(key_of[4], (NSEQ, LEN_LONG, D), 1.0, 6.0, ((0, 4), (1, 8))),
        "w_qkv": normal_values(key_of[5], (D, 3 * D), D ** -0.5, 0.21875, ((0, 32),)),
        "w_out": normal_values(key_of[6], (D, D), (D // 32) ** -0.5, 1.25, ((0, 32),)),
        "w_up": normal_values(key_of[7], (D, FF), D ** -0.5, 0.21875, ((0, 32),)),
        "w_down": normal_values(key_of[8], (FF, D), FF ** -0.5, 0.109375, ((0, 32),)),
        "conv_kernel": normal_values(key_of[9], (3, 3 * D), 0.6, 3.0, ((1, 32),)),
        "norm_params": draw_norm_params(jax.random.fold_in(key_of[11], 71), 0),
    }


EPS = 1e-05
NEG_FILL = -1e+30
HIGHEST = lax.Precision.HIGHEST

@jax.custom_vjp
def low(v):
    return lax.optimization_barrier(v.astype(jnp.bfloat16)).astype(jnp.float32)

@jax.custom_vjp
def low_back(v):
    return v

def low_keep(v):
    return (low(v), None)

def low_pass(kept, grad):
    return (grad,)

def back_keep(v):
    return (v, None)

def back_low(kept, grad):
    return (low(grad),)
low.defvjp(low_keep, low_pass)
low_back.defvjp(back_keep, back_low)

def matmul(left, right):
    return jnp.dot(left, right, precision=HIGHEST, preferred_element_type=jnp.float32)

def layer_norm(values, gain, offset_term):
    average = lax.optimization_barrier(jnp.mean(values, axis=-1, keepdims=True))
    centred = values - average
    variance = lax.optimization_barrier(jnp.mean(centred * centred, axis=-1, keepdims=True))
    return centred * lax.rsqrt(variance + EPS) * gain + offset_term

def conv_causal(projected, kernel):
    row_count = projected.shape[0]
    padded = jnp.concatenate([jnp.zeros((2, projected.shape[1]), jnp.float32), projected], axis=0)
    return kernel[0] * padded[2:] + kernel[1] * padded[1:row_count + 1] + kernel[2] * padded[:row_count]

def layer_sequence(inputs, length, weights):
    w_qkv, w_out, w_up, w_down, conv_kernel, norm_params = weights
    row_count, model_width = inputs.shape
    heads_total = model_width // HEAD_DIM
    normed = low(layer_norm(inputs, norm_params[0], norm_params[1]))
    projected = low(low_back(matmul(normed, w_qkv)))
    mixed = low(conv_causal(projected, conv_kernel))
    queries = mixed[:, :model_width].reshape(row_count, heads_total, HEAD_DIM)
    key_rows = mixed[:, model_width:2 * model_width].reshape(row_count, heads_total, HEAD_DIM)
    value_rows = mixed[:, 2 * model_width:].reshape(row_count, heads_total, HEAD_DIM)
    scores = low_back(jnp.einsum('qhd,khd->hqk', queries, key_rows, precision=HIGHEST))
    positions = jnp.arange(row_count, dtype=jnp.int32)
    usable = (positions[None, :] <= positions[:, None]) & (positions[None, :] < length)
    masked = jnp.where(usable[None], HEAD_DIM ** (-0.5) * scores, NEG_FILL)
    exp_terms = jnp.exp(masked - lax.optimization_barrier(jnp.max(masked, axis=-1, keepdims=True)))
    attn_probs = low(exp_terms / lax.optimization_barrier(jnp.sum(exp_terms, axis=-1, keepdims=True)))
    attended = low(low_back(jnp.einsum('hqk,khd->qhd', attn_probs, value_rows, precision=HIGHEST)))
    attended = attended.reshape(row_count, model_width)
    middle = inputs + low_back(matmul(attended, w_out))
    second = low(layer_norm(middle, norm_params[2], norm_params[3]))
    upper = low_back(matmul(second, w_up))
    hidden = low(jnp.square(jnp.maximum(upper, 0.0)))
    return middle + matmul(hidden, w_down)

def run_group(inputs, seq_lengths, weights):
    layer_saved = jax.checkpoint(layer_sequence)

    def stepper(carry, entry):
        return (carry, layer_saved(entry[0], entry[1], weights))
    return lax.scan(stepper, jnp.zeros((), jnp.float32), (inputs, seq_lengths))[1]

def reference(x_short, x_long, lengths, cot_short, cot_long, w_qkv, w_out, w_up, w_down, conv_kernel, norm_params):
    weights = tuple((item.astype(jnp.float32) for item in (w_qkv, w_out, w_up, w_down, conv_kernel, norm_params)))

    def forward(short_in, long_in, weight_set):
        return (run_group(short_in, lengths[0], weight_set), run_group(long_in, lengths[1], weight_set))
    outputs, pullback = jax.vjp(forward, x_short.astype(jnp.float32), x_long.astype(jnp.float32), weights)
    grad_short, grad_long, grad_weights = pullback((cot_short.astype(jnp.float32), cot_long.astype(jnp.float32)))
    return (outputs[0].astype(jnp.bfloat16), outputs[1].astype(jnp.bfloat16), grad_short.astype(jnp.float32), grad_long.astype(jnp.float32), grad_weights[0], grad_weights[1], grad_weights[2], grad_weights[3], grad_weights[4], grad_weights[5])
```

```python
import jax
import jax.numpy as jnp
from jax import lax
from jax.experimental import pallas as pl
from jax.experimental.pallas import tpu as pltpu
from jax.sharding import PartitionSpec as P

EPS = 1e-05
NEG_FILL = -1e30
HEAD_DIM = 64
LANES = 128
TILE = 256
PAD = 16
MESH = pl.DeviceIdType.MESH
F32 = jnp.float32
BF16 = jnp.bfloat16


def dot_nn(left, right):
    return lax.dot_general(left, right, (((1,), (0,)), ((), ())), preferred_element_type=F32)


def dot_nt(left, right):
    return lax.dot_general(left, right, (((1,), (1,)), ((), ())), preferred_element_type=F32)


def dot_tn(left, right):
    return lax.dot_general(left, right, (((0,), (0,)), ((), ())), preferred_element_type=F32)


def params_of(limit=58, **more):
    return pltpu.CompilerParams(vmem_limit_bytes=limit * 2**20, **more)


def vmem():
    return pl.BlockSpec(memory_space=pltpu.VMEM)


def smem():
    return pl.BlockSpec(memory_space=pltpu.SMEM)


def hbm():
    return pl.BlockSpec(memory_space=pl.ANY)


def normalise(values):
    average = jnp.mean(values, axis=-1, keepdims=True)
    centred = values - average
    inverse = lax.rsqrt(jnp.mean(centred * centred, axis=-1, keepdims=True) + EPS)
    return centred * inverse, inverse


def norm_back(grad, normal, inverse, gain):
    scaled_grad = grad * gain
    first_mean = jnp.mean(scaled_grad, axis=-1, keepdims=True)
    second_mean = jnp.mean(scaled_grad * normal, axis=-1, keepdims=True)
    return inverse * (scaled_grad - first_mean - normal * second_mean)


def lane_iota(rows):
    return lax.broadcasted_iota(jnp.int32, (rows, LANES), 1)


def position():
    index = lax.axis_index("seq")
    return index, lax.axis_index("batch"), index // 2, index % 2


def greet(others, count):
    barrier = pltpu.get_barrier_semaphore()
    for other in others:
        pl.semaphore_signal(barrier, inc=1, device_id=other, device_id_type=MESH)
    pl.semaphore_wait(barrier, count)


def exchange_kernel(x_ref, o_ref, local_sem, send_sem, recv_sem):
    index, batch, _, _ = position()
    count = x_ref.shape[0]
    others = [(lax.rem(index + step, count), batch) for step in range(1, count)]
    greet(others, count - 1)
    own = pltpu.make_async_copy(x_ref.at[index], o_ref.at[index], local_sem)
    own.start()
    copies = []
    for step in range(1, count):
        target = lax.rem(index + step, count)
        copy = pltpu.make_async_remote_copy(
            src_ref=x_ref.at[target],
            dst_ref=o_ref.at[index],
            send_sem=send_sem.at[target],
            recv_sem=recv_sem.at[index],
            device_id=(target, batch),
            device_id_type=MESH,
        )
        copy.start()
        copies.append(copy)
    for step in range(1, count):
        source = lax.rem(index + count - step, count)
        pltpu.make_async_remote_copy(
            src_ref=x_ref.at[source],
            dst_ref=o_ref.at[source],
            send_sem=send_sem.at[source],
            recv_sem=recv_sem.at[source],
            device_id=(source, batch),
            device_id_type=MESH,
        ).wait_recv()
    for copy in copies:
        copy.wait_send()
    own.wait()


def exchange(x, collective_id):
    count = x.shape[0]
    return pl.pallas_call(
        exchange_kernel,
        out_shape=jax.ShapeDtypeStruct(x.shape, x.dtype),
        in_specs=[hbm()],
        out_specs=hbm(),
        scratch_shapes=[
            pltpu.SemaphoreType.DMA,
            pltpu.SemaphoreType.DMA((count,)),
            pltpu.SemaphoreType.DMA((count,)),
        ],
        compiler_params=pltpu.CompilerParams(collective_id=collective_id, has_side_effects=True),
    )(x)


def roles():
    index, batch, z, core = position()
    half = index // 4
    near = jnp.where(half == 0, z, 3 - z)
    partner_z = jnp.where(half == 0, 1 - z, 5 - z)
    far_z = 2 - half
    return index, batch, z, core, half, near, partner_z, far_z


def z_of(half, place):
    return jnp.where(half == 0, place, 3 - place)


def greet_roles():
    index, batch, z, core, half, near, partner_z, far_z = roles()
    barrier = pltpu.get_barrier_semaphore()
    pl.semaphore_signal(barrier, inc=1, device_id=(z * 2 + 1 - core, batch), device_id_type=MESH)
    pl.semaphore_signal(barrier, inc=1, device_id=(partner_z * 2 + core, batch), device_id_type=MESH)

    @pl.when(near == 1)
    def _():
        for place in (2, 3):
            other = (z_of(half, place) * 2 + core, batch)
            pl.semaphore_signal(barrier, inc=1, device_id=other, device_id_type=MESH)

    pl.semaphore_wait(barrier, 3)


def gather_kernel(xs_ref, xl_ref, os_ref, ol_ref, own_sem, send_sem, recv_sem, sib_send, sib_recv):
    index, batch, z, core, half, near, partner_z, far_z = roles()
    greet_roles()
    sibling = (z * 2 + 1 - core, batch)
    partner = (partner_z * 2 + core, batch)
    far = (far_z * 2 + core, batch)
    started = []
    for part, (x_ref, o_ref) in enumerate(((xs_ref, os_ref), (xl_ref, ol_ref))):
        rows = x_ref.shape[1]

        def place_of(device, o_ref=o_ref, rows=rows):
            return o_ref.at[pl.ds(device * rows, rows)]

        def send(src, dst, send_s, recv_s, device):
            copy = pltpu.make_async_remote_copy(
                src_ref=src, dst_ref=dst, send_sem=send_s, recv_sem=recv_s,
                device_id=device, device_id_type=MESH,
            )
            copy.start()
            started.append(copy)

        send(x_ref.at[half], place_of(index), send_sem.at[part, 0], recv_sem.at[part, near], partner)
        send(x_ref.at[1 - half], place_of(index), send_sem.at[part, 1], recv_sem.at[part, 3 - near], far)
        send(x_ref.at[half], place_of(index), sib_send.at[part, 0], sib_recv.at[part, near], sibling)
        own = pltpu.make_async_copy(x_ref.at[half], place_of(index), own_sem.at[part])
        own.start()
        started.append(own)
    for part, (x_ref, o_ref) in enumerate(((xs_ref, os_ref), (xl_ref, ol_ref))):
        rows = x_ref.shape[1]
        for slot, place in enumerate((1 - near, 2, 3)):
            device = z_of(half, place) * 2 + core
            block = o_ref.at[pl.ds(device * rows, rows)]

            def wait_for(sem, block=block, device=device):
                pltpu.make_async_remote_copy(
                    src_ref=block, dst_ref=block, send_sem=send_sem.at[part, 0], recv_sem=sem,
                    device_id=(device, batch), device_id_type=MESH,
                ).wait_recv()

            wait_for(recv_sem.at[part, place])
            if slot > 0:
                onward = pltpu.make_async_remote_copy(
                    src_ref=block, dst_ref=block, send_sem=send_sem.at[part, 1 + slot],
                    recv_sem=recv_sem.at[part, place], device_id=partner, device_id_type=MESH,
                )

                @pl.when(near == 1)
                def _(onward=onward):
                    onward.start()
            across = pltpu.make_async_remote_copy(
                src_ref=block, dst_ref=block, send_sem=sib_send.at[part, 1 + slot],
                recv_sem=sib_recv.at[part, place], device_id=sibling, device_id_type=MESH,
            )
            across.start()
            started.append(across)
    for part, (x_ref, o_ref) in enumerate(((xs_ref, os_ref), (xl_ref, ol_ref))):
        rows = x_ref.shape[1]
        for place in range(4):
            device = z_of(half, place) * 2 + 1 - core
            block = o_ref.at[pl.ds(device * rows, rows)]
            pltpu.make_async_remote_copy(
                src_ref=block, dst_ref=block, send_sem=sib_send.at[part, 0],
                recv_sem=sib_recv.at[part, place], device_id=sibling, device_id_type=MESH,
            ).wait_recv()
        own_place = o_ref.at[pl.ds(index * rows, rows)]
        first, second, third, local = started[4 * part : 4 * part + 4]
        first.wait_send()
        second.wait_send()
        third.wait_send()
        local.wait()

        @pl.when(near == 1)
        def _(part=part, own_place=own_place):
            for slot in (1, 2):
                pltpu.make_async_remote_copy(
                    src_ref=own_place, dst_ref=own_place, send_sem=send_sem.at[part, 1 + slot],
                    recv_sem=recv_sem.at[part, 0], device_id=partner, device_id_type=MESH,
                ).wait_send()
    for copy in started[8:]:
        copy.wait_send()


def gather_rows(x_short, x_long, count):
    width = x_short.shape[2]
    return pl.pallas_call(
        gather_kernel,
        out_shape=(
            jax.ShapeDtypeStruct((count * x_short.shape[1], width), x_short.dtype),
            jax.ShapeDtypeStruct((count * x_long.shape[1], width), x_long.dtype),
        ),
        in_specs=[hbm(), hbm()],
        out_specs=(hbm(), hbm()),
        scratch_shapes=[
            pltpu.SemaphoreType.DMA((2,)),
            pltpu.SemaphoreType.DMA((2, 4)),
            pltpu.SemaphoreType.DMA((2, 4)),
            pltpu.SemaphoreType.DMA((2, 4)),
            pltpu.SemaphoreType.DMA((2, 4)),
        ],
        compiler_params=pltpu.CompilerParams(collective_id=0, has_side_effects=True),
    )(x_short, x_long)


def sum_kernel(g_ref, o_ref, sib, total, got, sib_send, sib_recv, send_sem, recv_sem, own_sem):
    index, batch, z, core, half, near, partner_z, far_z = roles()
    greet_roles_sum()
    sibling = (z * 2 + 1 - core, batch)
    partner = (partner_z * 2 + core, batch)
    order = (2, 3, 1, 0)

    def copy_of(src, dst, send_s, recv_s, device):
        return pltpu.make_async_remote_copy(
            src_ref=src, dst_ref=dst, send_sem=send_s, recv_sem=recv_s,
            device_id=device, device_id_type=MESH,
        )

    across = []
    for place in order:
        copy = copy_of(
            g_ref.at[z_of(half, place) * 2 + 1 - core], sib.at[place],
            sib_send.at[place], sib_recv.at[place], sibling,
        )
        copy.start()
        across.append(copy)

    def own_sum(place):
        across[order.index(place)].wait_recv()
        mine = g_ref[z_of(half, place) * 2 + core]
        return mine.astype(F32) + sib[place].astype(F32)

    @pl.when(near == 0)
    def _():
        out = []
        for place in (2, 3, 1):
            total[place] = own_sum(place).astype(BF16)
            copy = copy_of(total.at[place], got.at[place], send_sem.at[place], recv_sem.at[place], partner)
            copy.start()
            out.append(copy)
        mine = own_sum(0)
        copy_of(total.at[0], got.at[0], send_sem.at[0], recv_sem.at[0], partner).wait_recv()
        o_ref[half] = mine + got[0].astype(F32)
        for copy in out:
            copy.wait_send()

    @pl.when(near == 1)
    def _():
        total[0] = own_sum(0).astype(BF16)
        first = copy_of(total.at[0], got.at[0], send_sem.at[0], recv_sem.at[0], partner)
        first.start()
        out = [first]
        for place in (2, 3):
            mine = own_sum(place)
            copy_of(total.at[place], got.at[place], send_sem.at[place], recv_sem.at[place], partner).wait_recv()
            total[place] = (mine + got[place].astype(F32)).astype(BF16)
            copy = copy_of(
                total.at[place], got.at[4], send_sem.at[place], recv_sem.at[4],
                (z_of(half, place) * 2 + core, batch),
            )
            copy.start()
            out.append(copy)
        mine = own_sum(1)
        copy_of(total.at[1], got.at[1], send_sem.at[1], recv_sem.at[1], partner).wait_recv()
        o_ref[half] = mine + got[1].astype(F32)
        for copy in out:
            copy.wait_send()

    copy_of(total.at[0], got.at[4], send_sem.at[0], recv_sem.at[4], (far_z * 2 + core, batch)).wait_recv()
    o_ref[1 - half] = got[4].astype(F32)
    for copy in across:
        copy.wait_send()


def greet_roles_sum():
    index, batch, z, core, half, near, partner_z, far_z = roles()
    barrier = pltpu.get_barrier_semaphore()
    pl.semaphore_signal(barrier, inc=1, device_id=(z * 2 + 1 - core, batch), device_id_type=MESH)
    pl.semaphore_signal(barrier, inc=1, device_id=(partner_z * 2 + core, batch), device_id_type=MESH)
    pl.semaphore_signal(barrier, inc=1, device_id=(far_z * 2 + core, batch), device_id_type=MESH)

    @pl.when(near == 0)
    def _():
        pl.semaphore_wait(barrier, 2)

    @pl.when(near == 1)
    def _():
        pl.semaphore_wait(barrier, 4)


def sum_rows(grads):
    count, rows, width = grads.shape
    return pl.pallas_call(
        sum_kernel,
        out_shape=jax.ShapeDtypeStruct((2, rows, width), F32),
        in_specs=[vmem()],
        out_specs=vmem(),
        scratch_shapes=[
            pltpu.VMEM((4, rows, width), BF16),
            pltpu.VMEM((4, rows, width), BF16),
            pltpu.VMEM((5, rows, width), BF16),
            pltpu.SemaphoreType.DMA((4,)),
            pltpu.SemaphoreType.DMA((4,)),
            pltpu.SemaphoreType.DMA((4,)),
            pltpu.SemaphoreType.DMA((5,)),
            pltpu.SemaphoreType.DMA,
        ],
        compiler_params=params_of(collective_id=3, has_side_effects=True),
    )(grads)


def shifted(window, by):
    return pltpu.roll(window, by % window.shape[0], 0)


def front_kernel(
    lens_ref, xs_ref, xl_ref, wq_ref, ck_ref, np_ref,
    osend, qa, ka, vb, kt, proj, normed, lse,
    vt, ot,
):
    short_rows, long_rows = xs_ref.shape[0], xl_ref.shape[0]
    width = xs_ref.shape[1]
    parts = ((xs_ref, 0, PAD, short_rows), (xl_ref, short_rows, 2 * PAD + short_rows, long_rows))
    gain, offset = np_ref[0:1], np_ref[1:2]
    zeros = jnp.zeros((PAD, proj.shape[1]), BF16)
    proj[0:PAD] = zeros
    proj[PAD + short_rows : 2 * PAD + short_rows] = zeros
    lanes = lane_iota(TILE)
    low_half = lanes < HEAD_DIM
    for part, (x_ref, base, pbase, total) in enumerate(parts):
        length = lens_ref[part]

        @pl.loop(0, total // TILE)
        def _(step, x_ref=x_ref, base=base, pbase=pbase):
            start = pl.multiple_of(step * TILE, TILE)
            values = x_ref[pl.ds(start, TILE)].astype(F32)
            normal, _ = normalise(values)
            low = (normal * gain + offset).astype(BF16)
            normed[pl.ds(pl.multiple_of(base + start, TILE), TILE)] = low
            proj[pl.ds(pl.multiple_of(pbase + start, PAD), TILE)] = dot_nn(low, wq_ref[...]).astype(BF16)

        @pl.loop(0, total // TILE)
        def _(step, base=base, pbase=pbase, length=length):
            start = pl.multiple_of(step * TILE, TILE)
            window = proj[pl.ds(pl.multiple_of(pbase - PAD + start, PAD), TILE + PAD)].astype(F32)
            mixed = (
                ck_ref[0:1] * window[PAD:]
                + ck_ref[1:2] * shifted(window, 1)[PAD:]
                + ck_ref[2:3] * shifted(window, 2)[PAD:]
            ).astype(BF16).astype(F32)
            rows = pl.ds(pl.multiple_of(base + start, TILE), TILE)
            q_pair, q_one = mixed[:, 0:128] * 0.125, mixed[:, 128:256] * 0.125
            k_pair, k_one = mixed[:, 256:384], mixed[:, 384:512]
            v_pair, v_one = mixed[:, 512:640], mixed[:, 640:768]
            places = start + lax.broadcasted_iota(jnp.int32, (TILE, LANES), 0)
            bias = jnp.where(places < length, 0.0, NEG_FILL)
            at_zero = lanes == 0
            at_half = lanes == HEAD_DIM
            one_half = jnp.where(at_half, 1.0, 0.0)
            one_zero = jnp.where(at_zero, 1.0, 0.0)
            bias_half = jnp.where(at_half, bias, 0.0)
            bias_zero = jnp.where(at_zero, bias, 0.0)
            qa[0, rows] = jnp.where(low_half, q_pair, one_half).astype(BF16)
            qa[1, rows] = jnp.where(low_half, one_zero, q_pair).astype(BF16)
            qa[2, rows] = jnp.where(low_half, q_one, one_half).astype(BF16)
            ka[0, rows] = jnp.where(low_half, k_pair, bias_half).astype(BF16)
            ka[1, rows] = jnp.where(low_half, bias_zero, k_pair).astype(BF16)
            ka[2, rows] = jnp.where(low_half, k_one, bias_half).astype(BF16)
            vb[0, rows] = v_pair.astype(BF16)
            vb[1, rows] = v_one.astype(BF16)
            k_turned, k_turned_one = k_pair.T.astype(BF16), k_one.T.astype(BF16)
            v_turned, v_turned_one = v_pair.T.astype(BF16), v_one.T.astype(BF16)
            kt[0, :, rows] = k_turned[:HEAD_DIM]
            kt[1, :, rows] = k_turned[HEAD_DIM:]
            kt[2, :, rows] = k_turned_one[:HEAD_DIM]
            vt[0, :, rows] = v_turned[:HEAD_DIM]
            vt[1, :, rows] = v_turned[HEAD_DIM:]
            vt[2, :, rows] = v_turned_one[:HEAD_DIM]

    causal = lax.broadcasted_iota(jnp.int32, (TILE, TILE), 0) <= lax.broadcasted_iota(jnp.int32, (TILE, TILE), 1)

    @pl.loop(0, 3)
    def _(head):
        for _, base, _, total in parts:
            for block in range(total // TILE):
                rows = slice(base + block * TILE, base + (block + 1) * TILE)
                past = block * TILE
                query = qa[head, rows]
                diagonal = jnp.where(causal, dot_nt(ka[head, rows], query), NEG_FILL)
                top = jnp.max(diagonal, axis=0, keepdims=True)
                if past:
                    before = dot_nt(ka[head, base : base + past], query)
                    top = jnp.maximum(top, jnp.max(before, axis=0, keepdims=True))
                    exp_before = jnp.exp(before - top)
                exp_diagonal = jnp.exp(diagonal - top)
                norm = jnp.sum(exp_diagonal, axis=0, keepdims=True)
                if past:
                    norm = norm + jnp.sum(exp_before, axis=0, keepdims=True)
                lse[head, :, rows] = top + jnp.log(norm)
                inverse = 1.0 / norm
                result = dot_nn(vt[head, :, rows], (exp_diagonal * inverse).astype(BF16))
                if past:
                    result = result + dot_nn(
                        vt[head, :, base : base + past], (exp_before * inverse).astype(BF16)
                    )
                ot[head, :, rows] = result

    own_short, own_long = TILE // 2, TILE
    for _, base, _, total in parts:
        for block in range(total // TILE):
            rows = slice(base + block * TILE, base + (block + 1) * TILE)
            pair = jnp.concatenate([ot[0, :, rows], ot[1, :, rows]], axis=0).T.astype(BF16)
            single = ot[2, :, rows]
            if base:
                osend[block, own_short : own_short + own_long] = pair
                packed = jnp.concatenate([single[:, :LANES], single[:, LANES:]], axis=0).T
                osend[block, own_short + own_long + own_short // 2 :] = packed.astype(BF16)
            else:
                turned = jnp.concatenate([single, single], axis=0).T
                half = own_short // 2
                for side in range(2):
                    start = side * own_short
                    osend[2 * block + side, 0:own_short] = pair[start : start + own_short]
                    packed = jnp.where(
                        lane_iota(half) < HEAD_DIM,
                        turned[start : start + half],
                        turned[start + half : start + own_short],
                    )
                    osend[2 * block + side, own_short + own_long : own_short + own_long + half] = packed.astype(BF16)


def front(lens, xs, xl, wq, ck, norms, count):
    short_rows, long_rows = xs.shape[0], xl.shape[0]
    total = short_rows + long_rows
    owned = total // count
    out = jax.ShapeDtypeStruct
    return pl.pallas_call(
        front_kernel,
        out_shape=(
            out((count, owned * 3 // 2, LANES), BF16),
            out((3, total, LANES), BF16),
            out((3, total, LANES), BF16),
            out((2, total, LANES), BF16),
            out((3, HEAD_DIM, total), BF16),
            out((total + 2 * PAD, 6 * LANES), BF16),
            out((total, xs.shape[1]), BF16),
            out((3, 1, total), F32),
        ),
        in_specs=[smem()] + [vmem()] * 5,
        out_specs=tuple([vmem()] * 8),
        scratch_shapes=[pltpu.VMEM((3, HEAD_DIM, total), BF16), pltpu.VMEM((3, HEAD_DIM, total), F32)],
        compiler_params=params_of(),
    )(lens, xs, xl, wq, ck, norms)


def middle_kernel(
    xs_ref, xl_ref, recv, cs_ref, cl_ref, wo_ref, wu_ref, wd_ref, np_ref,
    ys_ref, yl_ref, gmid, gsend, gwo, gwu, gwd, gnorm,
    att, middle, normal_two, inverse_two, second, second_t, cot, y_acc, gsec, gml,
):
    short, long = xs_ref.shape[1], xl_ref.shape[1]
    owned = short + long
    rows_all = 2 * owned
    half = short // 2
    lanes = lane_iota(owned // 2)
    low_half = lanes < HEAD_DIM
    for seq in range(2):
        first = seq * owned
        cot[first : first + short] = cs_ref[seq]
        cot[first + short : first + owned] = cl_ref[seq]
        for chip in range(2):
            packs = []
            for core in range(2):
                source = recv.at[seq * 4 + chip * 2 + core]
                block = 3 * chip + core
                att[first : first + owned, block * LANES : (block + 1) * LANES] = source[0:owned]
                packs.append(source[owned:].astype(F32))
            swapped = [pltpu.roll(pack, HEAD_DIM, 1) for pack in packs]
            early = jnp.where(low_half, packs[0], swapped[1]).astype(BF16)
            late = jnp.where(low_half, swapped[0], packs[1]).astype(BF16)
            columns = slice((3 * chip + 2) * LANES, (3 * chip + 3) * LANES)
            att[first : first + half, columns] = early[:half]
            att[first + half : first + short, columns] = late[:half]
            att[first + short : first + short + long // 2, columns] = early[half:]
            att[first + short + long // 2 : first + owned, columns] = late[half:]
        middle[first : first + short] = xs_ref[seq].astype(F32)
        middle[first + short : first + owned] = xl_ref[seq].astype(F32)

    @pl.loop(0, rows_all // TILE)
    def _(step):
        rows = pl.ds(pl.multiple_of(step * TILE, TILE), TILE)
        values = middle[rows] + dot_nn(att[rows], wo_ref[...])
        middle[rows] = values
        normal, inverse = normalise(values)
        normal_two[rows] = normal
        inverse_two[rows] = inverse
        second[rows] = (normal * np_ref[2:3] + np_ref[3:4]).astype(BF16)
        y_acc[rows] = values
        gsec[rows] = jnp.zeros_like(values)

    second_t[...] = second[...].T
    inner = 512

    @pl.loop(0, wu_ref.shape[1] // inner)
    def _(step):
        columns = pl.ds(pl.multiple_of(step * inner, inner), inner)
        upper = jnp.maximum(dot_nn(second[...], wu_ref[:, columns]), 0.0)
        hidden = (upper * upper).astype(BF16)
        grad_hidden = dot_nt(cot[...], wd_ref[columns])
        grad_upper = (2.0 * upper * grad_hidden).astype(BF16)
        y_acc[...] += dot_nn(hidden, wd_ref[columns])
        gwd[columns] = dot_tn(hidden, cot[...]).astype(BF16)
        gwu[:, columns] = dot_nn(second_t[...], grad_upper).astype(BF16)
        gsec[...] += dot_nt(grad_upper, wu_ref[:, columns])

    gnorm[...] = jnp.zeros_like(gnorm)

    @pl.loop(0, rows_all // TILE)
    def _(step):
        rows = pl.ds(pl.multiple_of(step * TILE, TILE), TILE)
        grad = gsec[rows]
        normal = normal_two[rows]
        gnorm[0:1] += jnp.sum(grad * normal, axis=0, keepdims=True)
        gnorm[1:2] += jnp.sum(grad, axis=0, keepdims=True)
        total = cot[rows].astype(F32) + norm_back(grad, normal, inverse_two[rows], np_ref[2:3])
        gmid[rows] = total
        gml[rows] = total.astype(BF16)
        second[rows] = dot_nt(gml[rows], wo_ref[...]).astype(BF16)

    gwo[...] = dot_tn(att[...], gml[...]).astype(BF16)
    for seq in range(2):
        first = seq * owned
        ys_ref[seq] = y_acc[first : first + short].astype(BF16)
        yl_ref[seq] = y_acc[first + short : first + owned].astype(BF16)
        for chip in range(2):
            columns = slice((3 * chip + 2) * LANES, (3 * chip + 3) * LANES)
            one = second[first : first + owned, columns].astype(F32)
            early = jnp.concatenate([one[:half], one[short : short + long // 2]], axis=0)
            late = jnp.concatenate([one[half:short], one[short + long // 2 :]], axis=0)
            for core in range(2):
                target = seq * 4 + chip * 2 + core
                block = 3 * chip + core
                gsend[target, 0:owned] = second[first : first + owned, block * LANES : (block + 1) * LANES]
                if core == 0:
                    packed = jnp.where(low_half, early, pltpu.roll(late, HEAD_DIM, 1))
                else:
                    packed = jnp.where(low_half, pltpu.roll(early, HEAD_DIM, 1), late)
                gsend[target, owned:] = packed.astype(BF16)


def middle_part(x_short, x_long, recv, cot_short, cot_long, w_out, w_up, w_down, norms):
    width = x_short.shape[2]
    rows = 2 * (x_short.shape[1] + x_long.shape[1])
    out = jax.ShapeDtypeStruct
    return pl.pallas_call(
        middle_kernel,
        out_shape=(
            out(x_short.shape, BF16),
            out(x_long.shape, BF16),
            out((rows, width), F32),
            out(recv.shape, BF16),
            out(w_out.shape, BF16),
            out(w_up.shape, BF16),
            out(w_down.shape, BF16),
            out((8, width), F32),
        ),
        in_specs=[vmem()] * 9,
        out_specs=tuple([vmem()] * 8),
        scratch_shapes=[
            pltpu.VMEM((rows, width), BF16),
            pltpu.VMEM((rows, width), F32),
            pltpu.VMEM((rows, width), F32),
            pltpu.VMEM((rows, 1), F32),
            pltpu.VMEM((rows, width), BF16),
            pltpu.VMEM((width, rows), BF16),
            pltpu.VMEM((rows, width), BF16),
            pltpu.VMEM((rows, width), F32),
            pltpu.VMEM((rows, width), F32),
            pltpu.VMEM((rows, width), BF16),
        ],
        compiler_params=params_of(),
    )(x_short, x_long, recv, cot_short, cot_long, w_out, w_up, w_down, norms)


def back_kernel(
    xs_ref, xl_ref, normed, proj, qa, ka, vb, kt, lse, osend, grecv, wq_ref, ck_ref, np_ref,
    gn_ref, gwq, gck, gnp,
    do, delta, dqt, gm, gproj,
):
    short_rows, long_rows = xs_ref.shape[0], xl_ref.shape[0]
    parts = (
        (xs_ref, 0, PAD, 0, short_rows),
        (xl_ref, short_rows, 2 * PAD + short_rows, PAD + short_rows, long_rows),
    )
    own_short, own_long = TILE // 2, TILE
    owned = own_short + own_long
    quarter = own_short // 2
    gm[...] = jnp.zeros_like(gm)
    gck[...] = jnp.zeros_like(gck)
    gnp[...] = jnp.zeros_like(gnp)
    pick = jnp.where(
        (lax.broadcasted_iota(jnp.int32, (8, LANES), 1) < HEAD_DIM)
        == (lax.broadcasted_iota(jnp.int32, (8, LANES), 0) == 0),
        1.0,
        0.0,
    ).astype(F32)

    def row_sums(product):
        return lax.dot_general(
            pick, product, (((1,), (1,)), ((), ())),
            preferred_element_type=F32, precision=lax.Precision.HIGHEST,
        )

    def unpack(packed):
        wide = packed.astype(F32)
        return jnp.concatenate([wide, pltpu.roll(wide, HEAD_DIM, 1)], axis=0)

    for part, (_, base, _, _, total) in enumerate(parts):
        for block in range(total // TILE):
            rows = slice(base + block * TILE, base + (block + 1) * TILE)
            if part == 0:
                grad_pair = jnp.concatenate([grecv[2 * block, 0:own_short], grecv[2 * block + 1, 0:own_short]], axis=0)
                out_pair = jnp.concatenate([osend[2 * block, 0:own_short], osend[2 * block + 1, 0:own_short]], axis=0)
                grad_one = jnp.concatenate(
                    [unpack(grecv[2 * block + side, owned : owned + quarter]) for side in range(2)], axis=0
                )
                out_one = jnp.concatenate(
                    [unpack(osend[2 * block + side, owned : owned + quarter]) for side in range(2)], axis=0
                )
            else:
                grad_pair = grecv[block, own_short:owned]
                out_pair = osend[block, own_short:owned]
                grad_one = unpack(grecv[block, owned + quarter :])
                out_one = unpack(osend[block, owned + quarter :])
            low_half = lane_iota(TILE) < HEAD_DIM
            grad_pair = grad_pair.astype(F32)
            grad_one = jnp.where(low_half, grad_one, 0.0)
            do[0, rows] = jnp.where(low_half, grad_pair, 0.0).astype(BF16)
            do[1, rows] = jnp.where(low_half, 0.0, grad_pair).astype(BF16)
            do[2, rows] = grad_one.astype(BF16)
            sums = row_sums(grad_pair * out_pair.astype(F32))
            delta[0, :, rows] = sums[0:1]
            delta[1, :, rows] = sums[1:2]
            delta[2, :, rows] = row_sums(grad_one * out_one)[0:1]

    causal = lax.broadcasted_iota(jnp.int32, (TILE, TILE), 0) <= lax.broadcasted_iota(jnp.int32, (TILE, TILE), 1)

    @pl.loop(0, 3)
    def _(head):
        pair = head // 2
        own_lanes = (lane_iota(TILE) < HEAD_DIM) == (head != 1)
        k_lanes = pl.ds(pl.multiple_of((2 + pair) * LANES, LANES), LANES)
        v_lanes = pl.ds(pl.multiple_of((4 + pair) * LANES, LANES), LANES)
        for _, base, _, gbase, total in parts:
            for block in range(total // TILE):
                rows = slice(base + block * TILE, base + (block + 1) * TILE)
                query = qa[head, rows]
                bare = jnp.where(own_lanes, query.astype(F32), 0.0).astype(BF16)
                grad_out = do[head, rows]
                stat, less = lse[head, :, rows], delta[head, :, rows]
                spans = [(block * TILE, TILE, True)]
                if block:
                    spans.append((0, block * TILE, False))
                grad_q = jnp.zeros((HEAD_DIM, TILE), F32)
                for start, size, masked in spans:
                    keys = slice(base + start, base + start + size)
                    into = slice(gbase + start, gbase + start + size)
                    scores = dot_nt(ka[head, keys], query)
                    if masked:
                        scores = jnp.where(causal, scores, NEG_FILL)
                    probs = jnp.exp(scores - stat)
                    grad_probs = dot_nt(vb[pair, keys], grad_out)
                    gm[into, v_lanes] += dot_nn(probs.astype(BF16), grad_out)
                    grad_scores = (probs * (grad_probs - less)).astype(BF16)
                    gm[into, k_lanes] += dot_nn(grad_scores, bare)
                    grad_q = grad_q + dot_nn(kt[head, :, keys], grad_scores)
                dqt[head, :, rows] = 0.125 * grad_q

    for _, base, _, gbase, total in parts:

        @pl.loop(0, total // TILE)
        def _(step, base=base, gbase=gbase):
            start = pl.multiple_of(step * TILE, TILE)
            rows = pl.ds(pl.multiple_of(base + start, TILE), TILE)
            into = pl.ds(pl.multiple_of(gbase + start, PAD), TILE)
            gm[into, 0:128] = jnp.concatenate([dqt[0, :, rows], dqt[1, :, rows]], axis=0).T
            one = dqt[2, :, rows]
            gm[into, 128:256] = jnp.concatenate([one, jnp.zeros_like(one)], axis=0).T

    for part, (x_ref, base, pbase, gbase, total) in enumerate(parts):

        @pl.loop(0, total // TILE)
        def _(step, part=part, x_ref=x_ref, base=base, pbase=pbase, gbase=gbase):
            start = pl.multiple_of(step * TILE, TILE)
            rows = pl.ds(pl.multiple_of(base + start, TILE), TILE)
            window = gm[pl.ds(pl.multiple_of(gbase + start, PAD), TILE + PAD)]
            grad = window[:TILE]
            projected_grad = (
                ck_ref[0:1] * grad
                + ck_ref[1:2] * shifted(window, -1)[:TILE]
                + ck_ref[2:3] * shifted(window, -2)[:TILE]
            ).astype(BF16)
            gproj[rows] = projected_grad
            past = proj[pl.ds(pl.multiple_of(pbase - PAD + start, PAD), TILE + PAD)].astype(F32)
            gck[0:1] += jnp.sum(grad * past[PAD:], axis=0, keepdims=True)
            gck[1:2] += jnp.sum(grad * shifted(past, 1)[PAD:], axis=0, keepdims=True)
            gck[2:3] += jnp.sum(grad * shifted(past, 2)[PAD:], axis=0, keepdims=True)
            grad_normed = dot_nt(projected_grad, wq_ref[...])
            normal, _ = normalise(x_ref[pl.ds(start, TILE)].astype(F32))
            gnp[0:1] += jnp.sum(grad_normed * normal, axis=0, keepdims=True)
            gnp[1:2] += jnp.sum(grad_normed, axis=0, keepdims=True)
            low = grad_normed.astype(BF16)
            if part == 0:
                gn_ref[2 * step, 0:own_short] = low[:own_short]
                gn_ref[2 * step + 1, 0:own_short] = low[own_short:]
            else:
                gn_ref[step, own_short:] = low

    for start in range(0, normed.shape[1], TILE):
        gwq[start : start + TILE] = dot_tn(normed[:, start : start + TILE], gproj[...]).astype(BF16)


def back_part(xs, xl, normed, proj, qa, ka, vb, kt, lse, osend, grecv, wq, ck, norms, count):
    total = xs.shape[0] + xl.shape[0]
    width = xs.shape[1]
    out = jax.ShapeDtypeStruct
    return pl.pallas_call(
        back_kernel,
        out_shape=(
            out((count, total // count, width), BF16),
            out(wq.shape, BF16),
            out((8, wq.shape[1]), F32),
            out((8, width), F32),
        ),
        in_specs=[vmem()] * 14,
        out_specs=tuple([vmem()] * 4),
        scratch_shapes=[
            pltpu.VMEM((3, total, LANES), BF16),
            pltpu.VMEM((3, 1, total), F32),
            pltpu.VMEM((3, HEAD_DIM, total), F32),
            pltpu.VMEM((total + 2 * PAD, 6 * LANES), F32),
            pltpu.VMEM((total, 6 * LANES), BF16),
        ],
        compiler_params=params_of(),
    )(xs, xl, normed, proj, qa, ka, vb, kt, lse, osend, grecv, wq, ck, norms)


def take_columns(full, chip, core):
    rows = full.shape[0]
    blocks = full.reshape(rows, 3, 6, LANES)
    pair = lax.dynamic_index_in_dim(blocks, 3 * chip + core, 2, keepdims=False)
    shared = lax.dynamic_index_in_dim(blocks, 3 * chip + 2, 2, keepdims=False)
    one = lax.dynamic_index_in_dim(shared.reshape(rows, 3, 2, HEAD_DIM), core, 2, keepdims=False)
    one = jnp.concatenate([one, jnp.zeros_like(one)], axis=-1)
    return jnp.stack([pair, one], axis=2).reshape(rows, 6 * LANES)


def put_columns(group, chip, core):
    rows = group.shape[0]
    blocks = group.reshape(rows, 3, 2, LANES)
    at = (lax.broadcasted_iota(jnp.int32, (1, 1, 6, 1), 2) == 3 * chip + core)
    pairs = jnp.where(at, blocks[:, :, 0:1], 0)
    one = blocks[:, :, 1:2, :HEAD_DIM]
    zero = jnp.zeros_like(one)
    shared = jnp.where(
        core == 0, jnp.concatenate([one, zero], axis=-1), jnp.concatenate([zero, one], axis=-1)
    )
    at_one = (lax.broadcasted_iota(jnp.int32, (1, 1, 6, 1), 2) == 3 * chip + 2)
    return (pairs + jnp.where(at_one, shared, 0)).reshape(rows, 18 * LANES).astype(group.dtype)


def split_body(
    x_short, x_long, lengths, cot_short, cot_long, w_qkv, w_out, w_up, w_down, conv_kernel, norm_params
):
    both = ("seq", "batch")
    count = lax.axis_size("seq")
    index = lax.axis_index("seq")
    half, chip, core = index // 4, (index // 2) % 2, index % 2
    full_qkv = lax.all_gather(w_qkv, both, axis=0, tiled=True)
    kernel = lax.all_gather(conv_kernel, both, axis=1, tiled=True).astype(F32)
    norms = lax.all_gather(norm_params, both, axis=1, tiled=True).astype(F32)
    full_out = lax.all_gather(w_out, both, axis=0, tiled=True)
    full_up = lax.all_gather(w_up, both, axis=0, tiled=True)
    full_down = lax.all_gather(w_down, both, axis=0, tiled=True)
    xs, xl = gather_rows(x_short, x_long, count)
    wq = take_columns(full_qkv, chip, core)
    ck = take_columns(kernel, chip, core)
    lens = lax.dynamic_index_in_dim(lengths, half, 1, keepdims=False)
    osend, qa, ka, vb, kt, proj, normed, lse = front(lens, xs, xl, wq, ck, norms, count)
    recv = exchange(osend, 1)
    y_short, y_long, gmid, gsend, gwo, gwu, gwd, gnorm = middle_part(
        x_short, x_long, recv, cot_short, cot_long, full_out, full_up, full_down, norms
    )
    grecv = exchange(gsend, 2)
    gn, gwq, gck, gnp = back_part(
        xs, xl, normed, proj, qa, ka, vb, kt, lse, osend, grecv, wq, ck, norms, count
    )
    grad_normed = sum_rows(gn)
    short = x_short.shape[1]
    gmid = gmid.reshape(2, -1, gmid.shape[1])
    dx = []
    for x, rows in ((x_short, slice(0, short)), (x_long, slice(short, None))):
        normal, inverse = normalise(x.astype(F32))
        dx.append(gmid[:, rows] + norm_back(grad_normed[:, rows], normal, inverse, norms[0]))
    scatter = lambda value, axis: lax.psum_scatter(value, both, scatter_dimension=axis, tiled=True)
    grad_norm = jnp.concatenate([gnp[0:2], gnorm[0:2]], axis=0)
    return (
        y_short, y_long, dx[0], dx[1],
        scatter(put_columns(gwq, chip, core), 0).astype(F32),
        scatter(gwo, 0).astype(F32),
        scatter(gwu, 0).astype(F32),
        scatter(gwd, 0).astype(F32),
        scatter(put_columns(gck[0:3], chip, core), 1),
        scatter(grad_norm, 1),
    )


GROUP_HEADS = 2


def from_behind(value, axis, by):
    count = lax.axis_size(axis)
    pairs = [(i, i + by) for i in range(count) if 0 <= i + by < count]
    return lax.ppermute(value, axis, pairs)


def layer_norm(values, gain, offset_term):
    average = jnp.mean(values, axis=-1, keepdims=True)
    centred = values - average
    inverse = lax.rsqrt(jnp.mean(centred * centred, axis=-1, keepdims=True) + EPS)
    normal = centred * inverse
    return (normal * gain + offset_term, normal, inverse)


def norm_back_flat(grad, normal, inverse, gain):
    scaled_grad = grad * gain
    first_mean = jnp.mean(scaled_grad, axis=-1, keepdims=True)
    second_mean = jnp.mean(scaled_grad * normal, axis=-1, keepdims=True)
    return inverse * (scaled_grad - first_mean - normal * second_mean)


def front_part(inputs, full_weights):
    w_qkv = full_weights[0]
    kernel = full_weights[4].astype(jnp.float32)
    params = full_weights[5].astype(jnp.float32)
    saved = []
    tails = []
    for part_in in inputs:
        seq_count, block_rows, model_width = part_in.shape
        flat = part_in.reshape(seq_count * block_rows, model_width).astype(jnp.float32)
        normed, normal, inverse = layer_norm(flat, params[0], params[1])
        normed_low = normed.astype(jnp.bfloat16)
        projected = jnp.dot(normed_low, w_qkv, preferred_element_type=jnp.float32).astype(
            jnp.bfloat16
        )
        projected = projected.reshape(seq_count, block_rows, 3 * model_width)
        saved.append((flat, normal, inverse, normed_low, projected))
        tails.append(projected[:, block_rows - 2 :])
    received = from_behind((tails[0], tails[1]), "seq", 1)
    fronts = []
    for index_part in range(2):
        flat, normal, inverse, normed_low, projected = saved[index_part]
        block_rows = projected.shape[1]
        padded = jnp.concatenate([received[index_part], projected], axis=1).astype(jnp.float32)
        mixed = (
            kernel[0] * padded[:, 2:]
            + kernel[1] * padded[:, 1 : block_rows + 1]
            + kernel[2] * padded[:, :block_rows]
        )
        fronts.append((flat, normal, inverse, normed_low, padded, mixed.astype(jnp.bfloat16)))
    return fronts


def attend_block(queries, key_rows, value_rows, usable, grad_heads):
    scaling = queries.shape[-1] ** (-0.5)
    scores = jnp.einsum("sqhd,skhd->shqk", queries, key_rows, preferred_element_type=jnp.float32)
    masked = jnp.where(usable, scaling * scores, NEG_FILL)
    exp_terms = jnp.exp(masked - jnp.max(masked, axis=-1, keepdims=True))
    attn_probs = exp_terms / jnp.sum(exp_terms, axis=-1, keepdims=True)
    probs_low = attn_probs.astype(jnp.bfloat16)
    if grad_heads is None:
        attended = jnp.einsum(
            "shqk,skhd->sqhd", probs_low, value_rows, preferred_element_type=jnp.float32
        )
        return attended.astype(jnp.bfloat16)
    grad_probs = jnp.einsum(
        "sqhd,skhd->shqk", grad_heads, value_rows, preferred_element_type=jnp.float32
    )
    grad_values = jnp.einsum(
        "shqk,sqhd->skhd", probs_low, grad_heads, preferred_element_type=jnp.float32
    )
    row_delta = jnp.sum(attn_probs * grad_probs, axis=-1, keepdims=True)
    grad_scores = (scaling * attn_probs * (grad_probs - row_delta)).astype(jnp.bfloat16)
    grad_queries = jnp.einsum(
        "shqk,skhd->sqhd", grad_scores, key_rows, preferred_element_type=jnp.float32
    )
    grad_keys = jnp.einsum(
        "shqk,sqhd->skhd", grad_scores, queries, preferred_element_type=jnp.float32
    )
    return (grad_queries, grad_keys, grad_values)


def make_usable(query_pos, key_pos, seq_lengths):
    usable = (key_pos[None, None, :] <= query_pos[None, :, None]) & (
        key_pos[None, None, :] < seq_lengths[:, None, None]
    )
    return usable[:, None]


def attention(mixed, kv_full, seq_lengths, offset, grad_attended):
    seq_count, block_rows, three_width = mixed.shape
    model_width = three_width // 3
    full_len = kv_full.shape[1]
    queries = mixed[:, :, :model_width].reshape(seq_count, block_rows, -1, HEAD_DIM)
    key_rows = kv_full[:, :, :model_width].reshape(seq_count, full_len, -1, HEAD_DIM)
    value_rows = kv_full[:, :, model_width:].reshape(seq_count, full_len, -1, HEAD_DIM)
    positions = offset + jnp.arange(block_rows, dtype=jnp.int32)
    key_pos = jnp.arange(full_len, dtype=jnp.int32)
    usable = make_usable(positions, key_pos, seq_lengths)
    heads_total = queries.shape[2]
    grad_heads = None
    if grad_attended is not None:
        grad_heads = grad_attended.reshape(seq_count, block_rows, -1, HEAD_DIM)
    results = []
    for first_head in range(0, heads_total, GROUP_HEADS):
        last_head = first_head + GROUP_HEADS
        grad_part = None if grad_heads is None else grad_heads[:, :, first_head:last_head]
        results.append(
            attend_block(
                queries[:, :, first_head:last_head],
                key_rows[:, :, first_head:last_head],
                value_rows[:, :, first_head:last_head],
                usable,
                grad_part,
            )
        )
    if grad_heads is None:
        return jnp.concatenate(results, axis=2).reshape(seq_count, block_rows, model_width)
    grad_queries = jnp.concatenate([entry_set[0] for entry_set in results], axis=2).reshape(
        seq_count, block_rows, model_width
    )
    grad_keys = jnp.concatenate([entry_set[1] for entry_set in results], axis=2).reshape(
        seq_count, full_len, model_width
    )
    grad_values = jnp.concatenate([entry_set[2] for entry_set in results], axis=2).reshape(
        seq_count, full_len, model_width
    )
    return (grad_queries, grad_keys, grad_values)


def rest_part(front, kv_full, seq_lengths, offset, full_weights, cotangent_in):
    w_out, w_up, w_down = (full_weights[1], full_weights[2], full_weights[3])
    params = full_weights[5].astype(jnp.float32)
    flat, normal_one, inverse_one, normed_low, padded, mixed = front
    seq_count, block_rows, three_width = mixed.shape
    model_width = three_width // 3
    attended = attention(mixed, kv_full, seq_lengths, offset, None).reshape(
        seq_count * block_rows, model_width
    )
    middle = flat + jnp.dot(attended, w_out, preferred_element_type=jnp.float32)
    second, normal_two, inverse_two = layer_norm(middle, params[2], params[3])
    second_low = second.astype(jnp.bfloat16)
    upper = jnp.dot(second_low, w_up, preferred_element_type=jnp.float32)
    hidden = jnp.square(jnp.maximum(upper, 0.0)).astype(jnp.bfloat16)
    if cotangent_in is None:
        result_rows = middle + jnp.dot(hidden, w_down, preferred_element_type=jnp.float32)
        return result_rows.astype(jnp.bfloat16).reshape(seq_count, block_rows, model_width)
    cotangent = cotangent_in.reshape(seq_count * block_rows, model_width)
    grad_down = jnp.dot(hidden.T, cotangent, preferred_element_type=jnp.float32)
    grad_hidden = jnp.dot(cotangent, w_down.T, preferred_element_type=jnp.float32)
    grad_upper = (2.0 * jnp.maximum(upper, 0.0) * grad_hidden).astype(jnp.bfloat16)
    grad_up = jnp.dot(second_low.T, grad_upper, preferred_element_type=jnp.float32)
    grad_second = jnp.dot(grad_upper, w_up.T, preferred_element_type=jnp.float32)
    grad_middle = cotangent.astype(jnp.float32) + norm_back_flat(
        grad_second, normal_two, inverse_two, params[2]
    )
    grad_middle_low = grad_middle.astype(jnp.bfloat16)
    grad_out = jnp.dot(attended.T, grad_middle_low, preferred_element_type=jnp.float32)
    grad_attended = jnp.dot(grad_middle_low, w_out.T, preferred_element_type=jnp.float32).astype(
        jnp.bfloat16
    )
    grad_attended = grad_attended.reshape(seq_count, block_rows, model_width)
    grad_queries, grad_keys, grad_values = attention(
        mixed, kv_full, seq_lengths, offset, grad_attended
    )
    key_term = jnp.concatenate([grad_keys, grad_values], axis=-1)
    norm_two = (jnp.sum(grad_second * normal_two, axis=0), jnp.sum(grad_second, axis=0))
    return (grad_queries, key_term, grad_middle, grad_out, grad_up, grad_down, norm_two)


def general_body(
    x_short,
    x_long,
    lengths,
    cot_short,
    cot_long,
    w_qkv,
    w_out,
    w_up,
    w_down,
    conv_kernel,
    norm_params,
):
    full_weights = (
        lax.all_gather(w_qkv, ("seq", "batch"), axis=0, tiled=True),
        lax.all_gather(w_out, ("seq", "batch"), axis=0, tiled=True),
        lax.all_gather(w_up, ("seq", "batch"), axis=0, tiled=True),
        lax.all_gather(w_down, ("seq", "batch"), axis=0, tiled=True),
        lax.all_gather(conv_kernel, ("seq", "batch"), axis=1, tiled=True),
        lax.all_gather(norm_params, ("seq", "batch"), axis=1, tiled=True),
    )
    inputs = (x_short, x_long)
    cotangents = (cot_short, cot_long)
    model_width = x_short.shape[2]
    offsets = (lax.axis_index("seq") * x_short.shape[1], lax.axis_index("seq") * x_long.shape[1])
    fronts = front_part(inputs, full_weights)
    kv_fwd = (
        lax.all_gather(fronts[0][5][:, :, model_width:], "seq", axis=1, tiled=True),
        lax.all_gather(fronts[1][5][:, :, model_width:], "seq", axis=1, tiled=True),
    )
    outputs = [
        rest_part(
            fronts[index_part],
            kv_fwd[index_part],
            lengths[index_part],
            offsets[index_part],
            full_weights,
            None,
        )
        for index_part in range(2)
    ]
    back_weights = (
        lax.all_gather(w_qkv, ("seq", "batch"), axis=0, tiled=True),
        lax.all_gather(w_out, ("seq", "batch"), axis=0, tiled=True),
        lax.all_gather(w_up, ("seq", "batch"), axis=0, tiled=True),
        lax.all_gather(w_down, ("seq", "batch"), axis=0, tiled=True),
        lax.all_gather(conv_kernel, ("seq", "batch"), axis=1, tiled=True),
        lax.all_gather(norm_params, ("seq", "batch"), axis=1, tiled=True),
    )
    fronts_back = front_part(inputs, back_weights)
    kv_back = (
        lax.all_gather(fronts_back[0][5][:, :, model_width:], "seq", axis=1, tiled=True),
        lax.all_gather(fronts_back[1][5][:, :, model_width:], "seq", axis=1, tiled=True),
    )
    partials = [
        rest_part(
            fronts_back[index_part],
            kv_back[index_part],
            lengths[index_part],
            offsets[index_part],
            back_weights,
            cotangents[index_part],
        )
        for index_part in range(2)
    ]
    kv_grads = (
        lax.psum_scatter(
            partials[0][1].astype(jnp.bfloat16), "seq", scatter_dimension=1, tiled=True
        ).astype(jnp.float32),
        lax.psum_scatter(
            partials[1][1].astype(jnp.bfloat16), "seq", scatter_dimension=1, tiled=True
        ).astype(jnp.float32),
    )
    grad_mixed = [
        jnp.concatenate([partials[index_part][0], kv_grads[index_part]], axis=-1)
        for index_part in range(2)
    ]
    received = (
        from_behind(grad_mixed[0][:, :2].astype(jnp.bfloat16), "seq", -1).astype(jnp.float32),
        from_behind(grad_mixed[1][:, :2].astype(jnp.bfloat16), "seq", -1).astype(jnp.float32),
    )
    kernel = back_weights[4].astype(jnp.float32)
    params = back_weights[5].astype(jnp.float32)
    w_qkv_full = back_weights[0]
    grad_qkv = jnp.zeros(w_qkv_full.shape, jnp.float32)
    grad_kernel = jnp.zeros(kernel.shape, jnp.float32)
    grad_norm = jnp.zeros((4, model_width), jnp.float32)
    grad_out = partials[0][3] + partials[1][3]
    grad_up = partials[0][4] + partials[1][4]
    grad_down = partials[0][5] + partials[1][5]
    input_grads = []
    for index_part in range(2):
        flat, normal_one, inverse_one, normed_low, padded, mixed = fronts_back[index_part]
        seq_count, block_rows, three_width = mixed.shape
        mixed_grad = grad_mixed[index_part]
        extended = jnp.concatenate([mixed_grad, received[index_part]], axis=1)
        grad_projected = (
            kernel[0] * extended[:, :block_rows]
            + kernel[1] * extended[:, 1 : block_rows + 1]
            + kernel[2] * extended[:, 2:]
        ).astype(jnp.bfloat16)
        grad_kernel = grad_kernel + jnp.stack(
            [
                jnp.sum(mixed_grad * padded[:, 2:], axis=(0, 1)),
                jnp.sum(mixed_grad * padded[:, 1 : block_rows + 1], axis=(0, 1)),
                jnp.sum(mixed_grad * padded[:, :block_rows], axis=(0, 1)),
            ]
        )
        grad_flat = grad_projected.reshape(seq_count * block_rows, three_width)
        grad_qkv = grad_qkv + jnp.dot(normed_low.T, grad_flat, preferred_element_type=jnp.float32)
        grad_normed = jnp.dot(grad_flat, w_qkv_full.T, preferred_element_type=jnp.float32)
        grad_input = partials[index_part][2] + norm_back_flat(
            grad_normed, normal_one, inverse_one, params[0]
        )
        input_grads.append(grad_input.reshape(seq_count, block_rows, model_width))
        norm_two = partials[index_part][6]
        grad_norm = grad_norm + jnp.stack(
            [
                jnp.sum(grad_normed * normal_one, axis=0),
                jnp.sum(grad_normed, axis=0),
                norm_two[0],
                norm_two[1],
            ]
        )
    summed = (
        lax.psum_scatter(grad_qkv, ("seq", "batch"), scatter_dimension=0, tiled=True),
        lax.psum_scatter(grad_out, ("seq", "batch"), scatter_dimension=0, tiled=True),
        lax.psum_scatter(grad_up, ("seq", "batch"), scatter_dimension=0, tiled=True),
        lax.psum_scatter(grad_down, ("seq", "batch"), scatter_dimension=0, tiled=True),
        lax.psum_scatter(grad_kernel, ("seq", "batch"), scatter_dimension=1, tiled=True),
        lax.psum_scatter(grad_norm, ("seq", "batch"), scatter_dimension=1, tiled=True),
    )
    return (
        outputs[0],
        outputs[1],
        input_grads[0],
        input_grads[1],
        summed[0],
        summed[1],
        summed[2],
        summed[3],
        summed[4],
        summed[5],
    )


def solution(mesh):
    split = mesh.shape["seq"] == 8
    return jax.shard_map(
        split_body if split else general_body,
        mesh=mesh,
        in_specs=(
            P("batch", "seq", None),
            P("batch", "seq", None),
            P(None, "batch"),
            P("batch", "seq", None),
            P("batch", "seq", None),
            P(("seq", "batch"), None),
            P(("seq", "batch"), None),
            P(("seq", "batch"), None),
            P(("seq", "batch"), None),
            P(None, ("seq", "batch")),
            P(None, ("seq", "batch")),
        ),
        out_specs=(
            P("batch", "seq", None),
            P("batch", "seq", None),
            P("batch", "seq", None),
            P("batch", "seq", None),
            P(("seq", "batch"), None),
            P(("seq", "batch"), None),
            P(("seq", "batch"), None),
            P(("seq", "batch"), None),
            P(None, ("seq", "batch")),
            P(None, ("seq", "batch")),
        ),
        check_vma=False,
    )
```

```python
import functools

import jax
import jax.numpy as jnp
from jax import lax
from jax.experimental import pallas as pl
from jax.experimental.pallas import tpu as pltpu
from jax.sharding import PartitionSpec as P

EPS = 1e-05
NEG_FILL = -1e30
HEAD_DIM = 64
LANES = 128
TILE = 256
PAD = 16
MESH = pl.DeviceIdType.MESH
F32 = jnp.float32
BF16 = jnp.bfloat16


def dot_nn(left, right):
    return lax.dot_general(left, right, (((1,), (0,)), ((), ())), preferred_element_type=F32)


def dot_nt(left, right):
    return lax.dot_general(left, right, (((1,), (1,)), ((), ())), preferred_element_type=F32)


def dot_tn(left, right):
    return lax.dot_general(left, right, (((0,), (0,)), ((), ())), preferred_element_type=F32)


def params_of(limit=58, **more):
    return pltpu.CompilerParams(vmem_limit_bytes=limit * 2**20, **more)


def vmem():
    return pl.BlockSpec(memory_space=pltpu.VMEM)


def smem():
    return pl.BlockSpec(memory_space=pltpu.SMEM)


def hbm():
    return pl.BlockSpec(memory_space=pl.ANY)


def normalise(values):
    average = jnp.mean(values, axis=-1, keepdims=True)
    centred = values - average
    inverse = lax.rsqrt(jnp.mean(centred * centred, axis=-1, keepdims=True) + EPS)
    return centred * inverse, inverse


def norm_back(grad, normal, inverse, gain):
    scaled_grad = grad * gain
    first_mean = jnp.mean(scaled_grad, axis=-1, keepdims=True)
    second_mean = jnp.mean(scaled_grad * normal, axis=-1, keepdims=True)
    return inverse * (scaled_grad - first_mean - normal * second_mean)


def lane_iota(rows):
    return lax.broadcasted_iota(jnp.int32, (rows, LANES), 1)


def position():
    index, batch = lax.axis_index("seq"), lax.axis_index("batch")
    return index // 2, index % 2, batch // 2, batch % 2


def at(z, core, y, x):
    return (z * 2 + core, y * 2 + x)


def remote(src, dst, send, recv, device):
    return pltpu.make_async_remote_copy(
        src_ref=src, dst_ref=dst, send_sem=send, recv_sem=recv, device_id=device, device_id_type=MESH
    )


def greet(others):
    barrier = pltpu.get_barrier_semaphore()
    for other in others:
        pl.semaphore_signal(barrier, inc=1, device_id=other, device_id_type=MESH)
    pl.semaphore_wait(barrier, len(others))


def neighbours():
    z, core, y, x = position()
    line = [at(lax.rem(z + step, 4), core, y, x) for step in (1, 2, 3)]
    return line + [at(z, 1 - core, y, x), at(z, core, 1 - y, x), at(z, core, y, 1 - x)]


def roles():
    z = lax.axis_index("seq") // 2
    half = z // 2
    near = jnp.where(half == 0, z, 3 - z)
    partner_z = jnp.where(half == 0, 1 - z, 5 - z)
    return half, near, partner_z, 2 - half


def z_of(half, place):
    return jnp.where(half == 0, place, 3 - place)


def exchange_kernel(x_ref, o_ref, local_sem, send_sem, recv_sem):
    index, batch = lax.axis_index("seq"), lax.axis_index("batch")
    count = x_ref.shape[0]
    greet([(lax.rem(index + step, count), batch) for step in range(1, count)])
    own = pltpu.make_async_copy(x_ref.at[index], o_ref.at[index], local_sem)
    own.start()
    copies = []
    for step in range(1, count):
        target = lax.rem(index + step, count)
        copy = remote(
            x_ref.at[target], o_ref.at[index], send_sem.at[target], recv_sem.at[index], (target, batch)
        )
        copy.start()
        copies.append(copy)
    for step in range(1, count):
        source = lax.rem(index + count - step, count)
        remote(
            x_ref.at[source], o_ref.at[source], send_sem.at[source], recv_sem.at[source], (source, batch)
        ).wait_recv()
    for copy in copies:
        copy.wait_send()
    own.wait()


def exchange(x, collective_id):
    count = x.shape[0]
    return pl.pallas_call(
        exchange_kernel,
        out_shape=jax.ShapeDtypeStruct(x.shape, x.dtype),
        in_specs=[hbm()],
        out_specs=hbm(),
        scratch_shapes=[
            pltpu.SemaphoreType.DMA,
            pltpu.SemaphoreType.DMA((count,)),
            pltpu.SemaphoreType.DMA((count,)),
        ],
        compiler_params=pltpu.CompilerParams(collective_id=collective_id, has_side_effects=True),
    )(x)


class RowGather:
    def __init__(self, x_ref, o_ref, own_sem, send_sem, recv_sem, sib_send, sib_recv):
        self.x_ref, self.o_ref = x_ref, o_ref
        self.sems = (own_sem, send_sem, recv_sem, sib_send, sib_recv)
        self.rows = x_ref.shape[1]
        self.z, self.core, self.y, self.x = position()
        self.half, self.near, self.partner_z, self.far_z = roles()
        self.sibling = at(self.z, 1 - self.core, self.y, self.x)
        self.partner = at(self.partner_z, self.core, self.y, self.x)
        self.sent = []

    def block(self, z, core):
        return self.o_ref.at[pl.ds(pl.multiple_of((z * 2 + core) * self.rows, self.rows), self.rows)]

    def start(self):
        own_sem, send, recv, sib_send, sib_recv = self.sems
        mine, other = self.x_ref.at[self.half], self.x_ref.at[1 - self.half]
        place = self.block(self.z, self.core)
        far = at(self.far_z, self.core, self.y, self.x)
        self.own = pltpu.make_async_copy(mine, place, own_sem)
        self.sent = [
            remote(mine, place, send.at[0], recv.at[self.near], self.partner),
            remote(other, place, send.at[1], recv.at[3 - self.near], far),
            remote(mine, place, sib_send.at[0], sib_recv.at[self.near], self.sibling),
        ]
        for copy in self.sent:
            copy.start()
        self.own.start()

    def step(self, slot):
        _, send, recv, sib_send, sib_recv = self.sems
        place = (1 - self.near, 2, 3)[slot]
        block = self.block(z_of(self.half, place), self.core)
        remote(block, block, send.at[0], recv.at[place], self.partner).wait_recv()
        if slot:
            onward = remote(block, block, send.at[1 + slot], recv.at[place], self.partner)
            pl.when(self.near == 1)(onward.start)
        across = remote(block, block, sib_send.at[1 + slot], sib_recv.at[place], self.sibling)
        across.start()
        self.sent.append(across)

    def finish(self):
        _, send, recv, sib_send, sib_recv = self.sems
        for place in range(4):
            block = self.block(z_of(self.half, place), 1 - self.core)
            remote(block, block, sib_send.at[0], sib_recv.at[place], self.sibling).wait_recv()
        self.own.wait()
        for copy in self.sent:
            copy.wait_send()
        block = self.block(self.z, self.core)

        @pl.when(self.near == 1)
        def _():
            for slot in (1, 2):
                remote(block, block, send.at[1 + slot], recv.at[0], self.partner).wait_send()


class ShardGather:
    def __init__(self, shard, full, own_sem, send, recv, by_group=False):
        self.shard, self.full, self.own_sem, self.send_sem, self.recv_sem = shard, full, own_sem, send, recv
        self.z, self.core, self.y, self.x = position()
        self.by_group = by_group
        self.sent = []

    def go(self, src, dst, slot, device, recv_slot=None):
        copy = remote(src, dst, self.send_sem.at[slot], self.recv_sem.at[slot if recv_slot is None else recv_slot], device)
        copy.start()
        self.sent.append(copy)

    def arrived(self, dst, slot):
        remote(dst, dst, self.send_sem.at[0], self.recv_sem.at[slot], at(self.z, self.core, self.y, self.x)).wait_recv()

    def start(self):
        z, core, y, x = self.z, self.core, self.y, self.x
        pick = (lambda target: self.shard.at[lax.rem(target, 2)]) if self.by_group else (lambda target: self.shard)
        mine = self.full.at[z, core, y, x]
        for step in (1, 2, 3):
            target = lax.rem(z + step, 4)
            self.go(pick(target), mine, step, at(target, core, y, x))
        self.own = pltpu.make_async_copy(pick(z), mine, self.own_sem)
        self.own.start()

    def across(self, part, slot):
        zs, ys, xs = part
        ref = self.full.at[zs, self.core, ys, xs]
        if self.by_group:
            ref = self.full.at[zs, self.core, ys, xs, 1 - self.core]
        self.go(ref, ref, slot, at(self.z, 1 - self.core, self.y, self.x))

    def sides(self):
        first, second = pl.ds(0, 2), pl.ds(2, 2)
        return first, second

    def over(self):
        z, core, y, x = self.z, self.core, self.y, self.x
        for step in (1, 2, 3):
            source = lax.rem(z + 4 - step, 4)
            self.arrived(self.full.at[source, core, y, x], step)
        self.own.wait()
        first, second = self.sides()
        ref = self.full.at[first, core, y, x]
        self.go(ref, ref, 4, at(z, core, y, 1 - x))
        ref = self.full.at[second, core, y, x]
        self.go(ref, ref, 5, at(z, core, 1 - y, x))
        self.across((pl.ds(0, 4), y, x), 8)

    def turn(self):
        z, core, y, x = self.z, self.core, self.y, self.x
        first, second = self.sides()
        self.arrived(self.full.at[first, core, y, 1 - x], 4)
        ref = self.full.at[first, core, y]
        self.go(ref, ref, 6, at(z, core, 1 - y, x))
        self.across((first, y, 1 - x), 9)
        self.arrived(self.full.at[second, core, 1 - y, x], 5)
        ref = self.full.at[second, core, :, x]
        self.go(ref, ref, 7, at(z, core, y, 1 - x))
        self.across((second, 1 - y, x), 10)

    def last(self):
        z, core, y, x = self.z, self.core, self.y, self.x
        first, second = self.sides()
        self.arrived(self.full.at[first, core, 1 - y], 6)
        self.across((first, 1 - y, pl.ds(0, 2)), 11)
        self.arrived(self.full.at[second, core, :, 1 - x], 7)
        self.across((second, pl.ds(0, 2), 1 - x), 12)

    def finish(self):
        y, x, core, other = self.y, self.x, self.core, 1 - self.core
        first, second = self.sides()
        parts = (
            (pl.ds(0, 4), y, x),
            (first, y, 1 - x),
            (second, 1 - y, x),
            (first, 1 - y, pl.ds(0, 2)),
            (second, pl.ds(0, 2), 1 - x),
        )
        for slot, (zs, ys, xs) in enumerate(parts):
            ref = self.full.at[zs, other, ys, xs]
            if self.by_group:
                ref = self.full.at[zs, other, ys, xs, core]
            self.arrived(ref, 8 + slot)
        for copy in self.sent:
            copy.wait_send()


def gather_kernel(xs_ref, xl_ref, *refs, shards):
    ins, outs, sems = refs[:shards], refs[shards + 2 : 2 * shards + 2], refs[2 * shards + 2 :]
    os_ref, ol_ref = refs[shards : shards + 2]
    own_sem, send, recv, sib_send, sib_recv, shard_own, shard_send, shard_recv = sems
    greet(neighbours())
    rows = [
        RowGather(x, o, own_sem.at[i], send.at[i], recv.at[i], sib_send.at[i], sib_recv.at[i])
        for i, (x, o) in enumerate(((xs_ref, os_ref), (xl_ref, ol_ref)))
    ]
    weights = [
        ShardGather(a, f, shard_own.at[i], shard_send.at[i], shard_recv.at[i], by_group=i == 1)
        for i, (a, f) in enumerate(zip(ins, outs))
    ]
    for one in rows + weights:
        one.start()
    rows[0].step(0)
    rows[1].step(0)
    for one in weights[:2]:
        one.over()
    rows[0].step(1)
    rows[0].step(2)
    for one in weights[2:]:
        one.over()
    rows[1].step(1)
    for one in weights[:2]:
        one.turn()
    rows[1].step(2)
    for one in weights[:2]:
        one.last()
    for one in weights[2:]:
        one.turn()
    for one in weights[2:]:
        one.last()
    for one in rows + weights:
        one.finish()


def gather_all(x_short, x_long, shards, count):
    width = x_short.shape[2]
    n = len(shards)
    full = [
        jax.ShapeDtypeStruct((4, 2, 2, 2) + (s.shape[1:] if i == 1 else s.shape), s.dtype)
        for i, s in enumerate(shards)
    ]
    return pl.pallas_call(
        functools.partial(gather_kernel, shards=n),
        out_shape=(
            jax.ShapeDtypeStruct((count * x_short.shape[1], width), x_short.dtype),
            jax.ShapeDtypeStruct((count * x_long.shape[1], width), x_long.dtype),
            *full,
        ),
        in_specs=[hbm()] * (2 + n),
        out_specs=tuple([hbm()] * (2 + n)),
        scratch_shapes=[pltpu.SemaphoreType.DMA((2,))]
        + [pltpu.SemaphoreType.DMA((2, 4))] * 4
        + [pltpu.SemaphoreType.DMA((n,))]
        + [pltpu.SemaphoreType.DMA((n, 13))] * 2,
        compiler_params=pltpu.CompilerParams(collective_id=0, has_side_effects=True),
    )(x_short, x_long, *shards)


class RowSum:
    ORDER = (2, 3, 1, 0)

    def __init__(self, g_ref, o_ref, sib, total, got, sib_send, sib_recv, send, recv):
        self.g_ref, self.o_ref, self.sib, self.total, self.got = g_ref, o_ref, sib, total, got
        self.sib_send, self.sib_recv, self.send, self.recv = sib_send, sib_recv, send, recv
        self.z, self.core, self.y, self.x = position()
        self.half, self.near, self.partner_z, self.far_z = roles()
        self.partner = at(self.partner_z, self.core, self.y, self.x)
        self.sibling = at(self.z, 1 - self.core, self.y, self.x)

    def start(self):
        self.across = {}
        for place in self.ORDER:
            copy = remote(
                self.g_ref.at[z_of(self.half, place) * 2 + 1 - self.core], self.sib.at[place],
                self.sib_send.at[place], self.sib_recv.at[place], self.sibling,
            )
            copy.start()
            self.across[place] = copy

    def own_sum(self, place):
        self.across[place].wait_recv()
        mine = self.g_ref[z_of(self.half, place) * 2 + self.core]
        return mine.astype(F32) + self.sib[place].astype(F32)

    def to_partner(self, place):
        return remote(
            self.total.at[place], self.got.at[place], self.send.at[place], self.recv.at[place], self.partner
        )

    def first(self):
        @pl.when(self.near == 0)
        def _():
            for place in (2, 3, 1):
                self.total[place] = self.own_sum(place).astype(BF16)
                self.to_partner(place).start()

        @pl.when(self.near == 1)
        def _():
            self.total[0] = self.own_sum(0).astype(BF16)
            self.to_partner(0).start()

    def to_owner(self, place):
        owner = at(z_of(self.half, place), self.core, self.y, self.x)
        return remote(self.total.at[place], self.got.at[4], self.send.at[place], self.recv.at[4], owner)

    def second(self, place):
        @pl.when(self.near == 1)
        def _():
            mine = self.own_sum(place)
            self.to_partner(place).wait_recv()
            self.total[place] = (mine + self.got[place].astype(F32)).astype(BF16)
            self.to_owner(place).start()

    def finish(self):
        @pl.when(self.near == 0)
        def _():
            mine = self.own_sum(0)
            self.to_partner(0).wait_recv()
            self.o_ref[self.half] = mine + self.got[0].astype(F32)
            for place in (2, 3, 1):
                self.to_partner(place).wait_send()

        @pl.when(self.near == 1)
        def _():
            mine = self.own_sum(1)
            self.to_partner(1).wait_recv()
            self.o_ref[self.half] = mine + self.got[1].astype(F32)
            self.to_partner(0).wait_send()
            for place in (2, 3):
                self.to_owner(place).wait_send()

        far = at(self.far_z, self.core, self.y, self.x)
        remote(self.total.at[0], self.got.at[4], self.send.at[0], self.recv.at[4], far).wait_recv()
        self.o_ref[1 - self.half] = self.got[4].astype(F32)
        for place in self.ORDER:
            self.across[place].wait_send()


def add_into(total, part):
    total[...] = (total[...].astype(F32) + part[...].astype(F32)).astype(total.dtype)


class ShardSum:
    def __init__(self, grad, out, bufs, own_sem, send, recv):
        self.grad, self.out = grad, out
        self.tot, self.sib, self.one, self.two, self.line = bufs
        self.own_sem, self.send_sem, self.recv_sem = own_sem, send, recv
        self.z, self.core, self.y, self.x = position()
        self.sent = []

    def go(self, src, dst, slot, device):
        copy = remote(src, dst, self.send_sem.at[slot], self.recv_sem.at[slot], device)
        copy.start()
        self.sent.append(copy)

    def arrived(self, dst, slot):
        remote(dst, dst, self.send_sem.at[0], self.recv_sem.at[slot], at(self.z, self.core, self.y, self.x)).wait_recv()

    def start(self):
        z, core, y, x = self.z, self.core, self.y, self.x
        for side in (0, 1):
            zs = pl.ds(2 * side, 2)
            self.go(self.grad.at[zs, 1 - core], self.sib.at[zs], side, at(z, 1 - core, y, x))
        self.own = pltpu.make_async_copy(self.grad.at[:, core], self.tot, self.own_sem)
        self.own.start()

    def over(self):
        z, core, y, x = self.z, self.core, self.y, self.x
        self.own.wait()
        for side in (0, 1):
            zs = pl.ds(2 * side, 2)
            self.arrived(self.sib.at[zs], side)
            for zz in range(2):
                for ys in range(2):
                    for xs in range(2):
                        add_into(self.tot.at[2 * side + zz, ys, xs], self.sib.at[2 * side + zz, ys, xs])
            if side == 0:
                self.go(self.tot.at[zs, :, 1 - x], self.one.at[0], 2, at(z, core, y, 1 - x))
            else:
                self.go(self.tot.at[zs, 1 - y], self.one.at[1], 3, at(z, core, 1 - y, x))

    def turn(self):
        z, core, y, x = self.z, self.core, self.y, self.x
        self.arrived(self.one.at[0], 2)
        for zz in range(2):
            for ys in range(2):
                add_into(self.tot.at[zz, ys, x], self.one.at[0, zz, ys])
        self.go(self.tot.at[pl.ds(0, 2), 1 - y, x], self.two.at[0], 4, at(z, core, 1 - y, x))
        self.arrived(self.one.at[1], 3)
        for zz in range(2):
            for xs in range(2):
                add_into(self.tot.at[2 + zz, y, xs], self.one.at[1, zz, xs])
        self.go(self.tot.at[pl.ds(2, 2), y, 1 - x], self.two.at[1], 5, at(z, core, y, 1 - x))

    def last(self):
        z, core, y, x = self.z, self.core, self.y, self.x
        for side in (0, 1):
            self.arrived(self.two.at[side], 4 + side)
            for zz in range(2):
                add_into(self.tot.at[2 * side + zz, y, x], self.two.at[side, zz])
        for step in (1, 2, 3):
            target = lax.rem(z + step, 4)
            self.go(self.tot.at[target, y, x], self.line.at[step - 1], 5 + step, at(target, core, y, x))

    def finish(self):
        total = self.tot[self.z, self.y, self.x].astype(F32)
        for step in (1, 2, 3):
            self.arrived(self.line.at[step - 1], 5 + step)
            total = total + self.line[step - 1].astype(F32)
        self.out[...] = total
        for copy in self.sent:
            copy.wait_send()

    @staticmethod
    def buffers(grad):
        tail, kind = grad.shape[4:], grad.dtype
        return [
            pltpu.VMEM((4, 2, 2) + tail, kind),
            pltpu.VMEM((4, 2, 2) + tail, kind),
            pltpu.VMEM((2, 2, 2) + tail, kind),
            pltpu.VMEM((2, 2) + tail, kind),
            pltpu.VMEM((3,) + tail, kind),
        ]


class GroupSum:
    def __init__(self, grad, out, bufs, own_sem, send, recv):
        self.grad, self.out = grad, out
        self.tot, self.one, self.two, self.line = bufs
        self.own_sem, self.send_sem, self.recv_sem = own_sem, send, recv
        self.z, self.core, self.y, self.x = position()
        self.sent = []

    go = ShardSum.go
    arrived = ShardSum.arrived

    def start(self):
        z, core, y, x = self.z, self.core, self.y, self.x
        self.go(self.grad.at[pl.ds(0, 2), :, :, 1 - x], self.one.at[0], 0, at(z, core, y, 1 - x))
        self.go(self.grad.at[pl.ds(2, 2), :, 1 - y], self.one.at[1], 1, at(z, core, 1 - y, x))
        self.own = pltpu.make_async_copy(self.grad, self.tot, self.own_sem)
        self.own.start()

    def turn(self):
        z, core, y, x = self.z, self.core, self.y, self.x
        self.own.wait()
        self.arrived(self.one.at[0], 0)
        for zz in range(2):
            for cc in range(2):
                for ys in range(2):
                    add_into(self.tot.at[zz, cc, ys, x], self.one.at[0, zz, cc, ys])
        self.go(self.tot.at[pl.ds(0, 2), :, 1 - y, x], self.two.at[0], 2, at(z, core, 1 - y, x))
        self.arrived(self.one.at[1], 1)
        for zz in range(2):
            for cc in range(2):
                for xs in range(2):
                    add_into(self.tot.at[2 + zz, cc, y, xs], self.one.at[1, zz, cc, xs])
        self.go(self.tot.at[pl.ds(2, 2), :, y, 1 - x], self.two.at[1], 3, at(z, core, y, 1 - x))

    def last(self):
        z, core, y, x = self.z, self.core, self.y, self.x
        for side in (0, 1):
            self.arrived(self.two.at[side], 2 + side)
            for zz in range(2):
                for cc in range(2):
                    add_into(self.tot.at[2 * side + zz, cc, y, x], self.two.at[side, zz, cc])
        mine = z * 2 + core
        for step in range(1, 8):
            target = lax.rem(mine + step, 8)
            tz, tc = target // 2, target % 2
            self.go(self.tot.at[tz, tc, y, x], self.line.at[step - 1], 3 + step, at(tz, tc, y, x))

    def finish(self):
        z, core, y, x = self.z, self.core, self.y, self.x
        mine = z * 2 + core
        for step in range(1, 8):
            self.arrived(self.line.at[step - 1], 3 + step)
        self.line[7] = self.tot[z, core, y, x]
        for group in range(4):
            total = None
            for source in (group, group + 4):
                back = lax.rem(mine - source + 8 + 7, 8)
                term = self.line[back].astype(F32)
                total = term if total is None else total + term
            self.out[group] = total
        for copy in self.sent:
            copy.wait_send()

    @staticmethod
    def buffers(grad):
        tail, kind = grad.shape[4:], grad.dtype
        return [
            pltpu.VMEM((4, 2, 2, 2) + tail, kind),
            pltpu.VMEM((2, 2, 2, 2) + tail, kind),
            pltpu.VMEM((2, 2, 2) + tail, kind),
            pltpu.VMEM((8,) + tail, kind),
        ]


def sum_kernel(gn_ref, *refs, shards):
    grads, outs = refs[:shards], refs[shards : 2 * shards + 1]
    rest = refs[2 * shards + 1 :]
    sib, total, got, sib_send, sib_recv, send, recv, shard_own, shard_send, shard_recv = rest[:10]
    bufs = list(rest[10:])
    greet(neighbours() + extra_neighbours())
    rows = RowSum(gn_ref, outs[0], sib, total, got, sib_send, sib_recv, send, recv)
    sums = []
    for i, grad in enumerate(grads):
        kind = GroupSum if i == 0 else ShardSum
        size = 4 if i == 0 else 5
        mine, bufs = bufs[:size], bufs[size:]
        sums.append(kind(grad, outs[1 + i], mine, shard_own.at[i], shard_send.at[i], shard_recv.at[i]))
    rows.start()
    for one in sums:
        one.start()
    rows.first()
    for one in sums[1:]:
        one.over()
    rows.second(2)
    rows.second(3)
    for one in sums:
        one.turn()
    for one in sums:
        one.last()
    rows.finish()
    for one in sums:
        one.finish()


def extra_neighbours():
    z, core, y, x = position()
    return [at(lax.rem(z + step, 4), 1 - core, y, x) for step in (1, 2, 3)]


def sum_all(gn, grads):
    count, rows, width = gn.shape
    n = len(grads)
    tails = [((4,) if i == 0 else ()) + g.shape[4:] for i, g in enumerate(grads)]
    buffers = []
    for i, g in enumerate(grads):
        buffers += (GroupSum if i == 0 else ShardSum).buffers(g)
    return pl.pallas_call(
        functools.partial(sum_kernel, shards=n),
        out_shape=(
            jax.ShapeDtypeStruct((2, rows, width), F32),
            *[jax.ShapeDtypeStruct(tail, F32) for tail in tails],
        ),
        in_specs=[vmem()] + [hbm()] * n,
        out_specs=tuple([vmem()] * (1 + n)),
        scratch_shapes=[
            pltpu.VMEM((4, rows, width), BF16),
            pltpu.VMEM((4, rows, width), BF16),
            pltpu.VMEM((5, rows, width), BF16),
            pltpu.SemaphoreType.DMA((4,)),
            pltpu.SemaphoreType.DMA((4,)),
            pltpu.SemaphoreType.DMA((4,)),
            pltpu.SemaphoreType.DMA((5,)),
            pltpu.SemaphoreType.DMA((n,)),
            pltpu.SemaphoreType.DMA((n, 11)),
            pltpu.SemaphoreType.DMA((n, 11)),
        ]
        + buffers,
        compiler_params=params_of(collective_id=3, has_side_effects=True),
    )(gn, *grads)


def shifted(window, by):
    return pltpu.roll(window, by % window.shape[0], 0)


def front_kernel(
    lens_ref, xs_ref, xl_ref, wq_ref, ck_ref, np_ref,
    osend, qa, ka, vb, kt, proj, normed, lse,
    vt, ot,
):
    short_rows, long_rows = xs_ref.shape[0], xl_ref.shape[0]
    width = xs_ref.shape[1]
    parts = ((xs_ref, 0, PAD, short_rows), (xl_ref, short_rows, 2 * PAD + short_rows, long_rows))
    gain, offset = np_ref[0:1], np_ref[1:2]
    zeros = jnp.zeros((PAD, proj.shape[1]), BF16)
    proj[0:PAD] = zeros
    proj[PAD + short_rows : 2 * PAD + short_rows] = zeros
    lanes = lane_iota(TILE)
    low_half = lanes < HEAD_DIM
    for part, (x_ref, base, pbase, total) in enumerate(parts):
        length = lens_ref[part]

        @pl.loop(0, total // TILE)
        def _(step, x_ref=x_ref, base=base, pbase=pbase):
            start = pl.multiple_of(step * TILE, TILE)
            values = x_ref[pl.ds(start, TILE)].astype(F32)
            normal, _ = normalise(values)
            low = (normal * gain + offset).astype(BF16)
            normed[pl.ds(pl.multiple_of(base + start, TILE), TILE)] = low
            proj[pl.ds(pl.multiple_of(pbase + start, PAD), TILE)] = dot_nn(low, wq_ref[...]).astype(BF16)

        @pl.loop(0, total // TILE)
        def _(step, base=base, pbase=pbase, length=length):
            start = pl.multiple_of(step * TILE, TILE)
            window = proj[pl.ds(pl.multiple_of(pbase - PAD + start, PAD), TILE + PAD)].astype(F32)
            mixed = (
                ck_ref[0:1] * window[PAD:]
                + ck_ref[1:2] * shifted(window, 1)[PAD:]
                + ck_ref[2:3] * shifted(window, 2)[PAD:]
            ).astype(BF16).astype(F32)
            rows = pl.ds(pl.multiple_of(base + start, TILE), TILE)
            q_pair, q_one = mixed[:, 0:128] * 0.125, mixed[:, 128:256] * 0.125
            k_pair, k_one = mixed[:, 256:384], mixed[:, 384:512]
            v_pair, v_one = mixed[:, 512:640], mixed[:, 640:768]
            places = start + lax.broadcasted_iota(jnp.int32, (TILE, LANES), 0)
            bias = jnp.where(places < length, 0.0, NEG_FILL)
            at_zero = lanes == 0
            at_half = lanes == HEAD_DIM
            one_half = jnp.where(at_half, 1.0, 0.0)
            one_zero = jnp.where(at_zero, 1.0, 0.0)
            bias_half = jnp.where(at_half, bias, 0.0)
            bias_zero = jnp.where(at_zero, bias, 0.0)
            qa[0, rows] = jnp.where(low_half, q_pair, one_half).astype(BF16)
            qa[1, rows] = jnp.where(low_half, one_zero, q_pair).astype(BF16)
            qa[2, rows] = jnp.where(low_half, q_one, one_half).astype(BF16)
            ka[0, rows] = jnp.where(low_half, k_pair, bias_half).astype(BF16)
            ka[1, rows] = jnp.where(low_half, bias_zero, k_pair).astype(BF16)
            ka[2, rows] = jnp.where(low_half, k_one, bias_half).astype(BF16)
            vb[0, rows] = v_pair.astype(BF16)
            vb[1, rows] = v_one.astype(BF16)
            k_turned, k_turned_one = k_pair.T.astype(BF16), k_one.T.astype(BF16)
            v_turned, v_turned_one = v_pair.T.astype(BF16), v_one.T.astype(BF16)
            kt[0, :, rows] = k_turned[:HEAD_DIM]
            kt[1, :, rows] = k_turned[HEAD_DIM:]
            kt[2, :, rows] = k_turned_one[:HEAD_DIM]
            vt[0, :, rows] = v_turned[:HEAD_DIM]
            vt[1, :, rows] = v_turned[HEAD_DIM:]
            vt[2, :, rows] = v_turned_one[:HEAD_DIM]

    causal = lax.broadcasted_iota(jnp.int32, (TILE, TILE), 0) <= lax.broadcasted_iota(jnp.int32, (TILE, TILE), 1)

    @pl.loop(0, 3)
    def _(head):
        for _, base, _, total in parts:
            for block in range(total // TILE):
                rows = slice(base + block * TILE, base + (block + 1) * TILE)
                past = block * TILE
                query = qa[head, rows]
                diagonal = jnp.where(causal, dot_nt(ka[head, rows], query), NEG_FILL)
                top = jnp.max(diagonal, axis=0, keepdims=True)
                if past:
                    before = dot_nt(ka[head, base : base + past], query)
                    top = jnp.maximum(top, jnp.max(before, axis=0, keepdims=True))
                    exp_before = jnp.exp(before - top)
                exp_diagonal = jnp.exp(diagonal - top)
                norm = jnp.sum(exp_diagonal, axis=0, keepdims=True)
                if past:
                    norm = norm + jnp.sum(exp_before, axis=0, keepdims=True)
                lse[head, :, rows] = top + jnp.log(norm)
                inverse = 1.0 / norm
                result = dot_nn(vt[head, :, rows], (exp_diagonal * inverse).astype(BF16))
                if past:
                    result = result + dot_nn(
                        vt[head, :, base : base + past], (exp_before * inverse).astype(BF16)
                    )
                ot[head, :, rows] = result

    own_short, own_long = TILE // 2, TILE
    for _, base, _, total in parts:
        for block in range(total // TILE):
            rows = slice(base + block * TILE, base + (block + 1) * TILE)
            pair = jnp.concatenate([ot[0, :, rows], ot[1, :, rows]], axis=0).T.astype(BF16)
            single = ot[2, :, rows]
            if base:
                osend[block, own_short : own_short + own_long] = pair
                packed = jnp.concatenate([single[:, :LANES], single[:, LANES:]], axis=0).T
                osend[block, own_short + own_long + own_short // 2 :] = packed.astype(BF16)
            else:
                turned = jnp.concatenate([single, single], axis=0).T
                half = own_short // 2
                for side in range(2):
                    start = side * own_short
                    osend[2 * block + side, 0:own_short] = pair[start : start + own_short]
                    packed = jnp.where(
                        lane_iota(half) < HEAD_DIM,
                        turned[start : start + half],
                        turned[start + half : start + own_short],
                    )
                    osend[2 * block + side, own_short + own_long : own_short + own_long + half] = packed.astype(BF16)


def front(lens, xs, xl, wq, ck, norms, count):
    short_rows, long_rows = xs.shape[0], xl.shape[0]
    total = short_rows + long_rows
    owned = total // count
    out = jax.ShapeDtypeStruct
    return pl.pallas_call(
        front_kernel,
        out_shape=(
            out((count, owned * 3 // 2, LANES), BF16),
            out((3, total, LANES), BF16),
            out((3, total, LANES), BF16),
            out((2, total, LANES), BF16),
            out((3, HEAD_DIM, total), BF16),
            out((total + 2 * PAD, 6 * LANES), BF16),
            out((total, xs.shape[1]), BF16),
            out((3, 1, total), F32),
        ),
        in_specs=[smem()] + [vmem()] * 5,
        out_specs=tuple([vmem()] * 8),
        scratch_shapes=[pltpu.VMEM((3, HEAD_DIM, total), BF16), pltpu.VMEM((3, HEAD_DIM, total), F32)],
        compiler_params=params_of(),
    )(lens, xs, xl, wq, ck, norms)


def middle_kernel(
    xs_ref, xl_ref, recv, cs_ref, cl_ref, wo_ref, wu_ref, wd_ref, np_ref,
    ys_ref, yl_ref, gmid, gsend, gwo, gwu, gwd, gnorm,
    att, middle, normal_two, inverse_two, second, second_t, cot, y_acc, gsec, gml,
):
    short, long = xs_ref.shape[1], xl_ref.shape[1]
    owned = short + long
    rows_all = 2 * owned
    half = short // 2
    lanes = lane_iota(owned // 2)
    low_half = lanes < HEAD_DIM
    for seq in range(2):
        first = seq * owned
        cot[first : first + short] = cs_ref[seq]
        cot[first + short : first + owned] = cl_ref[seq]
        for chip in range(2):
            packs = []
            for core in range(2):
                source = recv.at[seq * 4 + chip * 2 + core]
                block = 3 * chip + core
                att[first : first + owned, block * LANES : (block + 1) * LANES] = source[0:owned]
                packs.append(source[owned:].astype(F32))
            swapped = [pltpu.roll(pack, HEAD_DIM, 1) for pack in packs]
            early = jnp.where(low_half, packs[0], swapped[1]).astype(BF16)
            late = jnp.where(low_half, swapped[0], packs[1]).astype(BF16)
            columns = slice((3 * chip + 2) * LANES, (3 * chip + 3) * LANES)
            att[first : first + half, columns] = early[:half]
            att[first + half : first + short, columns] = late[:half]
            att[first + short : first + short + long // 2, columns] = early[half:]
            att[first + short + long // 2 : first + owned, columns] = late[half:]
        middle[first : first + short] = xs_ref[seq].astype(F32)
        middle[first + short : first + owned] = xl_ref[seq].astype(F32)

    @pl.loop(0, rows_all // TILE)
    def _(step):
        rows = pl.ds(pl.multiple_of(step * TILE, TILE), TILE)
        values = middle[rows] + dot_nn(att[rows], wo_ref[...])
        middle[rows] = values
        normal, inverse = normalise(values)
        normal_two[rows] = normal
        inverse_two[rows] = inverse
        second[rows] = (normal * np_ref[2:3] + np_ref[3:4]).astype(BF16)
        y_acc[rows] = values
        gsec[rows] = jnp.zeros_like(values)

    second_t[...] = second[...].T
    inner = 512

    @pl.loop(0, wu_ref.shape[1] // inner)
    def _(step):
        columns = pl.ds(pl.multiple_of(step * inner, inner), inner)
        upper = jnp.maximum(dot_nn(second[...], wu_ref[:, columns]), 0.0)
        hidden = (upper * upper).astype(BF16)
        grad_hidden = dot_nt(cot[...], wd_ref[columns])
        grad_upper = (2.0 * upper * grad_hidden).astype(BF16)
        y_acc[...] += dot_nn(hidden, wd_ref[columns])
        gwd[columns] = dot_tn(hidden, cot[...]).astype(BF16)
        gwu[:, columns] = dot_nn(second_t[...], grad_upper).astype(BF16)
        gsec[...] += dot_nt(grad_upper, wu_ref[:, columns])

    gnorm[...] = jnp.zeros_like(gnorm)

    @pl.loop(0, rows_all // TILE)
    def _(step):
        rows = pl.ds(pl.multiple_of(step * TILE, TILE), TILE)
        grad = gsec[rows]
        normal = normal_two[rows]
        gnorm[0:1] += jnp.sum(grad * normal, axis=0, keepdims=True)
        gnorm[1:2] += jnp.sum(grad, axis=0, keepdims=True)
        total = cot[rows].astype(F32) + norm_back(grad, normal, inverse_two[rows], np_ref[2:3])
        gmid[rows] = total
        gml[rows] = total.astype(BF16)
        second[rows] = dot_nt(gml[rows], wo_ref[...]).astype(BF16)

    gwo[...] = dot_tn(att[...], gml[...]).astype(BF16)
    for seq in range(2):
        first = seq * owned
        ys_ref[seq] = y_acc[first : first + short].astype(BF16)
        yl_ref[seq] = y_acc[first + short : first + owned].astype(BF16)
        for chip in range(2):
            columns = slice((3 * chip + 2) * LANES, (3 * chip + 3) * LANES)
            one = second[first : first + owned, columns].astype(F32)
            early = jnp.concatenate([one[:half], one[short : short + long // 2]], axis=0)
            late = jnp.concatenate([one[half:short], one[short + long // 2 :]], axis=0)
            for core in range(2):
                target = seq * 4 + chip * 2 + core
                block = 3 * chip + core
                gsend[target, 0:owned] = second[first : first + owned, block * LANES : (block + 1) * LANES]
                if core == 0:
                    packed = jnp.where(low_half, early, pltpu.roll(late, HEAD_DIM, 1))
                else:
                    packed = jnp.where(low_half, pltpu.roll(early, HEAD_DIM, 1), late)
                gsend[target, owned:] = packed.astype(BF16)


def middle_part(x_short, x_long, recv, cot_short, cot_long, w_out, w_up, w_down, norms):
    width = x_short.shape[2]
    rows = 2 * (x_short.shape[1] + x_long.shape[1])
    out = jax.ShapeDtypeStruct
    return pl.pallas_call(
        middle_kernel,
        out_shape=(
            out(x_short.shape, BF16),
            out(x_long.shape, BF16),
            out((rows, width), F32),
            out(recv.shape, BF16),
            out(w_out.shape, BF16),
            out(w_up.shape, BF16),
            out(w_down.shape, BF16),
            out((8, width), F32),
        ),
        in_specs=[vmem()] * 9,
        out_specs=tuple([vmem()] * 8),
        scratch_shapes=[
            pltpu.VMEM((rows, width), BF16),
            pltpu.VMEM((rows, width), F32),
            pltpu.VMEM((rows, width), F32),
            pltpu.VMEM((rows, 1), F32),
            pltpu.VMEM((rows, width), BF16),
            pltpu.VMEM((width, rows), BF16),
            pltpu.VMEM((rows, width), BF16),
            pltpu.VMEM((rows, width), F32),
            pltpu.VMEM((rows, width), F32),
            pltpu.VMEM((rows, width), BF16),
        ],
        compiler_params=params_of(),
    )(x_short, x_long, recv, cot_short, cot_long, w_out, w_up, w_down, norms)


def back_kernel(
    xs_ref, xl_ref, normed, proj, qa, ka, vb, kt, lse, osend, grecv, wq_ref, ck_ref, np_ref,
    gn_ref, gwq, gck, gnp,
    do, delta, dqt, gm, gproj,
):
    short_rows, long_rows = xs_ref.shape[0], xl_ref.shape[0]
    parts = (
        (xs_ref, 0, PAD, 0, short_rows),
        (xl_ref, short_rows, 2 * PAD + short_rows, PAD + short_rows, long_rows),
    )
    own_short, own_long = TILE // 2, TILE
    owned = own_short + own_long
    quarter = own_short // 2
    gm[...] = jnp.zeros_like(gm)
    gck[...] = jnp.zeros_like(gck)
    gnp[...] = jnp.zeros_like(gnp)
    pick = jnp.where(
        (lax.broadcasted_iota(jnp.int32, (8, LANES), 1) < HEAD_DIM)
        == (lax.broadcasted_iota(jnp.int32, (8, LANES), 0) == 0),
        1.0,
        0.0,
    ).astype(F32)

    def row_sums(product):
        return lax.dot_general(
            pick, product, (((1,), (1,)), ((), ())),
            preferred_element_type=F32, precision=lax.Precision.HIGHEST,
        )

    def unpack(packed):
        wide = packed.astype(F32)
        return jnp.concatenate([wide, pltpu.roll(wide, HEAD_DIM, 1)], axis=0)

    for part, (_, base, _, _, total) in enumerate(parts):
        for block in range(total // TILE):
            rows = slice(base + block * TILE, base + (block + 1) * TILE)
            if part == 0:
                grad_pair = jnp.concatenate([grecv[2 * block, 0:own_short], grecv[2 * block + 1, 0:own_short]], axis=0)
                out_pair = jnp.concatenate([osend[2 * block, 0:own_short], osend[2 * block + 1, 0:own_short]], axis=0)
                grad_one = jnp.concatenate(
                    [unpack(grecv[2 * block + side, owned : owned + quarter]) for side in range(2)], axis=0
                )
                out_one = jnp.concatenate(
                    [unpack(osend[2 * block + side, owned : owned + quarter]) for side in range(2)], axis=0
                )
            else:
                grad_pair = grecv[block, own_short:owned]
                out_pair = osend[block, own_short:owned]
                grad_one = unpack(grecv[block, owned + quarter :])
                out_one = unpack(osend[block, owned + quarter :])
            low_half = lane_iota(TILE) < HEAD_DIM
            grad_pair = grad_pair.astype(F32)
            grad_one = jnp.where(low_half, grad_one, 0.0)
            do[0, rows] = jnp.where(low_half, grad_pair, 0.0).astype(BF16)
            do[1, rows] = jnp.where(low_half, 0.0, grad_pair).astype(BF16)
            do[2, rows] = grad_one.astype(BF16)
            sums = row_sums(grad_pair * out_pair.astype(F32))
            delta[0, :, rows] = sums[0:1]
            delta[1, :, rows] = sums[1:2]
            delta[2, :, rows] = row_sums(grad_one * out_one)[0:1]

    causal = lax.broadcasted_iota(jnp.int32, (TILE, TILE), 0) <= lax.broadcasted_iota(jnp.int32, (TILE, TILE), 1)

    @pl.loop(0, 3)
    def _(head):
        pair = head // 2
        own_lanes = (lane_iota(TILE) < HEAD_DIM) == (head != 1)
        k_lanes = pl.ds(pl.multiple_of((2 + pair) * LANES, LANES), LANES)
        v_lanes = pl.ds(pl.multiple_of((4 + pair) * LANES, LANES), LANES)
        for _, base, _, gbase, total in parts:
            for block in range(total // TILE):
                rows = slice(base + block * TILE, base + (block + 1) * TILE)
                query = qa[head, rows]
                bare = jnp.where(own_lanes, query.astype(F32), 0.0).astype(BF16)
                grad_out = do[head, rows]
                stat, less = lse[head, :, rows], delta[head, :, rows]
                spans = [(block * TILE, TILE, True)]
                if block:
                    spans.append((0, block * TILE, False))
                grad_q = jnp.zeros((HEAD_DIM, TILE), F32)
                for start, size, masked in spans:
                    keys = slice(base + start, base + start + size)
                    into = slice(gbase + start, gbase + start + size)
                    scores = dot_nt(ka[head, keys], query)
                    if masked:
                        scores = jnp.where(causal, scores, NEG_FILL)
                    probs = jnp.exp(scores - stat)
                    grad_probs = dot_nt(vb[pair, keys], grad_out)
                    gm[into, v_lanes] += dot_nn(probs.astype(BF16), grad_out)
                    grad_scores = (probs * (grad_probs - less)).astype(BF16)
                    gm[into, k_lanes] += dot_nn(grad_scores, bare)
                    grad_q = grad_q + dot_nn(kt[head, :, keys], grad_scores)
                dqt[head, :, rows] = 0.125 * grad_q

    for _, base, _, gbase, total in parts:

        @pl.loop(0, total // TILE)
        def _(step, base=base, gbase=gbase):
            start = pl.multiple_of(step * TILE, TILE)
            rows = pl.ds(pl.multiple_of(base + start, TILE), TILE)
            into = pl.ds(pl.multiple_of(gbase + start, PAD), TILE)
            gm[into, 0:128] = jnp.concatenate([dqt[0, :, rows], dqt[1, :, rows]], axis=0).T
            one = dqt[2, :, rows]
            gm[into, 128:256] = jnp.concatenate([one, jnp.zeros_like(one)], axis=0).T

    for part, (x_ref, base, pbase, gbase, total) in enumerate(parts):

        @pl.loop(0, total // TILE)
        def _(step, part=part, x_ref=x_ref, base=base, pbase=pbase, gbase=gbase):
            start = pl.multiple_of(step * TILE, TILE)
            rows = pl.ds(pl.multiple_of(base + start, TILE), TILE)
            window = gm[pl.ds(pl.multiple_of(gbase + start, PAD), TILE + PAD)]
            grad = window[:TILE]
            projected_grad = (
                ck_ref[0:1] * grad
                + ck_ref[1:2] * shifted(window, -1)[:TILE]
                + ck_ref[2:3] * shifted(window, -2)[:TILE]
            ).astype(BF16)
            gproj[rows] = projected_grad
            past = proj[pl.ds(pl.multiple_of(pbase - PAD + start, PAD), TILE + PAD)].astype(F32)
            gck[0:1] += jnp.sum(grad * past[PAD:], axis=0, keepdims=True)
            gck[1:2] += jnp.sum(grad * shifted(past, 1)[PAD:], axis=0, keepdims=True)
            gck[2:3] += jnp.sum(grad * shifted(past, 2)[PAD:], axis=0, keepdims=True)
            grad_normed = dot_nt(projected_grad, wq_ref[...])
            normal, _ = normalise(x_ref[pl.ds(start, TILE)].astype(F32))
            gnp[0:1] += jnp.sum(grad_normed * normal, axis=0, keepdims=True)
            gnp[1:2] += jnp.sum(grad_normed, axis=0, keepdims=True)
            low = grad_normed.astype(BF16)
            if part == 0:
                gn_ref[2 * step, 0:own_short] = low[:own_short]
                gn_ref[2 * step + 1, 0:own_short] = low[own_short:]
            else:
                gn_ref[step, own_short:] = low

    for start in range(0, normed.shape[1], TILE):
        gwq[start : start + TILE] = dot_tn(normed[:, start : start + TILE], gproj[...]).astype(BF16)


def back_part(xs, xl, normed, proj, qa, ka, vb, kt, lse, osend, grecv, wq, ck, norms, count):
    total = xs.shape[0] + xl.shape[0]
    width = xs.shape[1]
    out = jax.ShapeDtypeStruct
    return pl.pallas_call(
        back_kernel,
        out_shape=(
            out((count, total // count, width), BF16),
            out(wq.shape, BF16),
            out((8, wq.shape[1]), F32),
            out((8, width), F32),
        ),
        in_specs=[vmem()] * 14,
        out_specs=tuple([vmem()] * 4),
        scratch_shapes=[
            pltpu.VMEM((3, total, LANES), BF16),
            pltpu.VMEM((3, 1, total), F32),
            pltpu.VMEM((3, HEAD_DIM, total), F32),
            pltpu.VMEM((total + 2 * PAD, 6 * LANES), F32),
            pltpu.VMEM((total, 6 * LANES), BF16),
        ],
        compiler_params=params_of(),
    )(xs, xl, normed, proj, qa, ka, vb, kt, lse, osend, grecv, wq, ck, norms)


def group_blocks(rows_of):
    rows = rows_of.shape[0]
    blocks = rows_of.reshape(rows, 3, 2, 3, LANES)
    pair = blocks[:, :, :, 0:2]
    one = blocks[:, :, :, 2].reshape(rows, 3, 2, 2, HEAD_DIM)
    both = jnp.concatenate([pair, one, jnp.zeros_like(one)], axis=-1)
    return both.transpose(2, 3, 0, 1, 4).reshape(2, 2, rows, 6 * LANES)


def ungroup(groups):
    rows = groups.shape[1]
    blocks = groups.reshape(2, 2, rows, 3, 2, LANES).transpose(2, 3, 0, 1, 4, 5)
    pairs = blocks[:, :, :, :, 0].reshape(rows, 3, 2, 2 * LANES)
    ones = blocks[:, :, :, :, 1, :HEAD_DIM].reshape(rows, 3, 2, LANES)
    return jnp.concatenate([pairs, ones], axis=-1).reshape(rows, 18 * LANES)


def split_body(
    x_short, x_long, lengths, cot_short, cot_long, w_qkv, w_out, w_up, w_down, conv_kernel, norm_params
):
    count = lax.axis_size("seq")
    index = lax.axis_index("seq")
    half, chip, core = index // 4, (index // 2) % 2, index % 2
    taps, part = conv_kernel.shape
    width = x_short.shape[2]
    cut = norm_params.shape[1]
    small = jnp.zeros((8, LANES), F32)
    small = small.at[0:taps, 0:part].set(conv_kernel.astype(F32))
    small = small.at[taps : taps + 4, 0:cut].set(norm_params.astype(F32))
    xs, xl, smalls, wq, full_out, full_up, full_down = gather_all(
        x_short, x_long, (small, group_blocks(w_qkv), w_out, w_up, w_down), count
    )
    smalls = smalls.reshape(-1, 8, LANES)
    kernel = smalls[:, 0:taps, 0:part].transpose(1, 0, 2).reshape(taps, 3 * width)
    norms = smalls[:, taps : taps + 4, 0:cut].transpose(1, 0, 2).reshape(4, width)
    ck = lax.dynamic_index_in_dim(
        group_blocks(kernel).reshape(4, taps, 6 * LANES), 2 * chip + core, 0, keepdims=False
    )
    wq = lax.dynamic_index_in_dim(wq, core, 4, keepdims=False).reshape(width, 6 * LANES)
    lens = lax.dynamic_index_in_dim(lengths, half, 1, keepdims=False)
    osend, qa, ka, vb, kt, proj, normed, lse = front(lens, xs, xl, wq, ck, norms, count)
    recv = exchange(osend, 1)
    y_short, y_long, gmid, gsend, gwo, gwu, gwd, gnorm = middle_part(
        x_short, x_long, recv, cot_short, cot_long,
        full_out.reshape(width, -1), full_up.reshape(width, -1), full_down.reshape(-1, width), norms,
    )
    grecv = exchange(gsend, 2)
    gn, gwq, gck, gnp = back_part(
        xs, xl, normed, proj, qa, ka, vb, kt, lse, osend, grecv, wq, ck, norms, count
    )
    own = jnp.arange(4)[:, None, None] == 2 * chip + core
    grad_kernel = ungroup(jnp.where(own, gck[0:taps][None], 0.0))
    grad_norm = jnp.concatenate([gnp[0:2], gnorm[0:2]], axis=0)
    devices = smalls.shape[0]
    small_grads = jnp.zeros((devices, 8, LANES), F32)
    small_grads = small_grads.at[:, 0:taps, 0:part].set(grad_kernel.reshape(taps, devices, part).transpose(1, 0, 2))
    small_grads = small_grads.at[:, taps : taps + 4, 0:cut].set(grad_norm.reshape(4, devices, cut).transpose(1, 0, 2))

    def cut_up(value):
        return value.reshape(4, 2, 2, 2, value.shape[0] // devices, value.shape[1])

    grad_normed, sum_qkv, sum_out, sum_up, sum_down, sum_small = sum_all(
        gn, (cut_up(gwq), cut_up(gwo), cut_up(gwu), cut_up(gwd), small_grads.reshape(4, 2, 2, 2, 8, LANES))
    )
    short = x_short.shape[1]
    gmid = gmid.reshape(2, -1, gmid.shape[1])
    dx = []
    for x, rows in ((x_short, slice(0, short)), (x_long, slice(short, None))):
        normal, inverse = normalise(x.astype(F32))
        dx.append(gmid[:, rows] + norm_back(grad_normed[:, rows], normal, inverse, norms[0]))
    return (
        y_short, y_long, dx[0], dx[1], ungroup(sum_qkv), sum_out, sum_up, sum_down,
        sum_small[0:taps, 0:part], sum_small[taps : taps + 4, 0:cut],
    )


GROUP_HEADS = 2


def from_behind(value, axis, by):
    count = lax.axis_size(axis)
    pairs = [(i, i + by) for i in range(count) if 0 <= i + by < count]
    return lax.ppermute(value, axis, pairs)


def layer_norm(values, gain, offset_term):
    average = jnp.mean(values, axis=-1, keepdims=True)
    centred = values - average
    inverse = lax.rsqrt(jnp.mean(centred * centred, axis=-1, keepdims=True) + EPS)
    normal = centred * inverse
    return (normal * gain + offset_term, normal, inverse)


def norm_back_flat(grad, normal, inverse, gain):
    scaled_grad = grad * gain
    first_mean = jnp.mean(scaled_grad, axis=-1, keepdims=True)
    second_mean = jnp.mean(scaled_grad * normal, axis=-1, keepdims=True)
    return inverse * (scaled_grad - first_mean - normal * second_mean)


def front_part(inputs, full_weights):
    w_qkv = full_weights[0]
    kernel = full_weights[4].astype(jnp.float32)
    params = full_weights[5].astype(jnp.float32)
    saved = []
    tails = []
    for part_in in inputs:
        seq_count, block_rows, model_width = part_in.shape
        flat = part_in.reshape(seq_count * block_rows, model_width).astype(jnp.float32)
        normed, normal, inverse = layer_norm(flat, params[0], params[1])
        normed_low = normed.astype(jnp.bfloat16)
        projected = jnp.dot(normed_low, w_qkv, preferred_element_type=jnp.float32).astype(
            jnp.bfloat16
        )
        projected = projected.reshape(seq_count, block_rows, 3 * model_width)
        saved.append((flat, normal, inverse, normed_low, projected))
        tails.append(projected[:, block_rows - 2 :])
    received = from_behind((tails[0], tails[1]), "seq", 1)
    fronts = []
    for index_part in range(2):
        flat, normal, inverse, normed_low, projected = saved[index_part]
        block_rows = projected.shape[1]
        padded = jnp.concatenate([received[index_part], projected], axis=1).astype(jnp.float32)
        mixed = (
            kernel[0] * padded[:, 2:]
            + kernel[1] * padded[:, 1 : block_rows + 1]
            + kernel[2] * padded[:, :block_rows]
        )
        fronts.append((flat, normal, inverse, normed_low, padded, mixed.astype(jnp.bfloat16)))
    return fronts


def attend_block(queries, key_rows, value_rows, usable, grad_heads):
    scaling = queries.shape[-1] ** (-0.5)
    scores = jnp.einsum("sqhd,skhd->shqk", queries, key_rows, preferred_element_type=jnp.float32)
    masked = jnp.where(usable, scaling * scores, NEG_FILL)
    exp_terms = jnp.exp(masked - jnp.max(masked, axis=-1, keepdims=True))
    attn_probs = exp_terms / jnp.sum(exp_terms, axis=-1, keepdims=True)
    probs_low = attn_probs.astype(jnp.bfloat16)
    if grad_heads is None:
        attended = jnp.einsum(
            "shqk,skhd->sqhd", probs_low, value_rows, preferred_element_type=jnp.float32
        )
        return attended.astype(jnp.bfloat16)
    grad_probs = jnp.einsum(
        "sqhd,skhd->shqk", grad_heads, value_rows, preferred_element_type=jnp.float32
    )
    grad_values = jnp.einsum(
        "shqk,sqhd->skhd", probs_low, grad_heads, preferred_element_type=jnp.float32
    )
    row_delta = jnp.sum(attn_probs * grad_probs, axis=-1, keepdims=True)
    grad_scores = (scaling * attn_probs * (grad_probs - row_delta)).astype(jnp.bfloat16)
    grad_queries = jnp.einsum(
        "shqk,skhd->sqhd", grad_scores, key_rows, preferred_element_type=jnp.float32
    )
    grad_keys = jnp.einsum(
        "shqk,sqhd->skhd", grad_scores, queries, preferred_element_type=jnp.float32
    )
    return (grad_queries, grad_keys, grad_values)


def make_usable(query_pos, key_pos, seq_lengths):
    usable = (key_pos[None, None, :] <= query_pos[None, :, None]) & (
        key_pos[None, None, :] < seq_lengths[:, None, None]
    )
    return usable[:, None]


def attention(mixed, kv_full, seq_lengths, offset, grad_attended):
    seq_count, block_rows, three_width = mixed.shape
    model_width = three_width // 3
    full_len = kv_full.shape[1]
    queries = mixed[:, :, :model_width].reshape(seq_count, block_rows, -1, HEAD_DIM)
    key_rows = kv_full[:, :, :model_width].reshape(seq_count, full_len, -1, HEAD_DIM)
    value_rows = kv_full[:, :, model_width:].reshape(seq_count, full_len, -1, HEAD_DIM)
    positions = offset + jnp.arange(block_rows, dtype=jnp.int32)
    key_pos = jnp.arange(full_len, dtype=jnp.int32)
    usable = make_usable(positions, key_pos, seq_lengths)
    heads_total = queries.shape[2]
    grad_heads = None
    if grad_attended is not None:
        grad_heads = grad_attended.reshape(seq_count, block_rows, -1, HEAD_DIM)
    results = []
    for first_head in range(0, heads_total, GROUP_HEADS):
        last_head = first_head + GROUP_HEADS
        grad_part = None if grad_heads is None else grad_heads[:, :, first_head:last_head]
        results.append(
            attend_block(
                queries[:, :, first_head:last_head],
                key_rows[:, :, first_head:last_head],
                value_rows[:, :, first_head:last_head],
                usable,
                grad_part,
            )
        )
    if grad_heads is None:
        return jnp.concatenate(results, axis=2).reshape(seq_count, block_rows, model_width)
    grad_queries = jnp.concatenate([entry_set[0] for entry_set in results], axis=2).reshape(
        seq_count, block_rows, model_width
    )
    grad_keys = jnp.concatenate([entry_set[1] for entry_set in results], axis=2).reshape(
        seq_count, full_len, model_width
    )
    grad_values = jnp.concatenate([entry_set[2] for entry_set in results], axis=2).reshape(
        seq_count, full_len, model_width
    )
    return (grad_queries, grad_keys, grad_values)


def rest_part(front, kv_full, seq_lengths, offset, full_weights, cotangent_in):
    w_out, w_up, w_down = (full_weights[1], full_weights[2], full_weights[3])
    params = full_weights[5].astype(jnp.float32)
    flat, normal_one, inverse_one, normed_low, padded, mixed = front
    seq_count, block_rows, three_width = mixed.shape
    model_width = three_width // 3
    attended = attention(mixed, kv_full, seq_lengths, offset, None).reshape(
        seq_count * block_rows, model_width
    )
    middle = flat + jnp.dot(attended, w_out, preferred_element_type=jnp.float32)
    second, normal_two, inverse_two = layer_norm(middle, params[2], params[3])
    second_low = second.astype(jnp.bfloat16)
    upper = jnp.dot(second_low, w_up, preferred_element_type=jnp.float32)
    hidden = jnp.square(jnp.maximum(upper, 0.0)).astype(jnp.bfloat16)
    if cotangent_in is None:
        result_rows = middle + jnp.dot(hidden, w_down, preferred_element_type=jnp.float32)
        return result_rows.astype(jnp.bfloat16).reshape(seq_count, block_rows, model_width)
    cotangent = cotangent_in.reshape(seq_count * block_rows, model_width)
    grad_down = jnp.dot(hidden.T, cotangent, preferred_element_type=jnp.float32)
    grad_hidden = jnp.dot(cotangent, w_down.T, preferred_element_type=jnp.float32)
    grad_upper = (2.0 * jnp.maximum(upper, 0.0) * grad_hidden).astype(jnp.bfloat16)
    grad_up = jnp.dot(second_low.T, grad_upper, preferred_element_type=jnp.float32)
    grad_second = jnp.dot(grad_upper, w_up.T, preferred_element_type=jnp.float32)
    grad_middle = cotangent.astype(jnp.float32) + norm_back_flat(
        grad_second, normal_two, inverse_two, params[2]
    )
    grad_middle_low = grad_middle.astype(jnp.bfloat16)
    grad_out = jnp.dot(attended.T, grad_middle_low, preferred_element_type=jnp.float32)
    grad_attended = jnp.dot(grad_middle_low, w_out.T, preferred_element_type=jnp.float32).astype(
        jnp.bfloat16
    )
    grad_attended = grad_attended.reshape(seq_count, block_rows, model_width)
    grad_queries, grad_keys, grad_values = attention(
        mixed, kv_full, seq_lengths, offset, grad_attended
    )
    key_term = jnp.concatenate([grad_keys, grad_values], axis=-1)
    norm_two = (jnp.sum(grad_second * normal_two, axis=0), jnp.sum(grad_second, axis=0))
    return (grad_queries, key_term, grad_middle, grad_out, grad_up, grad_down, norm_two)


def general_body(
    x_short,
    x_long,
    lengths,
    cot_short,
    cot_long,
    w_qkv,
    w_out,
    w_up,
    w_down,
    conv_kernel,
    norm_params,
):
    full_weights = (
        lax.all_gather(w_qkv, ("seq", "batch"), axis=0, tiled=True),
        lax.all_gather(w_out, ("seq", "batch"), axis=0, tiled=True),
        lax.all_gather(w_up, ("seq", "batch"), axis=0, tiled=True),
        lax.all_gather(w_down, ("seq", "batch"), axis=0, tiled=True),
        lax.all_gather(conv_kernel, ("seq", "batch"), axis=1, tiled=True),
        lax.all_gather(norm_params, ("seq", "batch"), axis=1, tiled=True),
    )
    inputs = (x_short, x_long)
    cotangents = (cot_short, cot_long)
    model_width = x_short.shape[2]
    offsets = (lax.axis_index("seq") * x_short.shape[1], lax.axis_index("seq") * x_long.shape[1])
    fronts = front_part(inputs, full_weights)
    kv_fwd = (
        lax.all_gather(fronts[0][5][:, :, model_width:], "seq", axis=1, tiled=True),
        lax.all_gather(fronts[1][5][:, :, model_width:], "seq", axis=1, tiled=True),
    )
    outputs = [
        rest_part(
            fronts[index_part],
            kv_fwd[index_part],
            lengths[index_part],
            offsets[index_part],
            full_weights,
            None,
        )
        for index_part in range(2)
    ]
    back_weights = (
        lax.all_gather(w_qkv, ("seq", "batch"), axis=0, tiled=True),
        lax.all_gather(w_out, ("seq", "batch"), axis=0, tiled=True),
        lax.all_gather(w_up, ("seq", "batch"), axis=0, tiled=True),
        lax.all_gather(w_down, ("seq", "batch"), axis=0, tiled=True),
        lax.all_gather(conv_kernel, ("seq", "batch"), axis=1, tiled=True),
        lax.all_gather(norm_params, ("seq", "batch"), axis=1, tiled=True),
    )
    fronts_back = front_part(inputs, back_weights)
    kv_back = (
        lax.all_gather(fronts_back[0][5][:, :, model_width:], "seq", axis=1, tiled=True),
        lax.all_gather(fronts_back[1][5][:, :, model_width:], "seq", axis=1, tiled=True),
    )
    partials = [
        rest_part(
            fronts_back[index_part],
            kv_back[index_part],
            lengths[index_part],
            offsets[index_part],
            back_weights,
            cotangents[index_part],
        )
        for index_part in range(2)
    ]
    kv_grads = (
        lax.psum_scatter(
            partials[0][1].astype(jnp.bfloat16), "seq", scatter_dimension=1, tiled=True
        ).astype(jnp.float32),
        lax.psum_scatter(
            partials[1][1].astype(jnp.bfloat16), "seq", scatter_dimension=1, tiled=True
        ).astype(jnp.float32),
    )
    grad_mixed = [
        jnp.concatenate([partials[index_part][0], kv_grads[index_part]], axis=-1)
        for index_part in range(2)
    ]
    received = (
        from_behind(grad_mixed[0][:, :2].astype(jnp.bfloat16), "seq", -1).astype(jnp.float32),
        from_behind(grad_mixed[1][:, :2].astype(jnp.bfloat16), "seq", -1).astype(jnp.float32),
    )
    kernel = back_weights[4].astype(jnp.float32)
    params = back_weights[5].astype(jnp.float32)
    w_qkv_full = back_weights[0]
    grad_qkv = jnp.zeros(w_qkv_full.shape, jnp.float32)
    grad_kernel = jnp.zeros(kernel.shape, jnp.float32)
    grad_norm = jnp.zeros((4, model_width), jnp.float32)
    grad_out = partials[0][3] + partials[1][3]
    grad_up = partials[0][4] + partials[1][4]
    grad_down = partials[0][5] + partials[1][5]
    input_grads = []
    for index_part in range(2):
        flat, normal_one, inverse_one, normed_low, padded, mixed = fronts_back[index_part]
        seq_count, block_rows, three_width = mixed.shape
        mixed_grad = grad_mixed[index_part]
        extended = jnp.concatenate([mixed_grad, received[index_part]], axis=1)
        grad_projected = (
            kernel[0] * extended[:, :block_rows]
            + kernel[1] * extended[:, 1 : block_rows + 1]
            + kernel[2] * extended[:, 2:]
        ).astype(jnp.bfloat16)
        grad_kernel = grad_kernel + jnp.stack(
            [
                jnp.sum(mixed_grad * padded[:, 2:], axis=(0, 1)),
                jnp.sum(mixed_grad * padded[:, 1 : block_rows + 1], axis=(0, 1)),
                jnp.sum(mixed_grad * padded[:, :block_rows], axis=(0, 1)),
            ]
        )
        grad_flat = grad_projected.reshape(seq_count * block_rows, three_width)
        grad_qkv = grad_qkv + jnp.dot(normed_low.T, grad_flat, preferred_element_type=jnp.float32)
        grad_normed = jnp.dot(grad_flat, w_qkv_full.T, preferred_element_type=jnp.float32)
        grad_input = partials[index_part][2] + norm_back_flat(
            grad_normed, normal_one, inverse_one, params[0]
        )
        input_grads.append(grad_input.reshape(seq_count, block_rows, model_width))
        norm_two = partials[index_part][6]
        grad_norm = grad_norm + jnp.stack(
            [
                jnp.sum(grad_normed * normal_one, axis=0),
                jnp.sum(grad_normed, axis=0),
                norm_two[0],
                norm_two[1],
            ]
        )
    summed = (
        lax.psum_scatter(grad_qkv, ("seq", "batch"), scatter_dimension=0, tiled=True),
        lax.psum_scatter(grad_out, ("seq", "batch"), scatter_dimension=0, tiled=True),
        lax.psum_scatter(grad_up, ("seq", "batch"), scatter_dimension=0, tiled=True),
        lax.psum_scatter(grad_down, ("seq", "batch"), scatter_dimension=0, tiled=True),
        lax.psum_scatter(grad_kernel, ("seq", "batch"), scatter_dimension=1, tiled=True),
        lax.psum_scatter(grad_norm, ("seq", "batch"), scatter_dimension=1, tiled=True),
    )
    return (
        outputs[0],
        outputs[1],
        input_grads[0],
        input_grads[1],
        summed[0],
        summed[1],
        summed[2],
        summed[3],
        summed[4],
        summed[5],
    )


def solution(mesh):
    split = mesh.shape["seq"] == 8
    return jax.shard_map(
        split_body if split else general_body,
        mesh=mesh,
        in_specs=(
            P("batch", "seq", None),
            P("batch", "seq", None),
            P(None, "batch"),
            P("batch", "seq", None),
            P("batch", "seq", None),
            P(("seq", "batch"), None),
            P(("seq", "batch"), None),
            P(("seq", "batch"), None),
            P(("seq", "batch"), None),
            P(None, ("seq", "batch")),
            P(None, ("seq", "batch")),
        ),
        out_specs=(
            P("batch", "seq", None),
            P("batch", "seq", None),
            P("batch", "seq", None),
            P("batch", "seq", None),
            P(("seq", "batch"), None),
            P(("seq", "batch"), None),
            P(("seq", "batch"), None),
            P(("seq", "batch"), None),
            P(None, ("seq", "batch")),
            P(None, ("seq", "batch")),
        ),
        check_vma=False,
    )
```

```python
import functools

import jax
import jax.numpy as jnp
from jax import lax
from jax.experimental import pallas as pl
from jax.experimental.pallas import tpu as pltpu
from jax.sharding import PartitionSpec as P

EPS = 1e-05
NEG_FILL = -1e30
HEAD_DIM = 64
LANES = 128
TRIPLE = 3 * LANES
TILE = 256
PAD = 16
MESH = pl.DeviceIdType.MESH
F32 = jnp.float32
BF16 = jnp.bfloat16
DMA = pltpu.SemaphoreType.DMA


def dot_nn(left, right):
    return lax.dot_general(left, right, (((1,), (0,)), ((), ())), preferred_element_type=F32)


def dot_nt(left, right):
    return lax.dot_general(left, right, (((1,), (1,)), ((), ())), preferred_element_type=F32)


def dot_tn(left, right):
    return lax.dot_general(left, right, (((0,), (0,)), ((), ())), preferred_element_type=F32)


def params_of(limit=60, **more):
    return pltpu.CompilerParams(vmem_limit_bytes=limit * 2**20, **more)


def vmem():
    return pl.BlockSpec(memory_space=pltpu.VMEM)


def smem():
    return pl.BlockSpec(memory_space=pltpu.SMEM)


def hbm():
    return pl.BlockSpec(memory_space=pl.ANY)


def normalise(values):
    average = jnp.mean(values, axis=-1, keepdims=True)
    centred = values - average
    inverse = lax.rsqrt(jnp.mean(centred * centred, axis=-1, keepdims=True) + EPS)
    return centred * inverse, inverse


def norm_back(grad, normal, inverse, gain):
    scaled_grad = grad * gain
    first_mean = jnp.mean(scaled_grad, axis=-1, keepdims=True)
    second_mean = jnp.mean(scaled_grad * normal, axis=-1, keepdims=True)
    return inverse * (scaled_grad - first_mean - normal * second_mean)


def shifted(window, by):
    return pltpu.roll(window, by % window.shape[0], 0)


def iota(shape, axis):
    return lax.broadcasted_iota(jnp.int32, shape, axis)


def times(index, size):
    return pl.ds(pl.multiple_of(index * size, size), size)


def position():
    index, batch = lax.axis_index("seq"), lax.axis_index("batch")
    return index // 2, index % 2, batch // 2, batch % 2


def at(z, core, y, x):
    return (z * 2 + core, y * 2 + x)


def remote(src, dst, send, recv, device):
    return pltpu.make_async_remote_copy(
        src_ref=src, dst_ref=dst, send_sem=send, recv_sem=recv, device_id=device, device_id_type=MESH
    )


def greet(others):
    barrier = pltpu.get_barrier_semaphore()
    for other in others:
        pl.semaphore_signal(barrier, inc=1, device_id=other, device_id_type=MESH)
    pl.semaphore_wait(barrier, len(others))


def whole_line():
    z, core, y, x = position()
    line = [at(lax.rem(z + step, 4), (core + turn) % 2, y, x) for turn in (0, 1) for step in (0, 1, 2, 3)]
    return line[1:]


def greet_all():
    z, core, y, x = position()
    greet(whole_line() + [at(z, core, 1 - y, x), at(z, core, y, 1 - x)])


def roles():
    z = lax.axis_index("seq") // 2
    half = z // 2
    near = jnp.where(half == 0, z, 3 - z)
    partner_z = jnp.where(half == 0, 1 - z, 5 - z)
    return half, near, partner_z, 2 - half


def z_of(half, place):
    return jnp.where(half == 0, place, 3 - place)


def long_source(seq, pair):
    near = 1 if pair % 3 == 2 else 0
    z = near if seq == 0 else 3 - near
    return z * 2 + pair // 3, 0 if near else pair % 3


def short_source(seq, pair):
    return (1 if seq == 0 else 2) * 2 + pair // 3, pair % 3


class Copies:
    def __init__(self, sems):
        self.sems, self.count, self.open = sems, 0, []

    def start(self, src, dst):
        copy = pltpu.make_async_copy(src, dst, self.sems.at[self.count])
        self.count += 1
        copy.start()
        self.open.append(copy)
        return copy

    def finish(self):
        for copy in self.open:
            copy.wait()
        self.open = []


class RowGather:
    def __init__(self, x_ref, o_ref, own_sem, send, recv, sib_send, sib_recv, inner_only):
        self.x_ref, self.o_ref, self.inner_only = x_ref, o_ref, inner_only
        self.own_sem, self.send, self.recv, self.sib_send, self.sib_recv = own_sem, send, recv, sib_send, sib_recv
        self.rows = x_ref.shape[1]
        self.z, self.core, self.y, self.x = position()
        self.half, self.near, self.partner_z, far_z = roles()
        self.sibling = at(self.z, 1 - self.core, self.y, self.x)
        self.partner = at(self.partner_z, self.core, self.y, self.x)
        place = self.block(self.z, self.core)
        mine, other = self.x_ref.at[self.half], self.x_ref.at[1 - self.half]
        self.to_partner = remote(mine, place, send.at[0], recv.at[self.near], self.partner)
        self.to_far = remote(other, place, send.at[1], recv.at[3 - self.near], at(far_z, self.core, self.y, self.x))
        self.to_sibling = remote(mine, place, sib_send.at[0], sib_recv.at[self.near], self.sibling)
        self.own = pltpu.make_async_copy(mine, place, own_sem)

    def block(self, z, core):
        return self.o_ref.at[times(z * 2 + core, self.rows)]

    def at_inner(self, act):
        if self.inner_only:
            pl.when(self.near == 1)(act)
        else:
            act()

    def start(self):
        if self.inner_only:
            pl.when(self.near == 0)(self.to_partner.start)
        else:
            self.to_partner.start()
        self.to_far.start()

        def inside():
            self.to_sibling.start()
            self.own.start()

        self.at_inner(inside)

    def moves(self, slot):
        place = (1 - self.near, 2, 3)[slot]
        block = self.block(z_of(self.half, place), self.core)
        arrival = remote(block, block, self.send.at[0], self.recv.at[place], self.partner)
        onward = remote(block, block, self.send.at[1 + slot], self.recv.at[place], self.partner)
        across = remote(block, block, self.sib_send.at[1 + slot], self.sib_recv.at[place], self.sibling)
        return arrival, onward, across

    def step(self, slot):
        arrival, onward, across = self.moves(slot)

        def inside():
            arrival.wait_recv()
            if slot and not self.inner_only:
                pl.when(self.near == 1)(onward.start)
            across.start()

        self.at_inner(inside)

    def whole(self, place):
        where = (self.near, 1 - self.near, 2, 3)[place]
        block = self.block(z_of(self.half, where), 1 - self.core)

        def inside():
            remote(block, block, self.sib_send.at[0], self.sib_recv.at[where], self.sibling).wait_recv()
            if place == 0:
                self.own.wait()

        self.at_inner(inside)

    def chip_rows(self, place):
        return z_of(self.half, (self.near, 1 - self.near, 2, 3)[place])

    def finish(self):
        if self.inner_only:
            pl.when(self.near == 0)(self.to_partner.wait_send)
        else:
            self.to_partner.wait_send()
        self.to_far.wait_send()

        def inside():
            self.to_sibling.wait_send()
            for slot in range(3):
                _, onward, across = self.moves(slot)
                across.wait_send()
                if slot and not self.inner_only:
                    pl.when(self.near == 1)(onward.wait_send)

        self.at_inner(inside)


class ShardGather:
    def __init__(self, shard, full, own_sem, send, recv, halves=False):
        self.shard, self.full, self.own_sem, self.send_sem, self.recv_sem = shard, full, own_sem, send, recv
        self.z, self.core, self.y, self.x = position()
        self.halves = halves
        self.sent = []

    def go(self, src, dst, slot, device):
        copy = remote(src, dst, self.send_sem.at[slot], self.recv_sem.at[slot], device)
        copy.start()
        self.sent.append(copy)

    def arrived(self, dst, slot):
        remote(dst, dst, self.send_sem.at[0], self.recv_sem.at[slot], at(self.z, self.core, self.y, self.x)).wait_recv()

    def start(self):
        z, core, y, x = self.z, self.core, self.y, self.x
        mine = self.full.at[z, core, y, x]
        for step in (1, 2, 3):
            target = lax.rem(z + step, 4)
            self.go(self.shard, mine, step, at(target, core, y, x))
        self.own = pltpu.make_async_copy(self.shard, mine, self.own_sem)
        self.own.start()

    def part(self, core, zs, ys, xs, reader):
        ref = self.full.at[zs, core, ys, xs]
        return self.full.at[zs, core, ys, xs, reader] if self.halves else ref

    def across(self, zs, ys, xs, slot):
        ref = self.part(self.core, zs, ys, xs, 1 - self.core)
        self.go(ref, ref, slot, at(self.z, 1 - self.core, self.y, self.x))

    def over(self):
        z, core, y, x = self.z, self.core, self.y, self.x
        for step in (1, 2, 3):
            self.arrived(self.full.at[lax.rem(z + 4 - step, 4), core, y, x], step)
        self.own.wait()
        first, second = pl.ds(0, 2), pl.ds(2, 2)
        ref = self.full.at[first, core, y, x]
        self.go(ref, ref, 4, at(z, core, y, 1 - x))
        ref = self.full.at[second, core, y, x]
        self.go(ref, ref, 5, at(z, core, 1 - y, x))
        self.across(pl.ds(0, 4), y, x, 8)

    def turn(self):
        z, core, y, x = self.z, self.core, self.y, self.x
        first, second = pl.ds(0, 2), pl.ds(2, 2)
        self.arrived(self.full.at[first, core, y, 1 - x], 4)
        ref = self.full.at[first, core, y]
        self.go(ref, ref, 6, at(z, core, 1 - y, x))
        self.across(first, y, 1 - x, 9)
        self.arrived(self.full.at[second, core, 1 - y, x], 5)
        ref = self.full.at[second, core, :, x]
        self.go(ref, ref, 7, at(z, core, y, 1 - x))
        self.across(second, 1 - y, x, 10)

    def last(self):
        core, y, x = self.core, self.y, self.x
        first, second = pl.ds(0, 2), pl.ds(2, 2)
        self.arrived(self.full.at[first, core, 1 - y], 6)
        self.across(first, 1 - y, pl.ds(0, 2), 11)
        self.arrived(self.full.at[second, core, :, 1 - x], 7)
        self.across(second, pl.ds(0, 2), 1 - x, 12)

    def finish(self):
        y, x, core, other = self.y, self.x, self.core, 1 - self.core
        first, second, both = pl.ds(0, 2), pl.ds(2, 2), pl.ds(0, 2)
        parts = (
            (pl.ds(0, 4), y, x), (first, y, 1 - x), (second, 1 - y, x), (first, 1 - y, both), (second, both, 1 - x),
        )
        for slot, (zs, ys, xs) in enumerate(parts):
            self.arrived(self.part(other, zs, ys, xs, core), 8 + slot)

    def sends_done(self):
        for copy in self.sent:
            copy.wait_send()


def add_into(total, part):
    total[...] = (total[...].astype(F32) + part[...].astype(F32)).astype(total.dtype)


class ShardSum:
    def __init__(self, grad, out, bufs, own_sem, send, recv):
        self.grad, self.out = grad, out
        self.tot, self.sib, self.one, self.two, self.line = bufs
        self.own_sem, self.send_sem, self.recv_sem = own_sem, send, recv
        self.z, self.core, self.y, self.x = position()
        self.sent = []

    def go(self, src, dst, slot, device):
        copy = remote(src, dst, self.send_sem.at[slot], self.recv_sem.at[slot], device)
        copy.start()
        self.sent.append(copy)

    def arrived(self, dst, slot):
        remote(dst, dst, self.send_sem.at[0], self.recv_sem.at[slot], at(self.z, self.core, self.y, self.x)).wait_recv()

    def start(self):
        z, core, y, x = self.z, self.core, self.y, self.x
        for side in (0, 1):
            zs = pl.ds(2 * side, 2)
            self.go(self.grad.at[zs, 1 - core], self.sib.at[zs], side, at(z, 1 - core, y, x))
        self.own = pltpu.make_async_copy(self.grad.at[:, core], self.tot, self.own_sem)
        self.own.start()

    def over(self):
        z, core, y, x = self.z, self.core, self.y, self.x
        self.own.wait()
        for side in (0, 1):
            zs = pl.ds(2 * side, 2)
            self.arrived(self.sib.at[zs], side)

            @pl.loop(2 * side, 2 * side + 2)
            def _(zz):
                for ys in range(2):
                    for xs in range(2):
                        add_into(self.tot.at[zz, ys, xs], self.sib.at[zz, ys, xs])

            if side == 0:
                self.go(self.tot.at[zs, :, 1 - x], self.one.at[0], 2, at(z, core, y, 1 - x))
            else:
                self.go(self.tot.at[zs, 1 - y], self.one.at[1], 3, at(z, core, 1 - y, x))

    def turn(self):
        z, core, y, x = self.z, self.core, self.y, self.x
        self.arrived(self.one.at[0], 2)
        for zz in range(2):
            for ys in range(2):
                add_into(self.tot.at[zz, ys, x], self.one.at[0, zz, ys])
        self.go(self.tot.at[pl.ds(0, 2), 1 - y, x], self.two.at[0], 4, at(z, core, 1 - y, x))
        self.arrived(self.one.at[1], 3)
        for zz in range(2):
            for xs in range(2):
                add_into(self.tot.at[2 + zz, y, xs], self.one.at[1, zz, xs])
        self.go(self.tot.at[pl.ds(2, 2), y, 1 - x], self.two.at[1], 5, at(z, core, y, 1 - x))

    def last(self):
        z, core, y, x = self.z, self.core, self.y, self.x
        for side in (0, 1):
            self.arrived(self.two.at[side], 4 + side)
            for zz in range(2):
                add_into(self.tot.at[2 * side + zz, y, x], self.two.at[side, zz])
        for step in (1, 2, 3):
            target = lax.rem(z + step, 4)
            self.go(self.tot.at[target, y, x], self.line.at[step - 1], 5 + step, at(target, core, y, x))

    def finish(self):
        total = self.tot[self.z, self.y, self.x].astype(F32)
        for step in (1, 2, 3):
            self.arrived(self.line.at[step - 1], 5 + step)
            total = total + self.line[step - 1].astype(F32)
        self.out[...] = total
        for copy in self.sent:
            copy.wait_send()

    @staticmethod
    def buffers(grad):
        tail, kind = grad.shape[4:], grad.dtype
        return [
            pltpu.VMEM((4, 2, 2) + tail, kind),
            pltpu.VMEM((4, 2, 2) + tail, kind),
            pltpu.VMEM((2, 2, 2) + tail, kind),
            pltpu.VMEM((2, 2) + tail, kind),
            pltpu.VMEM((3,) + tail, kind),
        ]


class GroupSum:
    def __init__(self, bufs, send, recv):
        self.tot, self.one, self.two, self.line = bufs
        self.send_sem, self.recv_sem = send, recv
        self.z, self.core, self.y, self.x = position()
        self.sent = []

    go = ShardSum.go
    arrived = ShardSum.arrived

    def start(self, total):
        z, core, y, x = self.z, self.core, self.y, self.x
        rows = self.tot.shape[4]
        for zz in range(4):
            for cc in range(2):
                for yy in range(2):
                    for xx in range(2):
                        first = (((zz * 2 + cc) * 2 + yy) * 2 + xx) * rows
                        self.tot[zz, cc, yy, xx] = total[first : first + rows].astype(BF16)
        self.go(self.tot.at[pl.ds(0, 2), :, :, 1 - x], self.one.at[0], 0, at(z, core, y, 1 - x))
        self.go(self.tot.at[pl.ds(2, 2), :, 1 - y], self.one.at[1], 1, at(z, core, 1 - y, x))

    def turn(self):
        z, core, y, x = self.z, self.core, self.y, self.x
        self.arrived(self.one.at[0], 0)

        @pl.loop(0, 2)
        def _(zz):
            for cc in range(2):
                for ys in range(2):
                    add_into(self.tot.at[zz, cc, ys, x], self.one.at[0, zz, cc, ys])

        self.go(self.tot.at[pl.ds(0, 2), :, 1 - y, x], self.two.at[0], 2, at(z, core, 1 - y, x))
        self.arrived(self.one.at[1], 1)

        @pl.loop(0, 2)
        def _(zz):
            for cc in range(2):
                for xs in range(2):
                    add_into(self.tot.at[2 + zz, cc, y, xs], self.one.at[1, zz, cc, xs])

        self.go(self.tot.at[pl.ds(2, 2), :, y, 1 - x], self.two.at[1], 3, at(z, core, y, 1 - x))

    def last(self):
        z, core, y, x = self.z, self.core, self.y, self.x
        for side in (0, 1):
            self.arrived(self.two.at[side], 2 + side)

            @pl.loop(0, 2)
            def _(zz, side=side):
                for cc in range(2):
                    add_into(self.tot.at[2 * side + zz, cc, y, x], self.two.at[side, zz, cc])

        mine = z * 2 + core
        for step in range(1, 8):
            target = lax.rem(mine + step, 8)
            tz, tc = target // 2, target % 2
            self.go(self.tot.at[tz, tc, y, x], self.line.at[step - 1], 3 + step, at(tz, tc, y, x))

    def finish(self, out):
        z, core, y, x = self.z, self.core, self.y, self.x
        mine = z * 2 + core
        for step in range(1, 8):
            self.arrived(self.line.at[step - 1], 3 + step)
        own = self.tot[z, core, y, x].astype(F32)
        width = out.shape[1] // 3
        for side in (0, 1):
            total = None
            for source in (side, side + 2, side + 4, side + 6):
                back = lax.rem(mine - source + 8 + 7, 8)
                term = jnp.where(back == 7, own, self.line[jnp.minimum(back, 6)].astype(F32))
                total = term if total is None else total + term
            for j in range(3):
                for kind in range(3):
                    first = kind * width + (3 * side + j) * LANES
                    source = (3 * j + kind) * LANES
                    out[:, first : first + LANES] = total[:, source : source + LANES]
        for copy in self.sent:
            copy.wait_send()

    @staticmethod
    def buffers(rows, columns):
        return [
            pltpu.VMEM((4, 2, 2, 2, rows, columns), BF16),
            pltpu.VMEM((2, 2, 2, 2, rows, columns), BF16),
            pltpu.VMEM((2, 2, 2, rows, columns), BF16),
            pltpu.VMEM((7, rows, columns), BF16),
        ]


class SmallSum:
    def __init__(self, bufs, out, send, recv):
        self.norms, self.swap, self.acc, self.got, self.line = bufs
        self.out, self.send_sem, self.recv_sem = out, send, recv
        self.z, self.core, self.y, self.x = position()
        self.sent = []
        self.cut = self.norms.shape[2]

    go = ShardSum.go
    arrived = ShardSum.arrived

    def start(self, kernel_grad, norm_grad):
        z, core, y, x = self.z, self.core, self.y, self.x
        cut = self.cut
        self.norms[0] = norm_grad[:, :cut]
        self.norms[1] = norm_grad[:, cut:]
        self.acc[0, :, : kernel_grad.shape[1]] = kernel_grad
        self.go(self.norms.at[1 - core], self.swap, 0, at(z, 1 - core, y, x))

    def over(self):
        z, core, y, x = self.z, self.core, self.y, self.x
        self.arrived(self.swap, 0)
        self.acc[0, :, self.acc.shape[2] - self.cut :] = self.norms[core] + self.swap[...]
        self.go(self.acc.at[0], self.got.at[0], 1, at(z, core, y, 1 - x))

    def turn(self):
        z, core, y, x = self.z, self.core, self.y, self.x
        self.arrived(self.got.at[0], 1)
        self.acc[1] = self.acc[0] + self.got[0]
        self.go(self.acc.at[1], self.got.at[1], 2, at(z, core, 1 - y, x))

    def last(self):
        z, core, y, x = self.z, self.core, self.y, self.x
        self.arrived(self.got.at[1], 2)
        self.acc[2] = self.acc[1] + self.got[1]
        for step in (1, 2, 3):
            self.go(self.acc.at[2], self.line.at[step - 1], 2 + step, at(lax.rem(z + step, 4), core, y, x))

    def swap_back(self):
        z, core, y, x = self.z, self.core, self.y, self.x
        for step in (1, 2, 3):
            self.arrived(self.line.at[step - 1], 2 + step)
        total = None
        for source in range(4):
            back = lax.rem(z - source + 4, 4)
            term = jnp.where(back == 0, self.acc[2], self.line[jnp.maximum(back - 1, 0)])
            total = term if total is None else total + term
        self.out[core] = total
        self.go(self.out.at[core], self.out.at[core], 6, at(z, 1 - core, y, x))

    def finish(self):
        self.arrived(self.out.at[1 - self.core], 6)
        for copy in self.sent:
            copy.wait_send()

    @staticmethod
    def buffers(columns, norm_columns):
        wide = columns + norm_columns
        return [
            pltpu.VMEM((2, 8, norm_columns), F32),
            pltpu.VMEM((8, norm_columns), F32),
            pltpu.VMEM((3, 8, wide), F32),
            pltpu.VMEM((2, 8, wide), F32),
            pltpu.VMEM((3, 8, wide), F32),
        ]


def causal_mask():
    return iota((TILE, TILE), 0) <= iota((TILE, TILE), 1)


def place_small(smalls, kernel_out, norm_out, core, part, cut):
    wide, width = kernel_out.shape[1], norm_out.shape[1]
    column = iota((LANES, wide), 1)
    block, lane = column // LANES, column % LANES
    source = (block % 3) * width + (core * 3 + block // 3) * LANES + lane - iota((LANES, wide), 0)
    norm_source = iota((LANES, width), 1) - iota((LANES, width), 0)
    kernel_out[...] = jnp.zeros_like(kernel_out)
    norm_out[...] = jnp.zeros_like(norm_out)

    @pl.loop(0, smalls.shape[0])
    def _(device):
        low = smalls[device].astype(BF16)
        kernel_out[...] += dot_nn(low, jnp.where(source == device * part, 1.0, 0.0).astype(BF16))
        norm_out[...] += dot_nn(low, jnp.where(norm_source == device * cut, 1.0, 0.0).astype(BF16))

    norm_out[0:4] = norm_out[3:7]


def attend(query_ref, key_ref, value_t, lse, out_t, head, block):
    rows, past = slice(block * TILE, (block + 1) * TILE), slice(0, block * TILE)
    query = query_ref[head, rows]
    diagonal = jnp.where(causal_mask(), dot_nt(key_ref[head, rows], query), NEG_FILL)
    top = jnp.max(diagonal, axis=0, keepdims=True)
    if block:
        before = dot_nt(key_ref[head, past], query)
        top = jnp.maximum(top, jnp.max(before, axis=0, keepdims=True))
        exp_before = jnp.exp(before - top)
    exp_diagonal = jnp.exp(diagonal - top)
    norm = jnp.sum(exp_diagonal, axis=0, keepdims=True)
    if block:
        norm = norm + jnp.sum(exp_before, axis=0, keepdims=True)
    lse[head, :, rows] = top + jnp.log(norm)
    inverse = 1.0 / norm
    result = dot_nn(value_t[head, :, rows], (exp_diagonal * inverse).astype(BF16))
    if block:
        result = result + dot_nn(value_t[head, :, past], (exp_before * inverse).astype(BF16))
    out_t[head, :, rows] = result


def convolve(proj, taps, slot, local, start, length, query_ref, key_ref, value_ref, key_t, value_t):
    window = proj[slot, pl.ds(pl.multiple_of(start, PAD), TILE + PAD)].astype(F32)
    columns = times(local, TRIPLE)
    mixed = (
        taps[0:1, columns] * window[PAD:]
        + taps[1:2, columns] * shifted(window, 1)[PAD:]
        + taps[2:3, columns] * shifted(window, 2)[PAD:]
    ).astype(BF16).astype(F32)
    query, key, value = mixed[:, 0:LANES] * (HEAD_DIM**-0.5), mixed[:, LANES : 2 * LANES], mixed[:, 2 * LANES :]
    rows = pl.ds(pl.multiple_of(start, TILE), TILE)
    lanes = iota((TILE, LANES), 1)
    low_half = lanes < HEAD_DIM
    bias = jnp.where(start + iota((TILE, LANES), 0) < length, 0.0, NEG_FILL)
    at_zero, at_half = lanes == 0, lanes == HEAD_DIM
    query_ref[2 * slot, rows] = jnp.where(low_half, query, jnp.where(at_half, 1.0, 0.0)).astype(BF16)
    query_ref[2 * slot + 1, rows] = jnp.where(low_half, jnp.where(at_zero, 1.0, 0.0), query).astype(BF16)
    key_ref[2 * slot, rows] = jnp.where(low_half, key, jnp.where(at_half, bias, 0.0)).astype(BF16)
    key_ref[2 * slot + 1, rows] = jnp.where(low_half, jnp.where(at_zero, bias, 0.0), key).astype(BF16)
    value_ref[slot, rows] = value.astype(BF16)
    turned_key, turned_value = key.T.astype(BF16), value.T.astype(BF16)
    for head in range(2):
        part = slice(head * HEAD_DIM, (head + 1) * HEAD_DIM)
        key_t[2 * slot + head, :, rows] = turned_key[part]
        value_t[2 * slot + head, :, rows] = turned_value[part]


def first_kernel(
    lens, xs_ref, xl_ref, qkv_ref, conv_ref, norm_ref, out_s, up_s, down_s,
    att, full_out, full_up, full_down, xs_o, xl_o, wq_o, taps_o, norms_o,
    ql_o, kl_o, vl_o, ktl_o, lsel_o, pl_o, ol_o, qs_o, ks_o, vs_o, kts_o, lses_o, ps_o, os_o,
    xs, xl, small, smalls, shard, wq_parts, wq, taps, norms,
    ql, kl, vl, ktl, lsel, proj_l, ol, qs, ks, vs, kts, lses, proj_s, os,
    vtl, vts, otl, ots,
    own_sem, send, recv, sib_send, sib_recv, shard_own, shard_send, shard_recv,
    att_send_l, att_recv_l, att_send_s, att_recv_s, att_own_l, att_own_s, save_sem,
):
    z, core, y, x = position()
    half, near, _, _ = roles()
    index = z * 2 + core
    pairs_long = 2 - near
    own_short, own_long = xs_ref.shape[1], xl_ref.shape[1]
    owned = own_short + own_long
    long_rows, short_rows = xl.shape[0], xs.shape[0]
    part, cut = conv_ref.shape[1], norm_ref.shape[1]
    length_short = jnp.where(half == 0, lens[0, 0], lens[0, 1])
    length_long = jnp.where(half == 0, lens[1, 0], lens[1, 1])

    small[...] = jnp.zeros_like(small)
    small[0:3, 0:part] = conv_ref[...].astype(F32)
    small[3:7, 0:cut] = norm_ref[...].astype(F32)
    width = wq.shape[0]
    for side in range(2):
        for j in range(3):
            for kind in range(3):
                source = kind * width + (3 * side + j) * LANES
                target = (3 * j + kind) * LANES
                shard[side, :, target : target + LANES] = qkv_ref[:, source : source + LANES]
    greet_all()
    rows_short = RowGather(
        xs_ref, xs, own_sem.at[0], send.at[0], recv.at[0], sib_send.at[0], sib_recv.at[0], True
    )
    rows_long = RowGather(
        xl_ref, xl, own_sem.at[1], send.at[1], recv.at[1], sib_send.at[1], sib_recv.at[1], False
    )
    weights = [
        ShardGather(a, f, shard_own.at[i], shard_send.at[i], shard_recv.at[i], halves=i == 1)
        for i, (a, f) in enumerate(
            ((small, smalls), (shard, wq_parts), (out_s, full_out), (up_s, full_up), (down_s, full_down))
        )
    ]
    early, late = weights[:2], weights[2:]
    for one in early:
        one.start()
    rows_long.start()
    rows_short.start()
    zeros = jnp.zeros((PAD, TRIPLE), BF16)
    for slot in range(2):
        proj_l[slot, 0:PAD] = zeros
    for slot in range(3):
        proj_s[slot, 0:PAD] = zeros
    for one in early:
        one.over()
    for one in early:
        one.turn()
    for one in early:
        one.last()
    for one in early:
        one.finish()
    rows_long.step(0)
    rows_short.step(0)
    rows_short.step(1)
    for one in late[:1]:
        one.start()
    place_small(smalls.reshape(32, 8, LANES), taps, norms, core, part, cut)

    pieces = wq_parts.shape[5]
    for zz in range(4):
        for cc in range(2):
            for yy in range(2):
                first = ((zz * 2 + cc) * 2 + yy) * 2 * pieces
                both = jnp.concatenate(
                    [wq_parts[zz, cc, yy, xx, core].astype(F32) for xx in range(2)], axis=0
                )
                wq[first : first + 2 * pieces] = both.astype(BF16)
    gain, offset = norms[0:1], norms[1:2]

    def project(x_ref, proj, start, size, slots, first_pair):
        normal, _ = normalise(x_ref[pl.ds(pl.multiple_of(start, size), size)].astype(F32))
        low = (normal * gain + offset).astype(BF16)

        @pl.loop(0, slots)
        def _(slot):
            result = dot_nn(low, wq[:, times(slot + first_pair, TRIPLE)])
            proj[slot, pl.ds(pl.multiple_of(PAD + start, PAD), size)] = result.astype(BF16)

    def project_long(place):
        @pl.loop(0, 2)
        def _(side):
            project(xl, proj_l, rows_long.chip_rows(place) * 2 * own_long + side * TILE, TILE, pairs_long, 2 * near)

    def project_short(place):
        @pl.when(near == 1)
        def _():
            project(xs, proj_s, rows_short.chip_rows(place) * 2 * own_short, TILE, 3, 0)

    rows_short.whole(0)
    project_short(0)
    rows_long.whole(0)
    project_long(0)
    rows_short.whole(1)
    project_short(1)
    rows_short.step(2)
    rows_long.step(1)
    for one in late[1:]:
        one.start()
    rows_long.whole(1)
    project_long(1)
    rows_short.whole(2)
    project_short(2)
    rows_short.whole(3)
    project_short(3)

    @pl.when(near == 1)
    def _():
        @pl.loop(0, 3)
        def _(slot):
            @pl.loop(0, short_rows // TILE)
            def _(step):
                convolve(proj_s, taps, slot, slot, step * TILE, length_short, qs, ks, vs, kts, vts)

    saves = Copies(save_sem)

    def to_owner(o_ref, slot, first, rows, owner, row_in_owner, pair, send_sem, recv_sem, own_sem):
        source = o_ref.at[slot, pl.ds(first, rows)]
        target = att.at[
            pl.ds(pl.multiple_of(half * owned + row_in_owner, LANES), rows), times(pair, LANES)
        ]
        far = remote(source, target, send_sem, recv_sem, (owner, y * 2 + x))
        close = pltpu.make_async_copy(source, target, own_sem)
        return far, close

    def short_moves(slot, owner):
        return to_owner(
            os, slot, owner * own_short, own_short, owner, 0, 3 * core + slot,
            att_send_s.at[slot, owner], att_recv_s.at[half, 3 * core + slot], att_own_s.at[slot],
        )

    def long_moves(slot, owner):
        pair = 3 * core + slot + 2 * near
        return to_owner(
            ol, slot, owner * own_long, own_long, owner, own_short, pair,
            att_send_l.at[slot, owner], att_recv_l.at[half, pair], att_own_l.at[slot],
        )

    def send_block(o_ref, o_t, slot, block, moves, owners):
        rows = slice(block * TILE, (block + 1) * TILE)
        both = jnp.concatenate([o_t[2 * slot, :, rows], o_t[2 * slot + 1, :, rows]], axis=0)
        o_ref[slot, rows] = both.T.astype(BF16)
        for owner in owners:
            far, close = moves(slot, owner)
            pl.when(index != owner)(far.start)
            pl.when(index == owner)(close.start)

    for block in (0, 2, 1, 3):

        @pl.when(near == 1)
        def _(block=block):
            @pl.loop(0, 6)
            def _(head):
                attend(qs, ks, vts, lses, ots, head, block)

            @pl.loop(0, 3)
            def _(slot):
                send_block(os, ots, slot, block, short_moves, (2 * block, 2 * block + 1))

        if block == 0:
            rows_long.step(2)
            rows_long.whole(2)
            project_long(2)

    rows_long.whole(3)
    project_long(3)

    @pl.loop(0, pairs_long)
    def _(slot):
        @pl.loop(0, long_rows // TILE)
        def _(step):
            convolve(proj_l, taps, slot, slot + 2 * near, step * TILE, length_long, ql, kl, vl, ktl, vtl)

    for source, target in ((xl, xl_o), (wq, wq_o), (taps, taps_o), (norms, norms_o)):
        saves.start(source, target)
    for source, target in ((ql, ql_o), (kl, kl_o), (vl, vl_o), (ktl, ktl_o), (proj_l, pl_o)):
        saves.start(source, target)
    for source, target in ((xs, xs_o), (qs, qs_o), (ks, ks_o), (vs, vs_o), (kts, kts_o), (proj_s, ps_o), (lses, lses_o), (os, os_o)):
        saves.start(source, target)

    order = (0, 4, 1, 5, 2, 6, 3, 7)
    for step, block in enumerate(order):

        @pl.loop(0, 2 * pairs_long)
        def _(head, block=block):
            attend(ql, kl, vtl, lsel, otl, head, block)

        @pl.loop(0, pairs_long)
        def _(slot, block=block):
            send_block(ol, otl, slot, block, long_moves, (block,))

        if step == 2:
            late[0].over()
        if step == 3:
            late[0].turn()
        if step == 4:
            late[1].over()
        if step == 5:
            late[2].over()
            late[0].last()
        if step == 6:
            late[1].turn()
    late[2].turn()
    for source, target in ((lsel, lsel_o), (ol, ol_o)):
        saves.start(source, target)
    late[1].last()
    late[2].last()
    for one in late:
        one.finish()
    for one in weights:
        one.sends_done()

    def own_or_wait(source, moves, slot, arrival):
        @pl.when(index == source)
        def _():
            moves(slot, index)[1].wait()

        @pl.when(index != source)
        def _():
            arrival.wait_recv()

    me = (index, y * 2 + x)
    for seq in range(2):
        for pair in range(6):
            columns = pl.ds(pair * LANES, LANES)
            block = att.at[pl.ds(seq * owned + own_short, own_long), columns]
            source, slot = long_source(seq, pair)
            own_or_wait(
                source, long_moves, slot,
                remote(block, block, att_send_l.at[0, 0], att_recv_l.at[seq, pair], me),
            )
            block = att.at[pl.ds(seq * owned, own_short), columns]
            source, slot = short_source(seq, pair)
            own_or_wait(
                source, short_moves, slot,
                remote(block, block, att_send_s.at[0, 0], att_recv_s.at[seq, pair], me),
            )

    def sends_done(moves, slot):
        for owner in range(8):
            far, _ = moves(slot, owner)
            pl.when(index != owner)(far.wait_send)

    sends_done(long_moves, 0)
    pl.when(near == 0)(lambda: sends_done(long_moves, 1))

    @pl.when(near == 1)
    def _():
        for slot in range(3):
            sends_done(short_moves, slot)

    rows_long.finish()
    rows_short.finish()
    saves.finish()


def first_part(lengths, x_short, x_long, w_qkv, conv_kernel, norm_params, w_out, w_up, w_down, count):
    width = x_short.shape[2]
    short, long = count * x_short.shape[1], count * x_long.shape[1]
    owned = x_short.shape[1] + x_long.shape[1]
    wide = w_qkv.shape[1] // 2
    rows = w_qkv.shape[0]
    out = jax.ShapeDtypeStruct

    def saved(pairs, total):
        return [
            ((2 * pairs, total, LANES), BF16),
            ((2 * pairs, total, LANES), BF16),
            ((pairs, total, LANES), BF16),
            ((2 * pairs, HEAD_DIM, total), BF16),
            ((2 * pairs, 1, total), F32),
            ((pairs, PAD + total, TRIPLE), BF16),
            ((pairs, total, LANES), BF16),
        ]

    kept = saved(2, long) + saved(3, short)
    basic = [((short, width), BF16), ((long, width), BF16)]
    consts = [((width, wide), BF16), ((8, wide), F32), ((8, width), F32)]
    full = [((4, 2, 2, 2) + w.shape, BF16) for w in (w_out, w_up, w_down)]
    outs = [((2 * owned, width), BF16)] + full + basic + consts + kept
    scratch = (
        basic
        + [((8, LANES), F32), ((4, 2, 2, 2, 8, LANES), F32), ((2, rows, wide), BF16)]
        + [((4, 2, 2, 2, 2, rows, wide), BF16)]
        + consts
        + kept
        + [((4, HEAD_DIM, long), BF16), ((6, HEAD_DIM, short), BF16)]
        + [((4, HEAD_DIM, long), F32), ((6, HEAD_DIM, short), F32)]
    )
    return pl.pallas_call(
        first_kernel,
        out_shape=tuple(out(*one) for one in outs),
        in_specs=[smem(), hbm(), hbm(), vmem(), vmem(), vmem(), hbm(), hbm(), hbm()],
        out_specs=tuple([hbm()] * len(outs)),
        scratch_shapes=[pltpu.VMEM(*one) for one in scratch]
        + [DMA((2,))] + [DMA((2, 4))] * 4
        + [DMA((5,)), DMA((5, 13)), DMA((5, 13))]
        + [DMA((2, 8)), DMA((2, 6)), DMA((3, 8)), DMA((2, 6)), DMA((2,)), DMA((3,))]
        + [DMA((24,))],
        compiler_params=params_of(collective_id=0, has_side_effects=True),
    )(lengths, x_short, x_long, w_qkv, conv_kernel, norm_params, w_out, w_up, w_down)


def second_kernel(
    xs_ref, xl_ref, att, cs_ref, cl_ref, np_ref, wo_ref, wu_ref, wd_ref,
    ys_ref, yl_ref, gmid, gnorm, gwo_o, gwu_o, gwd_o, gl_o, gs_o,
    wo, wu, wd, middle, normal_two, inverse_two, second, second_t, cot, y_acc, gsec, gml, gwo, hid, gup,
    load_sem, save_sem, send_l, recv_l, send_s, recv_s,
):
    z, core, y, x = position()
    half, near, _, _ = roles()
    index = z * 2 + core
    pairs_long = 2 - near
    loads, saves = Copies(load_sem), Copies(save_sem)
    got_out = loads.start(wo_ref, wo)
    got_up = loads.start(wu_ref, wu)
    got_down = loads.start(wd_ref, wd)
    greet(whole_line())
    short, long = xs_ref.shape[1], xl_ref.shape[1]
    owned = short + long
    rows_all = 2 * owned
    for seq in range(2):
        first = seq * owned
        cot[first : first + short] = cs_ref[seq]
        cot[first + short : first + owned] = cl_ref[seq]
        middle[first : first + short] = xs_ref[seq].astype(F32)
        middle[first + short : first + owned] = xl_ref[seq].astype(F32)
    got_out.wait()

    @pl.loop(0, rows_all // TILE)
    def _(step):
        rows = times(step, TILE)
        values = middle[rows] + dot_nn(att[rows], wo[...])
        normal, inverse = normalise(values)
        normal_two[rows] = normal
        inverse_two[rows] = inverse
        second[rows] = (normal * np_ref[2:3] + np_ref[3:4]).astype(BF16)
        y_acc[rows] = values
        gsec[rows] = jnp.zeros_like(values)

    second_t[...] = second[...].T
    inner = 512
    got_up.wait()
    got_down.wait()

    @pl.loop(0, wu.shape[1] // inner)
    def _(step):
        columns = times(step, inner)
        upper = jnp.maximum(dot_nn(second[...], wu[:, columns]), 0.0)
        hidden = (upper * upper).astype(BF16)
        grad_hidden = dot_nt(cot[...], wd[columns])
        grad_upper = (2.0 * upper * grad_hidden).astype(BF16)
        hid[:, columns] = hidden
        gup[:, columns] = grad_upper
        y_acc[...] += dot_nn(hidden, wd[columns])
        gsec[...] += dot_nt(grad_upper, wu[:, columns])

    gnorm[...] = jnp.zeros_like(gnorm)

    @pl.loop(0, rows_all // TILE)
    def _(step):
        rows = times(step, TILE)
        grad = gsec[rows]
        normal = normal_two[rows]
        gnorm[2:3] += jnp.sum(grad * normal, axis=0, keepdims=True)
        gnorm[3:4] += jnp.sum(grad, axis=0, keepdims=True)
        total = cot[rows].astype(F32) + norm_back(grad, normal, inverse_two[rows], np_ref[2:3])
        gmid[rows] = total
        gml[rows] = total.astype(BF16)
        second[rows] = dot_nt(gml[rows], wo[...]).astype(BF16)

    def moves(seq, pair, is_long):
        target, slot = (long_source if is_long else short_source)(seq, pair)
        rows = long if is_long else short
        out, send, recv = (gl_o, send_l, recv_l) if is_long else (gs_o, send_s, recv_s)
        first = seq * owned + (short if is_long else 0)
        source = second.at[pl.ds(first, rows), pl.ds(pair * LANES, LANES)]
        place = out.at[slot, times(index, rows)]
        far = remote(source, place, send.at[seq, pair], recv.at[slot, index], (target, y * 2 + x))
        close = pltpu.make_async_copy(source, place, recv.at[slot, index])
        return target, far, close

    kinds = [(seq, pair, is_long) for is_long in (True, False) for pair in range(6) for seq in range(2)]
    for kind in kinds:
        target, far, close = moves(*kind)
        pl.when(index != target)(far.start)
        pl.when(index == target)(close.start)

    @pl.loop(0, wu.shape[1] // inner)
    def _(step):
        columns = times(step, inner)
        wd[columns] = dot_tn(hid[:, columns], cot[...]).astype(BF16)
        wu[:, columns] = dot_nn(second_t[...], gup[:, columns]).astype(BF16)

    saves.start(wd, gwd_o)
    saves.start(wu, gwu_o)
    gwo[...] = dot_tn(att[...], gml[...]).astype(BF16)
    saves.start(gwo, gwo_o)
    for seq in range(2):
        first = seq * owned
        ys_ref[seq] = y_acc[first : first + short].astype(BF16)
        yl_ref[seq] = y_acc[first + short : first + owned].astype(BF16)

    me = (index, y * 2 + x)

    def arrivals(out, recv, slot, rows):
        for source in range(8):
            block = out.at[slot, pl.ds(source * rows, rows)]

            @pl.when(index != source)
            def _(block=block, source=source):
                remote(block, block, send_l.at[0, 0], recv.at[slot, source], me).wait_recv()

    arrivals(gl_o, recv_l, 0, long)
    pl.when(near == 0)(lambda: arrivals(gl_o, recv_l, 1, long))

    @pl.when(near == 1)
    def _():
        for slot in range(3):
            arrivals(gs_o, recv_s, slot, short)

    for kind in kinds:
        target, far, close = moves(*kind)
        pl.when(index != target)(far.wait_send)
        pl.when(index == target)(close.wait)
    saves.finish()


def second_part(x_short, x_long, att, cot_short, cot_long, norms, w_out, w_up, w_down, count):
    width = x_short.shape[2]
    rows = att.shape[0]
    short, long = count * x_short.shape[1], count * x_long.shape[1]
    hidden = w_up.shape[1]
    out = jax.ShapeDtypeStruct
    return pl.pallas_call(
        second_kernel,
        out_shape=(
            out(x_short.shape, BF16),
            out(x_long.shape, BF16),
            out((rows, width), F32),
            out((8, width), F32),
            out(w_out.shape, BF16),
            out(w_up.shape, BF16),
            out(w_down.shape, BF16),
            out((2, long, LANES), BF16),
            out((3, short, LANES), BF16),
        ),
        in_specs=[vmem()] * 6 + [hbm()] * 3,
        out_specs=tuple([vmem()] * 4 + [hbm()] * 5),
        scratch_shapes=[
            pltpu.VMEM(w_out.shape, BF16),
            pltpu.VMEM(w_up.shape, BF16),
            pltpu.VMEM(w_down.shape, BF16),
            pltpu.VMEM((rows, width), F32),
            pltpu.VMEM((rows, width), F32),
            pltpu.VMEM((rows, 1), F32),
            pltpu.VMEM((rows, width), BF16),
            pltpu.VMEM((width, rows), BF16),
            pltpu.VMEM((rows, width), BF16),
            pltpu.VMEM((rows, width), F32),
            pltpu.VMEM((rows, width), F32),
            pltpu.VMEM((rows, width), BF16),
            pltpu.VMEM(w_out.shape, BF16),
            pltpu.VMEM((rows, hidden), BF16),
            pltpu.VMEM((rows, hidden), BF16),
            DMA((3,)), DMA((3,)), DMA((2, 6)), DMA((2, 8)), DMA((2, 6)), DMA((3, 8)),
        ],
        compiler_params=params_of(collective_id=1, has_side_effects=True),
    )(x_short, x_long, att, cot_short, cot_long, norms, w_out, w_up, w_down)


class RowSum:
    def __init__(self, long_bufs, short_bufs, sems):
        self.mine, self.out, self.sib, self.got, self.fin = long_bufs
        self.mine_s, self.out_s, self.sib_s, self.fin_s = short_bufs
        (
            self.sib_send, self.sib_recv, self.send, self.recv, self.on_send, self.fin_recv,
            self.sib_send_s, self.sib_recv_s, self.send_s, self.fin_recv_s,
        ) = sems
        self.z, self.core, self.y, self.x = position()
        self.half, self.near, partner_z, far_z = roles()
        self.partner = at(partner_z, self.core, self.y, self.x)
        self.sibling = at(self.z, 1 - self.core, self.y, self.x)
        self.far = at(far_z, self.core, self.y, self.x)

    def across(self, zz):
        return remote(self.out.at[zz % 2], self.sib.at[zz], self.sib_send.at[zz], self.sib_recv.at[zz], self.sibling)

    def put(self, block, value):
        zz, parity = block // 2, block % 2

        @pl.when(self.core == parity)
        def _():
            self.mine[zz] = value

        @pl.when(self.core != parity)
        def _():
            if zz < 2:
                self.across(zz + 2).wait_send()
            self.out[zz % 2] = value
            self.across(zz).start()

    def place(self, zz):
        return jnp.where(self.half == 0, zz, 3 - zz)

    def to_partner(self, zz):
        return remote(self.mine.at[zz], self.got.at[zz], self.send.at[zz], self.recv.at[zz], self.partner)

    def to_owner(self, zz):
        return remote(
            self.mine.at[zz], self.fin, self.on_send.at[zz], self.fin_recv, at(zz, self.core, self.y, self.x)
        )

    def sends_to_partner(self, zz):
        place = self.place(zz)
        return jnp.where(self.near == 0, place != 0, place == 0)

    def add_cores(self, zz):
        self.across(zz).wait_recv()
        add_into(self.mine.at[zz], self.sib.at[zz])
        pl.when(self.sends_to_partner(zz))(self.to_partner(zz).start)

    def sends_on(self, zz):
        return jnp.logical_and(self.near == 1, self.place(zz) >= 2)

    def add_chips(self, zz):
        @pl.when(self.sends_on(zz))
        def _():
            self.to_partner(zz).wait_recv()
            add_into(self.mine.at[zz], self.got.at[zz])
            self.to_owner(zz).start()

    def across_s(self, zz):
        return remote(
            self.out_s.at[zz], self.sib_s.at[zz], self.sib_send_s.at[zz], self.sib_recv_s.at[zz], self.sibling
        )

    def put_short(self, zz, value):
        rows = value.shape[0] // 2
        first, second = value[:rows], value[rows:]

        @pl.when(self.core == 0)
        def _():
            self.mine_s[zz] = first
            self.out_s[zz] = second

        @pl.when(self.core == 1)
        def _():
            self.mine_s[zz] = second
            self.out_s[zz] = first

        self.across_s(zz).start()

    def to_owner_s(self, zz):
        return remote(
            self.mine_s.at[zz], self.fin_s.at[self.half], self.send_s.at[zz], self.fin_recv_s.at[self.half],
            at(zz, self.core, self.y, self.x),
        )

    def add_short(self, zz):
        @pl.when(self.near == 1)
        def _():
            self.across_s(zz).wait_recv()
            add_into(self.mine_s.at[zz], self.sib_s.at[zz])
            pl.when(self.z != zz)(self.to_owner_s(zz).start)

    def own_long(self):
        self.to_partner(self.z).wait_recv()
        return self.mine[self.z].astype(F32) + self.got[self.z].astype(F32)

    def other_long(self):
        remote(self.fin, self.fin, self.on_send.at[0], self.fin_recv, self.far).wait_recv()
        return self.fin[...].astype(F32)

    def shorts(self):
        def arrival(seq):
            block = self.fin_s.at[seq]
            remote(block, block, self.send_s.at[0], self.fin_recv_s.at[seq], self.far).wait_recv()

        arrival(1 - self.half)
        pl.when(self.near == 0)(lambda: arrival(self.half))

        @pl.when(self.near == 1)
        def _():
            self.fin_s[self.half] = self.mine_s[self.z]

    def sends_done(self):
        for zz in range(4):
            if zz < 2:
                self.across(zz).wait_send()
            pl.when(self.sends_to_partner(zz))(self.to_partner(zz).wait_send)
            pl.when(self.sends_on(zz))(self.to_owner(zz).wait_send)

        @pl.when(self.near == 1)
        def _():
            for zz in range(4):
                self.across_s(zz).wait_send()
                pl.when(self.z != zz)(self.to_owner_s(zz).wait_send)


def third_kernel(
    xs_own, xl_own, gnorm, wq, taps, norms, gmid,
    xs_h, xl_h, ql_h, kl_h, vl_h, ktl_h, lsel_h, pl_h, ol_h, qs_h, ks_h, vs_h, kts_h, lses_h, ps_h, os_h,
    gl_h, gs_h, gwo_h, gwu_h, gwd_h,
    dxs_ref, dxl_ref, gwq_ref, gwo_ref, gwu_ref, gwd_ref, small_ref,
    ql, kl, vl, ktl, lsel, ol, gl, qs, ks, vs, kts, lses, os, gs,
    gm, dqt, delta, gp, gacc, dwq, dtaps, dnorms, x_tile, p_tile,
    mine, out, sib, got, fin, mine_s, out_s, sib_s, fin_s,
    load_sem, tile_sem,
    r0, r1, r2, r3, r4, r5, r6, r7, r8, r9,
    shard_own, shard_send, shard_recv, group_send, group_recv, small_send, small_recv,
    *bufs,
):
    z, core, y, x = position()
    half, near, _, _ = roles()
    pairs_long = 2 - near
    loads, tiles = Copies(load_sem), Copies(tile_sem)
    for source, target in (
        (ql_h, ql), (kl_h, kl), (vl_h, vl), (ktl_h, ktl), (lsel_h, lsel), (ol_h, ol), (gl_h, gl),
    ):
        loads.start(source, target)
    greet_all()
    bufs = list(bufs)
    sums = []
    for i, (grad, total) in enumerate(((gwo_h, gwo_ref), (gwu_h, gwu_ref), (gwd_h, gwd_ref))):
        sums.append(ShardSum(grad, total, bufs[5 * i : 5 * i + 5], shard_own.at[i], shard_send.at[i], shard_recv.at[i]))
    group = GroupSum(bufs[15:19], group_send, group_recv)
    small = SmallSum(bufs[19:24], small_ref, small_send, small_recv)
    rows_sum = RowSum((mine, out, sib, got, fin), (mine_s, out_s, sib_s, fin_s), (r0, r1, r2, r3, r4, r5, r6, r7, r8, r9))
    for one in sums:
        one.start()
    short, long = xs_own.shape[1], xl_own.shape[1]
    owned = short + long
    middles = [
        pltpu.make_async_copy(gmid.at[pl.ds(seq * owned + first, size)], dx.at[seq], load_sem.at[14 + 2 * seq + i])
        for seq in range(2)
        for i, (dx, first, size) in enumerate(((dxs_ref, 0, short), (dxl_ref, short, long)))
    ]
    for copy in middles:
        copy.start()
    gm[...] = jnp.zeros_like(gm)
    dwq[...] = jnp.zeros_like(dwq)
    dtaps[...] = jnp.zeros_like(dtaps)
    dnorms[...] = gnorm[...]
    gain, offset = norms[0:1], norms[1:2]
    pick = jnp.where((iota((8, LANES), 1) < HEAD_DIM) == (iota((8, LANES), 0) == 0), 1.0, 0.0).astype(F32)
    causal = causal_mask()
    first_lanes = iota((TILE, LANES), 1) < HEAD_DIM

    def grads_long(slot):
        return gm.at[slot, pl.ds(0, xl_h.shape[0] + PAD)]

    def grads_short(slot):
        size = xs_h.shape[0] + PAD
        return gm.at[lax.rem(slot, 2), pl.ds(pl.multiple_of(slot // 2 * size, PAD), size)]

    def back_head(q_ref, k_ref, v_ref, kt_ref, lse, g_ref, grads, head, block):
        slot, side = head // 2, head % 2
        grad_ref = grads(slot)
        own_lanes = first_lanes == (side == 0)
        rows = slice(block * TILE, (block + 1) * TILE)
        query = q_ref[head, rows]
        bare = jnp.where(own_lanes, query.astype(F32), 0.0).astype(BF16)
        grad_out = jnp.where(own_lanes, g_ref[slot, rows].astype(F32), 0.0).astype(BF16)
        stat, less = lse[head, :, rows], delta[head]
        spans = [(block * TILE, TILE, True)]
        if block:
            spans.append((0, block * TILE, False))
        grad_q = None
        for start, size, masked in spans:
            keys = slice(start, start + size)
            scores = dot_nt(k_ref[head, keys], query)
            if masked:
                scores = jnp.where(causal, scores, NEG_FILL)
            probs = jnp.exp(scores - stat)
            grad_probs = dot_nt(v_ref[slot, keys], grad_out)
            grad_ref[keys, 2 * LANES :] += dot_nn(probs.astype(BF16), grad_out)
            grad_scores = (probs * (grad_probs - less)).astype(BF16)
            grad_ref[keys, LANES : 2 * LANES] += dot_nn(grad_scores, bare)
            term = dot_nn(kt_ref[head, :, keys], grad_scores)
            grad_q = term if grad_q is None else grad_q + term
        dqt[head] = (HEAD_DIM**-0.5) * grad_q

    def back_block(refs, x_h, p_h, grads, pairs, slots, first_pair, block, total):
        q_ref, k_ref, v_ref, kt_ref, lse, o_ref, g_ref = refs
        rows = slice(block * TILE, (block + 1) * TILE)
        got_x = pltpu.make_async_copy(x_h.at[pl.ds(block * TILE, TILE)], x_tile, tile_sem.at[0])
        got_p = pltpu.make_async_copy(
            p_h.at[:, pl.ds(block * TILE, TILE + PAD)], p_tile.at[pl.ds(0, pairs)], tile_sem.at[1]
        )
        got_x.start()
        got_p.start()

        @pl.loop(0, slots)
        def _(slot):
            product = g_ref[slot, rows].astype(F32) * o_ref[slot, rows].astype(F32)
            both = lax.dot_general(
                pick, product, (((1,), (1,)), ((), ())), preferred_element_type=F32,
                precision=lax.Precision.HIGHEST,
            )
            delta[2 * slot] = both[0:1]
            delta[2 * slot + 1] = both[1:2]

        @pl.loop(0, 2 * slots)
        def _(head):
            back_head(q_ref, k_ref, v_ref, kt_ref, lse, g_ref, grads, head, block)

        got_x.wait()
        got_p.wait()
        normal, _ = normalise(x_tile[...].astype(F32))
        low = (normal * gain + offset).astype(BF16)
        gacc[...] = jnp.zeros_like(gacc)

        @pl.loop(0, slots)
        def _(slot):
            columns = times(slot + first_pair, TRIPLE)
            grad_ref = grads(slot)
            grad_ref[rows, 0:LANES] = jnp.concatenate([dqt[2 * slot], dqt[2 * slot + 1]], axis=0).T
            window = grad_ref[pl.ds(block * TILE, TILE + PAD)]
            grad = window[:TILE]
            kernel = taps[:, columns]
            grad_projected = (
                kernel[0:1] * grad + kernel[1:2] * shifted(window, -1)[:TILE] + kernel[2:3] * shifted(window, -2)[:TILE]
            ).astype(BF16)
            past = p_tile[slot].astype(F32)
            dtaps[0:1, columns] += jnp.sum(grad * past[PAD:], axis=0, keepdims=True)
            dtaps[1:2, columns] += jnp.sum(grad * shifted(past, 1)[PAD:], axis=0, keepdims=True)
            dtaps[2:3, columns] += jnp.sum(grad * shifted(past, 2)[PAD:], axis=0, keepdims=True)
            gacc[...] += dot_nt(grad_projected, wq[:, columns])
            dwq[:, columns] += dot_tn(low, grad_projected)

        grad_normed = gacc[...]
        dnorms[0:1] += jnp.sum(grad_normed * normal, axis=0, keepdims=True)
        dnorms[1:2] += jnp.sum(grad_normed, axis=0, keepdims=True)
        return grad_normed.astype(BF16)

    loads.finish()

    short_loads = [
        pltpu.make_async_copy(source, target, load_sem.at[7 + i])
        for i, (source, target) in enumerate(
            ((qs_h, qs), (ks_h, ks), (vs_h, vs), (kts_h, kts), (lses_h, lses), (os_h, os), (gs_h, gs))
        )
    ]

    @pl.when(near == 1)
    def _():
        for copy in short_loads:
            copy.start()

    long_refs = (ql, kl, vl, ktl, lsel, ol, gl)
    short_refs = (qs, ks, vs, kts, lses, os, gs)
    last_long = xl_h.shape[0] // TILE - 1
    for block in range(last_long, -1, -1):
        value = back_block(long_refs, xl_h, pl_h, grads_long, 2, pairs_long, 2 * near, block, last_long)
        rows_sum.put(block, value)
        if block % 2 == 1 and block != last_long:
            rows_sum.add_cores(block // 2 + 1)
        if block == 7:
            for one in sums:
                one.over()
        if block == 5:
            for one in sums:
                one.turn()
        if block == 3:
            for one in sums:
                one.last()
        if block == 1:
            for one in sums:
                one.finish()
    rows_sum.add_cores(0)

    @pl.when(near == 1)
    def _():
        for copy in short_loads:
            copy.wait()
        gm[...] = jnp.zeros_like(gm)

    last_short = xs_h.shape[0] // TILE - 1
    for block in range(last_short, -1, -1):

        @pl.when(near == 1)
        def _(block=block):
            value = back_block(short_refs, xs_h, ps_h, grads_short, 3, 3, 0, block, last_short)
            rows_sum.put_short(block, value)

        rows_sum.add_chips(block)
        if block != last_short:
            rows_sum.add_short(block + 1)
    rows_sum.add_short(0)
    group.start(dwq)
    small.start(dtaps[...], dnorms[...])
    small.over()
    group.turn()
    small.turn()
    group.last()
    small.last()

    for copy in middles:
        copy.wait()

    def finish_rows(seq, grad, x_ref, dx_ref):
        normal, inverse = normalise(x_ref[seq].astype(F32))
        dx_ref[seq] += norm_back(grad, normal, inverse, gain)

    rows_sum.shorts()
    finish_rows(half, rows_sum.fin_s[half].astype(F32), xs_own, dxs_ref)
    finish_rows(1 - half, rows_sum.fin_s[1 - half].astype(F32), xs_own, dxs_ref)
    finish_rows(half, rows_sum.own_long(), xl_own, dxl_ref)
    finish_rows(1 - half, rows_sum.other_long(), xl_own, dxl_ref)
    small.swap_back()
    group.finish(gwq_ref)
    small.finish()
    rows_sum.sends_done()


def third_part(x_short, x_long, gmid, gnorm, wq, taps, norms, kept, grads_in, weight_grads):
    width = x_short.shape[2]
    wide = wq.shape[1]
    count = 8
    short, long = count * x_short.shape[1], count * x_long.shape[1]
    own_short = x_short.shape[1]
    rows = weight_grads[0].shape[4]
    out = jax.ShapeDtypeStruct
    small_wide = wide + width // 2

    def saved(pairs, total):
        return [
            ((2 * pairs, total, LANES), BF16),
            ((2 * pairs, total, LANES), BF16),
            ((pairs, total, LANES), BF16),
            ((2 * pairs, HEAD_DIM, total), BF16),
            ((2 * pairs, 1, total), F32),
            ((pairs, total, LANES), BF16),
            ((pairs, total, LANES), BF16),
        ]

    scratch = (
        saved(2, long)
        + saved(3, short)
        + [
            ((2, max(long + PAD, 2 * (short + PAD)), TRIPLE), F32),
            ((6, HEAD_DIM, TILE), F32),
            ((6, 1, TILE), F32),
            ((3, TILE, TRIPLE), BF16),
            ((TILE, width), F32),
            ((width, wide), F32),
            ((8, wide), F32),
            ((8, width), F32),
            ((TILE, width), BF16),
            ((3, TILE + PAD, TRIPLE), BF16),
        ]
        + [((4, TILE, width), BF16), ((2, TILE, width), BF16)]
        + [((4, TILE, width), BF16)] * 2
        + [((TILE, width), BF16)]
        + [((4, own_short, width), BF16)] * 3
        + [((2, own_short, width), BF16)]
    )
    buffers = []
    for g in weight_grads:
        buffers += ShardSum.buffers(g)
    buffers += GroupSum.buffers(rows, wide) + SmallSum.buffers(wide, width // 2)
    return pl.pallas_call(
        third_kernel,
        out_shape=(
            out(x_short.shape, F32),
            out(x_long.shape, F32),
            out((rows, 2 * wide), F32),
            *[out(g.shape[4:], F32) for g in weight_grads],
            out((2, 8, small_wide), F32),
        ),
        in_specs=[vmem()] * 6 + [hbm()] * (1 + len(kept) + len(grads_in) + len(weight_grads)),
        out_specs=tuple([vmem()] * 7),
        scratch_shapes=[pltpu.VMEM(*one) for one in scratch]
        + [DMA((18,)), DMA((2,))]
        + [DMA((4,))] * 5 + [DMA] + [DMA((4,))] * 3 + [DMA((2,))]
        + [DMA((3,)), DMA((3, 9)), DMA((3, 9)), DMA((11,)), DMA((11,)), DMA((7,)), DMA((7,))]
        + buffers,
        compiler_params=params_of(63, collective_id=2, has_side_effects=True),
    )(x_short, x_long, gnorm, wq, taps, norms, gmid, *kept, *grads_in, *weight_grads)


def split_body(
    x_short, x_long, lengths, cot_short, cot_long, w_qkv, w_out, w_up, w_down, conv_kernel, norm_params
):
    count = lax.axis_size("seq")
    width = x_short.shape[2]
    att, full_out, full_up, full_down, xs, xl, wq, taps, norms, *kept = first_part(
        lengths, x_short, x_long, w_qkv, conv_kernel, norm_params, w_out, w_up, w_down, count
    )
    y_short, y_long, gmid, gnorm, gwo, gwu, gwd, gl, gs = second_part(
        x_short, x_long, att, cot_short, cot_long, norms,
        full_out.reshape(width, -1), full_up.reshape(width, -1), full_down.reshape(-1, width), count,
    )
    cuts = [g.reshape(w.shape) for g, w in ((gwo, full_out), (gwu, full_up), (gwd, full_down))]
    dx_short, dx_long, sum_qkv, sum_out, sum_up, sum_down, smalls = third_part(
        x_short, x_long, gmid, gnorm, wq, taps, norms, [xs, xl] + kept, [gl, gs], cuts
    )
    wide = wq.shape[1]
    number = lax.axis_index("seq") * lax.axis_size("batch") + lax.axis_index("batch")
    part, cut = conv_kernel.shape[1], norm_params.shape[1]
    kernel = smalls[:, 0:3, :wide].reshape(2, 3, 3, 3, LANES).transpose(1, 3, 0, 2, 4).reshape(3, 3 * width)
    norm = smalls[:, 0:4, wide:].transpose(1, 0, 2).reshape(4, width)
    return (
        y_short, y_long, dx_short, dx_long, sum_qkv, sum_out, sum_up, sum_down,
        lax.dynamic_slice_in_dim(kernel, number * part, part, 1),
        lax.dynamic_slice_in_dim(norm, number * cut, cut, 1),
    )


GROUP_HEADS = 2


def from_behind(value, axis, by):
    count = lax.axis_size(axis)
    pairs = [(i, i + by) for i in range(count) if 0 <= i + by < count]
    return lax.ppermute(value, axis, pairs)


def layer_norm(values, gain, offset_term):
    average = jnp.mean(values, axis=-1, keepdims=True)
    centred = values - average
    inverse = lax.rsqrt(jnp.mean(centred * centred, axis=-1, keepdims=True) + EPS)
    normal = centred * inverse
    return (normal * gain + offset_term, normal, inverse)


def norm_back_flat(grad, normal, inverse, gain):
    scaled_grad = grad * gain
    first_mean = jnp.mean(scaled_grad, axis=-1, keepdims=True)
    second_mean = jnp.mean(scaled_grad * normal, axis=-1, keepdims=True)
    return inverse * (scaled_grad - first_mean - normal * second_mean)


def front_part(inputs, full_weights):
    w_qkv = full_weights[0]
    kernel = full_weights[4].astype(jnp.float32)
    params = full_weights[5].astype(jnp.float32)
    saved = []
    tails = []
    for part_in in inputs:
        seq_count, block_rows, model_width = part_in.shape
        flat = part_in.reshape(seq_count * block_rows, model_width).astype(jnp.float32)
        normed, normal, inverse = layer_norm(flat, params[0], params[1])
        normed_low = normed.astype(jnp.bfloat16)
        projected = jnp.dot(normed_low, w_qkv, preferred_element_type=jnp.float32).astype(
            jnp.bfloat16
        )
        projected = projected.reshape(seq_count, block_rows, 3 * model_width)
        saved.append((flat, normal, inverse, normed_low, projected))
        tails.append(projected[:, block_rows - 2 :])
    received = from_behind((tails[0], tails[1]), "seq", 1)
    fronts = []
    for index_part in range(2):
        flat, normal, inverse, normed_low, projected = saved[index_part]
        block_rows = projected.shape[1]
        padded = jnp.concatenate([received[index_part], projected], axis=1).astype(jnp.float32)
        mixed = (
            kernel[0] * padded[:, 2:]
            + kernel[1] * padded[:, 1 : block_rows + 1]
            + kernel[2] * padded[:, :block_rows]
        )
        fronts.append((flat, normal, inverse, normed_low, padded, mixed.astype(jnp.bfloat16)))
    return fronts


def attend_block(queries, key_rows, value_rows, usable, grad_heads):
    scaling = queries.shape[-1] ** (-0.5)
    scores = jnp.einsum("sqhd,skhd->shqk", queries, key_rows, preferred_element_type=jnp.float32)
    masked = jnp.where(usable, scaling * scores, NEG_FILL)
    exp_terms = jnp.exp(masked - jnp.max(masked, axis=-1, keepdims=True))
    attn_probs = exp_terms / jnp.sum(exp_terms, axis=-1, keepdims=True)
    probs_low = attn_probs.astype(jnp.bfloat16)
    if grad_heads is None:
        attended = jnp.einsum(
            "shqk,skhd->sqhd", probs_low, value_rows, preferred_element_type=jnp.float32
        )
        return attended.astype(jnp.bfloat16)
    grad_probs = jnp.einsum(
        "sqhd,skhd->shqk", grad_heads, value_rows, preferred_element_type=jnp.float32
    )
    grad_values = jnp.einsum(
        "shqk,sqhd->skhd", probs_low, grad_heads, preferred_element_type=jnp.float32
    )
    row_delta = jnp.sum(attn_probs * grad_probs, axis=-1, keepdims=True)
    grad_scores = (scaling * attn_probs * (grad_probs - row_delta)).astype(jnp.bfloat16)
    grad_queries = jnp.einsum(
        "shqk,skhd->sqhd", grad_scores, key_rows, preferred_element_type=jnp.float32
    )
    grad_keys = jnp.einsum(
        "shqk,sqhd->skhd", grad_scores, queries, preferred_element_type=jnp.float32
    )
    return (grad_queries, grad_keys, grad_values)


def make_usable(query_pos, key_pos, seq_lengths):
    usable = (key_pos[None, None, :] <= query_pos[None, :, None]) & (
        key_pos[None, None, :] < seq_lengths[:, None, None]
    )
    return usable[:, None]


def attention(mixed, kv_full, seq_lengths, offset, grad_attended):
    seq_count, block_rows, three_width = mixed.shape
    model_width = three_width // 3
    full_len = kv_full.shape[1]
    queries = mixed[:, :, :model_width].reshape(seq_count, block_rows, -1, HEAD_DIM)
    key_rows = kv_full[:, :, :model_width].reshape(seq_count, full_len, -1, HEAD_DIM)
    value_rows = kv_full[:, :, model_width:].reshape(seq_count, full_len, -1, HEAD_DIM)
    positions = offset + jnp.arange(block_rows, dtype=jnp.int32)
    key_pos = jnp.arange(full_len, dtype=jnp.int32)
    usable = make_usable(positions, key_pos, seq_lengths)
    heads_total = queries.shape[2]
    grad_heads = None
    if grad_attended is not None:
        grad_heads = grad_attended.reshape(seq_count, block_rows, -1, HEAD_DIM)
    results = []
    for first_head in range(0, heads_total, GROUP_HEADS):
        last_head = first_head + GROUP_HEADS
        grad_part = None if grad_heads is None else grad_heads[:, :, first_head:last_head]
        results.append(
            attend_block(
                queries[:, :, first_head:last_head],
                key_rows[:, :, first_head:last_head],
                value_rows[:, :, first_head:last_head],
                usable,
                grad_part,
            )
        )
    if grad_heads is None:
        return jnp.concatenate(results, axis=2).reshape(seq_count, block_rows, model_width)
    grad_queries = jnp.concatenate([entry_set[0] for entry_set in results], axis=2).reshape(
        seq_count, block_rows, model_width
    )
    grad_keys = jnp.concatenate([entry_set[1] for entry_set in results], axis=2).reshape(
        seq_count, full_len, model_width
    )
    grad_values = jnp.concatenate([entry_set[2] for entry_set in results], axis=2).reshape(
        seq_count, full_len, model_width
    )
    return (grad_queries, grad_keys, grad_values)


def rest_part(front, kv_full, seq_lengths, offset, full_weights, cotangent_in):
    w_out, w_up, w_down = (full_weights[1], full_weights[2], full_weights[3])
    params = full_weights[5].astype(jnp.float32)
    flat, normal_one, inverse_one, normed_low, padded, mixed = front
    seq_count, block_rows, three_width = mixed.shape
    model_width = three_width // 3
    attended = attention(mixed, kv_full, seq_lengths, offset, None).reshape(
        seq_count * block_rows, model_width
    )
    middle = flat + jnp.dot(attended, w_out, preferred_element_type=jnp.float32)
    second, normal_two, inverse_two = layer_norm(middle, params[2], params[3])
    second_low = second.astype(jnp.bfloat16)
    upper = jnp.dot(second_low, w_up, preferred_element_type=jnp.float32)
    hidden = jnp.square(jnp.maximum(upper, 0.0)).astype(jnp.bfloat16)
    if cotangent_in is None:
        result_rows = middle + jnp.dot(hidden, w_down, preferred_element_type=jnp.float32)
        return result_rows.astype(jnp.bfloat16).reshape(seq_count, block_rows, model_width)
    cotangent = cotangent_in.reshape(seq_count * block_rows, model_width)
    grad_down = jnp.dot(hidden.T, cotangent, preferred_element_type=jnp.float32)
    grad_hidden = jnp.dot(cotangent, w_down.T, preferred_element_type=jnp.float32)
    grad_upper = (2.0 * jnp.maximum(upper, 0.0) * grad_hidden).astype(jnp.bfloat16)
    grad_up = jnp.dot(second_low.T, grad_upper, preferred_element_type=jnp.float32)
    grad_second = jnp.dot(grad_upper, w_up.T, preferred_element_type=jnp.float32)
    grad_middle = cotangent.astype(jnp.float32) + norm_back_flat(
        grad_second, normal_two, inverse_two, params[2]
    )
    grad_middle_low = grad_middle.astype(jnp.bfloat16)
    grad_out = jnp.dot(attended.T, grad_middle_low, preferred_element_type=jnp.float32)
    grad_attended = jnp.dot(grad_middle_low, w_out.T, preferred_element_type=jnp.float32).astype(
        jnp.bfloat16
    )
    grad_attended = grad_attended.reshape(seq_count, block_rows, model_width)
    grad_queries, grad_keys, grad_values = attention(
        mixed, kv_full, seq_lengths, offset, grad_attended
    )
    key_term = jnp.concatenate([grad_keys, grad_values], axis=-1)
    norm_two = (jnp.sum(grad_second * normal_two, axis=0), jnp.sum(grad_second, axis=0))
    return (grad_queries, key_term, grad_middle, grad_out, grad_up, grad_down, norm_two)


def general_body(
    x_short,
    x_long,
    lengths,
    cot_short,
    cot_long,
    w_qkv,
    w_out,
    w_up,
    w_down,
    conv_kernel,
    norm_params,
):
    full_weights = (
        lax.all_gather(w_qkv, ("seq", "batch"), axis=0, tiled=True),
        lax.all_gather(w_out, ("seq", "batch"), axis=0, tiled=True),
        lax.all_gather(w_up, ("seq", "batch"), axis=0, tiled=True),
        lax.all_gather(w_down, ("seq", "batch"), axis=0, tiled=True),
        lax.all_gather(conv_kernel, ("seq", "batch"), axis=1, tiled=True),
        lax.all_gather(norm_params, ("seq", "batch"), axis=1, tiled=True),
    )
    inputs = (x_short, x_long)
    cotangents = (cot_short, cot_long)
    model_width = x_short.shape[2]
    offsets = (lax.axis_index("seq") * x_short.shape[1], lax.axis_index("seq") * x_long.shape[1])
    fronts = front_part(inputs, full_weights)
    kv_fwd = (
        lax.all_gather(fronts[0][5][:, :, model_width:], "seq", axis=1, tiled=True),
        lax.all_gather(fronts[1][5][:, :, model_width:], "seq", axis=1, tiled=True),
    )
    outputs = [
        rest_part(
            fronts[index_part],
            kv_fwd[index_part],
            lengths[index_part],
            offsets[index_part],
            full_weights,
            None,
        )
        for index_part in range(2)
    ]
    back_weights = (
        lax.all_gather(w_qkv, ("seq", "batch"), axis=0, tiled=True),
        lax.all_gather(w_out, ("seq", "batch"), axis=0, tiled=True),
        lax.all_gather(w_up, ("seq", "batch"), axis=0, tiled=True),
        lax.all_gather(w_down, ("seq", "batch"), axis=0, tiled=True),
        lax.all_gather(conv_kernel, ("seq", "batch"), axis=1, tiled=True),
        lax.all_gather(norm_params, ("seq", "batch"), axis=1, tiled=True),
    )
    fronts_back = front_part(inputs, back_weights)
    kv_back = (
        lax.all_gather(fronts_back[0][5][:, :, model_width:], "seq", axis=1, tiled=True),
        lax.all_gather(fronts_back[1][5][:, :, model_width:], "seq", axis=1, tiled=True),
    )
    partials = [
        rest_part(
            fronts_back[index_part],
            kv_back[index_part],
            lengths[index_part],
            offsets[index_part],
            back_weights,
            cotangents[index_part],
        )
        for index_part in range(2)
    ]
    kv_grads = (
        lax.psum_scatter(
            partials[0][1].astype(jnp.bfloat16), "seq", scatter_dimension=1, tiled=True
        ).astype(jnp.float32),
        lax.psum_scatter(
            partials[1][1].astype(jnp.bfloat16), "seq", scatter_dimension=1, tiled=True
        ).astype(jnp.float32),
    )
    grad_mixed = [
        jnp.concatenate([partials[index_part][0], kv_grads[index_part]], axis=-1)
        for index_part in range(2)
    ]
    received = (
        from_behind(grad_mixed[0][:, :2].astype(jnp.bfloat16), "seq", -1).astype(jnp.float32),
        from_behind(grad_mixed[1][:, :2].astype(jnp.bfloat16), "seq", -1).astype(jnp.float32),
    )
    kernel = back_weights[4].astype(jnp.float32)
    params = back_weights[5].astype(jnp.float32)
    w_qkv_full = back_weights[0]
    grad_qkv = jnp.zeros(w_qkv_full.shape, jnp.float32)
    grad_kernel = jnp.zeros(kernel.shape, jnp.float32)
    grad_norm = jnp.zeros((4, model_width), jnp.float32)
    grad_out = partials[0][3] + partials[1][3]
    grad_up = partials[0][4] + partials[1][4]
    grad_down = partials[0][5] + partials[1][5]
    input_grads = []
    for index_part in range(2):
        flat, normal_one, inverse_one, normed_low, padded, mixed = fronts_back[index_part]
        seq_count, block_rows, three_width = mixed.shape
        mixed_grad = grad_mixed[index_part]
        extended = jnp.concatenate([mixed_grad, received[index_part]], axis=1)
        grad_projected = (
            kernel[0] * extended[:, :block_rows]
            + kernel[1] * extended[:, 1 : block_rows + 1]
            + kernel[2] * extended[:, 2:]
        ).astype(jnp.bfloat16)
        grad_kernel = grad_kernel + jnp.stack(
            [
                jnp.sum(mixed_grad * padded[:, 2:], axis=(0, 1)),
                jnp.sum(mixed_grad * padded[:, 1 : block_rows + 1], axis=(0, 1)),
                jnp.sum(mixed_grad * padded[:, :block_rows], axis=(0, 1)),
            ]
        )
        grad_flat = grad_projected.reshape(seq_count * block_rows, three_width)
        grad_qkv = grad_qkv + jnp.dot(normed_low.T, grad_flat, preferred_element_type=jnp.float32)
        grad_normed = jnp.dot(grad_flat, w_qkv_full.T, preferred_element_type=jnp.float32)
        grad_input = partials[index_part][2] + norm_back_flat(
            grad_normed, normal_one, inverse_one, params[0]
        )
        input_grads.append(grad_input.reshape(seq_count, block_rows, model_width))
        norm_two = partials[index_part][6]
        grad_norm = grad_norm + jnp.stack(
            [
                jnp.sum(grad_normed * normal_one, axis=0),
                jnp.sum(grad_normed, axis=0),
                norm_two[0],
                norm_two[1],
            ]
        )
    summed = (
        lax.psum_scatter(grad_qkv, ("seq", "batch"), scatter_dimension=0, tiled=True),
        lax.psum_scatter(grad_out, ("seq", "batch"), scatter_dimension=0, tiled=True),
        lax.psum_scatter(grad_up, ("seq", "batch"), scatter_dimension=0, tiled=True),
        lax.psum_scatter(grad_down, ("seq", "batch"), scatter_dimension=0, tiled=True),
        lax.psum_scatter(grad_kernel, ("seq", "batch"), scatter_dimension=1, tiled=True),
        lax.psum_scatter(grad_norm, ("seq", "batch"), scatter_dimension=1, tiled=True),
    )
    return (
        outputs[0],
        outputs[1],
        input_grads[0],
        input_grads[1],
        summed[0],
        summed[1],
        summed[2],
        summed[3],
        summed[4],
        summed[5],
    )


def solution(mesh):
    split = mesh.shape["seq"] == 8
    return jax.shard_map(
        split_body if split else general_body,
        mesh=mesh,
        in_specs=(
            P("batch", "seq", None),
            P("batch", "seq", None),
            P(None, "batch"),
            P("batch", "seq", None),
            P("batch", "seq", None),
            P(("seq", "batch"), None),
            P(("seq", "batch"), None),
            P(("seq", "batch"), None),
            P(("seq", "batch"), None),
            P(None, ("seq", "batch")),
            P(None, ("seq", "batch")),
        ),
        out_specs=(
            P("batch", "seq", None),
            P("batch", "seq", None),
            P("batch", "seq", None),
            P("batch", "seq", None),
            P(("seq", "batch"), None),
            P(("seq", "batch"), None),
            P(("seq", "batch"), None),
            P(("seq", "batch"), None),
            P(None, ("seq", "batch")),
            P(None, ("seq", "batch")),
        ),
        check_vma=False,
    )
```

```python
import functools

import jax
import jax.numpy as jnp
from jax import lax
from jax.experimental import pallas as pl
from jax.experimental.pallas import tpu as pltpu
from jax.sharding import PartitionSpec as P

EPS = 1e-05
NEG_FILL = -1e30
HEAD_DIM = 64
LANES = 128
TRIPLE = 3 * LANES
TILE = 256
PAD = 16
MESH = pl.DeviceIdType.MESH
F32 = jnp.float32
BF16 = jnp.bfloat16
DMA = pltpu.SemaphoreType.DMA


def dot_nn(left, right):
    return lax.dot_general(left, right, (((1,), (0,)), ((), ())), preferred_element_type=F32)


def dot_nt(left, right):
    return lax.dot_general(left, right, (((1,), (1,)), ((), ())), preferred_element_type=F32)


def dot_tn(left, right):
    return lax.dot_general(left, right, (((0,), (0,)), ((), ())), preferred_element_type=F32)


def params_of(limit=60, **more):
    return pltpu.CompilerParams(vmem_limit_bytes=limit * 2**20, **more)


def vmem():
    return pl.BlockSpec(memory_space=pltpu.VMEM)


def smem():
    return pl.BlockSpec(memory_space=pltpu.SMEM)


def hbm():
    return pl.BlockSpec(memory_space=pl.ANY)


def normalise(values):
    average = jnp.mean(values, axis=-1, keepdims=True)
    centred = values - average
    inverse = lax.rsqrt(jnp.mean(centred * centred, axis=-1, keepdims=True) + EPS)
    return centred * inverse, inverse


def norm_back(grad, normal, inverse, gain):
    scaled_grad = grad * gain
    first_mean = jnp.mean(scaled_grad, axis=-1, keepdims=True)
    second_mean = jnp.mean(scaled_grad * normal, axis=-1, keepdims=True)
    return inverse * (scaled_grad - first_mean - normal * second_mean)


def shifted(window, by):
    return pltpu.roll(window, by % window.shape[0], 0)


def iota(shape, axis):
    return lax.broadcasted_iota(jnp.int32, shape, axis)


def times(index, size):
    return pl.ds(pl.multiple_of(index * size, size), size)


def position():
    index, batch = lax.axis_index("seq"), lax.axis_index("batch")
    return index // 2, index % 2, batch // 2, batch % 2


def at(z, core, y, x):
    return (z * 2 + core, y * 2 + x)


def remote(src, dst, send, recv, device):
    return pltpu.make_async_remote_copy(
        src_ref=src, dst_ref=dst, send_sem=send, recv_sem=recv, device_id=device, device_id_type=MESH
    )


def greet(others):
    barrier = pltpu.get_barrier_semaphore()
    for other in others:
        pl.semaphore_signal(barrier, inc=1, device_id=other, device_id_type=MESH)
    pl.semaphore_wait(barrier, len(others))


def whole_line():
    z, core, y, x = position()
    line = [at(lax.rem(z + step, 4), (core + turn) % 2, y, x) for turn in (0, 1) for step in (0, 1, 2, 3)]
    return line[1:]


def greet_all():
    z, core, y, x = position()
    greet(whole_line() + [at(z, core, 1 - y, x), at(z, core, y, 1 - x)])


def roles():
    z = lax.axis_index("seq") // 2
    half = z // 2
    near = jnp.where(half == 0, z, 3 - z)
    partner_z = jnp.where(half == 0, 1 - z, 5 - z)
    return half, near, partner_z, 2 - half


def z_of(half, place):
    return jnp.where(half == 0, place, 3 - place)


def long_source(seq, pair):
    near = 1 if pair % 3 == 2 else 0
    z = near if seq == 0 else 3 - near
    return z * 2 + pair // 3, 0 if near else pair % 3


def short_source(seq, pair):
    return (1 if seq == 0 else 2) * 2 + pair // 3, pair % 3


class Copies:
    def __init__(self, sems):
        self.sems, self.count, self.open = sems, 0, []

    def start(self, src, dst):
        copy = pltpu.make_async_copy(src, dst, self.sems.at[self.count])
        self.count += 1
        copy.start()
        self.open.append(copy)
        return copy

    def finish(self):
        for copy in self.open:
            copy.wait()
        self.open = []


class RowGather:
    def __init__(self, x_ref, o_ref, own_sem, send, recv, sib_send, sib_recv, inner_only):
        self.x_ref, self.o_ref, self.inner_only = x_ref, o_ref, inner_only
        self.own_sem, self.send, self.recv, self.sib_send, self.sib_recv = own_sem, send, recv, sib_send, sib_recv
        self.rows = x_ref.shape[1]
        self.z, self.core, self.y, self.x = position()
        self.half, self.near, self.partner_z, far_z = roles()
        self.sibling = at(self.z, 1 - self.core, self.y, self.x)
        self.partner = at(self.partner_z, self.core, self.y, self.x)
        place = self.block(self.z, self.core)
        mine, other = self.x_ref.at[self.half], self.x_ref.at[1 - self.half]
        self.to_partner = remote(mine, place, send.at[0], recv.at[self.near], self.partner)
        self.to_far = remote(other, place, send.at[1], recv.at[3 - self.near], at(far_z, self.core, self.y, self.x))
        self.to_sibling = remote(mine, place, sib_send.at[0], sib_recv.at[self.near], self.sibling)
        self.own = pltpu.make_async_copy(mine, place, own_sem)

    def block(self, z, core):
        return self.o_ref.at[times(z * 2 + core, self.rows)]

    def at_inner(self, act):
        if self.inner_only:
            pl.when(self.near == 1)(act)
        else:
            act()

    def start(self):
        if self.inner_only:
            pl.when(self.near == 0)(self.to_partner.start)
        else:
            self.to_partner.start()
        pl.when(self.near == 1)(self.to_far.start)

        def inside():
            self.to_sibling.start()
            self.own.start()

        self.at_inner(inside)

    def start_far(self):
        @pl.when(self.near == 0)
        def _():
            self.to_partner.wait_send()
            self.to_far.start()

    def moves(self, slot):
        place = (1 - self.near, 2, 3)[slot]
        block = self.block(z_of(self.half, place), self.core)
        arrival = remote(block, block, self.send.at[0], self.recv.at[place], self.partner)
        onward = remote(block, block, self.send.at[1 + slot], self.recv.at[place], self.partner)
        across = remote(block, block, self.sib_send.at[1 + slot], self.sib_recv.at[place], self.sibling)
        return arrival, onward, across

    def step(self, slot):
        arrival, onward, across = self.moves(slot)

        def inside():
            arrival.wait_recv()
            if slot and not self.inner_only:
                pl.when(self.near == 1)(onward.start)
            across.start()

        self.at_inner(inside)

    def whole(self, place):
        where = (self.near, 1 - self.near, 2, 3)[place]
        block = self.block(z_of(self.half, where), 1 - self.core)

        def inside():
            remote(block, block, self.sib_send.at[0], self.sib_recv.at[where], self.sibling).wait_recv()
            if place == 0:
                self.own.wait()

        self.at_inner(inside)

    def chip_rows(self, place):
        return z_of(self.half, (self.near, 1 - self.near, 2, 3)[place])

    def finish(self):
        if not self.inner_only:
            pl.when(self.near == 1)(self.to_partner.wait_send)
        self.to_far.wait_send()

        def inside():
            self.to_sibling.wait_send()
            for slot in range(3):
                _, onward, across = self.moves(slot)
                across.wait_send()
                if slot and not self.inner_only:
                    pl.when(self.near == 1)(onward.wait_send)

        self.at_inner(inside)


class ShardGather:
    def __init__(self, shard, full, own_sem, send, recv, halves=False):
        self.shard, self.full, self.own_sem, self.send_sem, self.recv_sem = shard, full, own_sem, send, recv
        self.z, self.core, self.y, self.x = position()
        self.halves = halves
        self.sent = []

    def go(self, src, dst, slot, device):
        copy = remote(src, dst, self.send_sem.at[slot], self.recv_sem.at[slot], device)
        copy.start()
        self.sent.append(copy)

    def arrived(self, dst, slot):
        remote(dst, dst, self.send_sem.at[0], self.recv_sem.at[slot], at(self.z, self.core, self.y, self.x)).wait_recv()

    def start(self):
        z, core, y, x = self.z, self.core, self.y, self.x
        mine = self.full.at[z, core, y, x]
        for step in (1, 2, 3):
            target = lax.rem(z + step, 4)
            self.go(self.shard, mine, step, at(target, core, y, x))
        self.own = pltpu.make_async_copy(self.shard, mine, self.own_sem)
        self.own.start()

    def part(self, core, zs, ys, xs, reader):
        ref = self.full.at[zs, core, ys, xs]
        return self.full.at[zs, core, ys, xs, reader] if self.halves else ref

    def across(self, zs, ys, xs, slot):
        ref = self.part(self.core, zs, ys, xs, 1 - self.core)
        self.go(ref, ref, slot, at(self.z, 1 - self.core, self.y, self.x))

    def over(self):
        z, core, y, x = self.z, self.core, self.y, self.x
        for step in (1, 2, 3):
            self.arrived(self.full.at[lax.rem(z + 4 - step, 4), core, y, x], step)
        self.own.wait()
        first, second = pl.ds(0, 2), pl.ds(2, 2)
        ref = self.full.at[first, core, y, x]
        self.go(ref, ref, 4, at(z, core, y, 1 - x))
        ref = self.full.at[second, core, y, x]
        self.go(ref, ref, 5, at(z, core, 1 - y, x))
        self.across(pl.ds(0, 4), y, x, 8)

    def turn(self):
        z, core, y, x = self.z, self.core, self.y, self.x
        first, second = pl.ds(0, 2), pl.ds(2, 2)
        self.arrived(self.full.at[first, core, y, 1 - x], 4)
        ref = self.full.at[first, core, y]
        self.go(ref, ref, 6, at(z, core, 1 - y, x))
        self.across(first, y, 1 - x, 9)
        self.arrived(self.full.at[second, core, 1 - y, x], 5)
        ref = self.full.at[second, core, :, x]
        self.go(ref, ref, 7, at(z, core, y, 1 - x))
        self.across(second, 1 - y, x, 10)

    def last(self):
        core, y, x = self.core, self.y, self.x
        first, second = pl.ds(0, 2), pl.ds(2, 2)
        self.arrived(self.full.at[first, core, 1 - y], 6)
        self.across(first, 1 - y, pl.ds(0, 2), 11)
        self.arrived(self.full.at[second, core, :, 1 - x], 7)
        self.across(second, pl.ds(0, 2), 1 - x, 12)

    def finish(self):
        y, x, core, other = self.y, self.x, self.core, 1 - self.core
        first, second, both = pl.ds(0, 2), pl.ds(2, 2), pl.ds(0, 2)
        parts = (
            (pl.ds(0, 4), y, x), (first, y, 1 - x), (second, 1 - y, x), (first, 1 - y, both), (second, both, 1 - x),
        )
        for slot, (zs, ys, xs) in enumerate(parts):
            self.arrived(self.part(other, zs, ys, xs, core), 8 + slot)

    def sends_done(self):
        for copy in self.sent:
            copy.wait_send()


def add_into(total, part):
    total[...] = (total[...].astype(F32) + part[...].astype(F32)).astype(total.dtype)


class CoreSum:
    def __init__(self, grad, sib, out, send, recv, save):
        self.grad, self.sib, self.out, self.save = grad, sib, out, save
        z, self.core, y, x = position()
        self.copy = remote(grad.at[:, 1 - self.core], sib, send, recv, at(z, 1 - self.core, y, x))

    def start(self):
        self.copy.start()

    def add(self):
        self.copy.wait_recv()

        @pl.loop(0, 4)
        def _(zz):
            for ys in range(2):
                for xs in range(2):
                    add_into(self.sib.at[zz, ys, xs], self.grad.at[zz, self.core, ys, xs])

        self.kept = pltpu.make_async_copy(self.sib, self.out, self.save)
        self.kept.start()

    def finish(self):
        self.copy.wait_send()
        self.kept.wait()


class ShardSum:
    def __init__(self, grad, out, bufs, own_sem, send, recv):
        self.grad, self.out = grad, out
        self.near_x, self.near_y, self.one, self.two, self.line = bufs
        self.own_sem, self.send_sem, self.recv_sem = own_sem, send, recv
        self.z, self.core, self.y, self.x = position()
        self.sent = []
        first, second = pl.ds(0, 2), pl.ds(2, 2)
        self.loads = (
            pltpu.make_async_copy(grad.at[first, :, self.x], self.near_x, own_sem.at[0]),
            pltpu.make_async_copy(grad.at[second, self.y], self.near_y, own_sem.at[1]),
        )

    def copy(self, src, dst, slot, device):
        return remote(src, dst, self.send_sem.at[slot], self.recv_sem.at[slot], device)

    def go(self, src, dst, slot, device):
        copy = self.copy(src, dst, slot, device)
        copy.start()
        self.sent.append(copy)

    def arrived(self, dst, slot):
        remote(dst, dst, self.send_sem.at[0], self.recv_sem.at[slot], at(self.z, self.core, self.y, self.x)).wait_recv()

    def moves(self):
        z, core, y, x = self.z, self.core, self.y, self.x
        first, second = pl.ds(0, 2), pl.ds(2, 2)
        return [
            self.copy(self.grad.at[first, :, 1 - x], self.one.at[0], 2, at(z, core, y, 1 - x)),
            self.copy(self.grad.at[second, 1 - y], self.one.at[1], 3, at(z, core, 1 - y, x)),
            self.copy(self.near_x.at[:, 1 - y], self.two.at[0], 4, at(z, core, 1 - y, x)),
            self.copy(self.near_y.at[:, 1 - x], self.two.at[1], 5, at(z, core, y, 1 - x)),
        ]

    def to_line(self, step):
        z, core, y, x = self.z, self.core, self.y, self.x
        target = lax.rem(z + step, 4)
        device = at(target, core, y, x)
        low = self.copy(self.near_x.at[lax.rem(target, 2), y], self.line.at[step - 1], 5 + step, device)
        high = self.copy(self.near_y.at[lax.rem(target, 2), x], self.line.at[step - 1], 5 + step, device)
        return target, low, high

    def start(self):
        for copy in self.moves()[:2]:
            copy.start()
        for copy in self.loads:
            copy.start()

    def turn(self):
        moves = self.moves()
        self.loads[0].wait()
        self.arrived(self.one.at[0], 2)
        for zz in range(2):
            for ys in range(2):
                add_into(self.near_x.at[zz, ys], self.one.at[0, zz, ys])
        moves[2].start()
        self.loads[1].wait()
        self.arrived(self.one.at[1], 3)
        for zz in range(2):
            for xs in range(2):
                add_into(self.near_y.at[zz, xs], self.one.at[1, zz, xs])
        moves[3].start()

    def last(self):
        y, x = self.y, self.x
        self.arrived(self.two.at[0], 4)
        for zz in range(2):
            add_into(self.near_x.at[zz, y], self.two.at[0, zz])
        self.arrived(self.two.at[1], 5)
        for zz in range(2):
            add_into(self.near_y.at[zz, x], self.two.at[1, zz])
        for step in (1, 2, 3):
            target, low, high = self.to_line(step)
            pl.when(target < 2)(low.start)
            pl.when(target >= 2)(high.start)

    def finish(self):
        z, y, x = self.z, self.y, self.x
        low = self.near_x[lax.rem(z, 2), y].astype(F32)
        high = self.near_y[lax.rem(z, 2), x].astype(F32)
        total = jnp.where(z < 2, low, high)
        for step in (1, 2, 3):
            self.arrived(self.line.at[step - 1], 5 + step)
            total = total + self.line[step - 1].astype(F32)
        self.out[...] = total
        for copy in self.moves():
            copy.wait_send()
        for step in (1, 2, 3):
            target, low, high = self.to_line(step)
            pl.when(target < 2)(low.wait_send)
            pl.when(target >= 2)(high.wait_send)

    @staticmethod
    def buffers(grad):
        tail, kind = grad.shape[3:], grad.dtype
        return [
            pltpu.VMEM((2, 2) + tail, kind),
            pltpu.VMEM((2, 2) + tail, kind),
            pltpu.VMEM((2, 2, 2) + tail, kind),
            pltpu.VMEM((2, 2) + tail, kind),
            pltpu.VMEM((3,) + tail, kind),
        ]


class GroupSum:
    def __init__(self, bufs, send, recv):
        self.tot, self.one, self.two, self.line = bufs
        self.send_sem, self.recv_sem = send, recv
        self.z, self.core, self.y, self.x = position()
        self.sent = []

    copy = ShardSum.copy
    go = ShardSum.go
    arrived = ShardSum.arrived

    def start(self, total):
        z, core, y, x = self.z, self.core, self.y, self.x
        rows = self.tot.shape[4]
        for zz in range(4):
            for cc in range(2):
                for yy in range(2):
                    for xx in range(2):
                        first = (((zz * 2 + cc) * 2 + yy) * 2 + xx) * rows
                        self.tot[zz, cc, yy, xx] = total[first : first + rows].astype(BF16)
        self.go(self.tot.at[pl.ds(0, 2), :, :, 1 - x], self.one.at[0], 0, at(z, core, y, 1 - x))
        self.go(self.tot.at[pl.ds(2, 2), :, 1 - y], self.one.at[1], 1, at(z, core, 1 - y, x))

    def turn(self):
        z, core, y, x = self.z, self.core, self.y, self.x
        self.arrived(self.one.at[0], 0)

        @pl.loop(0, 2)
        def _(zz):
            for cc in range(2):
                for ys in range(2):
                    add_into(self.tot.at[zz, cc, ys, x], self.one.at[0, zz, cc, ys])

        self.go(self.tot.at[pl.ds(0, 2), :, 1 - y, x], self.two.at[0], 2, at(z, core, 1 - y, x))
        self.arrived(self.one.at[1], 1)

        @pl.loop(0, 2)
        def _(zz):
            for cc in range(2):
                for xs in range(2):
                    add_into(self.tot.at[2 + zz, cc, y, xs], self.one.at[1, zz, cc, xs])

        self.go(self.tot.at[pl.ds(2, 2), :, y, 1 - x], self.two.at[1], 3, at(z, core, y, 1 - x))

    def last(self):
        z, core, y, x = self.z, self.core, self.y, self.x
        for side in (0, 1):
            self.arrived(self.two.at[side], 2 + side)

            @pl.loop(0, 2)
            def _(zz, side=side):
                for cc in range(2):
                    add_into(self.tot.at[2 * side + zz, cc, y, x], self.two.at[side, zz, cc])

        mine = z * 2 + core
        for step in range(1, 8):
            target = lax.rem(mine + step, 8)
            tz, tc = target // 2, target % 2
            self.go(self.tot.at[tz, tc, y, x], self.line.at[step - 1], 3 + step, at(tz, tc, y, x))

    def finish(self, out):
        z, core, y, x = self.z, self.core, self.y, self.x
        mine = z * 2 + core
        for step in range(1, 8):
            self.arrived(self.line.at[step - 1], 3 + step)
        own = self.tot[z, core, y, x].astype(F32)
        width = out.shape[1] // 3
        for side in (0, 1):
            total = None
            for source in (side, side + 2, side + 4, side + 6):
                back = lax.rem(mine - source + 8 + 7, 8)
                term = jnp.where(back == 7, own, self.line[jnp.minimum(back, 6)].astype(F32))
                total = term if total is None else total + term
            for j in range(3):
                for kind in range(3):
                    first = kind * width + (3 * side + j) * LANES
                    source = (3 * j + kind) * LANES
                    out[:, first : first + LANES] = total[:, source : source + LANES]
        for copy in self.sent:
            copy.wait_send()

    @staticmethod
    def buffers(rows, columns):
        return [
            pltpu.VMEM((4, 2, 2, 2, rows, columns), BF16),
            pltpu.VMEM((2, 2, 2, 2, rows, columns), BF16),
            pltpu.VMEM((2, 2, 2, rows, columns), BF16),
            pltpu.VMEM((7, rows, columns), BF16),
        ]


class SmallSum:
    def __init__(self, bufs, out, send, recv):
        self.norms, self.swap, self.acc, self.got, self.line = bufs
        self.out, self.send_sem, self.recv_sem = out, send, recv
        self.z, self.core, self.y, self.x = position()
        self.sent = []
        self.cut = self.norms.shape[2]

    copy = ShardSum.copy
    go = ShardSum.go
    arrived = ShardSum.arrived

    def start(self, kernel_grad, norm_grad):
        z, core, y, x = self.z, self.core, self.y, self.x
        cut = self.cut
        self.norms[0] = norm_grad[:, :cut]
        self.norms[1] = norm_grad[:, cut:]
        self.acc[0, :, : kernel_grad.shape[1]] = kernel_grad
        self.go(self.norms.at[1 - core], self.swap, 0, at(z, 1 - core, y, x))

    def over(self):
        z, core, y, x = self.z, self.core, self.y, self.x
        self.arrived(self.swap, 0)
        self.acc[0, :, self.acc.shape[2] - self.cut :] = self.norms[core] + self.swap[...]
        self.go(self.acc.at[0], self.got.at[0], 1, at(z, core, y, 1 - x))

    def turn(self):
        z, core, y, x = self.z, self.core, self.y, self.x
        self.arrived(self.got.at[0], 1)
        self.acc[1] = self.acc[0] + self.got[0]
        self.go(self.acc.at[1], self.got.at[1], 2, at(z, core, 1 - y, x))

    def last(self):
        z, core, y, x = self.z, self.core, self.y, self.x
        self.arrived(self.got.at[1], 2)
        self.acc[2] = self.acc[1] + self.got[1]
        for step in (1, 2, 3):
            self.go(self.acc.at[2], self.line.at[step - 1], 2 + step, at(lax.rem(z + step, 4), core, y, x))

    def swap_back(self):
        z, core, y, x = self.z, self.core, self.y, self.x
        for step in (1, 2, 3):
            self.arrived(self.line.at[step - 1], 2 + step)
        total = None
        for source in range(4):
            back = lax.rem(z - source + 4, 4)
            term = jnp.where(back == 0, self.acc[2], self.line[jnp.maximum(back - 1, 0)])
            total = term if total is None else total + term
        self.out[core] = total
        self.go(self.out.at[core], self.out.at[core], 6, at(z, 1 - core, y, x))

    def finish(self):
        self.arrived(self.out.at[1 - self.core], 6)
        for copy in self.sent:
            copy.wait_send()

    @staticmethod
    def buffers(columns, norm_columns):
        wide = columns + norm_columns
        return [
            pltpu.VMEM((2, 8, norm_columns), F32),
            pltpu.VMEM((8, norm_columns), F32),
            pltpu.VMEM((3, 8, wide), F32),
            pltpu.VMEM((2, 8, wide), F32),
            pltpu.VMEM((3, 8, wide), F32),
        ]


def causal_mask():
    return iota((TILE, TILE), 0) <= iota((TILE, TILE), 1)


def place_small(smalls, kernel_out, norm_out, core, part, cut):
    wide, width = kernel_out.shape[1], norm_out.shape[1]
    column = iota((LANES, wide), 1)
    block, lane = column // LANES, column % LANES
    source = (block % 3) * width + (core * 3 + block // 3) * LANES + lane - iota((LANES, wide), 0)
    norm_source = iota((LANES, width), 1) - iota((LANES, width), 0)
    kernel_out[...] = jnp.zeros_like(kernel_out)
    norm_out[...] = jnp.zeros_like(norm_out)

    @pl.loop(0, smalls.shape[0])
    def _(device):
        low = smalls[device].astype(BF16)
        kernel_out[...] += dot_nn(low, jnp.where(source == device * part, 1.0, 0.0).astype(BF16))
        norm_out[...] += dot_nn(low, jnp.where(norm_source == device * cut, 1.0, 0.0).astype(BF16))

    norm_out[0:4] = norm_out[3:7]


def attend(query_ref, key_ref, value_t, lse, out_t, head, block):
    rows, past = slice(block * TILE, (block + 1) * TILE), slice(0, block * TILE)
    query = query_ref[head, rows]
    diagonal = jnp.where(causal_mask(), dot_nt(key_ref[head, rows], query), NEG_FILL)
    top = jnp.max(diagonal, axis=0, keepdims=True)
    if block:
        before = dot_nt(key_ref[head, past], query)
        top = jnp.maximum(top, jnp.max(before, axis=0, keepdims=True))
        exp_before = jnp.exp(before - top)
    exp_diagonal = jnp.exp(diagonal - top)
    norm = jnp.sum(exp_diagonal, axis=0, keepdims=True)
    if block:
        norm = norm + jnp.sum(exp_before, axis=0, keepdims=True)
    lse[head, :, rows] = top + jnp.log(norm)
    inverse = 1.0 / norm
    result = dot_nn(value_t[head, :, rows], (exp_diagonal * inverse).astype(BF16))
    if block:
        result = result + dot_nn(value_t[head, :, past], (exp_before * inverse).astype(BF16))
    out_t[head, :, rows] = result


def convolve(proj, taps, slot, local, start, length, query_ref, key_ref, value_ref, key_t, value_t):
    window = proj[slot, pl.ds(pl.multiple_of(start, PAD), TILE + PAD)].astype(F32)
    columns = times(local, TRIPLE)
    mixed = (
        taps[0:1, columns] * window[PAD:]
        + taps[1:2, columns] * shifted(window, 1)[PAD:]
        + taps[2:3, columns] * shifted(window, 2)[PAD:]
    ).astype(BF16).astype(F32)
    query, key, value = mixed[:, 0:LANES] * (HEAD_DIM**-0.5), mixed[:, LANES : 2 * LANES], mixed[:, 2 * LANES :]
    rows = pl.ds(pl.multiple_of(start, TILE), TILE)
    lanes = iota((TILE, LANES), 1)
    low_half = lanes < HEAD_DIM
    bias = jnp.where(start + iota((TILE, LANES), 0) < length, 0.0, NEG_FILL)
    at_zero, at_half = lanes == 0, lanes == HEAD_DIM
    query_ref[2 * slot, rows] = jnp.where(low_half, query, jnp.where(at_half, 1.0, 0.0)).astype(BF16)
    query_ref[2 * slot + 1, rows] = jnp.where(low_half, jnp.where(at_zero, 1.0, 0.0), query).astype(BF16)
    key_ref[2 * slot, rows] = jnp.where(low_half, key, jnp.where(at_half, bias, 0.0)).astype(BF16)
    key_ref[2 * slot + 1, rows] = jnp.where(low_half, jnp.where(at_zero, bias, 0.0), key).astype(BF16)
    value_ref[slot, rows] = value.astype(BF16)
    turned_key, turned_value = key.T.astype(BF16), value.T.astype(BF16)
    for head in range(2):
        part = slice(head * HEAD_DIM, (head + 1) * HEAD_DIM)
        key_t[2 * slot + head, :, rows] = turned_key[part]
        value_t[2 * slot + head, :, rows] = turned_value[part]


def first_kernel(
    lens, xs_ref, xl_ref, qkv_ref, conv_ref, norm_ref, out_s, up_s, down_s,
    att, full_out, full_up, full_down, xs_o, xl_o, wq_o, taps_o, norms_o,
    ql_o, kl_o, vl_o, ktl_o, lsel_o, pl_o, ol_o, qs_o, ks_o, vs_o, kts_o, lses_o, ps_o, os_o,
    xs, xl, small, smalls, shard, wq_parts, wq, taps, norms,
    ql, kl, vl, ktl, lsel, proj_l, ol, qs, ks, vs, kts, lses, proj_s, os,
    vtl, vts, otl, ots,
    own_sem, send, recv, sib_send, sib_recv, shard_own, shard_send, shard_recv,
    att_send_l, att_recv_l, att_send_s, att_recv_s, att_own_l, att_own_s, save_sem,
):
    z, core, y, x = position()
    half, near, _, _ = roles()
    index = z * 2 + core
    pairs_long = 2 - near
    own_short, own_long = xs_ref.shape[1], xl_ref.shape[1]
    owned = own_short + own_long
    long_rows, short_rows = xl.shape[0], xs.shape[0]
    part, cut = conv_ref.shape[1], norm_ref.shape[1]
    length_short = jnp.where(half == 0, lens[0, 0], lens[0, 1])
    length_long = jnp.where(half == 0, lens[1, 0], lens[1, 1])

    small[...] = jnp.zeros_like(small)
    small[0:3, 0:part] = conv_ref[...].astype(F32)
    small[3:7, 0:cut] = norm_ref[...].astype(F32)
    width = wq.shape[0]
    for side in range(2):
        for j in range(3):
            for kind in range(3):
                source = kind * width + (3 * side + j) * LANES
                target = (3 * j + kind) * LANES
                shard[side, :, target : target + LANES] = qkv_ref[:, source : source + LANES]
    greet_all()
    rows_short = RowGather(
        xs_ref, xs, own_sem.at[0], send.at[0], recv.at[0], sib_send.at[0], sib_recv.at[0], True
    )
    rows_long = RowGather(
        xl_ref, xl, own_sem.at[1], send.at[1], recv.at[1], sib_send.at[1], sib_recv.at[1], False
    )
    weights = [
        ShardGather(a, f, shard_own.at[i], shard_send.at[i], shard_recv.at[i], halves=i == 1)
        for i, (a, f) in enumerate(
            ((small, smalls), (shard, wq_parts), (out_s, full_out), (up_s, full_up), (down_s, full_down))
        )
    ]
    early, late = weights[:2], weights[2:]
    for one in early:
        one.start()
    rows_long.start()
    zeros = jnp.zeros((PAD, TRIPLE), BF16)
    for slot in range(2):
        proj_l[slot, 0:PAD] = zeros
    for slot in range(3):
        proj_s[slot, 0:PAD] = zeros
    rows_long.start_far()
    rows_short.start()
    for one in early:
        one.over()
    rows_long.step(0)
    for one in early:
        one.turn()
    rows_short.start_far()
    for one in late[:2]:
        one.start()
    rows_long.step(1)
    for one in early:
        one.last()
    rows_long.step(2)
    late[2].start()
    for one in early:
        one.finish()
    place_small(smalls.reshape(32, 8, LANES), taps, norms, core, part, cut)

    pieces = wq_parts.shape[5]
    for zz in range(4):
        for cc in range(2):
            for yy in range(2):
                first = ((zz * 2 + cc) * 2 + yy) * 2 * pieces
                both = jnp.concatenate(
                    [wq_parts[zz, cc, yy, xx, core].astype(F32) for xx in range(2)], axis=0
                )
                wq[first : first + 2 * pieces] = both.astype(BF16)
    gain, offset = norms[0:1], norms[1:2]

    def project(x_ref, proj, start, size, slots, first_pair):
        normal, _ = normalise(x_ref[pl.ds(pl.multiple_of(start, size), size)].astype(F32))
        low = (normal * gain + offset).astype(BF16)

        @pl.loop(0, slots)
        def _(slot):
            result = dot_nn(low, wq[:, times(slot + first_pair, TRIPLE)])
            proj[slot, pl.ds(pl.multiple_of(PAD + start, PAD), size)] = result.astype(BF16)

    def project_long(place):
        @pl.loop(0, 2)
        def _(side):
            project(xl, proj_l, rows_long.chip_rows(place) * 2 * own_long + side * TILE, TILE, pairs_long, 2 * near)

    def project_short(place):
        @pl.when(near == 1)
        def _():
            project(xs, proj_s, rows_short.chip_rows(place) * 2 * own_short, TILE, 3, 0)

    for place in range(3):
        rows_long.whole(place)
        project_long(place)
    for slot in range(3):
        rows_short.step(slot)
    for place in range(4):
        rows_short.whole(place)
        project_short(place)
    rows_long.whole(3)
    project_long(3)
    for one in late[:2]:
        one.over()

    @pl.when(near == 1)
    def _():
        @pl.loop(0, 3)
        def _(slot):
            @pl.loop(0, short_rows // TILE)
            def _(step):
                convolve(proj_s, taps, slot, slot, step * TILE, length_short, qs, ks, vs, kts, vts)

    saves = Copies(save_sem)

    def to_owner(o_ref, slot, first, rows, owner, row_in_owner, pair, send_sem, recv_sem, own_sem):
        source = o_ref.at[slot, pl.ds(first, rows)]
        target = att.at[
            pl.ds(pl.multiple_of(half * owned + row_in_owner, LANES), rows), times(pair, LANES)
        ]
        far = remote(source, target, send_sem, recv_sem, (owner, y * 2 + x))
        close = pltpu.make_async_copy(source, target, own_sem)
        return far, close

    def short_moves(slot, owner):
        return to_owner(
            os, slot, owner * own_short, own_short, owner, 0, 3 * core + slot,
            att_send_s.at[slot, owner], att_recv_s.at[half, 3 * core + slot], att_own_s.at[slot],
        )

    def long_moves(slot, owner):
        pair = 3 * core + slot + 2 * near
        return to_owner(
            ol, slot, owner * own_long, own_long, owner, own_short, pair,
            att_send_l.at[slot, owner], att_recv_l.at[half, pair], att_own_l.at[slot],
        )

    def send_block(o_ref, o_t, slot, block, moves, owners):
        rows = slice(block * TILE, (block + 1) * TILE)
        both = jnp.concatenate([o_t[2 * slot, :, rows], o_t[2 * slot + 1, :, rows]], axis=0)
        o_ref[slot, rows] = both.T.astype(BF16)
        for owner in owners:
            far, close = moves(slot, owner)
            pl.when(index != owner)(far.start)
            pl.when(index == owner)(close.start)

    for block in (0, 2, 1, 3):

        @pl.when(near == 1)
        def _(block=block):
            @pl.loop(0, 6)
            def _(head):
                attend(qs, ks, vts, lses, ots, head, block)

            @pl.loop(0, 3)
            def _(slot):
                send_block(os, ots, slot, block, short_moves, (2 * block, 2 * block + 1))


    @pl.loop(0, pairs_long)
    def _(slot):
        @pl.loop(0, long_rows // TILE)
        def _(step):
            convolve(proj_l, taps, slot, slot + 2 * near, step * TILE, length_long, ql, kl, vl, ktl, vtl)

    for source, target in ((xl, xl_o), (wq, wq_o), (taps, taps_o), (norms, norms_o)):
        saves.start(source, target)
    for source, target in ((ql, ql_o), (kl, kl_o), (vl, vl_o), (ktl, ktl_o), (proj_l, pl_o)):
        saves.start(source, target)
    for source, target in ((xs, xs_o), (qs, qs_o), (ks, ks_o), (vs, vs_o), (kts, kts_o), (proj_s, ps_o), (lses, lses_o), (os, os_o)):
        saves.start(source, target)

    order = (0, 4, 1, 5, 2, 6, 3, 7)
    for step, block in enumerate(order):

        @pl.loop(0, 2 * pairs_long)
        def _(head, block=block):
            attend(ql, kl, vtl, lsel, otl, head, block)

        @pl.loop(0, pairs_long)
        def _(slot, block=block):
            send_block(ol, otl, slot, block, long_moves, (block,))

        if step == 0:
            late[0].turn()
            late[1].turn()
        if step == 3:
            late[0].last()
            late[1].last()
            late[2].over()
        if step == 5:
            late[2].turn()
    for source, target in ((lsel, lsel_o), (ol, ol_o)):
        saves.start(source, target)
    late[2].last()
    for one in late:
        one.finish()
    for one in weights:
        one.sends_done()

    def own_or_wait(source, moves, slot, arrival):
        @pl.when(index == source)
        def _():
            moves(slot, index)[1].wait()

        @pl.when(index != source)
        def _():
            arrival.wait_recv()

    me = (index, y * 2 + x)
    for seq in range(2):
        for pair in range(6):
            columns = pl.ds(pair * LANES, LANES)
            block = att.at[pl.ds(seq * owned + own_short, own_long), columns]
            source, slot = long_source(seq, pair)
            own_or_wait(
                source, long_moves, slot,
                remote(block, block, att_send_l.at[0, 0], att_recv_l.at[seq, pair], me),
            )
            block = att.at[pl.ds(seq * owned, own_short), columns]
            source, slot = short_source(seq, pair)
            own_or_wait(
                source, short_moves, slot,
                remote(block, block, att_send_s.at[0, 0], att_recv_s.at[seq, pair], me),
            )

    def sends_done(moves, slot):
        for owner in range(8):
            far, _ = moves(slot, owner)
            pl.when(index != owner)(far.wait_send)

    sends_done(long_moves, 0)
    pl.when(near == 0)(lambda: sends_done(long_moves, 1))

    @pl.when(near == 1)
    def _():
        for slot in range(3):
            sends_done(short_moves, slot)

    rows_long.finish()
    rows_short.finish()
    saves.finish()


def first_part(lengths, x_short, x_long, w_qkv, conv_kernel, norm_params, w_out, w_up, w_down, count):
    width = x_short.shape[2]
    short, long = count * x_short.shape[1], count * x_long.shape[1]
    owned = x_short.shape[1] + x_long.shape[1]
    wide = w_qkv.shape[1] // 2
    rows = w_qkv.shape[0]
    out = jax.ShapeDtypeStruct

    def saved(pairs, total):
        return [
            ((2 * pairs, total, LANES), BF16),
            ((2 * pairs, total, LANES), BF16),
            ((pairs, total, LANES), BF16),
            ((2 * pairs, HEAD_DIM, total), BF16),
            ((2 * pairs, 1, total), F32),
            ((pairs, PAD + total, TRIPLE), BF16),
            ((pairs, total, LANES), BF16),
        ]

    kept = saved(2, long) + saved(3, short)
    basic = [((short, width), BF16), ((long, width), BF16)]
    consts = [((width, wide), BF16), ((8, wide), F32), ((8, width), F32)]
    full = [((4, 2, 2, 2) + w.shape, BF16) for w in (w_out, w_up, w_down)]
    outs = [((2 * owned, width), BF16)] + full + basic + consts + kept
    scratch = (
        basic
        + [((8, LANES), F32), ((4, 2, 2, 2, 8, LANES), F32), ((2, rows, wide), BF16)]
        + [((4, 2, 2, 2, 2, rows, wide), BF16)]
        + consts
        + kept
        + [((4, HEAD_DIM, long), BF16), ((6, HEAD_DIM, short), BF16)]
        + [((4, HEAD_DIM, long), F32), ((6, HEAD_DIM, short), F32)]
    )
    return pl.pallas_call(
        first_kernel,
        out_shape=tuple(out(*one) for one in outs),
        in_specs=[smem(), hbm(), hbm(), vmem(), vmem(), vmem(), hbm(), hbm(), hbm()],
        out_specs=tuple([hbm()] * len(outs)),
        scratch_shapes=[pltpu.VMEM(*one) for one in scratch]
        + [DMA((2,))] + [DMA((2, 4))] * 4
        + [DMA((5,)), DMA((5, 13)), DMA((5, 13))]
        + [DMA((2, 8)), DMA((2, 6)), DMA((3, 8)), DMA((2, 6)), DMA((2,)), DMA((3,))]
        + [DMA((24,))],
        compiler_params=params_of(collective_id=0, has_side_effects=True),
    )(lengths, x_short, x_long, w_qkv, conv_kernel, norm_params, w_out, w_up, w_down)


def second_kernel(
    xs_ref, xl_ref, att, cs_ref, cl_ref, np_ref, wo_ref, wu_ref, wd_ref,
    ys_ref, yl_ref, gmid, gnorm, gwo_o, gwu_o, gwd_o, gl_o, gs_o,
    wo, wu, wd, middle, normal_two, inverse_two, second, second_t, cot, y_acc, gsec, gml, hid, gup,
    gwo, gwu, gwd, sib_out, sib_up, sib_down,
    load_sem, save_sem, send_l, recv_l, send_s, recv_s, core_send, core_recv,
):
    z, core, y, x = position()
    half, near, _, _ = roles()
    index = z * 2 + core
    pairs_long = 2 - near
    loads = Copies(load_sem)
    got_out = loads.start(wo_ref, wo)
    got_up = loads.start(wu_ref, wu)
    got_down = loads.start(wd_ref, wd)
    greet(whole_line())
    short, long = xs_ref.shape[1], xl_ref.shape[1]
    owned = short + long
    rows_all = 2 * owned
    for seq in range(2):
        first = seq * owned
        cot[first : first + short] = cs_ref[seq]
        cot[first + short : first + owned] = cl_ref[seq]
        middle[first : first + short] = xs_ref[seq].astype(F32)
        middle[first + short : first + owned] = xl_ref[seq].astype(F32)
    got_out.wait()

    @pl.loop(0, rows_all // TILE)
    def _(step):
        rows = times(step, TILE)
        values = middle[rows] + dot_nn(att[rows], wo[...])
        normal, inverse = normalise(values)
        normal_two[rows] = normal
        inverse_two[rows] = inverse
        second[rows] = (normal * np_ref[2:3] + np_ref[3:4]).astype(BF16)
        y_acc[rows] = values
        gsec[rows] = jnp.zeros_like(values)

    second_t[...] = second[...].T
    inner = 512
    got_up.wait()
    got_down.wait()

    @pl.loop(0, wu.shape[1] // inner)
    def _(step):
        columns = times(step, inner)
        upper = jnp.maximum(dot_nn(second[...], wu[:, columns]), 0.0)
        hidden = (upper * upper).astype(BF16)
        grad_hidden = dot_nt(cot[...], wd[columns])
        grad_upper = (2.0 * upper * grad_hidden).astype(BF16)
        hid[:, columns] = hidden
        gup[:, columns] = grad_upper
        y_acc[...] += dot_nn(hidden, wd[columns])
        gsec[...] += dot_nt(grad_upper, wu[:, columns])

    gnorm[...] = jnp.zeros_like(gnorm)

    @pl.loop(0, rows_all // TILE)
    def _(step):
        rows = times(step, TILE)
        grad = gsec[rows]
        normal = normal_two[rows]
        gnorm[2:3] += jnp.sum(grad * normal, axis=0, keepdims=True)
        gnorm[3:4] += jnp.sum(grad, axis=0, keepdims=True)
        total = cot[rows].astype(F32) + norm_back(grad, normal, inverse_two[rows], np_ref[2:3])
        gmid[rows] = total
        gml[rows] = total.astype(BF16)
        second[rows] = dot_nt(gml[rows], wo[...]).astype(BF16)

    def moves(seq, pair, is_long):
        target, slot = (long_source if is_long else short_source)(seq, pair)
        rows = long if is_long else short
        out, send, recv = (gl_o, send_l, recv_l) if is_long else (gs_o, send_s, recv_s)
        first = seq * owned + (short if is_long else 0)
        source = second.at[pl.ds(first, rows), pl.ds(pair * LANES, LANES)]
        place = out.at[slot, times(index, rows)]
        far = remote(source, place, send.at[seq, pair], recv.at[slot, index], (target, y * 2 + x))
        close = pltpu.make_async_copy(source, place, recv.at[slot, index])
        return target, far, close

    kinds = [(seq, pair, is_long) for is_long in (True, False) for pair in range(6) for seq in range(2)]
    for kind in kinds:
        target, far, close = moves(*kind)
        pl.when(index != target)(far.start)
        pl.when(index == target)(close.start)

    sums = [
        CoreSum(grad, sib, total, core_send.at[i], core_recv.at[i], save_sem.at[i])
        for i, (grad, sib, total) in enumerate(
            ((gwu, sib_up, gwu_o), (gwd, sib_down, gwd_o), (gwo, sib_out, gwo_o))
        )
    ]

    def cut(value, grad):
        return value.reshape(grad.shape[:5] + value.shape[1:]).astype(BF16)

    @pl.loop(0, wu.shape[1] // inner)
    def _(step):
        columns = times(step, inner)
        gwu[:, :, :, :, :, columns] = cut(dot_nn(second_t[...], gup[:, columns]), gwu)

    sums[0].start()
    per = gwd.shape[4]
    slabs = gwd.shape[2] * gwd.shape[3]

    @pl.loop(0, gwd.shape[0])
    def _(zz):
        for cc in range(2):
            columns = times(zz * 2 + cc, slabs * per)
            value = dot_tn(hid[:, columns], cot[...])
            gwd[zz, cc] = value.reshape(gwd.shape[2:]).astype(BF16)

    sums[1].start()
    gwo[...] = cut(dot_tn(att[...], gml[...]), gwo)
    sums[2].start()
    for seq in range(2):
        first = seq * owned
        ys_ref[seq] = y_acc[first : first + short].astype(BF16)
        yl_ref[seq] = y_acc[first + short : first + owned].astype(BF16)

    for one in sums:
        one.add()
    me = (index, y * 2 + x)

    def arrivals(out, recv, slot, rows):
        for source in range(8):
            block = out.at[slot, pl.ds(source * rows, rows)]

            @pl.when(index != source)
            def _(block=block, source=source):
                remote(block, block, send_l.at[0, 0], recv.at[slot, source], me).wait_recv()

    arrivals(gl_o, recv_l, 0, long)
    pl.when(near == 0)(lambda: arrivals(gl_o, recv_l, 1, long))

    @pl.when(near == 1)
    def _():
        for slot in range(3):
            arrivals(gs_o, recv_s, slot, short)

    for kind in kinds:
        target, far, close = moves(*kind)
        pl.when(index != target)(far.wait_send)
        pl.when(index == target)(close.wait)
    for one in sums:
        one.finish()


def second_part(x_short, x_long, att, cot_short, cot_long, norms, w_out, w_up, w_down, count):
    width = x_short.shape[2]
    rows = att.shape[0]
    short, long = count * x_short.shape[1], count * x_long.shape[1]
    hidden = w_up.shape[1]
    out = jax.ShapeDtypeStruct
    devices = 4 * count

    def shards(w):
        return (4, 2, 2, 2, w.shape[0] // devices, w.shape[1])

    def halves(w):
        return (4, 2, 2, w.shape[0] // devices, w.shape[1])

    return pl.pallas_call(
        second_kernel,
        out_shape=(
            out(x_short.shape, BF16),
            out(x_long.shape, BF16),
            out((rows, width), F32),
            out((8, width), F32),
            out(halves(w_out), BF16),
            out(halves(w_up), BF16),
            out(halves(w_down), BF16),
            out((2, long, LANES), BF16),
            out((3, short, LANES), BF16),
        ),
        in_specs=[vmem()] * 6 + [hbm()] * 3,
        out_specs=tuple([vmem()] * 4 + [hbm()] * 5),
        scratch_shapes=[
            pltpu.VMEM(w_out.shape, BF16),
            pltpu.VMEM(w_up.shape, BF16),
            pltpu.VMEM(w_down.shape, BF16),
            pltpu.VMEM((rows, width), F32),
            pltpu.VMEM((rows, width), F32),
            pltpu.VMEM((rows, 1), F32),
            pltpu.VMEM((rows, width), BF16),
            pltpu.VMEM((width, rows), BF16),
            pltpu.VMEM((rows, width), BF16),
            pltpu.VMEM((rows, width), F32),
            pltpu.VMEM((rows, width), F32),
            pltpu.VMEM((rows, width), BF16),
            pltpu.VMEM((rows, hidden), BF16),
            pltpu.VMEM((rows, hidden), BF16),
            *[pltpu.VMEM(shards(w), BF16) for w in (w_out, w_up, w_down)],
            *[pltpu.VMEM(halves(w), BF16) for w in (w_out, w_up, w_down)],
            DMA((3,)), DMA((3,)), DMA((2, 6)), DMA((2, 8)), DMA((2, 6)), DMA((3, 8)), DMA((3,)), DMA((3,)),
        ],
        compiler_params=params_of(collective_id=1, has_side_effects=True),
    )(x_short, x_long, att, cot_short, cot_long, norms, w_out, w_up, w_down)


class RowSum:
    def __init__(self, long_bufs, short_bufs, sems):
        self.mine, self.out, self.sib, self.got, self.fin = long_bufs
        self.mine_s, self.out_s, self.sib_s, self.fin_s = short_bufs
        (
            self.sib_send, self.sib_recv, self.send, self.recv, self.on_send, self.fin_recv,
            self.sib_send_s, self.sib_recv_s, self.send_s, self.fin_recv_s,
        ) = sems
        self.z, self.core, self.y, self.x = position()
        self.half, self.near, partner_z, far_z = roles()
        self.partner = at(partner_z, self.core, self.y, self.x)
        self.sibling = at(self.z, 1 - self.core, self.y, self.x)
        self.far = at(far_z, self.core, self.y, self.x)

    def across(self, zz):
        return remote(self.out.at[zz % 2], self.sib.at[zz], self.sib_send.at[zz], self.sib_recv.at[zz], self.sibling)

    def put(self, block, value):
        zz, parity = block // 2, block % 2

        @pl.when(self.core == parity)
        def _():
            self.mine[zz] = value

        @pl.when(self.core != parity)
        def _():
            if zz < 2:
                self.across(zz + 2).wait_send()
            self.out[zz % 2] = value
            self.across(zz).start()

    def place(self, zz):
        return jnp.where(self.half == 0, zz, 3 - zz)

    def to_partner(self, zz):
        return remote(self.mine.at[zz], self.got.at[zz], self.send.at[zz], self.recv.at[zz], self.partner)

    def to_owner(self, zz):
        return remote(
            self.mine.at[zz], self.fin, self.on_send.at[zz], self.fin_recv, at(zz, self.core, self.y, self.x)
        )

    def sends_to_partner(self, zz):
        place = self.place(zz)
        return jnp.where(self.near == 0, place != 0, place == 0)

    def add_cores(self, zz):
        self.across(zz).wait_recv()
        add_into(self.mine.at[zz], self.sib.at[zz])
        pl.when(self.sends_to_partner(zz))(self.to_partner(zz).start)

    def sends_on(self, zz):
        return jnp.logical_and(self.near == 1, self.place(zz) >= 2)

    def add_chips(self, zz):
        @pl.when(self.sends_on(zz))
        def _():
            self.to_partner(zz).wait_recv()
            add_into(self.mine.at[zz], self.got.at[zz])
            self.to_owner(zz).start()

    def across_s(self, zz):
        return remote(
            self.out_s.at[zz], self.sib_s.at[zz], self.sib_send_s.at[zz], self.sib_recv_s.at[zz], self.sibling
        )

    def put_short(self, zz, value):
        rows = value.shape[0] // 2
        first, second = value[:rows], value[rows:]

        @pl.when(self.core == 0)
        def _():
            self.mine_s[zz] = first
            self.out_s[zz] = second

        @pl.when(self.core == 1)
        def _():
            self.mine_s[zz] = second
            self.out_s[zz] = first

        self.across_s(zz).start()

    def to_owner_s(self, zz):
        return remote(
            self.mine_s.at[zz], self.fin_s.at[self.half], self.send_s.at[zz], self.fin_recv_s.at[self.half],
            at(zz, self.core, self.y, self.x),
        )

    def add_short(self, zz):
        @pl.when(self.near == 1)
        def _():
            self.across_s(zz).wait_recv()
            add_into(self.mine_s.at[zz], self.sib_s.at[zz])
            pl.when(self.z != zz)(self.to_owner_s(zz).start)

    def own_long(self):
        self.to_partner(self.z).wait_recv()
        return self.mine[self.z].astype(F32) + self.got[self.z].astype(F32)

    def other_long(self):
        remote(self.fin, self.fin, self.on_send.at[0], self.fin_recv, self.far).wait_recv()
        return self.fin[...].astype(F32)

    def shorts(self):
        def arrival(seq):
            block = self.fin_s.at[seq]
            remote(block, block, self.send_s.at[0], self.fin_recv_s.at[seq], self.far).wait_recv()

        arrival(1 - self.half)
        pl.when(self.near == 0)(lambda: arrival(self.half))

        @pl.when(self.near == 1)
        def _():
            self.fin_s[self.half] = self.mine_s[self.z]

    def sends_done(self):
        for zz in range(4):
            if zz < 2:
                self.across(zz).wait_send()
            pl.when(self.sends_to_partner(zz))(self.to_partner(zz).wait_send)
            pl.when(self.sends_on(zz))(self.to_owner(zz).wait_send)

        @pl.when(self.near == 1)
        def _():
            for zz in range(4):
                self.across_s(zz).wait_send()
                pl.when(self.z != zz)(self.to_owner_s(zz).wait_send)


def third_kernel(
    xs_own, xl_own, gnorm, wq, taps, norms, gmid,
    xs_h, xl_h, ql_h, kl_h, vl_h, ktl_h, lsel_h, pl_h, ol_h, qs_h, ks_h, vs_h, kts_h, lses_h, ps_h, os_h,
    gl_h, gs_h, gwo_h, gwu_h, gwd_h,
    dxs_ref, dxl_ref, gwq_ref, gwo_ref, gwu_ref, gwd_ref, small_ref,
    ql, kl, vl, ktl, lsel, ol, gl, qs, ks, vs, kts, lses, os, gs,
    gm, dqt, delta, gp, gacc, dwq, dtaps, dnorms, x_tile, p_tile,
    mine, out, sib, got, fin, mine_s, out_s, sib_s, fin_s,
    load_sem, tile_sem,
    r0, r1, r2, r3, r4, r5, r6, r7, r8, r9,
    shard_own, shard_send, shard_recv, group_send, group_recv, small_send, small_recv,
    *bufs,
):
    z, core, y, x = position()
    half, near, _, _ = roles()
    pairs_long = 2 - near
    loads, tiles = Copies(load_sem), Copies(tile_sem)
    for source, target in (
        (ql_h, ql), (kl_h, kl), (vl_h, vl), (ktl_h, ktl), (lsel_h, lsel), (ol_h, ol), (gl_h, gl),
    ):
        loads.start(source, target)
    greet_all()
    bufs = list(bufs)
    sums = []
    for i, (grad, total) in enumerate(((gwo_h, gwo_ref), (gwu_h, gwu_ref), (gwd_h, gwd_ref))):
        sums.append(ShardSum(grad, total, bufs[5 * i : 5 * i + 5], shard_own.at[i], shard_send.at[i], shard_recv.at[i]))
    group = GroupSum(bufs[15:19], group_send, group_recv)
    small = SmallSum(bufs[19:24], small_ref, small_send, small_recv)
    rows_sum = RowSum((mine, out, sib, got, fin), (mine_s, out_s, sib_s, fin_s), (r0, r1, r2, r3, r4, r5, r6, r7, r8, r9))
    sum_out, sum_up, sum_down = sums
    sum_up.start()
    short, long = xs_own.shape[1], xl_own.shape[1]
    owned = short + long
    middles = [
        pltpu.make_async_copy(gmid.at[pl.ds(seq * owned + first, size)], dx.at[seq], load_sem.at[14 + 2 * seq + i])
        for seq in range(2)
        for i, (dx, first, size) in enumerate(((dxs_ref, 0, short), (dxl_ref, short, long)))
    ]
    for copy in middles:
        copy.start()
    gm[...] = jnp.zeros_like(gm)
    dwq[...] = jnp.zeros_like(dwq)
    dtaps[...] = jnp.zeros_like(dtaps)
    dnorms[...] = gnorm[...]
    gain, offset = norms[0:1], norms[1:2]
    pick = jnp.where((iota((8, LANES), 1) < HEAD_DIM) == (iota((8, LANES), 0) == 0), 1.0, 0.0).astype(F32)
    causal = causal_mask()
    first_lanes = iota((TILE, LANES), 1) < HEAD_DIM

    def grads_long(slot):
        return gm.at[slot, pl.ds(0, xl_h.shape[0] + PAD)]

    def grads_short(slot):
        size = xs_h.shape[0] + PAD
        return gm.at[lax.rem(slot, 2), pl.ds(pl.multiple_of(slot // 2 * size, PAD), size)]

    def back_head(q_ref, k_ref, v_ref, kt_ref, lse, g_ref, grads, head, block):
        slot, side = head // 2, head % 2
        grad_ref = grads(slot)
        own_lanes = first_lanes == (side == 0)
        rows = slice(block * TILE, (block + 1) * TILE)
        query = q_ref[head, rows]
        bare = jnp.where(own_lanes, query.astype(F32), 0.0).astype(BF16)
        grad_out = jnp.where(own_lanes, g_ref[slot, rows].astype(F32), 0.0).astype(BF16)
        stat, less = lse[head, :, rows], delta[head]
        spans = [(block * TILE, TILE, True)]
        if block:
            spans.append((0, block * TILE, False))
        grad_q = None
        for start, size, masked in spans:
            keys = slice(start, start + size)
            scores = dot_nt(k_ref[head, keys], query)
            if masked:
                scores = jnp.where(causal, scores, NEG_FILL)
            probs = jnp.exp(scores - stat)
            grad_probs = dot_nt(v_ref[slot, keys], grad_out)
            grad_ref[keys, 2 * LANES :] += dot_nn(probs.astype(BF16), grad_out)
            grad_scores = (probs * (grad_probs - less)).astype(BF16)
            grad_ref[keys, LANES : 2 * LANES] += dot_nn(grad_scores, bare)
            term = dot_nn(kt_ref[head, :, keys], grad_scores)
            grad_q = term if grad_q is None else grad_q + term
        dqt[head] = (HEAD_DIM**-0.5) * grad_q

    def back_block(refs, x_h, p_h, grads, pairs, slots, first_pair, block, total):
        q_ref, k_ref, v_ref, kt_ref, lse, o_ref, g_ref = refs
        rows = slice(block * TILE, (block + 1) * TILE)
        got_x = pltpu.make_async_copy(x_h.at[pl.ds(block * TILE, TILE)], x_tile, tile_sem.at[0])
        got_p = pltpu.make_async_copy(
            p_h.at[:, pl.ds(block * TILE, TILE + PAD)], p_tile.at[pl.ds(0, pairs)], tile_sem.at[1]
        )
        got_x.start()
        got_p.start()

        @pl.loop(0, slots)
        def _(slot):
            product = g_ref[slot, rows].astype(F32) * o_ref[slot, rows].astype(F32)
            both = lax.dot_general(
                pick, product, (((1,), (1,)), ((), ())), preferred_element_type=F32,
                precision=lax.Precision.HIGHEST,
            )
            delta[2 * slot] = both[0:1]
            delta[2 * slot + 1] = both[1:2]

        @pl.loop(0, 2 * slots)
        def _(head):
            back_head(q_ref, k_ref, v_ref, kt_ref, lse, g_ref, grads, head, block)

        got_x.wait()
        got_p.wait()
        normal, _ = normalise(x_tile[...].astype(F32))
        low = (normal * gain + offset).astype(BF16)
        gacc[...] = jnp.zeros_like(gacc)

        @pl.loop(0, slots)
        def _(slot):
            columns = times(slot + first_pair, TRIPLE)
            grad_ref = grads(slot)
            grad_ref[rows, 0:LANES] = jnp.concatenate([dqt[2 * slot], dqt[2 * slot + 1]], axis=0).T
            window = grad_ref[pl.ds(block * TILE, TILE + PAD)]
            grad = window[:TILE]
            kernel = taps[:, columns]
            grad_projected = (
                kernel[0:1] * grad + kernel[1:2] * shifted(window, -1)[:TILE] + kernel[2:3] * shifted(window, -2)[:TILE]
            ).astype(BF16)
            past = p_tile[slot].astype(F32)
            dtaps[0:1, columns] += jnp.sum(grad * past[PAD:], axis=0, keepdims=True)
            dtaps[1:2, columns] += jnp.sum(grad * shifted(past, 1)[PAD:], axis=0, keepdims=True)
            dtaps[2:3, columns] += jnp.sum(grad * shifted(past, 2)[PAD:], axis=0, keepdims=True)
            gacc[...] += dot_nt(grad_projected, wq[:, columns])
            dwq[:, columns] += dot_tn(low, grad_projected)

        grad_normed = gacc[...]
        dnorms[0:1] += jnp.sum(grad_normed * normal, axis=0, keepdims=True)
        dnorms[1:2] += jnp.sum(grad_normed, axis=0, keepdims=True)
        return grad_normed.astype(BF16)

    loads.finish()

    short_loads = [
        pltpu.make_async_copy(source, target, load_sem.at[7 + i])
        for i, (source, target) in enumerate(
            ((qs_h, qs), (ks_h, ks), (vs_h, vs), (kts_h, kts), (lses_h, lses), (os_h, os), (gs_h, gs))
        )
    ]

    @pl.when(near == 1)
    def _():
        for copy in short_loads:
            copy.start()

    def hook_one():
        sum_up.turn()
        sum_down.start()
        sum_out.start()

    def hook_two():
        sum_up.last()
        sum_down.turn()
        sum_out.turn()

    def hook_three():
        sum_down.last()
        sum_out.last()

    long_refs = (ql, kl, vl, ktl, lsel, ol, gl)
    short_refs = (qs, ks, vs, kts, lses, os, gs)
    last_long = xl_h.shape[0] // TILE - 1
    for block in range(last_long, -1, -1):
        value = back_block(long_refs, xl_h, pl_h, grads_long, 2, pairs_long, 2 * near, block, last_long)
        rows_sum.put(block, value)
        if block % 2 == 1 and block != last_long:
            rows_sum.add_cores(block // 2 + 1)
        if block == 7:
            pl.when(near == 0)(hook_one)
        if block == 5:
            pl.when(near == 1)(hook_one)
            pl.when(near == 0)(hook_two)
        if block == 3:
            pl.when(near == 0)(hook_three)
    rows_sum.add_cores(0)

    @pl.when(near == 1)
    def _():
        for copy in short_loads:
            copy.wait()
        gm[...] = jnp.zeros_like(gm)

    last_short = xs_h.shape[0] // TILE - 1
    for block in range(last_short, -1, -1):

        @pl.when(near == 1)
        def _(block=block):
            value = back_block(short_refs, xs_h, ps_h, grads_short, 3, 3, 0, block, last_short)
            rows_sum.put_short(block, value)

        if block == 3:
            pl.when(near == 1)(hook_two)
        if block == 1:
            pl.when(near == 1)(hook_three)
        rows_sum.add_chips(block)
        if block != last_short:
            rows_sum.add_short(block + 1)
    rows_sum.add_short(0)
    group.start(dwq)
    small.start(dtaps[...], dnorms[...])
    small.over()
    group.turn()
    small.turn()
    group.last()
    small.last()

    for copy in middles:
        copy.wait()

    def finish_rows(seq, grad, x_ref, dx_ref):
        normal, inverse = normalise(x_ref[seq].astype(F32))
        dx_ref[seq] += norm_back(grad, normal, inverse, gain)

    rows_sum.shorts()
    finish_rows(half, rows_sum.fin_s[half].astype(F32), xs_own, dxs_ref)
    finish_rows(1 - half, rows_sum.fin_s[1 - half].astype(F32), xs_own, dxs_ref)
    finish_rows(half, rows_sum.own_long(), xl_own, dxl_ref)
    finish_rows(1 - half, rows_sum.other_long(), xl_own, dxl_ref)
    small.swap_back()
    for one in sums:
        one.finish()
    group.finish(gwq_ref)
    small.finish()
    rows_sum.sends_done()


def third_part(x_short, x_long, gmid, gnorm, wq, taps, norms, kept, grads_in, weight_grads):
    width = x_short.shape[2]
    wide = wq.shape[1]
    count = 8
    short, long = count * x_short.shape[1], count * x_long.shape[1]
    own_short = x_short.shape[1]
    rows = weight_grads[0].shape[3]
    out = jax.ShapeDtypeStruct
    small_wide = wide + width // 2

    def saved(pairs, total):
        return [
            ((2 * pairs, total, LANES), BF16),
            ((2 * pairs, total, LANES), BF16),
            ((pairs, total, LANES), BF16),
            ((2 * pairs, HEAD_DIM, total), BF16),
            ((2 * pairs, 1, total), F32),
            ((pairs, total, LANES), BF16),
            ((pairs, total, LANES), BF16),
        ]

    scratch = (
        saved(2, long)
        + saved(3, short)
        + [
            ((2, max(long + PAD, 2 * (short + PAD)), TRIPLE), F32),
            ((6, HEAD_DIM, TILE), F32),
            ((6, 1, TILE), F32),
            ((3, TILE, TRIPLE), BF16),
            ((TILE, width), F32),
            ((width, wide), F32),
            ((8, wide), F32),
            ((8, width), F32),
            ((TILE, width), BF16),
            ((3, TILE + PAD, TRIPLE), BF16),
        ]
        + [((4, TILE, width), BF16), ((2, TILE, width), BF16)]
        + [((4, TILE, width), BF16)] * 2
        + [((TILE, width), BF16)]
        + [((4, own_short, width), BF16)] * 3
        + [((2, own_short, width), BF16)]
    )
    buffers = []
    for g in weight_grads:
        buffers += ShardSum.buffers(g)
    buffers += GroupSum.buffers(rows, wide) + SmallSum.buffers(wide, width // 2)
    return pl.pallas_call(
        third_kernel,
        out_shape=(
            out(x_short.shape, F32),
            out(x_long.shape, F32),
            out((rows, 2 * wide), F32),
            *[out(g.shape[3:], F32) for g in weight_grads],
            out((2, 8, small_wide), F32),
        ),
        in_specs=[vmem()] * 6 + [hbm()] * (1 + len(kept) + len(grads_in) + len(weight_grads)),
        out_specs=tuple([vmem()] * 7),
        scratch_shapes=[pltpu.VMEM(*one) for one in scratch]
        + [DMA((18,)), DMA((2,))]
        + [DMA((4,))] * 5 + [DMA] + [DMA((4,))] * 3 + [DMA((2,))]
        + [DMA((3, 2)), DMA((3, 9)), DMA((3, 9)), DMA((11,)), DMA((11,)), DMA((7,)), DMA((7,))]
        + buffers,
        compiler_params=params_of(63, collective_id=2, has_side_effects=True),
    )(x_short, x_long, gnorm, wq, taps, norms, gmid, *kept, *grads_in, *weight_grads)


def split_body(
    x_short, x_long, lengths, cot_short, cot_long, w_qkv, w_out, w_up, w_down, conv_kernel, norm_params
):
    count = lax.axis_size("seq")
    width = x_short.shape[2]
    att, full_out, full_up, full_down, xs, xl, wq, taps, norms, *kept = first_part(
        lengths, x_short, x_long, w_qkv, conv_kernel, norm_params, w_out, w_up, w_down, count
    )
    y_short, y_long, gmid, gnorm, gwo, gwu, gwd, gl, gs = second_part(
        x_short, x_long, att, cot_short, cot_long, norms,
        full_out.reshape(width, -1), full_up.reshape(width, -1), full_down.reshape(-1, width), count,
    )
    dx_short, dx_long, sum_qkv, sum_out, sum_up, sum_down, smalls = third_part(
        x_short, x_long, gmid, gnorm, wq, taps, norms, [xs, xl] + kept, [gl, gs], [gwo, gwu, gwd]
    )
    wide = wq.shape[1]
    number = lax.axis_index("seq") * lax.axis_size("batch") + lax.axis_index("batch")
    part, cut = conv_kernel.shape[1], norm_params.shape[1]
    kernel = smalls[:, 0:3, :wide].reshape(2, 3, 3, 3, LANES).transpose(1, 3, 0, 2, 4).reshape(3, 3 * width)
    norm = smalls[:, 0:4, wide:].transpose(1, 0, 2).reshape(4, width)
    return (
        y_short, y_long, dx_short, dx_long, sum_qkv, sum_out, sum_up, sum_down,
        lax.dynamic_slice_in_dim(kernel, number * part, part, 1),
        lax.dynamic_slice_in_dim(norm, number * cut, cut, 1),
    )


GROUP_HEADS = 2


def from_behind(value, axis, by):
    count = lax.axis_size(axis)
    pairs = [(i, i + by) for i in range(count) if 0 <= i + by < count]
    return lax.ppermute(value, axis, pairs)


def layer_norm(values, gain, offset_term):
    average = jnp.mean(values, axis=-1, keepdims=True)
    centred = values - average
    inverse = lax.rsqrt(jnp.mean(centred * centred, axis=-1, keepdims=True) + EPS)
    normal = centred * inverse
    return (normal * gain + offset_term, normal, inverse)


def norm_back_flat(grad, normal, inverse, gain):
    scaled_grad = grad * gain
    first_mean = jnp.mean(scaled_grad, axis=-1, keepdims=True)
    second_mean = jnp.mean(scaled_grad * normal, axis=-1, keepdims=True)
    return inverse * (scaled_grad - first_mean - normal * second_mean)


def front_part(inputs, full_weights):
    w_qkv = full_weights[0]
    kernel = full_weights[4].astype(jnp.float32)
    params = full_weights[5].astype(jnp.float32)
    saved = []
    tails = []
    for part_in in inputs:
        seq_count, block_rows, model_width = part_in.shape
        flat = part_in.reshape(seq_count * block_rows, model_width).astype(jnp.float32)
        normed, normal, inverse = layer_norm(flat, params[0], params[1])
        normed_low = normed.astype(jnp.bfloat16)
        projected = jnp.dot(normed_low, w_qkv, preferred_element_type=jnp.float32).astype(
            jnp.bfloat16
        )
        projected = projected.reshape(seq_count, block_rows, 3 * model_width)
        saved.append((flat, normal, inverse, normed_low, projected))
        tails.append(projected[:, block_rows - 2 :])
    received = from_behind((tails[0], tails[1]), "seq", 1)
    fronts = []
    for index_part in range(2):
        flat, normal, inverse, normed_low, projected = saved[index_part]
        block_rows = projected.shape[1]
        padded = jnp.concatenate([received[index_part], projected], axis=1).astype(jnp.float32)
        mixed = (
            kernel[0] * padded[:, 2:]
            + kernel[1] * padded[:, 1 : block_rows + 1]
            + kernel[2] * padded[:, :block_rows]
        )
        fronts.append((flat, normal, inverse, normed_low, padded, mixed.astype(jnp.bfloat16)))
    return fronts


def attend_block(queries, key_rows, value_rows, usable, grad_heads):
    scaling = queries.shape[-1] ** (-0.5)
    scores = jnp.einsum("sqhd,skhd->shqk", queries, key_rows, preferred_element_type=jnp.float32)
    masked = jnp.where(usable, scaling * scores, NEG_FILL)
    exp_terms = jnp.exp(masked - jnp.max(masked, axis=-1, keepdims=True))
    attn_probs = exp_terms / jnp.sum(exp_terms, axis=-1, keepdims=True)
    probs_low = attn_probs.astype(jnp.bfloat16)
    if grad_heads is None:
        attended = jnp.einsum(
            "shqk,skhd->sqhd", probs_low, value_rows, preferred_element_type=jnp.float32
        )
        return attended.astype(jnp.bfloat16)
    grad_probs = jnp.einsum(
        "sqhd,skhd->shqk", grad_heads, value_rows, preferred_element_type=jnp.float32
    )
    grad_values = jnp.einsum(
        "shqk,sqhd->skhd", probs_low, grad_heads, preferred_element_type=jnp.float32
    )
    row_delta = jnp.sum(attn_probs * grad_probs, axis=-1, keepdims=True)
    grad_scores = (scaling * attn_probs * (grad_probs - row_delta)).astype(jnp.bfloat16)
    grad_queries = jnp.einsum(
        "shqk,skhd->sqhd", grad_scores, key_rows, preferred_element_type=jnp.float32
    )
    grad_keys = jnp.einsum(
        "shqk,sqhd->skhd", grad_scores, queries, preferred_element_type=jnp.float32
    )
    return (grad_queries, grad_keys, grad_values)


def make_usable(query_pos, key_pos, seq_lengths):
    usable = (key_pos[None, None, :] <= query_pos[None, :, None]) & (
        key_pos[None, None, :] < seq_lengths[:, None, None]
    )
    return usable[:, None]


def attention(mixed, kv_full, seq_lengths, offset, grad_attended):
    seq_count, block_rows, three_width = mixed.shape
    model_width = three_width // 3
    full_len = kv_full.shape[1]
    queries = mixed[:, :, :model_width].reshape(seq_count, block_rows, -1, HEAD_DIM)
    key_rows = kv_full[:, :, :model_width].reshape(seq_count, full_len, -1, HEAD_DIM)
    value_rows = kv_full[:, :, model_width:].reshape(seq_count, full_len, -1, HEAD_DIM)
    positions = offset + jnp.arange(block_rows, dtype=jnp.int32)
    key_pos = jnp.arange(full_len, dtype=jnp.int32)
    usable = make_usable(positions, key_pos, seq_lengths)
    heads_total = queries.shape[2]
    grad_heads = None
    if grad_attended is not None:
        grad_heads = grad_attended.reshape(seq_count, block_rows, -1, HEAD_DIM)
    results = []
    for first_head in range(0, heads_total, GROUP_HEADS):
        last_head = first_head + GROUP_HEADS
        grad_part = None if grad_heads is None else grad_heads[:, :, first_head:last_head]
        results.append(
            attend_block(
                queries[:, :, first_head:last_head],
                key_rows[:, :, first_head:last_head],
                value_rows[:, :, first_head:last_head],
                usable,
                grad_part,
            )
        )
    if grad_heads is None:
        return jnp.concatenate(results, axis=2).reshape(seq_count, block_rows, model_width)
    grad_queries = jnp.concatenate([entry_set[0] for entry_set in results], axis=2).reshape(
        seq_count, block_rows, model_width
    )
    grad_keys = jnp.concatenate([entry_set[1] for entry_set in results], axis=2).reshape(
        seq_count, full_len, model_width
    )
    grad_values = jnp.concatenate([entry_set[2] for entry_set in results], axis=2).reshape(
        seq_count, full_len, model_width
    )
    return (grad_queries, grad_keys, grad_values)


def rest_part(front, kv_full, seq_lengths, offset, full_weights, cotangent_in):
    w_out, w_up, w_down = (full_weights[1], full_weights[2], full_weights[3])
    params = full_weights[5].astype(jnp.float32)
    flat, normal_one, inverse_one, normed_low, padded, mixed = front
    seq_count, block_rows, three_width = mixed.shape
    model_width = three_width // 3
    attended = attention(mixed, kv_full, seq_lengths, offset, None).reshape(
        seq_count * block_rows, model_width
    )
    middle = flat + jnp.dot(attended, w_out, preferred_element_type=jnp.float32)
    second, normal_two, inverse_two = layer_norm(middle, params[2], params[3])
    second_low = second.astype(jnp.bfloat16)
    upper = jnp.dot(second_low, w_up, preferred_element_type=jnp.float32)
    hidden = jnp.square(jnp.maximum(upper, 0.0)).astype(jnp.bfloat16)
    if cotangent_in is None:
        result_rows = middle + jnp.dot(hidden, w_down, preferred_element_type=jnp.float32)
        return result_rows.astype(jnp.bfloat16).reshape(seq_count, block_rows, model_width)
    cotangent = cotangent_in.reshape(seq_count * block_rows, model_width)
    grad_down = jnp.dot(hidden.T, cotangent, preferred_element_type=jnp.float32)
    grad_hidden = jnp.dot(cotangent, w_down.T, preferred_element_type=jnp.float32)
    grad_upper = (2.0 * jnp.maximum(upper, 0.0) * grad_hidden).astype(jnp.bfloat16)
    grad_up = jnp.dot(second_low.T, grad_upper, preferred_element_type=jnp.float32)
    grad_second = jnp.dot(grad_upper, w_up.T, preferred_element_type=jnp.float32)
    grad_middle = cotangent.astype(jnp.float32) + norm_back_flat(
        grad_second, normal_two, inverse_two, params[2]
    )
    grad_middle_low = grad_middle.astype(jnp.bfloat16)
    grad_out = jnp.dot(attended.T, grad_middle_low, preferred_element_type=jnp.float32)
    grad_attended = jnp.dot(grad_middle_low, w_out.T, preferred_element_type=jnp.float32).astype(
        jnp.bfloat16
    )
    grad_attended = grad_attended.reshape(seq_count, block_rows, model_width)
    grad_queries, grad_keys, grad_values = attention(
        mixed, kv_full, seq_lengths, offset, grad_attended
    )
    key_term = jnp.concatenate([grad_keys, grad_values], axis=-1)
    norm_two = (jnp.sum(grad_second * normal_two, axis=0), jnp.sum(grad_second, axis=0))
    return (grad_queries, key_term, grad_middle, grad_out, grad_up, grad_down, norm_two)


def general_body(
    x_short,
    x_long,
    lengths,
    cot_short,
    cot_long,
    w_qkv,
    w_out,
    w_up,
    w_down,
    conv_kernel,
    norm_params,
):
    full_weights = (
        lax.all_gather(w_qkv, ("seq", "batch"), axis=0, tiled=True),
        lax.all_gather(w_out, ("seq", "batch"), axis=0, tiled=True),
        lax.all_gather(w_up, ("seq", "batch"), axis=0, tiled=True),
        lax.all_gather(w_down, ("seq", "batch"), axis=0, tiled=True),
        lax.all_gather(conv_kernel, ("seq", "batch"), axis=1, tiled=True),
        lax.all_gather(norm_params, ("seq", "batch"), axis=1, tiled=True),
    )
    inputs = (x_short, x_long)
    cotangents = (cot_short, cot_long)
    model_width = x_short.shape[2]
    offsets = (lax.axis_index("seq") * x_short.shape[1], lax.axis_index("seq") * x_long.shape[1])
    fronts = front_part(inputs, full_weights)
    kv_fwd = (
        lax.all_gather(fronts[0][5][:, :, model_width:], "seq", axis=1, tiled=True),
        lax.all_gather(fronts[1][5][:, :, model_width:], "seq", axis=1, tiled=True),
    )
    outputs = [
        rest_part(
            fronts[index_part],
            kv_fwd[index_part],
            lengths[index_part],
            offsets[index_part],
            full_weights,
            None,
        )
        for index_part in range(2)
    ]
    back_weights = (
        lax.all_gather(w_qkv, ("seq", "batch"), axis=0, tiled=True),
        lax.all_gather(w_out, ("seq", "batch"), axis=0, tiled=True),
        lax.all_gather(w_up, ("seq", "batch"), axis=0, tiled=True),
        lax.all_gather(w_down, ("seq", "batch"), axis=0, tiled=True),
        lax.all_gather(conv_kernel, ("seq", "batch"), axis=1, tiled=True),
        lax.all_gather(norm_params, ("seq", "batch"), axis=1, tiled=True),
    )
    fronts_back = front_part(inputs, back_weights)
    kv_back = (
        lax.all_gather(fronts_back[0][5][:, :, model_width:], "seq", axis=1, tiled=True),
        lax.all_gather(fronts_back[1][5][:, :, model_width:], "seq", axis=1, tiled=True),
    )
    partials = [
        rest_part(
            fronts_back[index_part],
            kv_back[index_part],
            lengths[index_part],
            offsets[index_part],
            back_weights,
            cotangents[index_part],
        )
        for index_part in range(2)
    ]
    kv_grads = (
        lax.psum_scatter(
            partials[0][1].astype(jnp.bfloat16), "seq", scatter_dimension=1, tiled=True
        ).astype(jnp.float32),
        lax.psum_scatter(
            partials[1][1].astype(jnp.bfloat16), "seq", scatter_dimension=1, tiled=True
        ).astype(jnp.float32),
    )
    grad_mixed = [
        jnp.concatenate([partials[index_part][0], kv_grads[index_part]], axis=-1)
        for index_part in range(2)
    ]
    received = (
        from_behind(grad_mixed[0][:, :2].astype(jnp.bfloat16), "seq", -1).astype(jnp.float32),
        from_behind(grad_mixed[1][:, :2].astype(jnp.bfloat16), "seq", -1).astype(jnp.float32),
    )
    kernel = back_weights[4].astype(jnp.float32)
    params = back_weights[5].astype(jnp.float32)
    w_qkv_full = back_weights[0]
    grad_qkv = jnp.zeros(w_qkv_full.shape, jnp.float32)
    grad_kernel = jnp.zeros(kernel.shape, jnp.float32)
    grad_norm = jnp.zeros((4, model_width), jnp.float32)
    grad_out = partials[0][3] + partials[1][3]
    grad_up = partials[0][4] + partials[1][4]
    grad_down = partials[0][5] + partials[1][5]
    input_grads = []
    for index_part in range(2):
        flat, normal_one, inverse_one, normed_low, padded, mixed = fronts_back[index_part]
        seq_count, block_rows, three_width = mixed.shape
        mixed_grad = grad_mixed[index_part]
        extended = jnp.concatenate([mixed_grad, received[index_part]], axis=1)
        grad_projected = (
            kernel[0] * extended[:, :block_rows]
            + kernel[1] * extended[:, 1 : block_rows + 1]
            + kernel[2] * extended[:, 2:]
        ).astype(jnp.bfloat16)
        grad_kernel = grad_kernel + jnp.stack(
            [
                jnp.sum(mixed_grad * padded[:, 2:], axis=(0, 1)),
                jnp.sum(mixed_grad * padded[:, 1 : block_rows + 1], axis=(0, 1)),
                jnp.sum(mixed_grad * padded[:, :block_rows], axis=(0, 1)),
            ]
        )
        grad_flat = grad_projected.reshape(seq_count * block_rows, three_width)
        grad_qkv = grad_qkv + jnp.dot(normed_low.T, grad_flat, preferred_element_type=jnp.float32)
        grad_normed = jnp.dot(grad_flat, w_qkv_full.T, preferred_element_type=jnp.float32)
        grad_input = partials[index_part][2] + norm_back_flat(
            grad_normed, normal_one, inverse_one, params[0]
        )
        input_grads.append(grad_input.reshape(seq_count, block_rows, model_width))
        norm_two = partials[index_part][6]
        grad_norm = grad_norm + jnp.stack(
            [
                jnp.sum(grad_normed * normal_one, axis=0),
                jnp.sum(grad_normed, axis=0),
                norm_two[0],
                norm_two[1],
            ]
        )
    summed = (
        lax.psum_scatter(grad_qkv, ("seq", "batch"), scatter_dimension=0, tiled=True),
        lax.psum_scatter(grad_out, ("seq", "batch"), scatter_dimension=0, tiled=True),
        lax.psum_scatter(grad_up, ("seq", "batch"), scatter_dimension=0, tiled=True),
        lax.psum_scatter(grad_down, ("seq", "batch"), scatter_dimension=0, tiled=True),
        lax.psum_scatter(grad_kernel, ("seq", "batch"), scatter_dimension=1, tiled=True),
        lax.psum_scatter(grad_norm, ("seq", "batch"), scatter_dimension=1, tiled=True),
    )
    return (
        outputs[0],
        outputs[1],
        input_grads[0],
        input_grads[1],
        summed[0],
        summed[1],
        summed[2],
        summed[3],
        summed[4],
        summed[5],
    )


def solution(mesh):
    split = mesh.shape["seq"] == 8
    return jax.shard_map(
        split_body if split else general_body,
        mesh=mesh,
        in_specs=(
            P("batch", "seq", None),
            P("batch", "seq", None),
            P(None, "batch"),
            P("batch", "seq", None),
            P("batch", "seq", None),
            P(("seq", "batch"), None),
            P(("seq", "batch"), None),
            P(("seq", "batch"), None),
            P(("seq", "batch"), None),
            P(None, ("seq", "batch")),
            P(None, ("seq", "batch")),
        ),
        out_specs=(
            P("batch", "seq", None),
            P("batch", "seq", None),
            P("batch", "seq", None),
            P("batch", "seq", None),
            P(("seq", "batch"), None),
            P(("seq", "batch"), None),
            P(("seq", "batch"), None),
            P(("seq", "batch"), None),
            P(None, ("seq", "batch")),
            P(None, ("seq", "batch")),
        ),
        check_vma=False,
    )
```

```python
import functools

import jax
import jax.numpy as jnp
from jax import lax
from jax.experimental import pallas as pl
from jax.experimental.pallas import tpu as pltpu
from jax.sharding import PartitionSpec as P

EPS = 1e-05
NEG_FILL = -1e30
HEAD_DIM = 64
LANES = 128
TRIPLE = 3 * LANES
TILE = 256
PAD = 16
MESH = pl.DeviceIdType.MESH
F32 = jnp.float32
BF16 = jnp.bfloat16
DMA = pltpu.SemaphoreType.DMA


def dot_nn(left, right):
    return lax.dot_general(left, right, (((1,), (0,)), ((), ())), preferred_element_type=F32)


def dot_nt(left, right):
    return lax.dot_general(left, right, (((1,), (1,)), ((), ())), preferred_element_type=F32)


def dot_tn(left, right):
    return lax.dot_general(left, right, (((0,), (0,)), ((), ())), preferred_element_type=F32)


def params_of(limit=60, **more):
    return pltpu.CompilerParams(vmem_limit_bytes=limit * 2**20, **more)


def vmem():
    return pl.BlockSpec(memory_space=pltpu.VMEM)


def smem():
    return pl.BlockSpec(memory_space=pltpu.SMEM)


def hbm():
    return pl.BlockSpec(memory_space=pl.ANY)


def normalise(values):
    average = jnp.mean(values, axis=-1, keepdims=True)
    centred = values - average
    inverse = lax.rsqrt(jnp.mean(centred * centred, axis=-1, keepdims=True) + EPS)
    return centred * inverse, inverse


def norm_back(grad, normal, inverse, gain):
    scaled_grad = grad * gain
    first_mean = jnp.mean(scaled_grad, axis=-1, keepdims=True)
    second_mean = jnp.mean(scaled_grad * normal, axis=-1, keepdims=True)
    return inverse * (scaled_grad - first_mean - normal * second_mean)


def shifted(window, by):
    return pltpu.roll(window, by % window.shape[0], 0)


def iota(shape, axis):
    return lax.broadcasted_iota(jnp.int32, shape, axis)


def times(index, size):
    return pl.ds(pl.multiple_of(index * size, size), size)


def position():
    index, batch = lax.axis_index("seq"), lax.axis_index("batch")
    return index // 2, index % 2, batch // 2, batch % 2


def at(z, core, y, x):
    return (z * 2 + core, y * 2 + x)


def remote(src, dst, send, recv, device):
    return pltpu.make_async_remote_copy(
        src_ref=src, dst_ref=dst, send_sem=send, recv_sem=recv, device_id=device, device_id_type=MESH
    )


def greet(others):
    barrier = pltpu.get_barrier_semaphore()
    for other in others:
        pl.semaphore_signal(barrier, inc=1, device_id=other, device_id_type=MESH)
    pl.semaphore_wait(barrier, len(others))


def whole_line():
    z, core, y, x = position()
    line = [at(lax.rem(z + step, 4), (core + turn) % 2, y, x) for turn in (0, 1) for step in (0, 1, 2, 3)]
    return line[1:]


def greet_all():
    z, core, y, x = position()
    greet(whole_line() + [at(z, core, 1 - y, x), at(z, core, y, 1 - x)])


def roles():
    z = lax.axis_index("seq") // 2
    half = z // 2
    near = jnp.where(half == 0, z, 3 - z)
    partner_z = jnp.where(half == 0, 1 - z, 5 - z)
    return half, near, partner_z, 2 - half


def z_of(half, place):
    return jnp.where(half == 0, place, 3 - place)


def long_source(seq, pair):
    near = 1 if pair % 3 == 2 else 0
    z = near if seq == 0 else 3 - near
    return z * 2 + pair // 3, 0 if near else pair % 3


def short_source(seq, pair):
    return (1 if seq == 0 else 2) * 2 + pair // 3, pair % 3


class Copies:
    def __init__(self, sems):
        self.sems, self.count, self.open = sems, 0, []

    def start(self, src, dst):
        copy = pltpu.make_async_copy(src, dst, self.sems.at[self.count])
        self.count += 1
        copy.start()
        self.open.append(copy)
        return copy

    def finish(self):
        for copy in self.open:
            copy.wait()
        self.open = []


class RowGather:
    def __init__(self, x_ref, o_ref, own_sem, send, recv, sib_send, sib_recv, inner_only):
        self.x_ref, self.o_ref, self.inner_only = x_ref, o_ref, inner_only
        self.own_sem, self.send, self.recv, self.sib_send, self.sib_recv = own_sem, send, recv, sib_send, sib_recv
        self.rows = x_ref.shape[1]
        self.z, self.core, self.y, self.x = position()
        self.half, self.near, self.partner_z, far_z = roles()
        self.sibling = at(self.z, 1 - self.core, self.y, self.x)
        self.partner = at(self.partner_z, self.core, self.y, self.x)
        place = self.block(self.z, self.core)
        mine, other = self.x_ref.at[self.half], self.x_ref.at[1 - self.half]
        self.to_partner = remote(mine, place, send.at[0], recv.at[self.near], self.partner)
        self.to_far = remote(other, place, send.at[1], recv.at[3 - self.near], at(far_z, self.core, self.y, self.x))
        self.to_sibling = remote(mine, place, sib_send.at[0], sib_recv.at[self.near], self.sibling)
        self.own = pltpu.make_async_copy(mine, place, own_sem)

    def block(self, z, core):
        return self.o_ref.at[times(z * 2 + core, self.rows)]

    def at_inner(self, act):
        if self.inner_only:
            pl.when(self.near == 1)(act)
        else:
            act()

    def start(self):
        if self.inner_only:
            pl.when(self.near == 0)(self.to_partner.start)
        else:
            self.to_partner.start()
        pl.when(self.near == 1)(self.to_far.start)

        def inside():
            self.to_sibling.start()
            self.own.start()

        self.at_inner(inside)

    def start_far(self):
        @pl.when(self.near == 0)
        def _():
            self.to_partner.wait_send()
            self.to_far.start()

    def moves(self, slot):
        place = (1 - self.near, 2, 3)[slot]
        block = self.block(z_of(self.half, place), self.core)
        arrival = remote(block, block, self.send.at[0], self.recv.at[place], self.partner)
        onward = remote(block, block, self.send.at[1 + slot], self.recv.at[place], self.partner)
        across = remote(block, block, self.sib_send.at[1 + slot], self.sib_recv.at[place], self.sibling)
        return arrival, onward, across

    def step(self, slot):
        arrival, onward, across = self.moves(slot)

        def inside():
            arrival.wait_recv()
            if slot and not self.inner_only:
                pl.when(self.near == 1)(onward.start)
            across.start()

        self.at_inner(inside)

    def whole(self, place):
        where = (self.near, 1 - self.near, 2, 3)[place]
        block = self.block(z_of(self.half, where), 1 - self.core)

        def inside():
            remote(block, block, self.sib_send.at[0], self.sib_recv.at[where], self.sibling).wait_recv()
            if place == 0:
                self.own.wait()

        self.at_inner(inside)

    def chip_rows(self, place):
        return z_of(self.half, (self.near, 1 - self.near, 2, 3)[place])

    def finish(self):
        if not self.inner_only:
            pl.when(self.near == 1)(self.to_partner.wait_send)
        self.to_far.wait_send()

        def inside():
            self.to_sibling.wait_send()
            for slot in range(3):
                _, onward, across = self.moves(slot)
                across.wait_send()
                if slot and not self.inner_only:
                    pl.when(self.near == 1)(onward.wait_send)

        self.at_inner(inside)


class ShardGather:
    def __init__(self, shard, full, own_sem, send, recv, halves=False):
        self.shard, self.full, self.own_sem, self.send_sem, self.recv_sem = shard, full, own_sem, send, recv
        self.z, self.core, self.y, self.x = position()
        self.halves = halves
        self.sent = []

    def go(self, src, dst, slot, device):
        copy = remote(src, dst, self.send_sem.at[slot], self.recv_sem.at[slot], device)
        copy.start()
        self.sent.append(copy)

    def arrived(self, dst, slot):
        remote(dst, dst, self.send_sem.at[0], self.recv_sem.at[slot], at(self.z, self.core, self.y, self.x)).wait_recv()

    def start(self):
        z, core, y, x = self.z, self.core, self.y, self.x
        mine = self.full.at[z, core, y, x]
        for step in (1, 2, 3):
            target = lax.rem(z + step, 4)
            self.go(self.shard, mine, step, at(target, core, y, x))
        self.own = pltpu.make_async_copy(self.shard, mine, self.own_sem)
        self.own.start()

    def part(self, core, zs, ys, xs, reader):
        ref = self.full.at[zs, core, ys, xs]
        return self.full.at[zs, core, ys, xs, reader] if self.halves else ref

    def across(self, zs, ys, xs, slot):
        ref = self.part(self.core, zs, ys, xs, 1 - self.core)
        self.go(ref, ref, slot, at(self.z, 1 - self.core, self.y, self.x))

    def over(self):
        z, core, y, x = self.z, self.core, self.y, self.x
        for step in (1, 2, 3):
            self.arrived(self.full.at[lax.rem(z + 4 - step, 4), core, y, x], step)
        self.own.wait()
        first, second = pl.ds(0, 2), pl.ds(2, 2)
        ref = self.full.at[first, core, y, x]
        self.go(ref, ref, 4, at(z, core, y, 1 - x))
        ref = self.full.at[second, core, y, x]
        self.go(ref, ref, 5, at(z, core, 1 - y, x))
        self.across(pl.ds(0, 4), y, x, 8)

    def turn(self):
        z, core, y, x = self.z, self.core, self.y, self.x
        first, second = pl.ds(0, 2), pl.ds(2, 2)
        self.arrived(self.full.at[first, core, y, 1 - x], 4)
        ref = self.full.at[first, core, y]
        self.go(ref, ref, 6, at(z, core, 1 - y, x))
        self.across(first, y, 1 - x, 9)
        self.arrived(self.full.at[second, core, 1 - y, x], 5)
        ref = self.full.at[second, core, :, x]
        self.go(ref, ref, 7, at(z, core, y, 1 - x))
        self.across(second, 1 - y, x, 10)

    def last(self):
        core, y, x = self.core, self.y, self.x
        first, second = pl.ds(0, 2), pl.ds(2, 2)
        self.arrived(self.full.at[first, core, 1 - y], 6)
        self.across(first, 1 - y, pl.ds(0, 2), 11)
        self.arrived(self.full.at[second, core, :, 1 - x], 7)
        self.across(second, pl.ds(0, 2), 1 - x, 12)

    def finish(self):
        y, x, core, other = self.y, self.x, self.core, 1 - self.core
        first, second, both = pl.ds(0, 2), pl.ds(2, 2), pl.ds(0, 2)
        parts = (
            (pl.ds(0, 4), y, x), (first, y, 1 - x), (second, 1 - y, x), (first, 1 - y, both), (second, both, 1 - x),
        )
        for slot, (zs, ys, xs) in enumerate(parts):
            self.arrived(self.part(other, zs, ys, xs, core), 8 + slot)

    def sends_done(self):
        for copy in self.sent:
            copy.wait_send()


def add_into(total, part):
    total[...] = (total[...].astype(F32) + part[...].astype(F32)).astype(total.dtype)


class CoreSum:
    def __init__(self, grad, sib, out, send, recv, save, hop=None):
        self.grad, self.sib, self.out, self.save = grad, sib, out, save
        self.z, self.core, self.y, self.x = position()
        z, core, y, x = position()
        self.copy = remote(grad.at[:, 1 - core], sib, send.at[0], recv.at[0], at(z, 1 - core, y, x))
        self.hop = hop
        first, second = pl.ds(0, 2), pl.ds(2, 2)
        if hop is not None:
            self.hops = (
                remote(sib.at[first, :, 1 - x], hop.at[0], send.at[1], recv.at[1], at(z, core, y, 1 - x)),
                remote(sib.at[second, 1 - y], hop.at[1], send.at[2], recv.at[2], at(z, core, 1 - y, x)),
            )

    def start(self):
        self.copy.start()

    def keep(self, *moves):
        self.kept = [pltpu.make_async_copy(src, dst, self.save.at[i]) for i, (src, dst) in enumerate(moves)]
        for copy in self.kept:
            copy.start()

    def add(self):
        self.copy.wait_recv()

        @pl.loop(0, 4)
        def _(zz):
            for ys in range(2):
                for xs in range(2):
                    add_into(self.sib.at[zz, ys, xs], self.grad.at[zz, self.core, ys, xs])

        if self.hop is None:
            self.keep((self.sib, self.out))
        else:
            for copy in self.hops:
                copy.start()

    def add_hop(self):
        x, y = self.x, self.y
        self.hops[0].wait_recv()
        for zz in range(2):
            for ys in range(2):
                add_into(self.sib.at[zz, ys, x], self.hop.at[0, zz, ys])
        self.hops[1].wait_recv()
        for zz in range(2):
            for xs in range(2):
                add_into(self.sib.at[2 + zz, y, xs], self.hop.at[1, zz, xs])
        self.keep(
            (self.sib.at[pl.ds(0, 2), :, x], self.out.at[0]),
            (self.sib.at[pl.ds(2, 2), y], self.out.at[1]),
        )

    def finish(self):
        self.copy.wait_send()
        for copy in self.kept:
            copy.wait()
        if self.hop is not None:
            for copy in self.hops:
                copy.wait_send()


class ShardSum:
    def __init__(self, grad, out, bufs, own_sem, send, recv, begun=False):
        self.grad, self.out, self.begun = grad, out, begun
        self.near_x, self.near_y, self.two, self.line = bufs[:4]
        self.one = None if begun else bufs[4]
        self.own_sem, self.send_sem, self.recv_sem = own_sem, send, recv
        self.z, self.core, self.y, self.x = position()
        self.sent = []
        first, second = pl.ds(0, 2), pl.ds(2, 2)
        self.loads = (
            pltpu.make_async_copy(grad.at[0] if begun else grad.at[first, :, self.x], self.near_x, own_sem.at[0]),
            pltpu.make_async_copy(grad.at[1] if begun else grad.at[second, self.y], self.near_y, own_sem.at[1]),
        )

    def copy(self, src, dst, slot, device):
        return remote(src, dst, self.send_sem.at[slot], self.recv_sem.at[slot], device)

    def go(self, src, dst, slot, device):
        copy = self.copy(src, dst, slot, device)
        copy.start()
        self.sent.append(copy)

    def arrived(self, dst, slot):
        remote(dst, dst, self.send_sem.at[0], self.recv_sem.at[slot], at(self.z, self.core, self.y, self.x)).wait_recv()

    def moves(self):
        z, core, y, x = self.z, self.core, self.y, self.x
        first, second = pl.ds(0, 2), pl.ds(2, 2)
        return ([] if self.begun else [
            self.copy(self.grad.at[first, :, 1 - x], self.one.at[0], 2, at(z, core, y, 1 - x)),
            self.copy(self.grad.at[second, 1 - y], self.one.at[1], 3, at(z, core, 1 - y, x)),
        ]) + [
            self.copy(self.near_x.at[:, 1 - y], self.two.at[0], 4, at(z, core, 1 - y, x)),
            self.copy(self.near_y.at[:, 1 - x], self.two.at[1], 5, at(z, core, y, 1 - x)),
        ]

    def to_line(self, step):
        z, core, y, x = self.z, self.core, self.y, self.x
        target = lax.rem(z + step, 4)
        device = at(target, core, y, x)
        low = self.copy(self.near_x.at[lax.rem(target, 2), y], self.line.at[step - 1], 5 + step, device)
        high = self.copy(self.near_y.at[lax.rem(target, 2), x], self.line.at[step - 1], 5 + step, device)
        return target, low, high

    def start(self):
        for copy in self.moves()[:-2]:
            copy.start()
        for copy in self.loads:
            copy.start()

    def turn(self):
        moves = self.moves()
        for side, near in enumerate((self.near_x, self.near_y)):
            self.loads[side].wait()
            if not self.begun:
                self.arrived(self.one.at[side], 2 + side)
                for zz in range(2):
                    for other in range(2):
                        add_into(near.at[zz, other], self.one.at[side, zz, other])
            moves[side - 2].start()

    def last(self):
        y, x = self.y, self.x
        self.arrived(self.two.at[0], 4)
        for zz in range(2):
            add_into(self.near_x.at[zz, y], self.two.at[0, zz])
        self.arrived(self.two.at[1], 5)
        for zz in range(2):
            add_into(self.near_y.at[zz, x], self.two.at[1, zz])
        for step in (1, 2, 3):
            target, low, high = self.to_line(step)
            pl.when(target < 2)(low.start)
            pl.when(target >= 2)(high.start)

    def finish(self):
        z, y, x = self.z, self.y, self.x
        low = self.near_x[lax.rem(z, 2), y].astype(F32)
        high = self.near_y[lax.rem(z, 2), x].astype(F32)
        total = jnp.where(z < 2, low, high)
        for step in (1, 2, 3):
            self.arrived(self.line.at[step - 1], 5 + step)
            total = total + self.line[step - 1].astype(F32)
        self.out[...] = total
        for copy in self.moves():
            copy.wait_send()
        for step in (1, 2, 3):
            target, low, high = self.to_line(step)
            pl.when(target < 2)(low.wait_send)
            pl.when(target >= 2)(high.wait_send)

    @staticmethod
    def buffers(grad, begun=False):
        tail, kind = grad.shape[3:], grad.dtype
        shapes = [(2, 2), (2, 2), (2, 2), (3,)] + ([] if begun else [(2, 2, 2)])
        return [pltpu.VMEM(shape + tail, kind) for shape in shapes]


class GroupSum:
    def __init__(self, bufs, send, recv):
        self.tot, self.one, self.two, self.line = bufs
        self.send_sem, self.recv_sem = send, recv
        self.z, self.core, self.y, self.x = position()
        self.sent = []

    copy = ShardSum.copy
    go = ShardSum.go
    arrived = ShardSum.arrived

    def start(self, total, columns):
        z, core, y, x = self.z, self.core, self.y, self.x
        rows = self.tot.shape[4]

        @pl.loop(0, 4)
        def _(zz):
            for cc in range(2):
                for yy in range(2):
                    for xx in range(2):
                        first = pl.multiple_of(zz * 8 * rows, 8) + ((cc * 2 + yy) * 2 + xx) * rows
                        part = total[pl.ds(pl.multiple_of(first, 8), rows), columns]
                        self.tot[zz, cc, yy, xx] = part.astype(BF16)

        self.go(self.tot.at[pl.ds(0, 2), :, :, 1 - x], self.one.at[0], 0, at(z, core, y, 1 - x))
        self.go(self.tot.at[pl.ds(2, 2), :, 1 - y], self.one.at[1], 1, at(z, core, 1 - y, x))

    def turn(self):
        z, core, y, x = self.z, self.core, self.y, self.x
        self.arrived(self.one.at[0], 0)

        @pl.loop(0, 2)
        def _(zz):
            for cc in range(2):
                for ys in range(2):
                    add_into(self.tot.at[zz, cc, ys, x], self.one.at[0, zz, cc, ys])

        self.go(self.tot.at[pl.ds(0, 2), :, 1 - y, x], self.two.at[0], 2, at(z, core, 1 - y, x))
        self.arrived(self.one.at[1], 1)

        @pl.loop(0, 2)
        def _(zz):
            for cc in range(2):
                for xs in range(2):
                    add_into(self.tot.at[2 + zz, cc, y, xs], self.one.at[1, zz, cc, xs])

        self.go(self.tot.at[pl.ds(2, 2), :, y, 1 - x], self.two.at[1], 3, at(z, core, y, 1 - x))

    def last(self):
        z, core, y, x = self.z, self.core, self.y, self.x
        for side in (0, 1):
            self.arrived(self.two.at[side], 2 + side)

            @pl.loop(0, 2)
            def _(zz, side=side):
                for cc in range(2):
                    add_into(self.tot.at[2 * side + zz, cc, y, x], self.two.at[side, zz, cc])

        mine = z * 2 + core
        for step in range(1, 8):
            target = lax.rem(mine + step, 8)
            tz, tc = target // 2, target % 2
            self.go(self.tot.at[tz, tc, y, x], self.line.at[step - 1], 3 + step, at(tz, tc, y, x))

    def finish(self):
        for step in range(1, 8):
            self.arrived(self.line.at[step - 1], 3 + step)
        for copy in self.sent:
            copy.wait_send()

    def term(self, source):
        z, core, y, x = self.z, self.core, self.y, self.x
        back = lax.rem(z * 2 + core - source + 8 + 7, 8)
        own = self.tot[z, core, y, x].astype(F32)
        return jnp.where(back == 7, own, self.line[jnp.minimum(back, 6)].astype(F32))

    @staticmethod
    def buffers(rows, columns):
        return [
            pltpu.VMEM((4, 2, 2, 2, rows, columns), BF16),
            pltpu.VMEM((2, 2, 2, 2, rows, columns), BF16),
            pltpu.VMEM((2, 2, 2, rows, columns), BF16),
            pltpu.VMEM((7, rows, columns), BF16),
        ]


def join_groups(first, second, out):
    width = out.shape[1] // 3
    for side in range(2):
        early = None
        for z in range(4):
            term = first.term(z * 2 + side)
            early = term if early is None else early + term
        outer = second.term(side) + second.term(6 + side)
        inner = second.term(2 + side) + second.term(4 + side)
        pairs = (early[:, :TRIPLE], early[:, TRIPLE:] + outer, inner)
        for j, pair in enumerate(pairs):
            for kind in range(3):
                target = kind * width + (3 * side + j) * LANES
                out[:, target : target + LANES] = pair[:, kind * LANES : (kind + 1) * LANES]


class SmallSum:
    def __init__(self, bufs, out, send, recv):
        self.norms, self.swap, self.acc, self.got, self.line = bufs
        self.out, self.send_sem, self.recv_sem = out, send, recv
        self.z, self.core, self.y, self.x = position()
        self.sent = []
        self.cut = self.norms.shape[2]

    copy = ShardSum.copy
    go = ShardSum.go
    arrived = ShardSum.arrived

    def start(self, kernel_grad, norm_grad):
        z, core, y, x = self.z, self.core, self.y, self.x
        cut = self.cut
        self.norms[0] = norm_grad[:, :cut]
        self.norms[1] = norm_grad[:, cut:]
        self.acc[0, :, : kernel_grad.shape[1]] = kernel_grad
        self.go(self.norms.at[1 - core], self.swap, 0, at(z, 1 - core, y, x))

    def over(self):
        z, core, y, x = self.z, self.core, self.y, self.x
        self.arrived(self.swap, 0)
        self.acc[0, :, self.acc.shape[2] - self.cut :] = self.norms[core] + self.swap[...]
        self.go(self.acc.at[0], self.got.at[0], 1, at(z, core, y, 1 - x))

    def turn(self):
        z, core, y, x = self.z, self.core, self.y, self.x
        self.arrived(self.got.at[0], 1)
        self.acc[1] = self.acc[0] + self.got[0]
        self.go(self.acc.at[1], self.got.at[1], 2, at(z, core, 1 - y, x))

    def last(self):
        z, core, y, x = self.z, self.core, self.y, self.x
        self.arrived(self.got.at[1], 2)
        self.acc[2] = self.acc[1] + self.got[1]
        for step in (1, 2, 3):
            self.go(self.acc.at[2], self.line.at[step - 1], 2 + step, at(lax.rem(z + step, 4), core, y, x))

    def swap_back(self):
        z, core, y, x = self.z, self.core, self.y, self.x
        for step in (1, 2, 3):
            self.arrived(self.line.at[step - 1], 2 + step)
        total = None
        for source in range(4):
            back = lax.rem(z - source + 4, 4)
            term = jnp.where(back == 0, self.acc[2], self.line[jnp.maximum(back - 1, 0)])
            total = term if total is None else total + term
        self.out[core] = total
        self.go(self.out.at[core], self.out.at[core], 6, at(z, 1 - core, y, x))

    def finish(self):
        self.arrived(self.out.at[1 - self.core], 6)
        for copy in self.sent:
            copy.wait_send()

    @staticmethod
    def buffers(columns, norm_columns):
        wide = columns + norm_columns
        return [
            pltpu.VMEM((2, 8, norm_columns), F32),
            pltpu.VMEM((8, norm_columns), F32),
            pltpu.VMEM((3, 8, wide), F32),
            pltpu.VMEM((2, 8, wide), F32),
            pltpu.VMEM((3, 8, wide), F32),
        ]


def causal_mask():
    return iota((TILE, TILE), 0) <= iota((TILE, TILE), 1)


def place_small(smalls, kernel_out, norm_out, core, part, cut):
    wide, width = kernel_out.shape[1], norm_out.shape[1]
    column = iota((LANES, wide), 1)
    block, lane = column // LANES, column % LANES
    source = (block % 3) * width + (core * 3 + block // 3) * LANES + lane - iota((LANES, wide), 0)
    norm_source = iota((LANES, width), 1) - iota((LANES, width), 0)
    kernel_out[...] = jnp.zeros_like(kernel_out)
    norm_out[...] = jnp.zeros_like(norm_out)

    @pl.loop(0, smalls.shape[0])
    def _(device):
        low = smalls[device].astype(BF16)
        kernel_out[...] += dot_nn(low, jnp.where(source == device * part, 1.0, 0.0).astype(BF16))
        norm_out[...] += dot_nn(low, jnp.where(norm_source == device * cut, 1.0, 0.0).astype(BF16))

    norm_out[0:4] = norm_out[3:7]


def attend(query_ref, key_ref, value_t, lse, out_t, head, block):
    rows, past = slice(block * TILE, (block + 1) * TILE), slice(0, block * TILE)
    query = query_ref[head, rows]
    diagonal = jnp.where(causal_mask(), dot_nt(key_ref[head, rows], query), NEG_FILL)
    top = jnp.max(diagonal, axis=0, keepdims=True)
    if block:
        before = dot_nt(key_ref[head, past], query)
        top = jnp.maximum(top, jnp.max(before, axis=0, keepdims=True))
        exp_before = jnp.exp(before - top)
    exp_diagonal = jnp.exp(diagonal - top)
    norm = jnp.sum(exp_diagonal, axis=0, keepdims=True)
    if block:
        norm = norm + jnp.sum(exp_before, axis=0, keepdims=True)
    lse[head, :, rows] = top + jnp.log(norm)
    inverse = 1.0 / norm
    result = dot_nn(value_t[head, :, rows], (exp_diagonal * inverse).astype(BF16))
    if block:
        result = result + dot_nn(value_t[head, :, past], (exp_before * inverse).astype(BF16))
    out_t[head, :, rows] = result


def convolve(proj, taps, slot, local, start, length, query_ref, key_ref, value_ref, key_t, value_t):
    window = proj[slot, pl.ds(pl.multiple_of(start, PAD), TILE + PAD)].astype(F32)
    columns = times(local, TRIPLE)
    mixed = (
        taps[0:1, columns] * window[PAD:]
        + taps[1:2, columns] * shifted(window, 1)[PAD:]
        + taps[2:3, columns] * shifted(window, 2)[PAD:]
    ).astype(BF16).astype(F32)
    query, key, value = mixed[:, 0:LANES] * (HEAD_DIM**-0.5), mixed[:, LANES : 2 * LANES], mixed[:, 2 * LANES :]
    rows = pl.ds(pl.multiple_of(start, TILE), TILE)
    lanes = iota((TILE, LANES), 1)
    low_half = lanes < HEAD_DIM
    bias = jnp.where(start + iota((TILE, LANES), 0) < length, 0.0, NEG_FILL)
    at_zero, at_half = lanes == 0, lanes == HEAD_DIM
    query_ref[2 * slot, rows] = jnp.where(low_half, query, jnp.where(at_half, 1.0, 0.0)).astype(BF16)
    query_ref[2 * slot + 1, rows] = jnp.where(low_half, jnp.where(at_zero, 1.0, 0.0), query).astype(BF16)
    key_ref[2 * slot, rows] = jnp.where(low_half, key, jnp.where(at_half, bias, 0.0)).astype(BF16)
    key_ref[2 * slot + 1, rows] = jnp.where(low_half, jnp.where(at_zero, bias, 0.0), key).astype(BF16)
    value_ref[slot, rows] = value.astype(BF16)
    turned_key, turned_value = key.T.astype(BF16), value.T.astype(BF16)
    for head in range(2):
        part = slice(head * HEAD_DIM, (head + 1) * HEAD_DIM)
        key_t[2 * slot + head, :, rows] = turned_key[part]
        value_t[2 * slot + head, :, rows] = turned_value[part]


def first_kernel(
    lens, xs_ref, xl_ref, qkv_ref, conv_ref, norm_ref, out_s, up_s, down_s,
    att, full_out, full_up, full_down, xs_o, xl_o, wq_o, taps_o, norms_o,
    ql_o, kl_o, vl_o, ktl_o, lsel_o, pl_o, ol_o, qs_o, ks_o, vs_o, kts_o, lses_o, ps_o, os_o,
    xs, xl, small, smalls, shard, wq_parts, wq, taps, norms,
    ql, kl, vl, ktl, lsel, proj_l, ol, qs, ks, vs, kts, lses, proj_s, os,
    vtl, vts, otl, ots,
    own_sem, send, recv, sib_send, sib_recv, shard_own, shard_send, shard_recv,
    att_send_l, att_recv_l, att_send_s, att_recv_s, att_own_l, att_own_s, save_sem,
):
    z, core, y, x = position()
    half, near, _, _ = roles()
    index = z * 2 + core
    pairs_long = 2 - near
    own_short, own_long = xs_ref.shape[1], xl_ref.shape[1]
    owned = own_short + own_long
    long_rows, short_rows = xl.shape[0], xs.shape[0]
    part, cut = conv_ref.shape[1], norm_ref.shape[1]
    length_short = jnp.where(half == 0, lens[0, 0], lens[0, 1])
    length_long = jnp.where(half == 0, lens[1, 0], lens[1, 1])

    small[...] = jnp.zeros_like(small)
    small[0:3, 0:part] = conv_ref[...].astype(F32)
    small[3:7, 0:cut] = norm_ref[...].astype(F32)
    width = wq.shape[0]
    for side in range(2):
        for j in range(3):
            for kind in range(3):
                source = kind * width + (3 * side + j) * LANES
                target = (3 * j + kind) * LANES
                shard[side, :, target : target + LANES] = qkv_ref[:, source : source + LANES]
    greet_all()
    rows_short = RowGather(
        xs_ref, xs, own_sem.at[0], send.at[0], recv.at[0], sib_send.at[0], sib_recv.at[0], True
    )
    rows_long = RowGather(
        xl_ref, xl, own_sem.at[1], send.at[1], recv.at[1], sib_send.at[1], sib_recv.at[1], False
    )
    weights = [
        ShardGather(a, f, shard_own.at[i], shard_send.at[i], shard_recv.at[i], halves=i == 1)
        for i, (a, f) in enumerate(
            ((small, smalls), (shard, wq_parts), (out_s, full_out), (up_s, full_up), (down_s, full_down))
        )
    ]
    small_w, qkv_w, out_w, up_w, down_w = weights

    def place():
        place_small(smalls.reshape(32, 8, LANES), taps, norms, core, part, cut)

    def join_weights():
        pieces = wq_parts.shape[5]
        for zz in range(4):
            for cc in range(2):
                for yy in range(2):
                    first = ((zz * 2 + cc) * 2 + yy) * 2 * pieces
                    both = jnp.concatenate([wq_parts[zz, cc, yy, xx, core].astype(F32) for xx in range(2)], axis=0)
                    wq[first : first + 2 * pieces] = both.astype(BF16)

    def project(x_ref, proj, start, size, slots, first_pair):
        normal, _ = normalise(x_ref[pl.ds(pl.multiple_of(start, size), size)].astype(F32))
        low = (normal * norms[0:1] + norms[1:2]).astype(BF16)

        @pl.loop(0, slots)
        def _(slot):
            result = dot_nn(low, wq[:, times(slot + first_pair, TRIPLE)])
            proj[slot, pl.ds(pl.multiple_of(PAD + start, PAD), size)] = result.astype(BF16)

    def project_long(place):
        @pl.loop(0, 2)
        def _(side):
            project(xl, proj_l, rows_long.chip_rows(place) * 2 * own_long + side * TILE, TILE, pairs_long, 2 * near)

    def project_short(place):
        @pl.when(near == 1)
        def _():
            project(xs, proj_s, rows_short.chip_rows(place) * 2 * own_short, TILE, 3, 0)

    def conv_short():
        @pl.when(near == 1)
        def _():
            @pl.loop(0, 3)
            def _(slot):
                @pl.loop(0, short_rows // TILE)
                def _(step):
                    convolve(proj_s, taps, slot, slot, step * TILE, length_short, qs, ks, vs, kts, vts)

    def conv_long():
        @pl.loop(0, pairs_long)
        def _(slot):
            @pl.loop(0, long_rows // TILE)
            def _(step):
                convolve(proj_l, taps, slot, slot + 2 * near, step * TILE, length_long, ql, kl, vl, ktl, vtl)

    saves = Copies(save_sem)

    def save(*moves):
        for source, target in moves:
            saves.start(source, target)

    def save_long():
        save((xl, xl_o), (wq, wq_o), (taps, taps_o), (norms, norms_o))
        save((ql, ql_o), (kl, kl_o), (vl, vl_o), (ktl, ktl_o), (proj_l, pl_o))

    def save_short():
        save((xs, xs_o), (qs, qs_o), (ks, ks_o), (vs, vs_o))
        save((kts, kts_o), (proj_s, ps_o), (lses, lses_o), (os, os_o))

    def save_last():
        save((lsel, lsel_o), (ol, ol_o))

    def to_owner(o_ref, slot, first, rows, owner, row_in_owner, pair, send_sem, recv_sem, own_sem):
        source = o_ref.at[slot, pl.ds(first, rows)]
        target = att.at[
            pl.ds(pl.multiple_of(half * owned + row_in_owner, LANES), rows), times(pair, LANES)
        ]
        far = remote(source, target, send_sem, recv_sem, (owner, y * 2 + x))
        close = pltpu.make_async_copy(source, target, own_sem)
        return far, close

    def short_moves(slot, owner):
        return to_owner(
            os, slot, owner * own_short, own_short, owner, 0, 3 * core + slot,
            att_send_s.at[slot, owner], att_recv_s.at[half, 3 * core + slot], att_own_s.at[slot],
        )

    def long_moves(slot, owner):
        pair = 3 * core + slot + 2 * near
        return to_owner(
            ol, slot, owner * own_long, own_long, owner, own_short, pair,
            att_send_l.at[slot, owner], att_recv_l.at[half, pair], att_own_l.at[slot],
        )

    def send_block(o_ref, o_t, slot, block, moves, owners):
        rows = slice(block * TILE, (block + 1) * TILE)
        both = jnp.concatenate([o_t[2 * slot, :, rows], o_t[2 * slot + 1, :, rows]], axis=0)
        o_ref[slot, rows] = both.T.astype(BF16)
        for owner in owners:
            far, close = moves(slot, owner)
            pl.when(index != owner)(far.start)
            pl.when(index == owner)(close.start)

    def attend_short(block):
        @pl.when(near == 1)
        def _():
            @pl.loop(0, 6)
            def _(head):
                attend(qs, ks, vts, lses, ots, head, block)

    def send_short(block):
        @pl.when(near == 1)
        def _():
            @pl.loop(0, 3)
            def _(slot):
                send_block(os, ots, slot, block, short_moves, (2 * block, 2 * block + 1))

    def attend_long(block):
        @pl.loop(0, 2 * pairs_long)
        def _(head):
            attend(ql, kl, vtl, lsel, otl, head, block)

    def send_long(block):
        @pl.loop(0, pairs_long)
        def _(slot):
            send_block(ol, otl, slot, block, long_moves, (block,))

    zeros = jnp.zeros((PAD, TRIPLE), BF16)
    for slot in range(2):
        proj_l[slot, 0:PAD] = zeros
    for slot in range(3):
        proj_s[slot, 0:PAD] = zeros
    small_w.start()
    qkv_w.start()
    rows_long.start()
    rows_long.start_far()
    rows_short.start()
    small_w.over()
    small_w.turn()
    small_w.last()
    small_w.finish()
    place()
    qkv_w.over()
    rows_long.step(0)
    qkv_w.turn()
    rows_short.start_far()
    up_w.start()
    out_w.start()
    rows_long.step(1)
    qkv_w.last()
    rows_long.step(2)
    down_w.start()
    qkv_w.finish()
    join_weights()
    rows_long.whole(0)
    project_long(0)
    rows_long.whole(1)
    project_long(1)
    rows_long.whole(2)
    project_long(2)
    rows_short.step(0)
    rows_short.step(1)
    rows_short.step(2)
    rows_short.whole(0)
    project_short(0)
    rows_short.whole(1)
    project_short(1)
    rows_short.whole(2)
    project_short(2)
    rows_short.whole(3)
    project_short(3)
    rows_long.whole(3)
    project_long(3)
    up_w.over()
    out_w.over()
    conv_short()
    attend_short(0)
    send_short(0)
    attend_short(2)
    send_short(2)
    attend_short(1)
    send_short(1)
    attend_short(3)
    send_short(3)
    save_short()
    conv_long()
    save_long()
    attend_long(0)
    send_long(0)
    up_w.turn()
    attend_long(4)
    send_long(4)
    out_w.turn()
    attend_long(1)
    send_long(1)
    attend_long(5)
    send_long(5)
    down_w.over()
    up_w.last()
    out_w.last()
    attend_long(2)
    send_long(2)
    attend_long(6)
    send_long(6)
    down_w.turn()
    attend_long(3)
    send_long(3)
    attend_long(7)
    send_long(7)
    save_last()
    down_w.last()
    out_w.finish()
    up_w.finish()
    down_w.finish()
    for one in weights:
        one.sends_done()

    def own_or_wait(source, moves, slot, arrival):
        @pl.when(index == source)
        def _():
            moves(slot, index)[1].wait()

        @pl.when(index != source)
        def _():
            arrival.wait_recv()

    me = (index, y * 2 + x)
    for seq in range(2):
        for pair in range(6):
            columns = pl.ds(pair * LANES, LANES)
            block = att.at[pl.ds(seq * owned + own_short, own_long), columns]
            source, slot = long_source(seq, pair)
            own_or_wait(
                source, long_moves, slot,
                remote(block, block, att_send_l.at[0, 0], att_recv_l.at[seq, pair], me),
            )
            block = att.at[pl.ds(seq * owned, own_short), columns]
            source, slot = short_source(seq, pair)
            own_or_wait(
                source, short_moves, slot,
                remote(block, block, att_send_s.at[0, 0], att_recv_s.at[seq, pair], me),
            )

    def sends_done(moves, slot):
        for owner in range(8):
            far, _ = moves(slot, owner)
            pl.when(index != owner)(far.wait_send)

    sends_done(long_moves, 0)
    pl.when(near == 0)(lambda: sends_done(long_moves, 1))

    @pl.when(near == 1)
    def _():
        for slot in range(3):
            sends_done(short_moves, slot)

    rows_long.finish()
    rows_short.finish()
    saves.finish()


def first_part(lengths, x_short, x_long, w_qkv, conv_kernel, norm_params, w_out, w_up, w_down, count):
    width = x_short.shape[2]
    short, long = count * x_short.shape[1], count * x_long.shape[1]
    owned = x_short.shape[1] + x_long.shape[1]
    wide = w_qkv.shape[1] // 2
    rows = w_qkv.shape[0]
    out = jax.ShapeDtypeStruct

    def saved(pairs, total):
        return [
            ((2 * pairs, total, LANES), BF16),
            ((2 * pairs, total, LANES), BF16),
            ((pairs, total, LANES), BF16),
            ((2 * pairs, HEAD_DIM, total), BF16),
            ((2 * pairs, 1, total), F32),
            ((pairs, PAD + total, TRIPLE), BF16),
            ((pairs, total, LANES), BF16),
        ]

    kept = saved(2, long) + saved(3, short)
    basic = [((short, width), BF16), ((long, width), BF16)]
    consts = [((width, wide), BF16), ((8, wide), F32), ((8, width), F32)]
    full = [((4, 2, 2, 2) + w.shape, BF16) for w in (w_out, w_up, w_down)]
    outs = [((2 * owned, width), BF16)] + full + basic + consts + kept
    scratch = (
        basic
        + [((8, LANES), F32), ((4, 2, 2, 2, 8, LANES), F32), ((2, rows, wide), BF16)]
        + [((4, 2, 2, 2, 2, rows, wide), BF16)]
        + consts
        + kept
        + [((4, HEAD_DIM, long), BF16), ((6, HEAD_DIM, short), BF16)]
        + [((4, HEAD_DIM, long), F32), ((6, HEAD_DIM, short), F32)]
    )
    return pl.pallas_call(
        first_kernel,
        out_shape=tuple(out(*one) for one in outs),
        in_specs=[smem(), hbm(), hbm(), vmem(), vmem(), vmem(), hbm(), hbm(), hbm()],
        out_specs=tuple([hbm()] * len(outs)),
        scratch_shapes=[pltpu.VMEM(*one) for one in scratch]
        + [DMA((2,))] + [DMA((2, 4))] * 4
        + [DMA((5,)), DMA((5, 13)), DMA((5, 13))]
        + [DMA((2, 8)), DMA((2, 6)), DMA((3, 8)), DMA((2, 6)), DMA((2,)), DMA((3,))]
        + [DMA((24,))],
        compiler_params=params_of(collective_id=0, has_side_effects=True),
    )(lengths, x_short, x_long, w_qkv, conv_kernel, norm_params, w_out, w_up, w_down)


def second_kernel(
    xs_ref, xl_ref, att, cs_ref, cl_ref, np_ref, wo_ref, wu_ref, wd_ref,
    ys_ref, yl_ref, gmid, gnorm, gwo_o, gwu_o, gwd_o, gl_o, gs_o,
    wo, wu, wd, middle, normal_two, inverse_two, second, second_t, cot, y_acc, gsec, gml, hid, gup,
    gwo, gwu, gwd, sib_out, sib_up, sib_down, hop_up,
    load_sem, save_sem, send_l, recv_l, send_s, recv_s, core_send, core_recv,
):
    z, core, y, x = position()
    half, near, _, _ = roles()
    index = z * 2 + core
    pairs_long = 2 - near
    loads = Copies(load_sem)
    got_out = loads.start(wo_ref, wo)
    got_up = loads.start(wu_ref, wu)
    got_down = loads.start(wd_ref, wd)
    greet_all()
    short, long = xs_ref.shape[1], xl_ref.shape[1]
    owned = short + long
    rows_all = 2 * owned
    for seq in range(2):
        first = seq * owned
        cot[first : first + short] = cs_ref[seq]
        cot[first + short : first + owned] = cl_ref[seq]
        middle[first : first + short] = xs_ref[seq].astype(F32)
        middle[first + short : first + owned] = xl_ref[seq].astype(F32)
    got_out.wait()

    @pl.loop(0, rows_all // TILE)
    def _(step):
        rows = times(step, TILE)
        values = middle[rows] + dot_nn(att[rows], wo[...])
        normal, inverse = normalise(values)
        normal_two[rows] = normal
        inverse_two[rows] = inverse
        second[rows] = (normal * np_ref[2:3] + np_ref[3:4]).astype(BF16)
        y_acc[rows] = values
        gsec[rows] = jnp.zeros_like(values)

    second_t[...] = second[...].T
    inner = 512
    got_up.wait()
    got_down.wait()

    @pl.loop(0, wu.shape[1] // inner)
    def _(step):
        columns = times(step, inner)
        upper = jnp.maximum(dot_nn(second[...], wu[:, columns]), 0.0)
        hidden = (upper * upper).astype(BF16)
        grad_hidden = dot_nt(cot[...], wd[columns])
        grad_upper = (2.0 * upper * grad_hidden).astype(BF16)
        hid[:, columns] = hidden
        gup[:, columns] = grad_upper
        y_acc[...] += dot_nn(hidden, wd[columns])
        gsec[...] += dot_nt(grad_upper, wu[:, columns])

    gnorm[...] = jnp.zeros_like(gnorm)

    @pl.loop(0, rows_all // TILE)
    def _(step):
        rows = times(step, TILE)
        grad = gsec[rows]
        normal = normal_two[rows]
        gnorm[2:3] += jnp.sum(grad * normal, axis=0, keepdims=True)
        gnorm[3:4] += jnp.sum(grad, axis=0, keepdims=True)
        total = cot[rows].astype(F32) + norm_back(grad, normal, inverse_two[rows], np_ref[2:3])
        gmid[rows] = total
        gml[rows] = total.astype(BF16)
        second[rows] = dot_nt(gml[rows], wo[...]).astype(BF16)

    def moves(seq, pair, is_long):
        target, slot = (long_source if is_long else short_source)(seq, pair)
        rows = long if is_long else short
        out, send, recv = (gl_o, send_l, recv_l) if is_long else (gs_o, send_s, recv_s)
        first = seq * owned + (short if is_long else 0)
        source = second.at[pl.ds(first, rows), pl.ds(pair * LANES, LANES)]
        place = out.at[slot, times(index, rows)]
        far = remote(source, place, send.at[seq, pair], recv.at[slot, index], (target, y * 2 + x))
        close = pltpu.make_async_copy(source, place, recv.at[slot, index])
        return target, far, close

    kinds = [(seq, pair, is_long) for is_long in (True, False) for pair in range(6) for seq in range(2)]
    for kind in kinds:
        target, far, close = moves(*kind)
        pl.when(index != target)(far.start)
        pl.when(index == target)(close.start)

    sums = [
        CoreSum(grad, sib, total, core_send.at[i], core_recv.at[i], save_sem.at[i], hop)
        for i, (grad, sib, total, hop) in enumerate(
            ((gwu, sib_up, gwu_o, hop_up), (gwd, sib_down, gwd_o, None), (gwo, sib_out, gwo_o, None))
        )
    ]

    def cut(value, grad):
        return value.reshape(grad.shape[:5] + value.shape[1:]).astype(BF16)

    @pl.loop(0, wu.shape[1] // inner)
    def _(step):
        columns = times(step, inner)
        gwu[:, :, :, :, :, columns] = cut(dot_nn(second_t[...], gup[:, columns]), gwu)

    sums[0].start()
    per = gwd.shape[4]
    slabs = gwd.shape[2] * gwd.shape[3]

    @pl.loop(0, gwd.shape[0])
    def _(zz):
        for cc in range(2):
            columns = times(zz * 2 + cc, slabs * per)
            value = dot_tn(hid[:, columns], cot[...])
            gwd[zz, cc] = value.reshape(gwd.shape[2:]).astype(BF16)

    sums[1].start()
    sums[0].add()
    gwo[...] = cut(dot_tn(att[...], gml[...]), gwo)
    sums[2].start()
    for seq in range(2):
        first = seq * owned
        ys_ref[seq] = y_acc[first : first + short].astype(BF16)
        yl_ref[seq] = y_acc[first + short : first + owned].astype(BF16)

    sums[1].add()
    sums[2].add()
    sums[0].add_hop()
    me = (index, y * 2 + x)

    def arrivals(out, recv, slot, rows):
        for source in range(8):
            block = out.at[slot, pl.ds(source * rows, rows)]

            @pl.when(index != source)
            def _(block=block, source=source):
                remote(block, block, send_l.at[0, 0], recv.at[slot, source], me).wait_recv()

    arrivals(gl_o, recv_l, 0, long)
    pl.when(near == 0)(lambda: arrivals(gl_o, recv_l, 1, long))

    @pl.when(near == 1)
    def _():
        for slot in range(3):
            arrivals(gs_o, recv_s, slot, short)

    for kind in kinds:
        target, far, close = moves(*kind)
        pl.when(index != target)(far.wait_send)
        pl.when(index == target)(close.wait)
    for one in sums:
        one.finish()


def second_part(x_short, x_long, att, cot_short, cot_long, norms, w_out, w_up, w_down, count):
    width = x_short.shape[2]
    rows = att.shape[0]
    short, long = count * x_short.shape[1], count * x_long.shape[1]
    hidden = w_up.shape[1]
    out = jax.ShapeDtypeStruct
    devices = 4 * count

    def shards(w):
        return (4, 2, 2, 2, w.shape[0] // devices, w.shape[1])

    def halves(w):
        return (4, 2, 2, w.shape[0] // devices, w.shape[1])

    return pl.pallas_call(
        second_kernel,
        out_shape=(
            out(x_short.shape, BF16),
            out(x_long.shape, BF16),
            out((rows, width), F32),
            out((8, width), F32),
            out(halves(w_out), BF16),
            out((2, 2, 2) + halves(w_up)[3:], BF16),
            out(halves(w_down), BF16),
            out((2, long, LANES), BF16),
            out((3, short, LANES), BF16),
        ),
        in_specs=[vmem()] * 6 + [hbm()] * 3,
        out_specs=tuple([vmem()] * 4 + [hbm()] * 5),
        scratch_shapes=[
            pltpu.VMEM(w_out.shape, BF16),
            pltpu.VMEM(w_up.shape, BF16),
            pltpu.VMEM(w_down.shape, BF16),
            pltpu.VMEM((rows, width), F32),
            pltpu.VMEM((rows, width), F32),
            pltpu.VMEM((rows, 1), F32),
            pltpu.VMEM((rows, width), BF16),
            pltpu.VMEM((width, rows), BF16),
            pltpu.VMEM((rows, width), BF16),
            pltpu.VMEM((rows, width), F32),
            pltpu.VMEM((rows, width), F32),
            pltpu.VMEM((rows, width), BF16),
            pltpu.VMEM((rows, hidden), BF16),
            pltpu.VMEM((rows, hidden), BF16),
            *[pltpu.VMEM(shards(w), BF16) for w in (w_out, w_up, w_down)],
            *[pltpu.VMEM(halves(w), BF16) for w in (w_out, w_up, w_down)],
            pltpu.VMEM((2, 2, 2) + halves(w_up)[3:], BF16),
            DMA((3,)), DMA((3, 2)), DMA((2, 6)), DMA((2, 8)), DMA((2, 6)), DMA((3, 8)), DMA((3, 3)), DMA((3, 3)),
        ],
        compiler_params=params_of(collective_id=1, has_side_effects=True),
    )(x_short, x_long, att, cot_short, cot_long, norms, w_out, w_up, w_down)


class RowSum:
    def __init__(self, long_bufs, short_bufs, sems):
        self.mine, self.out, self.sib, self.got, self.fin = long_bufs
        self.mine_s, self.out_s, self.sib_s, self.fin_s = short_bufs
        (
            self.sib_send, self.sib_recv, self.send, self.recv, self.on_send, self.fin_recv,
            self.sib_send_s, self.sib_recv_s, self.send_s, self.fin_recv_s,
        ) = sems
        self.z, self.core, self.y, self.x = position()
        self.half, self.near, partner_z, far_z = roles()
        self.partner = at(partner_z, self.core, self.y, self.x)
        self.sibling = at(self.z, 1 - self.core, self.y, self.x)
        self.far = at(far_z, self.core, self.y, self.x)

    def across(self, zz):
        return remote(self.out.at[zz % 2], self.sib.at[zz], self.sib_send.at[zz], self.sib_recv.at[zz], self.sibling)

    def put(self, block, value):
        zz, parity = block // 2, block % 2

        @pl.when(self.core == parity)
        def _():
            self.mine[zz] = value

        @pl.when(self.core != parity)
        def _():
            if zz < 2:
                self.across(zz + 2).wait_send()
            self.out[zz % 2] = value
            self.across(zz).start()

    def place(self, zz):
        return jnp.where(self.half == 0, zz, 3 - zz)

    def part(self, side):
        rows = self.fin.shape[0] // 2
        return pl.ds(side * rows, rows)

    def to_partner(self, zz, side):
        rows = self.part(side)
        return remote(
            self.mine.at[zz, rows], self.got.at[zz, rows], self.send.at[zz, side], self.recv.at[zz, side], self.partner
        )

    def to_owner(self, zz, side):
        rows = self.part(side)
        return remote(
            self.mine.at[zz, rows], self.fin.at[rows], self.on_send.at[zz, side], self.fin_recv.at[side],
            at(zz, self.core, self.y, self.x),
        )

    def sends_to_partner(self, zz):
        place = self.place(zz)
        return jnp.where(self.near == 0, place != 0, place == 0)

    def add_cores(self, zz):
        self.across(zz).wait_recv()
        for side in range(2):
            rows = self.part(side)
            add_into(self.mine.at[zz, rows], self.sib.at[zz, rows])
            pl.when(self.sends_to_partner(zz))(self.to_partner(zz, side).start)

    def sends_on(self, zz):
        return jnp.logical_and(self.near == 1, self.place(zz) >= 2)

    def add_chips(self, zz):
        @pl.when(self.sends_on(zz))
        def _():
            for side in range(2):
                rows = self.part(side)
                self.to_partner(zz, side).wait_recv()
                add_into(self.mine.at[zz, rows], self.got.at[zz, rows])
                self.to_owner(zz, side).start()

    def across_s(self, zz):
        return remote(
            self.out_s.at[zz], self.sib_s.at[zz], self.sib_send_s.at[zz], self.sib_recv_s.at[zz], self.sibling
        )

    def put_short(self, zz, value):
        rows = value.shape[0] // 2
        first, second = value[:rows], value[rows:]

        @pl.when(self.core == 0)
        def _():
            self.mine_s[zz] = first
            self.out_s[zz] = second

        @pl.when(self.core == 1)
        def _():
            self.mine_s[zz] = second
            self.out_s[zz] = first

        self.across_s(zz).start()

    def to_owner_s(self, zz):
        return remote(
            self.mine_s.at[zz], self.fin_s.at[self.half], self.send_s.at[zz], self.fin_recv_s.at[self.half],
            at(zz, self.core, self.y, self.x),
        )

    def add_short(self, zz):
        @pl.when(self.near == 1)
        def _():
            self.across_s(zz).wait_recv()
            add_into(self.mine_s.at[zz], self.sib_s.at[zz])
            pl.when(self.z != zz)(self.to_owner_s(zz).start)

    def own_long(self):
        for side in range(2):
            self.to_partner(self.z, side).wait_recv()
        return self.mine[self.z].astype(F32) + self.got[self.z].astype(F32)

    def other_long(self):
        for side in range(2):
            block = self.fin.at[self.part(side)]
            remote(block, block, self.on_send.at[0, 0], self.fin_recv.at[side], self.far).wait_recv()
        return self.fin[...].astype(F32)

    def shorts(self):
        def arrival(seq):
            block = self.fin_s.at[seq]
            remote(block, block, self.send_s.at[0], self.fin_recv_s.at[seq], self.far).wait_recv()

        arrival(1 - self.half)
        pl.when(self.near == 0)(lambda: arrival(self.half))

        @pl.when(self.near == 1)
        def _():
            self.fin_s[self.half] = self.mine_s[self.z]

    def sends_done(self):
        for zz in range(4):
            if zz < 2:
                self.across(zz).wait_send()
            for side in range(2):
                pl.when(self.sends_to_partner(zz))(self.to_partner(zz, side).wait_send)
                pl.when(self.sends_on(zz))(self.to_owner(zz, side).wait_send)

        @pl.when(self.near == 1)
        def _():
            for zz in range(4):
                self.across_s(zz).wait_send()
                pl.when(self.z != zz)(self.to_owner_s(zz).wait_send)


def third_kernel(
    xs_own, xl_own, gnorm, wq, taps, norms, gmid,
    xs_h, xl_h, ql_h, kl_h, vl_h, ktl_h, lsel_h, pl_h, ol_h, qs_h, ks_h, vs_h, kts_h, lses_h, ps_h, os_h,
    gl_h, gs_h, gwo_h, gwu_h, gwd_h,
    dxs_ref, dxl_ref, gwq_ref, gwo_ref, gwu_ref, gwd_ref, small_ref,
    ql, kl, vl, ktl, lsel, ol, gl, qs, ks, vs, kts, lses, os, gs,
    gm, dqt, delta, gp, early_gn, dwq, dtaps, dnorms, x_tile, p_tile,
    mine, out, sib, got, fin, mine_s, out_s, sib_s, fin_s,
    load_sem, tile_sem,
    r0, r1, r2, r3, r4, r5, r6, r7, r8, r9,
    shard_own, shard_send, shard_recv, group_send, group_recv, small_send, small_recv,
    *bufs,
):
    z, core, y, x = position()
    half, near, _, _ = roles()
    long_moves = (
        (ql_h, ql), (kl_h, kl), (vl_h, vl), (ktl_h, ktl), (lsel_h, lsel), (ol_h, ol), (gl_h, gl),
    )
    short_moves = (
        (qs_h, qs), (ks_h, ks), (vs_h, vs), (kts_h, kts), (lses_h, lses), (os_h, os), (gs_h, gs),
    )
    loads = [
        pltpu.make_async_copy(source, target, load_sem.at[i])
        for i, (source, target) in enumerate(long_moves + short_moves)
    ]
    long_loads, short_loads = loads[:7], loads[7:]

    @pl.when(near == 1)
    def _():
        for copy in short_loads:
            copy.start()

    for copy in long_loads:
        copy.start()
    greet_all()
    bufs = list(bufs)
    sums = []
    for i, (grad, total, begun) in enumerate(
        ((gwo_h, gwo_ref, False), (gwu_h, gwu_ref, True), (gwd_h, gwd_ref, False))
    ):
        size = 4 if begun else 5
        mine_bufs, bufs = bufs[:size], bufs[size:]
        sums.append(ShardSum(grad, total, mine_bufs, shard_own.at[i], shard_send.at[i], shard_recv.at[i], begun))
    group_early = GroupSum(bufs[0:4], group_send.at[0], group_recv.at[0])
    group_late = GroupSum(bufs[4:8], group_send.at[1], group_recv.at[1])
    small = SmallSum(bufs[8:13], small_ref, small_send, small_recv)
    rows_sum = RowSum((mine, out, sib, got, fin), (mine_s, out_s, sib_s, fin_s), (r0, r1, r2, r3, r4, r5, r6, r7, r8, r9))
    sum_out, sum_up, sum_down = sums
    for one in sums:
        one.start()
    short, long = xs_own.shape[1], xl_own.shape[1]
    owned = short + long
    middles = [
        pltpu.make_async_copy(gmid.at[pl.ds(seq * owned + first, size)], dx.at[seq], load_sem.at[14 + 2 * seq + i])
        for seq in range(2)
        for i, (dx, first, size) in enumerate(((dxs_ref, 0, short), (dxl_ref, short, long)))
    ]
    for copy in middles:
        copy.start()
    gm[...] = jnp.zeros_like(gm)
    dwq[...] = jnp.zeros_like(dwq)
    dtaps[...] = jnp.zeros_like(dtaps)
    dnorms[...] = gnorm[...]
    sum_up.turn()
    gain, offset = norms[0:1], norms[1:2]
    causal = causal_mask()
    first_lanes = iota((TILE, LANES), 1) < HEAD_DIM

    def back_head(refs, grad_ref, slot, side, local, block):
        q_ref, k_ref, v_ref, kt_ref, lse, _, g_ref = refs
        head = 2 * slot + side
        own_lanes = first_lanes == (side == 0)
        rows = slice(block * TILE, (block + 1) * TILE)
        query = q_ref[head, rows]
        bare = jnp.where(own_lanes, query.astype(F32), 0.0).astype(BF16)
        grad_out = jnp.where(own_lanes, g_ref[slot, rows].astype(F32), 0.0).astype(BF16)
        stat, less = lse[head, :, rows], delta[local]
        spans = [(block * TILE, TILE, True)]
        if block:
            spans.append((0, block * TILE, False))
        grad_q = None
        for start, size, masked in spans:
            keys = slice(start, start + size)
            scores = dot_nt(k_ref[head, keys], query)
            if masked:
                scores = jnp.where(causal, scores, NEG_FILL)
            probs = jnp.exp(scores - stat)
            grad_probs = dot_nt(v_ref[slot, keys], grad_out)
            grad_ref[keys, 2 * LANES :] += dot_nn(probs.astype(BF16), grad_out)
            grad_scores = (probs * (grad_probs - less)).astype(BF16)
            grad_ref[keys, LANES : 2 * LANES] += dot_nn(grad_scores, bare)
            term = dot_nn(kt_ref[head, :, keys], grad_scores)
            grad_q = term if grad_q is None else grad_q + term
        dqt[local] = (HEAD_DIM**-0.5) * grad_q

    def back_block(refs, x_h, p_h, count, first_slot, first_pair, block):
        o_ref, g_ref = refs[5], refs[6]
        rows = slice(block * TILE, (block + 1) * TILE)
        span = x_h.shape[0] + PAD
        got_x = pltpu.make_async_copy(x_h.at[pl.ds(block * TILE, TILE)], x_tile, tile_sem.at[0])
        got_p = pltpu.make_async_copy(
            p_h.at[pl.ds(first_slot, count), pl.ds(block * TILE, TILE + PAD)], p_tile.at[pl.ds(0, count)], tile_sem.at[1]
        )
        got_x.start()
        got_p.start()
        for local in range(count):
            product = g_ref[first_slot + local, rows].astype(F32) * o_ref[first_slot + local, rows].astype(F32)
            turned = product.T
            delta[2 * local] = jnp.sum(turned[:HEAD_DIM], axis=0, keepdims=True)
            delta[2 * local + 1] = jnp.sum(turned[HEAD_DIM:], axis=0, keepdims=True)

        @pl.loop(0, 2 * count)
        def _(local):
            slot = local // 2
            grad_ref = gm.at[pl.ds(pl.multiple_of(slot * span, PAD), span)]
            back_head(refs, grad_ref, first_slot + slot, local % 2, local, block)

        got_x.wait()
        got_p.wait()
        normal, _ = normalise(x_tile[...].astype(F32))
        low = (normal * gain + offset).astype(BF16)
        for local in range(count):
            grad_ref = gm.at[pl.ds(local * span, span)]
            grad_ref[rows, 0:LANES] = jnp.concatenate([dqt[2 * local], dqt[2 * local + 1]], axis=0).T
            window = grad_ref[pl.ds(block * TILE, TILE + PAD)]
            grad = window[:TILE]
            columns = pl.ds(pl.multiple_of((first_pair + local) * TRIPLE, TRIPLE), TRIPLE)
            kernel = taps[:, columns]
            grad_projected = (
                kernel[0:1] * grad + kernel[1:2] * shifted(window, -1)[:TILE] + kernel[2:3] * shifted(window, -2)[:TILE]
            ).astype(BF16)
            past = p_tile[local].astype(F32)
            dtaps[0:1, columns] += jnp.sum(grad * past[PAD:], axis=0, keepdims=True)
            dtaps[1:2, columns] += jnp.sum(grad * shifted(past, 1)[PAD:], axis=0, keepdims=True)
            dtaps[2:3, columns] += jnp.sum(grad * shifted(past, 2)[PAD:], axis=0, keepdims=True)
            gp[:, local * TRIPLE : (local + 1) * TRIPLE] = grad_projected
        grads = gp[:, : count * TRIPLE]
        columns = pl.ds(pl.multiple_of(first_pair * TRIPLE, TRIPLE), count * TRIPLE)
        grad_normed = dot_nt(grads, wq[:, columns])
        dwq[:, columns] += dot_tn(low, grads)
        dnorms[0:1] += jnp.sum(grad_normed * normal, axis=0, keepdims=True)
        dnorms[1:2] += jnp.sum(grad_normed, axis=0, keepdims=True)
        return grad_normed

    def hook_one():
        sum_up.last()

    def hook_two():
        sum_down.turn()
        sum_out.turn()

    def hook_three():
        sum_down.last()
        sum_out.last()

    def finish_rows(seq, grad, x_ref, dx_ref):
        normal, inverse = normalise(x_ref[seq].astype(F32))
        dx_ref[seq] += norm_back(grad, normal, inverse, gain)

    long_refs = (ql, kl, vl, ktl, lsel, ol, gl)
    short_refs = (qs, ks, vs, kts, lses, os, gs)
    last_long = xl_h.shape[0] // TILE - 1
    last_short = xs_h.shape[0] // TILE - 1

    @pl.when(near == 0)
    def _():
        for copy in long_loads:
            copy.wait()
        for block in range(last_long, -1, -1):
            value = back_block(long_refs, xl_h, pl_h, 1, 0, 0, block)
            early_gn[block * TILE : (block + 1) * TILE] = value.astype(BF16)
            if block == 5:
                hook_one()
            if block == 4:
                hook_two()

    @pl.when(near == 1)
    def _():
        for copy in short_loads:
            copy.wait()
        for block in range(last_short, -1, -1):
            value = back_block(short_refs, xs_h, ps_h, 3, 0, 0, block)
            rows_sum.put_short(block, value.astype(BF16))
            if block == 2:
                hook_one()
            if block == 1:
                hook_two()
        for copy in long_loads:
            copy.wait()

    group_early.start(dwq, pl.ds(0, 2 * TRIPLE))
    hook_three()
    gm[...] = jnp.zeros_like(gm)

    for block in range(last_long, -1, -1):
        value = back_block(long_refs, xl_h, pl_h, 1, 1 - near, 1 + near, block)
        early = early_gn[block * TILE : (block + 1) * TILE].astype(F32)
        rows_sum.put(block, (value + jnp.where(near == 0, early, 0.0)).astype(BF16))
        if block % 2 == 1 and block != last_long:
            rows_sum.add_cores(block // 2 + 1)
        if block > 3:
            rows_sum.add_short(block - 4)
        if block == 6:
            group_early.turn()
        if block == 5:
            group_early.last()
        if block == 2:
            rows_sum.add_chips(3)
    group_late.start(dwq, pl.ds(pl.multiple_of((1 + near) * TRIPLE, TRIPLE), TRIPLE))
    small.start(dtaps[...], dnorms[...])
    rows_sum.add_cores(0)
    rows_sum.add_chips(2)
    small.over()
    group_late.turn()
    rows_sum.add_chips(1)
    small.turn()
    for copy in middles:
        copy.wait()
    rows_sum.shorts()
    finish_rows(half, rows_sum.fin_s[half].astype(F32), xs_own, dxs_ref)
    group_late.last()
    small.last()
    rows_sum.add_chips(0)
    finish_rows(1 - half, rows_sum.fin_s[1 - half].astype(F32), xs_own, dxs_ref)
    finish_rows(half, rows_sum.own_long(), xl_own, dxl_ref)
    for one in sums:
        one.finish()
    group_early.finish()
    small.swap_back()
    group_late.finish()
    join_groups(group_early, group_late, gwq_ref)
    finish_rows(1 - half, rows_sum.other_long(), xl_own, dxl_ref)
    small.finish()
    rows_sum.sends_done()


def third_part(x_short, x_long, gmid, gnorm, wq, taps, norms, kept, grads_in, weight_grads):
    width = x_short.shape[2]
    wide = wq.shape[1]
    count = 8
    short, long = count * x_short.shape[1], count * x_long.shape[1]
    own_short = x_short.shape[1]
    rows = weight_grads[0].shape[3]
    out = jax.ShapeDtypeStruct
    small_wide = wide + width // 2

    def saved(pairs, total):
        return [
            ((2 * pairs, total, LANES), BF16),
            ((2 * pairs, total, LANES), BF16),
            ((pairs, total, LANES), BF16),
            ((2 * pairs, HEAD_DIM, total), BF16),
            ((2 * pairs, 1, total), F32),
            ((pairs, total, LANES), BF16),
            ((pairs, total, LANES), BF16),
        ]

    scratch = (
        saved(2, long)
        + saved(3, short)
        + [
            ((max(long + PAD, 3 * (short + PAD)), TRIPLE), F32),
            ((6, HEAD_DIM, TILE), F32),
            ((6, 1, TILE), F32),
            ((TILE, wide), BF16),
            ((long, width), BF16),
            ((width, wide), F32),
            ((8, wide), F32),
            ((8, width), F32),
            ((TILE, width), BF16),
            ((3, TILE + PAD, TRIPLE), BF16),
        ]
        + [((4, TILE, width), BF16), ((2, TILE, width), BF16)]
        + [((4, TILE, width), BF16)] * 2
        + [((TILE, width), BF16)]
        + [((4, own_short, width), BF16)] * 3
        + [((2, own_short, width), BF16)]
    )
    buffers = []
    for i, g in enumerate(weight_grads):
        buffers += ShardSum.buffers(g, i == 1)
    buffers += GroupSum.buffers(rows, 2 * TRIPLE) + GroupSum.buffers(rows, TRIPLE) + SmallSum.buffers(wide, width // 2)
    return pl.pallas_call(
        third_kernel,
        out_shape=(
            out(x_short.shape, F32),
            out(x_long.shape, F32),
            out((rows, 2 * wide), F32),
            *[out(g.shape[3:], F32) for g in weight_grads],
            out((2, 8, small_wide), F32),
        ),
        in_specs=[vmem()] * 6 + [hbm()] * (1 + len(kept) + len(grads_in) + len(weight_grads)),
        out_specs=tuple([vmem()] * 7),
        scratch_shapes=[pltpu.VMEM(*one) for one in scratch]
        + [DMA((18,)), DMA((2,))]
        + [DMA((4,))] * 2 + [DMA((4, 2))] * 3 + [DMA((2,))] + [DMA((4,))] * 3 + [DMA((2,))]
        + [DMA((3, 2)), DMA((3, 9)), DMA((3, 9)), DMA((2, 11)), DMA((2, 11)), DMA((7,)), DMA((7,))]
        + buffers,
        compiler_params=params_of(63, collective_id=2, has_side_effects=True),
    )(x_short, x_long, gnorm, wq, taps, norms, gmid, *kept, *grads_in, *weight_grads)


def last_kernel(*refs):
    *arrays, smalls = refs[:9]
    outs, kernel_out, norm_out = refs[9:17], refs[17], refs[18]
    held, sems = refs[19:27], refs[27]
    loads = [pltpu.make_async_copy(a, h, sems.at[0, i]) for i, (a, h) in enumerate(zip(arrays, held))]
    copies = [pltpu.make_async_copy(h, o, sems.at[1, i]) for i, (h, o) in enumerate(zip(held, outs))]
    for copy in loads:
        copy.start()
    number = lax.axis_index("seq") * lax.axis_size("batch") + lax.axis_index("batch")
    (taps, part), (norms, cut) = kernel_out.shape, norm_out.shape
    norm_columns = norm_out.shape[1] * 32 // 2
    wide = smalls.shape[2] - norm_columns
    width = 2 * wide // 3

    def pick(values, source, first):
        chosen = jnp.where(source == first + iota(source.shape, 1), 1.0, 0.0)
        return lax.dot_general(
            values, chosen, (((1,), (0,)), ((), ())), preferred_element_type=F32, precision=lax.Precision.HIGHEST
        )

    row = iota((wide, LANES), 0)
    block = row // LANES
    norm_row = iota((norm_columns, LANES), 0)
    kernel_sum, norm_sum = None, None
    for load, copy in zip(loads, copies):
        load.wait()
        copy.start()
    for side in range(2):
        source = (block % 3) * width + (3 * side + block // 3) * LANES + row % LANES
        term = pick(smalls[side, :, :wide], source, number * part)
        norm_term = pick(smalls[side, :, wide:], norm_row + side * norm_columns, number * cut)
        kernel_sum = term if side == 0 else kernel_sum + term
        norm_sum = norm_term if side == 0 else norm_sum + norm_term
    kernel_out[...] = kernel_sum[:taps, :part]
    norm_out[...] = norm_sum[:norms, :cut]
    for copy in copies:
        copy.wait()


def last_part(arrays, smalls, taps, part, cut):
    out = jax.ShapeDtypeStruct
    return pl.pallas_call(
        last_kernel,
        out_shape=(*[out(a.shape, a.dtype) for a in arrays], out((taps, part), F32), out((4, cut), F32)),
        in_specs=[hbm()] * 8 + [vmem()],
        out_specs=tuple([hbm()] * 8 + [vmem()] * 2),
        scratch_shapes=[pltpu.VMEM(a.shape, a.dtype) for a in arrays] + [DMA((2, 8))],
        compiler_params=params_of(),
    )(*arrays, smalls)


def split_body(
    x_short, x_long, lengths, cot_short, cot_long, w_qkv, w_out, w_up, w_down, conv_kernel, norm_params
):
    count = lax.axis_size("seq")
    width = x_short.shape[2]
    att, full_out, full_up, full_down, xs, xl, wq, taps, norms, *kept = first_part(
        lengths, x_short, x_long, w_qkv, conv_kernel, norm_params, w_out, w_up, w_down, count
    )
    y_short, y_long, gmid, gnorm, gwo, gwu, gwd, gl, gs = second_part(
        x_short, x_long, att, cot_short, cot_long, norms,
        full_out.reshape(width, -1), full_up.reshape(width, -1), full_down.reshape(-1, width), count,
    )
    dx_short, dx_long, sum_qkv, sum_out, sum_up, sum_down, smalls = third_part(
        x_short, x_long, gmid, gnorm, wq, taps, norms, [xs, xl] + kept, [gl, gs], [gwo, gwu, gwd]
    )
    return last_part(
        (y_short, y_long, dx_short, dx_long, sum_qkv, sum_out, sum_up, sum_down), smalls,
        conv_kernel.shape[0], conv_kernel.shape[1], norm_params.shape[1],
    )


GROUP_HEADS = 2


def from_behind(value, axis, by):
    count = lax.axis_size(axis)
    pairs = [(i, i + by) for i in range(count) if 0 <= i + by < count]
    return lax.ppermute(value, axis, pairs)


def layer_norm(values, gain, offset_term):
    average = jnp.mean(values, axis=-1, keepdims=True)
    centred = values - average
    inverse = lax.rsqrt(jnp.mean(centred * centred, axis=-1, keepdims=True) + EPS)
    normal = centred * inverse
    return (normal * gain + offset_term, normal, inverse)


def norm_back_flat(grad, normal, inverse, gain):
    scaled_grad = grad * gain
    first_mean = jnp.mean(scaled_grad, axis=-1, keepdims=True)
    second_mean = jnp.mean(scaled_grad * normal, axis=-1, keepdims=True)
    return inverse * (scaled_grad - first_mean - normal * second_mean)


def front_part(inputs, full_weights):
    w_qkv = full_weights[0]
    kernel = full_weights[4].astype(jnp.float32)
    params = full_weights[5].astype(jnp.float32)
    saved = []
    tails = []
    for part_in in inputs:
        seq_count, block_rows, model_width = part_in.shape
        flat = part_in.reshape(seq_count * block_rows, model_width).astype(jnp.float32)
        normed, normal, inverse = layer_norm(flat, params[0], params[1])
        normed_low = normed.astype(jnp.bfloat16)
        projected = jnp.dot(normed_low, w_qkv, preferred_element_type=jnp.float32).astype(
            jnp.bfloat16
        )
        projected = projected.reshape(seq_count, block_rows, 3 * model_width)
        saved.append((flat, normal, inverse, normed_low, projected))
        tails.append(projected[:, block_rows - 2 :])
    received = from_behind((tails[0], tails[1]), "seq", 1)
    fronts = []
    for index_part in range(2):
        flat, normal, inverse, normed_low, projected = saved[index_part]
        block_rows = projected.shape[1]
        padded = jnp.concatenate([received[index_part], projected], axis=1).astype(jnp.float32)
        mixed = (
            kernel[0] * padded[:, 2:]
            + kernel[1] * padded[:, 1 : block_rows + 1]
            + kernel[2] * padded[:, :block_rows]
        )
        fronts.append((flat, normal, inverse, normed_low, padded, mixed.astype(jnp.bfloat16)))
    return fronts


def attend_block(queries, key_rows, value_rows, usable, grad_heads):
    scaling = queries.shape[-1] ** (-0.5)
    scores = jnp.einsum("sqhd,skhd->shqk", queries, key_rows, preferred_element_type=jnp.float32)
    masked = jnp.where(usable, scaling * scores, NEG_FILL)
    exp_terms = jnp.exp(masked - jnp.max(masked, axis=-1, keepdims=True))
    attn_probs = exp_terms / jnp.sum(exp_terms, axis=-1, keepdims=True)
    probs_low = attn_probs.astype(jnp.bfloat16)
    if grad_heads is None:
        attended = jnp.einsum(
            "shqk,skhd->sqhd", probs_low, value_rows, preferred_element_type=jnp.float32
        )
        return attended.astype(jnp.bfloat16)
    grad_probs = jnp.einsum(
        "sqhd,skhd->shqk", grad_heads, value_rows, preferred_element_type=jnp.float32
    )
    grad_values = jnp.einsum(
        "shqk,sqhd->skhd", probs_low, grad_heads, preferred_element_type=jnp.float32
    )
    row_delta = jnp.sum(attn_probs * grad_probs, axis=-1, keepdims=True)
    grad_scores = (scaling * attn_probs * (grad_probs - row_delta)).astype(jnp.bfloat16)
    grad_queries = jnp.einsum(
        "shqk,skhd->sqhd", grad_scores, key_rows, preferred_element_type=jnp.float32
    )
    grad_keys = jnp.einsum(
        "shqk,sqhd->skhd", grad_scores, queries, preferred_element_type=jnp.float32
    )
    return (grad_queries, grad_keys, grad_values)


def make_usable(query_pos, key_pos, seq_lengths):
    usable = (key_pos[None, None, :] <= query_pos[None, :, None]) & (
        key_pos[None, None, :] < seq_lengths[:, None, None]
    )
    return usable[:, None]


def attention(mixed, kv_full, seq_lengths, offset, grad_attended):
    seq_count, block_rows, three_width = mixed.shape
    model_width = three_width // 3
    full_len = kv_full.shape[1]
    queries = mixed[:, :, :model_width].reshape(seq_count, block_rows, -1, HEAD_DIM)
    key_rows = kv_full[:, :, :model_width].reshape(seq_count, full_len, -1, HEAD_DIM)
    value_rows = kv_full[:, :, model_width:].reshape(seq_count, full_len, -1, HEAD_DIM)
    positions = offset + jnp.arange(block_rows, dtype=jnp.int32)
    key_pos = jnp.arange(full_len, dtype=jnp.int32)
    usable = make_usable(positions, key_pos, seq_lengths)
    heads_total = queries.shape[2]
    grad_heads = None
    if grad_attended is not None:
        grad_heads = grad_attended.reshape(seq_count, block_rows, -1, HEAD_DIM)
    results = []
    for first_head in range(0, heads_total, GROUP_HEADS):
        last_head = first_head + GROUP_HEADS
        grad_part = None if grad_heads is None else grad_heads[:, :, first_head:last_head]
        results.append(
            attend_block(
                queries[:, :, first_head:last_head],
                key_rows[:, :, first_head:last_head],
                value_rows[:, :, first_head:last_head],
                usable,
                grad_part,
            )
        )
    if grad_heads is None:
        return jnp.concatenate(results, axis=2).reshape(seq_count, block_rows, model_width)
    grad_queries = jnp.concatenate([entry_set[0] for entry_set in results], axis=2).reshape(
        seq_count, block_rows, model_width
    )
    grad_keys = jnp.concatenate([entry_set[1] for entry_set in results], axis=2).reshape(
        seq_count, full_len, model_width
    )
    grad_values = jnp.concatenate([entry_set[2] for entry_set in results], axis=2).reshape(
        seq_count, full_len, model_width
    )
    return (grad_queries, grad_keys, grad_values)


def rest_part(front, kv_full, seq_lengths, offset, full_weights, cotangent_in):
    w_out, w_up, w_down = (full_weights[1], full_weights[2], full_weights[3])
    params = full_weights[5].astype(jnp.float32)
    flat, normal_one, inverse_one, normed_low, padded, mixed = front
    seq_count, block_rows, three_width = mixed.shape
    model_width = three_width // 3
    attended = attention(mixed, kv_full, seq_lengths, offset, None).reshape(
        seq_count * block_rows, model_width
    )
    middle = flat + jnp.dot(attended, w_out, preferred_element_type=jnp.float32)
    second, normal_two, inverse_two = layer_norm(middle, params[2], params[3])
    second_low = second.astype(jnp.bfloat16)
    upper = jnp.dot(second_low, w_up, preferred_element_type=jnp.float32)
    hidden = jnp.square(jnp.maximum(upper, 0.0)).astype(jnp.bfloat16)
    if cotangent_in is None:
        result_rows = middle + jnp.dot(hidden, w_down, preferred_element_type=jnp.float32)
        return result_rows.astype(jnp.bfloat16).reshape(seq_count, block_rows, model_width)
    cotangent = cotangent_in.reshape(seq_count * block_rows, model_width)
    grad_down = jnp.dot(hidden.T, cotangent, preferred_element_type=jnp.float32)
    grad_hidden = jnp.dot(cotangent, w_down.T, preferred_element_type=jnp.float32)
    grad_upper = (2.0 * jnp.maximum(upper, 0.0) * grad_hidden).astype(jnp.bfloat16)
    grad_up = jnp.dot(second_low.T, grad_upper, preferred_element_type=jnp.float32)
    grad_second = jnp.dot(grad_upper, w_up.T, preferred_element_type=jnp.float32)
    grad_middle = cotangent.astype(jnp.float32) + norm_back_flat(
        grad_second, normal_two, inverse_two, params[2]
    )
    grad_middle_low = grad_middle.astype(jnp.bfloat16)
    grad_out = jnp.dot(attended.T, grad_middle_low, preferred_element_type=jnp.float32)
    grad_attended = jnp.dot(grad_middle_low, w_out.T, preferred_element_type=jnp.float32).astype(
        jnp.bfloat16
    )
    grad_attended = grad_attended.reshape(seq_count, block_rows, model_width)
    grad_queries, grad_keys, grad_values = attention(
        mixed, kv_full, seq_lengths, offset, grad_attended
    )
    key_term = jnp.concatenate([grad_keys, grad_values], axis=-1)
    norm_two = (jnp.sum(grad_second * normal_two, axis=0), jnp.sum(grad_second, axis=0))
    return (grad_queries, key_term, grad_middle, grad_out, grad_up, grad_down, norm_two)


def general_body(
    x_short,
    x_long,
    lengths,
    cot_short,
    cot_long,
    w_qkv,
    w_out,
    w_up,
    w_down,
    conv_kernel,
    norm_params,
):
    full_weights = (
        lax.all_gather(w_qkv, ("seq", "batch"), axis=0, tiled=True),
        lax.all_gather(w_out, ("seq", "batch"), axis=0, tiled=True),
        lax.all_gather(w_up, ("seq", "batch"), axis=0, tiled=True),
        lax.all_gather(w_down, ("seq", "batch"), axis=0, tiled=True),
        lax.all_gather(conv_kernel, ("seq", "batch"), axis=1, tiled=True),
        lax.all_gather(norm_params, ("seq", "batch"), axis=1, tiled=True),
    )
    inputs = (x_short, x_long)
    cotangents = (cot_short, cot_long)
    model_width = x_short.shape[2]
    offsets = (lax.axis_index("seq") * x_short.shape[1], lax.axis_index("seq") * x_long.shape[1])
    fronts = front_part(inputs, full_weights)
    kv_fwd = (
        lax.all_gather(fronts[0][5][:, :, model_width:], "seq", axis=1, tiled=True),
        lax.all_gather(fronts[1][5][:, :, model_width:], "seq", axis=1, tiled=True),
    )
    outputs = [
        rest_part(
            fronts[index_part],
            kv_fwd[index_part],
            lengths[index_part],
            offsets[index_part],
            full_weights,
            None,
        )
        for index_part in range(2)
    ]
    back_weights = (
        lax.all_gather(w_qkv, ("seq", "batch"), axis=0, tiled=True),
        lax.all_gather(w_out, ("seq", "batch"), axis=0, tiled=True),
        lax.all_gather(w_up, ("seq", "batch"), axis=0, tiled=True),
        lax.all_gather(w_down, ("seq", "batch"), axis=0, tiled=True),
        lax.all_gather(conv_kernel, ("seq", "batch"), axis=1, tiled=True),
        lax.all_gather(norm_params, ("seq", "batch"), axis=1, tiled=True),
    )
    fronts_back = front_part(inputs, back_weights)
    kv_back = (
        lax.all_gather(fronts_back[0][5][:, :, model_width:], "seq", axis=1, tiled=True),
        lax.all_gather(fronts_back[1][5][:, :, model_width:], "seq", axis=1, tiled=True),
    )
    partials = [
        rest_part(
            fronts_back[index_part],
            kv_back[index_part],
            lengths[index_part],
            offsets[index_part],
            back_weights,
            cotangents[index_part],
        )
        for index_part in range(2)
    ]
    kv_grads = (
        lax.psum_scatter(
            partials[0][1].astype(jnp.bfloat16), "seq", scatter_dimension=1, tiled=True
        ).astype(jnp.float32),
        lax.psum_scatter(
            partials[1][1].astype(jnp.bfloat16), "seq", scatter_dimension=1, tiled=True
        ).astype(jnp.float32),
    )
    grad_mixed = [
        jnp.concatenate([partials[index_part][0], kv_grads[index_part]], axis=-1)
        for index_part in range(2)
    ]
    received = (
        from_behind(grad_mixed[0][:, :2].astype(jnp.bfloat16), "seq", -1).astype(jnp.float32),
        from_behind(grad_mixed[1][:, :2].astype(jnp.bfloat16), "seq", -1).astype(jnp.float32),
    )
    kernel = back_weights[4].astype(jnp.float32)
    params = back_weights[5].astype(jnp.float32)
    w_qkv_full = back_weights[0]
    grad_qkv = jnp.zeros(w_qkv_full.shape, jnp.float32)
    grad_kernel = jnp.zeros(kernel.shape, jnp.float32)
    grad_norm = jnp.zeros((4, model_width), jnp.float32)
    grad_out = partials[0][3] + partials[1][3]
    grad_up = partials[0][4] + partials[1][4]
    grad_down = partials[0][5] + partials[1][5]
    input_grads = []
    for index_part in range(2):
        flat, normal_one, inverse_one, normed_low, padded, mixed = fronts_back[index_part]
        seq_count, block_rows, three_width = mixed.shape
        mixed_grad = grad_mixed[index_part]
        extended = jnp.concatenate([mixed_grad, received[index_part]], axis=1)
        grad_projected = (
            kernel[0] * extended[:, :block_rows]
            + kernel[1] * extended[:, 1 : block_rows + 1]
            + kernel[2] * extended[:, 2:]
        ).astype(jnp.bfloat16)
        grad_kernel = grad_kernel + jnp.stack(
            [
                jnp.sum(mixed_grad * padded[:, 2:], axis=(0, 1)),
                jnp.sum(mixed_grad * padded[:, 1 : block_rows + 1], axis=(0, 1)),
                jnp.sum(mixed_grad * padded[:, :block_rows], axis=(0, 1)),
            ]
        )
        grad_flat = grad_projected.reshape(seq_count * block_rows, three_width)
        grad_qkv = grad_qkv + jnp.dot(normed_low.T, grad_flat, preferred_element_type=jnp.float32)
        grad_normed = jnp.dot(grad_flat, w_qkv_full.T, preferred_element_type=jnp.float32)
        grad_input = partials[index_part][2] + norm_back_flat(
            grad_normed, normal_one, inverse_one, params[0]
        )
        input_grads.append(grad_input.reshape(seq_count, block_rows, model_width))
        norm_two = partials[index_part][6]
        grad_norm = grad_norm + jnp.stack(
            [
                jnp.sum(grad_normed * normal_one, axis=0),
                jnp.sum(grad_normed, axis=0),
                norm_two[0],
                norm_two[1],
            ]
        )
    summed = (
        lax.psum_scatter(grad_qkv, ("seq", "batch"), scatter_dimension=0, tiled=True),
        lax.psum_scatter(grad_out, ("seq", "batch"), scatter_dimension=0, tiled=True),
        lax.psum_scatter(grad_up, ("seq", "batch"), scatter_dimension=0, tiled=True),
        lax.psum_scatter(grad_down, ("seq", "batch"), scatter_dimension=0, tiled=True),
        lax.psum_scatter(grad_kernel, ("seq", "batch"), scatter_dimension=1, tiled=True),
        lax.psum_scatter(grad_norm, ("seq", "batch"), scatter_dimension=1, tiled=True),
    )
    return (
        outputs[0],
        outputs[1],
        input_grads[0],
        input_grads[1],
        summed[0],
        summed[1],
        summed[2],
        summed[3],
        summed[4],
        summed[5],
    )


def solution(mesh):
    split = mesh.shape["seq"] == 8
    return jax.shard_map(
        split_body if split else general_body,
        mesh=mesh,
        in_specs=(
            P("batch", "seq", None),
            P("batch", "seq", None),
            P(None, "batch"),
            P("batch", "seq", None),
            P("batch", "seq", None),
            P(("seq", "batch"), None),
            P(("seq", "batch"), None),
            P(("seq", "batch"), None),
            P(("seq", "batch"), None),
            P(None, ("seq", "batch")),
            P(None, ("seq", "batch")),
        ),
        out_specs=(
            P("batch", "seq", None),
            P("batch", "seq", None),
            P("batch", "seq", None),
            P("batch", "seq", None),
            P(("seq", "batch"), None),
            P(("seq", "batch"), None),
            P(("seq", "batch"), None),
            P(("seq", "batch"), None),
            P(None, ("seq", "batch")),
            P(None, ("seq", "batch")),
        ),
        check_vma=False,
    )
```

```python
import functools

import jax
import jax.numpy as jnp
from jax import lax
from jax.experimental import pallas as pl
from jax.experimental.pallas import tpu as pltpu
from jax.sharding import PartitionSpec as P

EPS = 1e-05
NEG_FILL = -1e30
HEAD_DIM = 64
LANES = 128
TRIPLE = 3 * LANES
TILE = 256
PAD = 16
MESH = pl.DeviceIdType.MESH
F32 = jnp.float32
BF16 = jnp.bfloat16
DMA = pltpu.SemaphoreType.DMA


def dot_nn(left, right):
    return lax.dot_general(left, right, (((1,), (0,)), ((), ())), preferred_element_type=F32)


def dot_nt(left, right):
    return lax.dot_general(left, right, (((1,), (1,)), ((), ())), preferred_element_type=F32)


def dot_tn(left, right):
    return lax.dot_general(left, right, (((0,), (0,)), ((), ())), preferred_element_type=F32)


def params_of(limit=60, **more):
    return pltpu.CompilerParams(vmem_limit_bytes=limit * 2**20, **more)


def vmem():
    return pl.BlockSpec(memory_space=pltpu.VMEM)


def smem():
    return pl.BlockSpec(memory_space=pltpu.SMEM)


def hbm():
    return pl.BlockSpec(memory_space=pl.ANY)


def normalise(values):
    average = jnp.mean(values, axis=-1, keepdims=True)
    centred = values - average
    inverse = lax.rsqrt(jnp.mean(centred * centred, axis=-1, keepdims=True) + EPS)
    return centred * inverse, inverse


def norm_back(grad, normal, inverse, gain):
    scaled_grad = grad * gain
    first_mean = jnp.mean(scaled_grad, axis=-1, keepdims=True)
    second_mean = jnp.mean(scaled_grad * normal, axis=-1, keepdims=True)
    return inverse * (scaled_grad - first_mean - normal * second_mean)


def shifted(window, by):
    return pltpu.roll(window, by % window.shape[0], 0)


def iota(shape, axis):
    return lax.broadcasted_iota(jnp.int32, shape, axis)


def times(index, size):
    return pl.ds(pl.multiple_of(index * size, size), size)


def position():
    index, batch = lax.axis_index("seq"), lax.axis_index("batch")
    return index // 2, index % 2, batch // 2, batch % 2


def at(z, core, y, x):
    return (z * 2 + core, y * 2 + x)


def remote(src, dst, send, recv, device):
    return pltpu.make_async_remote_copy(
        src_ref=src, dst_ref=dst, send_sem=send, recv_sem=recv, device_id=device, device_id_type=MESH
    )


def greet(others):
    barrier = pltpu.get_barrier_semaphore()
    for other in others:
        pl.semaphore_signal(barrier, inc=1, device_id=other, device_id_type=MESH)
    pl.semaphore_wait(barrier, len(others))


def whole_line():
    z, core, y, x = position()
    line = [at(lax.rem(z + step, 4), (core + turn) % 2, y, x) for turn in (0, 1) for step in (0, 1, 2, 3)]
    return line[1:]


def greet_all():
    z, core, y, x = position()
    greet(whole_line() + [at(z, core, 1 - y, x), at(z, core, y, 1 - x)])


def roles():
    z = lax.axis_index("seq") // 2
    half = z // 2
    near = jnp.where(half == 0, z, 3 - z)
    partner_z = jnp.where(half == 0, 1 - z, 5 - z)
    return half, near, partner_z, 2 - half


def z_of(half, place):
    return jnp.where(half == 0, place, 3 - place)


def long_source(seq, pair):
    near = 1 if pair % 3 == 2 else 0
    z = near if seq == 0 else 3 - near
    return z * 2 + pair // 3, 0 if near else pair % 3


def short_source(seq, pair):
    return (1 if seq == 0 else 2) * 2 + pair // 3, pair % 3


class Copies:
    def __init__(self, sems):
        self.sems, self.count, self.open = sems, 0, []

    def start(self, src, dst):
        copy = pltpu.make_async_copy(src, dst, self.sems.at[self.count])
        self.count += 1
        copy.start()
        self.open.append(copy)
        return copy

    def finish(self):
        for copy in self.open:
            copy.wait()
        self.open = []


class RowGather:
    def __init__(self, x_ref, o_ref, own_sem, send, recv, sib_send, sib_recv, inner_only):
        self.x_ref, self.o_ref, self.inner_only = x_ref, o_ref, inner_only
        self.own_sem, self.send, self.recv, self.sib_send, self.sib_recv = own_sem, send, recv, sib_send, sib_recv
        self.rows = x_ref.shape[1]
        self.z, self.core, self.y, self.x = position()
        self.half, self.near, self.partner_z, far_z = roles()
        self.sibling = at(self.z, 1 - self.core, self.y, self.x)
        self.partner = at(self.partner_z, self.core, self.y, self.x)
        place = self.block(self.z, self.core)
        mine, other = self.x_ref.at[self.half], self.x_ref.at[1 - self.half]
        self.to_partner = remote(mine, place, send.at[0], recv.at[self.near], self.partner)
        self.to_far = remote(other, place, send.at[1], recv.at[3 - self.near], at(far_z, self.core, self.y, self.x))
        self.to_sibling = remote(mine, place, sib_send.at[0], sib_recv.at[self.near], self.sibling)
        self.own = pltpu.make_async_copy(mine, place, own_sem)

    def block(self, z, core):
        return self.o_ref.at[times(z * 2 + core, self.rows)]

    def at_inner(self, act):
        if self.inner_only:
            pl.when(self.near == 1)(act)
        else:
            act()

    def start(self):
        if self.inner_only:
            pl.when(self.near == 0)(self.to_partner.start)
        else:
            self.to_partner.start()
        pl.when(self.near == 1)(self.to_far.start)

        def inside():
            self.to_sibling.start()
            self.own.start()

        self.at_inner(inside)

    def start_far(self):
        @pl.when(self.near == 0)
        def _():
            self.to_partner.wait_send()
            self.to_far.start()

    def moves(self, slot):
        place = (1 - self.near, 2, 3)[slot]
        block = self.block(z_of(self.half, place), self.core)
        arrival = remote(block, block, self.send.at[0], self.recv.at[place], self.partner)
        onward = remote(block, block, self.send.at[1 + slot], self.recv.at[place], self.partner)
        across = remote(block, block, self.sib_send.at[1 + slot], self.sib_recv.at[place], self.sibling)
        return arrival, onward, across

    def step(self, slot):
        arrival, onward, across = self.moves(slot)

        def inside():
            arrival.wait_recv()
            if slot and not self.inner_only:
                pl.when(self.near == 1)(onward.start)
            across.start()

        self.at_inner(inside)

    def whole(self, place):
        where = (self.near, 1 - self.near, 2, 3)[place]
        block = self.block(z_of(self.half, where), 1 - self.core)

        def inside():
            remote(block, block, self.sib_send.at[0], self.sib_recv.at[where], self.sibling).wait_recv()
            if place == 0:
                self.own.wait()

        self.at_inner(inside)

    def chip_rows(self, place):
        return z_of(self.half, (self.near, 1 - self.near, 2, 3)[place])

    def finish(self):
        if not self.inner_only:
            pl.when(self.near == 1)(self.to_partner.wait_send)
        self.to_far.wait_send()

        def inside():
            self.to_sibling.wait_send()
            for slot in range(3):
                _, onward, across = self.moves(slot)
                across.wait_send()
                if slot and not self.inner_only:
                    pl.when(self.near == 1)(onward.wait_send)

        self.at_inner(inside)


class ShardGather:
    def __init__(self, shard, full, own_sem, send, recv, halves=False):
        self.shard, self.full, self.own_sem, self.send_sem, self.recv_sem = shard, full, own_sem, send, recv
        self.z, self.core, self.y, self.x = position()
        self.halves = halves
        self.sent = []

    def go(self, src, dst, slot, device):
        copy = remote(src, dst, self.send_sem.at[slot], self.recv_sem.at[slot], device)
        copy.start()
        self.sent.append(copy)

    def arrived(self, dst, slot):
        remote(dst, dst, self.send_sem.at[0], self.recv_sem.at[slot], at(self.z, self.core, self.y, self.x)).wait_recv()

    def start(self):
        z, core, y, x = self.z, self.core, self.y, self.x
        mine = self.full.at[z, core, y, x]
        for step in (1, 2, 3):
            target = lax.rem(z + step, 4)
            self.go(self.shard, mine, step, at(target, core, y, x))
        self.own = pltpu.make_async_copy(self.shard, mine, self.own_sem)
        self.own.start()

    def part(self, core, zs, ys, xs, reader):
        ref = self.full.at[zs, core, ys, xs]
        return self.full.at[zs, core, ys, xs, reader] if self.halves else ref

    def across(self, zs, ys, xs, slot):
        ref = self.part(self.core, zs, ys, xs, 1 - self.core)
        self.go(ref, ref, slot, at(self.z, 1 - self.core, self.y, self.x))

    def over(self):
        z, core, y, x = self.z, self.core, self.y, self.x
        for step in (1, 2, 3):
            self.arrived(self.full.at[lax.rem(z + 4 - step, 4), core, y, x], step)
        self.own.wait()
        first, second = pl.ds(0, 2), pl.ds(2, 2)
        ref = self.full.at[first, core, y, x]
        self.go(ref, ref, 4, at(z, core, y, 1 - x))
        ref = self.full.at[second, core, y, x]
        self.go(ref, ref, 5, at(z, core, 1 - y, x))
        self.across(pl.ds(0, 4), y, x, 8)

    def turn(self):
        z, core, y, x = self.z, self.core, self.y, self.x
        first, second = pl.ds(0, 2), pl.ds(2, 2)
        self.arrived(self.full.at[first, core, y, 1 - x], 4)
        ref = self.full.at[first, core, y]
        self.go(ref, ref, 6, at(z, core, 1 - y, x))
        self.across(first, y, 1 - x, 9)
        self.arrived(self.full.at[second, core, 1 - y, x], 5)
        ref = self.full.at[second, core, :, x]
        self.go(ref, ref, 7, at(z, core, y, 1 - x))
        self.across(second, 1 - y, x, 10)

    def last(self):
        core, y, x = self.core, self.y, self.x
        first, second = pl.ds(0, 2), pl.ds(2, 2)
        self.arrived(self.full.at[first, core, 1 - y], 6)
        self.across(first, 1 - y, pl.ds(0, 2), 11)
        self.arrived(self.full.at[second, core, :, 1 - x], 7)
        self.across(second, pl.ds(0, 2), 1 - x, 12)

    def finish(self):
        y, x, core, other = self.y, self.x, self.core, 1 - self.core
        first, second, both = pl.ds(0, 2), pl.ds(2, 2), pl.ds(0, 2)
        parts = (
            (pl.ds(0, 4), y, x), (first, y, 1 - x), (second, 1 - y, x), (first, 1 - y, both), (second, both, 1 - x),
        )
        for slot, (zs, ys, xs) in enumerate(parts):
            self.arrived(self.part(other, zs, ys, xs, core), 8 + slot)

    def sends_done(self):
        for copy in self.sent:
            copy.wait_send()


def add_into(total, part):
    total[...] = (total[...].astype(F32) + part[...].astype(F32)).astype(total.dtype)


class CoreSum:
    def __init__(self, grad, sib, out, send, recv, save, hop=None):
        self.grad, self.sib, self.out, self.save = grad, sib, out, save
        self.z, self.core, self.y, self.x = position()
        z, core, y, x = position()
        self.copy = remote(grad.at[:, 1 - core], sib, send.at[0], recv.at[0], at(z, 1 - core, y, x))
        self.hop = hop
        first, second = pl.ds(0, 2), pl.ds(2, 2)
        if hop is not None:
            self.hops = (
                remote(sib.at[first, :, 1 - x], hop.at[0], send.at[1], recv.at[1], at(z, core, y, 1 - x)),
                remote(sib.at[second, 1 - y], hop.at[1], send.at[2], recv.at[2], at(z, core, 1 - y, x)),
            )

    def start(self):
        self.copy.start()

    def keep(self, *moves):
        self.kept = [pltpu.make_async_copy(src, dst, self.save.at[i]) for i, (src, dst) in enumerate(moves)]
        for copy in self.kept:
            copy.start()

    def add(self):
        self.copy.wait_recv()

        @pl.loop(0, 4)
        def _(zz):
            for ys in range(2):
                for xs in range(2):
                    add_into(self.sib.at[zz, ys, xs], self.grad.at[zz, self.core, ys, xs])

        if self.hop is None:
            self.keep((self.sib, self.out))
        else:
            for copy in self.hops:
                copy.start()

    def add_hop(self):
        x, y = self.x, self.y
        self.hops[0].wait_recv()
        for zz in range(2):
            for ys in range(2):
                add_into(self.sib.at[zz, ys, x], self.hop.at[0, zz, ys])
        self.hops[1].wait_recv()
        for zz in range(2):
            for xs in range(2):
                add_into(self.sib.at[2 + zz, y, xs], self.hop.at[1, zz, xs])
        self.keep(
            (self.sib.at[pl.ds(0, 2), :, x], self.out.at[0]),
            (self.sib.at[pl.ds(2, 2), y], self.out.at[1]),
        )

    def finish(self):
        self.copy.wait_send()
        for copy in self.kept:
            copy.wait()
        if self.hop is not None:
            for copy in self.hops:
                copy.wait_send()


class ShardSum:
    def __init__(self, grad, out, bufs, own_sem, send, recv, begun=False):
        self.grad, self.out, self.begun = grad, out, begun
        self.near_x, self.near_y, self.two, self.line = bufs[:4]
        self.one = None if begun else bufs[4]
        self.own_sem, self.send_sem, self.recv_sem = own_sem, send, recv
        self.z, self.core, self.y, self.x = position()
        self.sent = []
        first, second = pl.ds(0, 2), pl.ds(2, 2)
        self.loads = (
            pltpu.make_async_copy(grad.at[0] if begun else grad.at[first, :, self.x], self.near_x, own_sem.at[0]),
            pltpu.make_async_copy(grad.at[1] if begun else grad.at[second, self.y], self.near_y, own_sem.at[1]),
        )

    def copy(self, src, dst, slot, device):
        return remote(src, dst, self.send_sem.at[slot], self.recv_sem.at[slot], device)

    def go(self, src, dst, slot, device):
        copy = self.copy(src, dst, slot, device)
        copy.start()
        self.sent.append(copy)

    def arrived(self, dst, slot):
        remote(dst, dst, self.send_sem.at[0], self.recv_sem.at[slot], at(self.z, self.core, self.y, self.x)).wait_recv()

    def moves(self):
        z, core, y, x = self.z, self.core, self.y, self.x
        first, second = pl.ds(0, 2), pl.ds(2, 2)
        return ([] if self.begun else [
            self.copy(self.grad.at[first, :, 1 - x], self.one.at[0], 2, at(z, core, y, 1 - x)),
            self.copy(self.grad.at[second, 1 - y], self.one.at[1], 3, at(z, core, 1 - y, x)),
        ]) + [
            self.copy(self.near_x.at[:, 1 - y], self.two.at[0], 4, at(z, core, 1 - y, x)),
            self.copy(self.near_y.at[:, 1 - x], self.two.at[1], 5, at(z, core, y, 1 - x)),
        ]

    def to_line(self, step):
        z, core, y, x = self.z, self.core, self.y, self.x
        target = lax.rem(z + step, 4)
        device = at(target, core, y, x)
        low = self.copy(self.near_x.at[lax.rem(target, 2), y], self.line.at[step - 1], 5 + step, device)
        high = self.copy(self.near_y.at[lax.rem(target, 2), x], self.line.at[step - 1], 5 + step, device)
        return target, low, high

    def start(self):
        for copy in self.moves()[:-2]:
            copy.start()
        for copy in self.loads:
            copy.start()

    def turn(self):
        moves = self.moves()
        for side, near in enumerate((self.near_x, self.near_y)):
            self.loads[side].wait()
            if not self.begun:
                self.arrived(self.one.at[side], 2 + side)
                for zz in range(2):
                    for other in range(2):
                        add_into(near.at[zz, other], self.one.at[side, zz, other])
            moves[side - 2].start()

    def last(self):
        y, x = self.y, self.x
        self.arrived(self.two.at[0], 4)
        for zz in range(2):
            add_into(self.near_x.at[zz, y], self.two.at[0, zz])
        self.arrived(self.two.at[1], 5)
        for zz in range(2):
            add_into(self.near_y.at[zz, x], self.two.at[1, zz])
        for step in (1, 2, 3):
            target, low, high = self.to_line(step)
            pl.when(target < 2)(low.start)
            pl.when(target >= 2)(high.start)

    def finish(self):
        z, y, x = self.z, self.y, self.x
        low = self.near_x[lax.rem(z, 2), y].astype(F32)
        high = self.near_y[lax.rem(z, 2), x].astype(F32)
        total = jnp.where(z < 2, low, high)
        for step in (1, 2, 3):
            self.arrived(self.line.at[step - 1], 5 + step)
            total = total + self.line[step - 1].astype(F32)
        self.out[...] = total
        for copy in self.moves():
            copy.wait_send()
        for step in (1, 2, 3):
            target, low, high = self.to_line(step)
            pl.when(target < 2)(low.wait_send)
            pl.when(target >= 2)(high.wait_send)

    @staticmethod
    def buffers(grad, begun=False):
        tail, kind = grad.shape[3:], grad.dtype
        shapes = [(2, 2), (2, 2), (2, 2), (3,)] + ([] if begun else [(2, 2, 2)])
        return [pltpu.VMEM(shape + tail, kind) for shape in shapes]


class GroupSum:
    def __init__(self, bufs, send, recv):
        self.tot, self.one, self.two, self.line = bufs
        self.send_sem, self.recv_sem = send, recv
        self.z, self.core, self.y, self.x = position()
        self.sent = []

    copy = ShardSum.copy
    go = ShardSum.go
    arrived = ShardSum.arrived

    def start(self, total, columns):
        z, core, y, x = self.z, self.core, self.y, self.x
        rows = self.tot.shape[4]

        @pl.loop(0, 4)
        def _(zz):
            for cc in range(2):
                for yy in range(2):
                    for xx in range(2):
                        first = pl.multiple_of(zz * 8 * rows, 8) + ((cc * 2 + yy) * 2 + xx) * rows
                        part = total[pl.ds(pl.multiple_of(first, 8), rows), columns]
                        self.tot[zz, cc, yy, xx] = part.astype(BF16)

        self.go(self.tot.at[pl.ds(0, 2), :, :, 1 - x], self.one.at[0], 0, at(z, core, y, 1 - x))
        self.go(self.tot.at[pl.ds(2, 2), :, 1 - y], self.one.at[1], 1, at(z, core, 1 - y, x))

    def turn(self):
        z, core, y, x = self.z, self.core, self.y, self.x
        self.arrived(self.one.at[0], 0)

        @pl.loop(0, 2)
        def _(zz):
            for cc in range(2):
                for ys in range(2):
                    add_into(self.tot.at[zz, cc, ys, x], self.one.at[0, zz, cc, ys])

        self.go(self.tot.at[pl.ds(0, 2), :, 1 - y, x], self.two.at[0], 2, at(z, core, 1 - y, x))
        self.arrived(self.one.at[1], 1)

        @pl.loop(0, 2)
        def _(zz):
            for cc in range(2):
                for xs in range(2):
                    add_into(self.tot.at[2 + zz, cc, y, xs], self.one.at[1, zz, cc, xs])

        self.go(self.tot.at[pl.ds(2, 2), :, y, 1 - x], self.two.at[1], 3, at(z, core, y, 1 - x))

    def last(self):
        z, core, y, x = self.z, self.core, self.y, self.x
        for side in (0, 1):
            self.arrived(self.two.at[side], 2 + side)

            @pl.loop(0, 2)
            def _(zz, side=side):
                for cc in range(2):
                    add_into(self.tot.at[2 * side + zz, cc, y, x], self.two.at[side, zz, cc])

        mine = z * 2 + core
        for step in range(1, 8):
            target = lax.rem(mine + step, 8)
            tz, tc = target // 2, target % 2
            self.go(self.tot.at[tz, tc, y, x], self.line.at[step - 1], 3 + step, at(tz, tc, y, x))

    def finish(self):
        for step in range(1, 8):
            self.arrived(self.line.at[step - 1], 3 + step)
        for copy in self.sent:
            copy.wait_send()

    def term(self, source):
        z, core, y, x = self.z, self.core, self.y, self.x
        back = lax.rem(z * 2 + core - source + 8 + 7, 8)
        own = self.tot[z, core, y, x].astype(F32)
        return jnp.where(back == 7, own, self.line[jnp.minimum(back, 6)].astype(F32))

    @staticmethod
    def buffers(rows, columns):
        return [
            pltpu.VMEM((4, 2, 2, 2, rows, columns), BF16),
            pltpu.VMEM((2, 2, 2, 2, rows, columns), BF16),
            pltpu.VMEM((2, 2, 2, rows, columns), BF16),
            pltpu.VMEM((7, rows, columns), BF16),
        ]


def join_groups(first, second, out):
    width = out.shape[1] // 3
    for side in range(2):
        early = None
        for z in range(4):
            term = first.term(z * 2 + side)
            early = term if early is None else early + term
        outer = second.term(side) + second.term(6 + side)
        inner = second.term(2 + side) + second.term(4 + side)
        pairs = (early[:, :TRIPLE], early[:, TRIPLE:] + outer, inner)
        for j, pair in enumerate(pairs):
            for kind in range(3):
                target = kind * width + (3 * side + j) * LANES
                out[:, target : target + LANES] = pair[:, kind * LANES : (kind + 1) * LANES]


class SmallSum:
    def __init__(self, bufs, out, send, recv):
        self.norms, self.swap, self.acc, self.got, self.line = bufs
        self.out, self.send_sem, self.recv_sem = out, send, recv
        self.z, self.core, self.y, self.x = position()
        self.sent = []
        self.cut = self.norms.shape[2]

    copy = ShardSum.copy
    go = ShardSum.go
    arrived = ShardSum.arrived

    def start(self, kernel_grad, norm_grad):
        z, core, y, x = self.z, self.core, self.y, self.x
        cut = self.cut
        self.norms[0] = norm_grad[:, :cut]
        self.norms[1] = norm_grad[:, cut:]
        self.acc[0, :, : kernel_grad.shape[1]] = kernel_grad
        self.go(self.norms.at[1 - core], self.swap, 0, at(z, 1 - core, y, x))

    def over(self):
        z, core, y, x = self.z, self.core, self.y, self.x
        self.arrived(self.swap, 0)
        self.acc[0, :, self.acc.shape[2] - self.cut :] = self.norms[core] + self.swap[...]
        self.go(self.acc.at[0], self.got.at[0], 1, at(z, core, y, 1 - x))

    def turn(self):
        z, core, y, x = self.z, self.core, self.y, self.x
        self.arrived(self.got.at[0], 1)
        self.acc[1] = self.acc[0] + self.got[0]
        self.go(self.acc.at[1], self.got.at[1], 2, at(z, core, 1 - y, x))

    def last(self):
        z, core, y, x = self.z, self.core, self.y, self.x
        self.arrived(self.got.at[1], 2)
        self.acc[2] = self.acc[1] + self.got[1]
        for step in (1, 2, 3):
            self.go(self.acc.at[2], self.line.at[step - 1], 2 + step, at(lax.rem(z + step, 4), core, y, x))

    def swap_back(self):
        z, core, y, x = self.z, self.core, self.y, self.x
        for step in (1, 2, 3):
            self.arrived(self.line.at[step - 1], 2 + step)
        total = None
        for source in range(4):
            back = lax.rem(z - source + 4, 4)
            term = jnp.where(back == 0, self.acc[2], self.line[jnp.maximum(back - 1, 0)])
            total = term if total is None else total + term
        self.out[core] = total
        self.go(self.out.at[core], self.out.at[core], 6, at(z, 1 - core, y, x))

    def finish(self):
        self.arrived(self.out.at[1 - self.core], 6)
        for copy in self.sent:
            copy.wait_send()

    @staticmethod
    def buffers(columns, norm_columns):
        wide = columns + norm_columns
        return [
            pltpu.VMEM((2, 8, norm_columns), F32),
            pltpu.VMEM((8, norm_columns), F32),
            pltpu.VMEM((3, 8, wide), F32),
            pltpu.VMEM((2, 8, wide), F32),
            pltpu.VMEM((3, 8, wide), F32),
        ]


def causal_mask():
    return iota((TILE, TILE), 0) <= iota((TILE, TILE), 1)


def place_small(smalls, kernel_out, norm_out, core, part, cut):
    wide, width = kernel_out.shape[1], norm_out.shape[1]
    column = iota((LANES, wide), 1)
    block, lane = column // LANES, column % LANES
    source = (block % 3) * width + (core * 3 + block // 3) * LANES + lane - iota((LANES, wide), 0)
    norm_source = iota((LANES, width), 1) - iota((LANES, width), 0)
    kernel_out[...] = jnp.zeros_like(kernel_out)
    norm_out[...] = jnp.zeros_like(norm_out)

    @pl.loop(0, smalls.shape[0])
    def _(device):
        low = smalls[device].astype(BF16)
        kernel_out[...] += dot_nn(low, jnp.where(source == device * part, 1.0, 0.0).astype(BF16))
        norm_out[...] += dot_nn(low, jnp.where(norm_source == device * cut, 1.0, 0.0).astype(BF16))

    norm_out[0:4] = norm_out[3:7]


def attend(query_ref, key_ref, value_t, lse, out_t, head, block):
    rows, past = slice(block * TILE, (block + 1) * TILE), slice(0, block * TILE)
    query = query_ref[head, rows]
    diagonal = jnp.where(causal_mask(), dot_nt(key_ref[head, rows], query), NEG_FILL)
    top = jnp.max(diagonal, axis=0, keepdims=True)
    if block:
        before = dot_nt(key_ref[head, past], query)
        top = jnp.maximum(top, jnp.max(before, axis=0, keepdims=True))
        exp_before = jnp.exp(before - top)
    exp_diagonal = jnp.exp(diagonal - top)
    norm = jnp.sum(exp_diagonal, axis=0, keepdims=True)
    if block:
        norm = norm + jnp.sum(exp_before, axis=0, keepdims=True)
    lse[head, :, rows] = top + jnp.log(norm)
    inverse = 1.0 / norm
    result = dot_nn(value_t[head, :, rows], (exp_diagonal * inverse).astype(BF16))
    if block:
        result = result + dot_nn(value_t[head, :, past], (exp_before * inverse).astype(BF16))
    out_t[head, :, rows] = result


def convolve(proj, taps, slot, local, start, length, query_ref, key_ref, value_ref, key_t, value_t):
    window = proj[slot, pl.ds(pl.multiple_of(start, PAD), TILE + PAD)].astype(F32)
    columns = times(local, TRIPLE)
    mixed = (
        taps[0:1, columns] * window[PAD:]
        + taps[1:2, columns] * shifted(window, 1)[PAD:]
        + taps[2:3, columns] * shifted(window, 2)[PAD:]
    ).astype(BF16).astype(F32)
    query, key, value = mixed[:, 0:LANES] * (HEAD_DIM**-0.5), mixed[:, LANES : 2 * LANES], mixed[:, 2 * LANES :]
    rows = pl.ds(pl.multiple_of(start, TILE), TILE)
    lanes = iota((TILE, LANES), 1)
    low_half = lanes < HEAD_DIM
    bias = jnp.where(start + iota((TILE, LANES), 0) < length, 0.0, NEG_FILL)
    at_zero, at_half = lanes == 0, lanes == HEAD_DIM
    query_ref[2 * slot, rows] = jnp.where(low_half, query, jnp.where(at_half, 1.0, 0.0)).astype(BF16)
    query_ref[2 * slot + 1, rows] = jnp.where(low_half, jnp.where(at_zero, 1.0, 0.0), query).astype(BF16)
    key_ref[2 * slot, rows] = jnp.where(low_half, key, jnp.where(at_half, bias, 0.0)).astype(BF16)
    key_ref[2 * slot + 1, rows] = jnp.where(low_half, jnp.where(at_zero, bias, 0.0), key).astype(BF16)
    value_ref[slot, rows] = value.astype(BF16)
    turned_key, turned_value = key.T.astype(BF16), value.T.astype(BF16)
    for head in range(2):
        part = slice(head * HEAD_DIM, (head + 1) * HEAD_DIM)
        key_t[2 * slot + head, :, rows] = turned_key[part]
        value_t[2 * slot + head, :, rows] = turned_value[part]


def first_kernel(
    lens, xs_ref, xl_ref, qkv_ref, conv_ref, norm_ref, out_s, up_s, down_s,
    att, full_out, full_up, full_down, xs_o, xl_o, wq_o, taps_o, norms_o,
    ql_o, kl_o, vl_o, ktl_o, lsel_o, pl_o, ol_o, qs_o, ks_o, vs_o, kts_o, lses_o, ps_o, os_o,
    xs, xl, small, smalls, shard, wq_parts, wq, taps, norms,
    ql, kl, vl, ktl, lsel, proj_l, ol, qs, ks, vs, kts, lses, proj_s, os,
    vtl, vts, otl, ots,
    own_sem, send, recv, sib_send, sib_recv, shard_own, shard_send, shard_recv,
    att_send_l, att_recv_l, att_send_s, att_recv_s, att_own_l, att_own_s, save_sem,
):
    z, core, y, x = position()
    half, near, _, _ = roles()
    index = z * 2 + core
    pairs_long = 2 - near
    own_short, own_long = xs_ref.shape[1], xl_ref.shape[1]
    long_rows, short_rows = xl.shape[0], xs.shape[0]
    part, cut = conv_ref.shape[1], norm_ref.shape[1]
    length_short = jnp.where(half == 0, lens[0, 0], lens[0, 1])
    length_long = jnp.where(half == 0, lens[1, 0], lens[1, 1])

    small[...] = jnp.zeros_like(small)
    small[0:3, 0:part] = conv_ref[...].astype(F32)
    small[3:7, 0:cut] = norm_ref[...].astype(F32)
    width = wq.shape[0]
    for side in range(2):
        for j in range(3):
            for kind in range(3):
                source = kind * width + (3 * side + j) * LANES
                target = (3 * j + kind) * LANES
                shard[side, :, target : target + LANES] = qkv_ref[:, source : source + LANES]
    greet_all()
    rows_short = RowGather(
        xs_ref, xs, own_sem.at[0], send.at[0], recv.at[0], sib_send.at[0], sib_recv.at[0], True
    )
    rows_long = RowGather(
        xl_ref, xl, own_sem.at[1], send.at[1], recv.at[1], sib_send.at[1], sib_recv.at[1], False
    )
    weights = [
        ShardGather(a, f, shard_own.at[i], shard_send.at[i], shard_recv.at[i], halves=i == 1)
        for i, (a, f) in enumerate(
            ((small, smalls), (shard, wq_parts), (out_s, full_out), (up_s, full_up), (down_s, full_down))
        )
    ]
    small_w, qkv_w, out_w, up_w, down_w = weights

    def place():
        place_small(smalls.reshape(32, 8, LANES), taps, norms, core, part, cut)

    def join_weights():
        pieces = wq_parts.shape[5]
        for zz in range(4):
            for cc in range(2):
                for yy in range(2):
                    first = ((zz * 2 + cc) * 2 + yy) * 2 * pieces
                    both = jnp.concatenate([wq_parts[zz, cc, yy, xx, core].astype(F32) for xx in range(2)], axis=0)
                    wq[first : first + 2 * pieces] = both.astype(BF16)

    def project(x_ref, proj, start, size, slots, first_pair):
        normal, _ = normalise(x_ref[pl.ds(pl.multiple_of(start, size), size)].astype(F32))
        low = (normal * norms[0:1] + norms[1:2]).astype(BF16)

        @pl.loop(0, slots)
        def _(slot):
            result = dot_nn(low, wq[:, times(slot + first_pair, TRIPLE)])
            proj[slot, pl.ds(pl.multiple_of(PAD + start, PAD), size)] = result.astype(BF16)

    def project_long(place):
        @pl.loop(0, 2)
        def _(side):
            project(xl, proj_l, rows_long.chip_rows(place) * 2 * own_long + side * TILE, TILE, pairs_long, 2 * near)

    def project_short(place):
        @pl.when(near == 1)
        def _():
            project(xs, proj_s, rows_short.chip_rows(place) * 2 * own_short, TILE, 3, 0)

    def conv_short():
        @pl.when(near == 1)
        def _():
            @pl.loop(0, 3)
            def _(slot):
                @pl.loop(0, short_rows // TILE)
                def _(step):
                    convolve(proj_s, taps, slot, slot, step * TILE, length_short, qs, ks, vs, kts, vts)

    def conv_long():
        @pl.loop(0, pairs_long)
        def _(slot):
            @pl.loop(0, long_rows // TILE)
            def _(step):
                convolve(proj_l, taps, slot, slot + 2 * near, step * TILE, length_long, ql, kl, vl, ktl, vtl)

    saves = Copies(save_sem)

    def save(*moves):
        for source, target in moves:
            saves.start(source, target)

    def save_long():
        save((xl, xl_o), (wq, wq_o), (taps, taps_o), (norms, norms_o))
        save((ql, ql_o), (kl, kl_o), (vl, vl_o), (ktl, ktl_o), (proj_l, pl_o))

    def save_short():
        save((xs, xs_o), (qs, qs_o), (ks, ks_o), (vs, vs_o))
        save((kts, kts_o), (proj_s, ps_o), (lses, lses_o), (os, os_o))

    def save_last():
        save((lsel, lsel_o), (ol, ol_o))

    def to_owner(o_ref, slot, first, rows, owner, row_in_owner, pair, send_sem, recv_sem, own_sem):
        source = o_ref.at[slot, pl.ds(first, rows)]
        target = att.at[
            pl.ds(pl.multiple_of(row_in_owner, LANES), rows), times(pair, LANES)
        ]
        far = remote(source, target, send_sem, recv_sem, (owner, y * 2 + x))
        close = pltpu.make_async_copy(source, target, own_sem)
        return far, close

    def short_moves(slot, owner):
        return to_owner(
            os, slot, owner * own_short, own_short, owner, 2 * own_long + half * own_short, 3 * core + slot,
            att_send_s.at[slot, owner], att_recv_s.at[half, 3 * core + slot], att_own_s.at[slot],
        )

    def long_moves(slot, owner):
        pair = 3 * core + slot + 2 * near
        return to_owner(
            ol, slot, owner * own_long, own_long, owner, half * own_long, pair,
            att_send_l.at[slot, owner], att_recv_l.at[half, pair], att_own_l.at[slot],
        )

    def send_block(o_ref, o_t, slot, block, moves, owners):
        rows = slice(block * TILE, (block + 1) * TILE)
        both = jnp.concatenate([o_t[2 * slot, :, rows], o_t[2 * slot + 1, :, rows]], axis=0)
        o_ref[slot, rows] = both.T.astype(BF16)
        for owner in owners:
            far, close = moves(slot, owner)
            pl.when(index != owner)(far.start)
            pl.when(index == owner)(close.start)

    def attend_short(block):
        @pl.when(near == 1)
        def _():
            @pl.loop(0, 6)
            def _(head):
                attend(qs, ks, vts, lses, ots, head, block)

    def send_short(block):
        @pl.when(near == 1)
        def _():
            @pl.loop(0, 3)
            def _(slot):
                send_block(os, ots, slot, block, short_moves, (2 * block, 2 * block + 1))

    def attend_long(block):
        @pl.loop(0, 2 * pairs_long)
        def _(head):
            attend(ql, kl, vtl, lsel, otl, head, block)

    def send_long(block):
        @pl.loop(0, pairs_long)
        def _(slot):
            send_block(ol, otl, slot, block, long_moves, (block,))

    zeros = jnp.zeros((PAD, TRIPLE), BF16)
    for slot in range(2):
        proj_l[slot, 0:PAD] = zeros
    for slot in range(3):
        proj_s[slot, 0:PAD] = zeros
    small_w.start()
    qkv_w.start()
    rows_long.start()
    rows_long.start_far()
    rows_short.start()
    small_w.over()
    small_w.turn()
    small_w.last()
    small_w.finish()
    place()
    qkv_w.over()
    rows_long.step(0)
    qkv_w.turn()
    rows_short.start_far()
    up_w.start()
    out_w.start()
    rows_long.step(1)
    qkv_w.last()
    rows_long.step(2)
    down_w.start()
    qkv_w.finish()
    join_weights()
    rows_long.whole(0)
    project_long(0)
    rows_long.whole(1)
    project_long(1)
    rows_long.whole(2)
    project_long(2)
    rows_short.step(0)
    rows_short.step(1)
    rows_short.step(2)
    rows_short.whole(0)
    project_short(0)
    rows_short.whole(1)
    project_short(1)
    rows_short.whole(2)
    project_short(2)
    rows_short.whole(3)
    project_short(3)
    rows_long.whole(3)
    project_long(3)
    up_w.over()
    out_w.over()
    conv_short()
    attend_short(0)
    send_short(0)
    attend_short(2)
    send_short(2)
    attend_short(1)
    send_short(1)
    attend_short(3)
    send_short(3)
    save_short()
    conv_long()
    save_long()
    attend_long(0)
    send_long(0)
    up_w.turn()
    attend_long(4)
    send_long(4)
    out_w.turn()
    attend_long(1)
    send_long(1)
    attend_long(5)
    send_long(5)
    down_w.over()
    up_w.last()
    out_w.last()
    attend_long(2)
    send_long(2)
    attend_long(6)
    send_long(6)
    down_w.turn()
    attend_long(3)
    send_long(3)
    attend_long(7)
    send_long(7)
    save_last()
    down_w.last()
    out_w.finish()
    up_w.finish()
    down_w.finish()
    for one in weights:
        one.sends_done()

    def own_or_wait(source, moves, slot, arrival):
        @pl.when(index == source)
        def _():
            moves(slot, index)[1].wait()

        @pl.when(index != source)
        def _():
            arrival.wait_recv()

    me = (index, y * 2 + x)
    for seq in range(2):
        for pair in range(6):
            columns = pl.ds(pair * LANES, LANES)
            block = att.at[pl.ds(seq * own_long, own_long), columns]
            source, slot = long_source(seq, pair)
            own_or_wait(
                source, long_moves, slot,
                remote(block, block, att_send_l.at[0, 0], att_recv_l.at[seq, pair], me),
            )
            block = att.at[pl.ds(2 * own_long + seq * own_short, own_short), columns]
            source, slot = short_source(seq, pair)
            own_or_wait(
                source, short_moves, slot,
                remote(block, block, att_send_s.at[0, 0], att_recv_s.at[seq, pair], me),
            )

    def sends_done(moves, slot):
        for owner in range(8):
            far, _ = moves(slot, owner)
            pl.when(index != owner)(far.wait_send)

    sends_done(long_moves, 0)
    pl.when(near == 0)(lambda: sends_done(long_moves, 1))

    @pl.when(near == 1)
    def _():
        for slot in range(3):
            sends_done(short_moves, slot)

    rows_long.finish()
    rows_short.finish()
    saves.finish()


def first_part(lengths, x_short, x_long, w_qkv, conv_kernel, norm_params, w_out, w_up, w_down, count):
    width = x_short.shape[2]
    short, long = count * x_short.shape[1], count * x_long.shape[1]
    owned = x_short.shape[1] + x_long.shape[1]
    wide = w_qkv.shape[1] // 2
    rows = w_qkv.shape[0]
    out = jax.ShapeDtypeStruct

    def saved(pairs, total):
        return [
            ((2 * pairs, total, LANES), BF16),
            ((2 * pairs, total, LANES), BF16),
            ((pairs, total, LANES), BF16),
            ((2 * pairs, HEAD_DIM, total), BF16),
            ((2 * pairs, 1, total), F32),
            ((pairs, PAD + total, TRIPLE), BF16),
            ((pairs, total, LANES), BF16),
        ]

    kept = saved(2, long) + saved(3, short)
    basic = [((short, width), BF16), ((long, width), BF16)]
    consts = [((width, wide), BF16), ((8, wide), F32), ((8, width), F32)]
    full = [((4, 2, 2, 2) + w.shape, BF16) for w in (w_out, w_up, w_down)]
    outs = [((2 * owned, width), BF16)] + full + basic + consts + kept
    scratch = (
        basic
        + [((8, LANES), F32), ((4, 2, 2, 2, 8, LANES), F32), ((2, rows, wide), BF16)]
        + [((4, 2, 2, 2, 2, rows, wide), BF16)]
        + consts
        + kept
        + [((4, HEAD_DIM, long), BF16), ((6, HEAD_DIM, short), BF16)]
        + [((4, HEAD_DIM, long), F32), ((6, HEAD_DIM, short), F32)]
    )
    return pl.pallas_call(
        first_kernel,
        out_shape=tuple(out(*one) for one in outs),
        in_specs=[smem(), hbm(), hbm(), vmem(), vmem(), vmem(), hbm(), hbm(), hbm()],
        out_specs=tuple([hbm()] * len(outs)),
        scratch_shapes=[pltpu.VMEM(*one) for one in scratch]
        + [DMA((2,))] + [DMA((2, 4))] * 4
        + [DMA((5,)), DMA((5, 13)), DMA((5, 13))]
        + [DMA((2, 8)), DMA((2, 6)), DMA((3, 8)), DMA((2, 6)), DMA((2,)), DMA((3,))]
        + [DMA((24,))],
        compiler_params=params_of(collective_id=0, has_side_effects=True),
    )(lengths, x_short, x_long, w_qkv, conv_kernel, norm_params, w_out, w_up, w_down)


def second_kernel(
    xs_ref, xl_ref, att, cs_ref, cl_ref, np_ref, wo_ref, wu_ref, wd_ref,
    ys_ref, yl_ref, gmid, gnorm, gwo_o, gwu_o, gwd_o, gl_o, gs_o,
    wo, wu, wd, middle, normal_two, inverse_two, second, second_t, cot, y_acc, gsec, gml, hid, gup,
    gwo, gwu, gwd, sib_out, sib_up, sib_down,
    load_sem, save_sem, send_l, recv_l, send_s, recv_s, core_send, core_recv,
):
    z, core, y, x = position()
    half, near, _, _ = roles()
    index = z * 2 + core
    pairs_long = 2 - near
    loads = Copies(load_sem)
    got_out = loads.start(wo_ref, wo)
    got_up = loads.start(wu_ref, wu)
    got_down = loads.start(wd_ref, wd)
    greet_all()
    short, long = xs_ref.shape[1], xl_ref.shape[1]
    first_short = 2 * long
    for seq in range(2):
        rows = slice(seq * long, (seq + 1) * long)
        cot[rows] = cl_ref[seq]
        middle[rows] = xl_ref[seq].astype(F32)
        rows = slice(first_short + seq * short, first_short + (seq + 1) * short)
        cot[rows] = cs_ref[seq]
        middle[rows] = xs_ref[seq].astype(F32)
    gnorm[...] = jnp.zeros_like(gnorm)
    inner = 512

    def through(part, size):
        @pl.loop(0, size // TILE)
        def _(step):
            rows = pl.ds(pl.multiple_of(part + step * TILE, TILE), TILE)
            values = middle[rows] + dot_nn(att[rows], wo[...])
            normal, inverse = normalise(values)
            normal_two[rows] = normal
            inverse_two[rows] = inverse
            second[rows] = (normal * np_ref[2:3] + np_ref[3:4]).astype(BF16)
            y_acc[rows] = values
            gsec[rows] = jnp.zeros_like(values)

        all_rows = slice(part, part + size)
        second_t[:, all_rows] = second[all_rows].T
        if part == 0:
            got_up.wait()
            got_down.wait()

        @pl.loop(0, wu.shape[1] // inner)
        def _(step):
            columns = times(step, inner)
            upper = jnp.maximum(dot_nn(second[all_rows], wu[:, columns]), 0.0)
            hidden = (upper * upper).astype(BF16)
            grad_hidden = dot_nt(cot[all_rows], wd[columns])
            grad_upper = (2.0 * upper * grad_hidden).astype(BF16)
            hid[all_rows, columns] = hidden
            gup[all_rows, columns] = grad_upper
            y_acc[all_rows] += dot_nn(hidden, wd[columns])
            gsec[all_rows] += dot_nt(grad_upper, wu[:, columns])

        @pl.loop(0, size // TILE)
        def _(step):
            rows = pl.ds(pl.multiple_of(part + step * TILE, TILE), TILE)
            grad = gsec[rows]
            normal = normal_two[rows]
            gnorm[2:3] += jnp.sum(grad * normal, axis=0, keepdims=True)
            gnorm[3:4] += jnp.sum(grad, axis=0, keepdims=True)
            total = cot[rows].astype(F32) + norm_back(grad, normal, inverse_two[rows], np_ref[2:3])
            gmid[rows] = total
            gml[rows] = total.astype(BF16)
            second[rows] = dot_nt(gml[rows], wo[...]).astype(BF16)

    def moves(seq, pair, is_long):
        target, slot = (long_source if is_long else short_source)(seq, pair)
        rows = long if is_long else short
        out, send, recv = (gl_o, send_l, recv_l) if is_long else (gs_o, send_s, recv_s)
        first = seq * long if is_long else first_short + seq * short
        source = second.at[pl.ds(first, rows), pl.ds(pair * LANES, LANES)]
        place = out.at[slot, times(index, rows)]
        far = remote(source, place, send.at[seq, pair], recv.at[slot, index], (target, y * 2 + x))
        close = pltpu.make_async_copy(source, place, recv.at[slot, index])
        return target, far, close

    kinds = [(seq, pair, is_long) for is_long in (True, False) for pair in range(6) for seq in range(2)]

    def send_part(is_long):
        for kind in kinds:
            if kind[2] == is_long:
                target, far, close = moves(*kind)
                pl.when(index != target)(far.start)
                pl.when(index == target)(close.start)

    got_out.wait()
    through(0, first_short)
    send_part(True)
    through(first_short, 2 * short)
    send_part(False)

    sums = [
        CoreSum(grad, sib, total, core_send.at[i], core_recv.at[i], save_sem.at[i], hop)
        for i, (grad, sib, total, hop) in enumerate(
            ((gwu, sib_up, gwu_o, None), (gwd, sib_down, gwd_o, None), (gwo, sib_out, gwo_o, None))
        )
    ]

    def cut(value, grad):
        return value.reshape(grad.shape[:5] + value.shape[1:]).astype(BF16)

    @pl.loop(0, wu.shape[1] // inner)
    def _(step):
        columns = times(step, inner)
        gwu[:, :, :, :, :, columns] = cut(dot_nn(second_t[...], gup[:, columns]), gwu)

    sums[0].start()
    per = gwd.shape[4]
    slabs = gwd.shape[2] * gwd.shape[3]

    @pl.loop(0, gwd.shape[0])
    def _(zz):
        for cc in range(2):
            columns = times(zz * 2 + cc, slabs * per)
            value = dot_tn(hid[:, columns], cot[...])
            gwd[zz, cc] = value.reshape(gwd.shape[2:]).astype(BF16)

    sums[1].start()
    sums[0].add()
    gwo[...] = cut(dot_tn(att[...], gml[...]), gwo)
    sums[2].start()
    for seq in range(2):
        ys_ref[seq] = y_acc[first_short + seq * short : first_short + (seq + 1) * short].astype(BF16)
        yl_ref[seq] = y_acc[seq * long : (seq + 1) * long].astype(BF16)

    sums[1].add()
    sums[2].add()
    me = (index, y * 2 + x)

    def arrivals(out, recv, slot, rows):
        for source in range(8):
            block = out.at[slot, pl.ds(source * rows, rows)]

            @pl.when(index != source)
            def _(block=block, source=source):
                remote(block, block, send_l.at[0, 0], recv.at[slot, source], me).wait_recv()

    arrivals(gl_o, recv_l, 0, long)
    pl.when(near == 0)(lambda: arrivals(gl_o, recv_l, 1, long))

    @pl.when(near == 1)
    def _():
        for slot in range(3):
            arrivals(gs_o, recv_s, slot, short)

    for kind in kinds:
        target, far, close = moves(*kind)
        pl.when(index != target)(far.wait_send)
        pl.when(index == target)(close.wait)
    for one in sums:
        one.finish()


def second_part(x_short, x_long, att, cot_short, cot_long, norms, w_out, w_up, w_down, count):
    width = x_short.shape[2]
    rows = att.shape[0]
    short, long = count * x_short.shape[1], count * x_long.shape[1]
    hidden = w_up.shape[1]
    out = jax.ShapeDtypeStruct
    devices = 4 * count

    def shards(w):
        return (4, 2, 2, 2, w.shape[0] // devices, w.shape[1])

    def halves(w):
        return (4, 2, 2, w.shape[0] // devices, w.shape[1])

    return pl.pallas_call(
        second_kernel,
        out_shape=(
            out(x_short.shape, BF16),
            out(x_long.shape, BF16),
            out((rows, width), F32),
            out((8, width), F32),
            out(halves(w_out), BF16),
            out(halves(w_up), BF16),
            out(halves(w_down), BF16),
            out((2, long, LANES), BF16),
            out((3, short, LANES), BF16),
        ),
        in_specs=[vmem()] * 6 + [hbm()] * 3,
        out_specs=tuple([vmem()] * 4 + [hbm()] * 5),
        scratch_shapes=[
            pltpu.VMEM(w_out.shape, BF16),
            pltpu.VMEM(w_up.shape, BF16),
            pltpu.VMEM(w_down.shape, BF16),
            pltpu.VMEM((rows, width), F32),
            pltpu.VMEM((rows, width), F32),
            pltpu.VMEM((rows, 1), F32),
            pltpu.VMEM((rows, width), BF16),
            pltpu.VMEM((width, rows), BF16),
            pltpu.VMEM((rows, width), BF16),
            pltpu.VMEM((rows, width), F32),
            pltpu.VMEM((rows, width), F32),
            pltpu.VMEM((rows, width), BF16),
            pltpu.VMEM((rows, hidden), BF16),
            pltpu.VMEM((rows, hidden), BF16),
            *[pltpu.VMEM(shards(w), BF16) for w in (w_out, w_up, w_down)],
            *[pltpu.VMEM(halves(w), BF16) for w in (w_out, w_up, w_down)],
            DMA((3,)), DMA((3, 2)), DMA((2, 6)), DMA((2, 8)), DMA((2, 6)), DMA((3, 8)), DMA((3, 3)), DMA((3, 3)),
        ],
        compiler_params=params_of(collective_id=1, has_side_effects=True),
    )(x_short, x_long, att, cot_short, cot_long, norms, w_out, w_up, w_down)


class RowSum:
    def __init__(self, long_bufs, short_bufs, sems):
        self.mine, self.out, self.sib, self.got, self.fin = long_bufs
        self.mine_s, self.out_s, self.sib_s, self.fin_s = short_bufs
        (
            self.sib_send, self.sib_recv, self.send, self.recv, self.on_send, self.fin_recv,
            self.sib_send_s, self.sib_recv_s, self.send_s, self.fin_recv_s,
        ) = sems
        self.z, self.core, self.y, self.x = position()
        self.half, self.near, partner_z, far_z = roles()
        self.partner = at(partner_z, self.core, self.y, self.x)
        self.sibling = at(self.z, 1 - self.core, self.y, self.x)
        self.far = at(far_z, self.core, self.y, self.x)

    def across(self, zz):
        return remote(self.out.at[zz % 2], self.sib.at[zz], self.sib_send.at[zz], self.sib_recv.at[zz], self.sibling)

    def put(self, block, value):
        zz, parity = block // 2, block % 2

        @pl.when(self.core == parity)
        def _():
            self.mine[zz] = value

        @pl.when(self.core != parity)
        def _():
            if zz < 2:
                self.across(zz + 2).wait_send()
            self.out[zz % 2] = value
            self.across(zz).start()

    def place(self, zz):
        return jnp.where(self.half == 0, zz, 3 - zz)

    def part(self, side):
        rows = self.fin.shape[0] // 2
        return pl.ds(side * rows, rows)

    def to_partner(self, zz, side):
        rows = self.part(side)
        return remote(
            self.mine.at[zz, rows], self.got.at[zz, rows], self.send.at[zz, side], self.recv.at[zz, side], self.partner
        )

    def to_owner(self, zz, side):
        rows = self.part(side)
        return remote(
            self.mine.at[zz, rows], self.fin.at[rows], self.on_send.at[zz, side], self.fin_recv.at[side],
            at(zz, self.core, self.y, self.x),
        )

    def sends_to_partner(self, zz):
        place = self.place(zz)
        return jnp.where(self.near == 0, place != 0, place == 0)

    def add_cores(self, zz):
        self.across(zz).wait_recv()
        for side in range(2):
            rows = self.part(side)
            add_into(self.mine.at[zz, rows], self.sib.at[zz, rows])
            pl.when(self.sends_to_partner(zz))(self.to_partner(zz, side).start)

    def sends_on(self, zz):
        return jnp.logical_and(self.near == 1, self.place(zz) >= 2)

    def add_chips(self, zz):
        @pl.when(self.sends_on(zz))
        def _():
            for side in range(2):
                rows = self.part(side)
                self.to_partner(zz, side).wait_recv()
                add_into(self.mine.at[zz, rows], self.got.at[zz, rows])
                self.to_owner(zz, side).start()

    def across_s(self, zz):
        return remote(
            self.out_s.at[zz], self.sib_s.at[zz], self.sib_send_s.at[zz], self.sib_recv_s.at[zz], self.sibling
        )

    def put_short(self, zz, value):
        rows = value.shape[0] // 2
        first, second = value[:rows], value[rows:]

        @pl.when(self.core == 0)
        def _():
            self.mine_s[zz] = first
            self.out_s[zz] = second

        @pl.when(self.core == 1)
        def _():
            self.mine_s[zz] = second
            self.out_s[zz] = first

        self.across_s(zz).start()

    def to_owner_s(self, zz):
        return remote(
            self.mine_s.at[zz], self.fin_s.at[self.half], self.send_s.at[zz], self.fin_recv_s.at[self.half],
            at(zz, self.core, self.y, self.x),
        )

    def add_short(self, zz):
        @pl.when(self.near == 1)
        def _():
            self.across_s(zz).wait_recv()
            add_into(self.mine_s.at[zz], self.sib_s.at[zz])
            pl.when(self.z != zz)(self.to_owner_s(zz).start)

    def own_long(self):
        for side in range(2):
            self.to_partner(self.z, side).wait_recv()
        return self.mine[self.z].astype(F32) + self.got[self.z].astype(F32)

    def other_long(self):
        for side in range(2):
            block = self.fin.at[self.part(side)]
            remote(block, block, self.on_send.at[0, 0], self.fin_recv.at[side], self.far).wait_recv()
        return self.fin[...].astype(F32)

    def shorts(self):
        def arrival(seq):
            block = self.fin_s.at[seq]
            remote(block, block, self.send_s.at[0], self.fin_recv_s.at[seq], self.far).wait_recv()

        arrival(1 - self.half)
        pl.when(self.near == 0)(lambda: arrival(self.half))

        @pl.when(self.near == 1)
        def _():
            self.fin_s[self.half] = self.mine_s[self.z]

    def sends_done(self):
        for zz in range(4):
            if zz < 2:
                self.across(zz).wait_send()
            for side in range(2):
                pl.when(self.sends_to_partner(zz))(self.to_partner(zz, side).wait_send)
                pl.when(self.sends_on(zz))(self.to_owner(zz, side).wait_send)

        @pl.when(self.near == 1)
        def _():
            for zz in range(4):
                self.across_s(zz).wait_send()
                pl.when(self.z != zz)(self.to_owner_s(zz).wait_send)


def third_kernel(
    xs_own, xl_own, gnorm, wq, taps, norms, gmid,
    xs_h, xl_h, ql_h, kl_h, vl_h, ktl_h, lsel_h, pl_h, ol_h, qs_h, ks_h, vs_h, kts_h, lses_h, ps_h, os_h,
    gl_h, gs_h, gwo_h, gwu_h, gwd_h,
    dxs_ref, dxl_ref, gwq_ref, gwo_ref, gwu_ref, gwd_ref, small_ref,
    ql, kl, vl, ktl, lsel, ol, gl, qs, ks, vs, kts, lses, os, gs,
    gm, dqt, delta, gp, early_gn, dwq, dtaps, dnorms, x_tile, p_tile,
    mine, out, sib, got, fin, mine_s, out_s, sib_s, fin_s,
    load_sem, tile_sem,
    r0, r1, r2, r3, r4, r5, r6, r7, r8, r9,
    shard_own, shard_send, shard_recv, group_send, group_recv, small_send, small_recv,
    *bufs,
):
    z, core, y, x = position()
    half, near, _, _ = roles()
    long_moves = (
        (ql_h, ql), (kl_h, kl), (vl_h, vl), (ktl_h, ktl), (lsel_h, lsel), (ol_h, ol), (gl_h, gl),
    )
    short_moves = (
        (qs_h, qs), (ks_h, ks), (vs_h, vs), (kts_h, kts), (lses_h, lses), (os_h, os), (gs_h, gs),
    )
    loads = [
        pltpu.make_async_copy(source, target, load_sem.at[i])
        for i, (source, target) in enumerate(long_moves + short_moves)
    ]
    long_loads, short_loads = loads[:7], loads[7:]

    @pl.when(near == 1)
    def _():
        for copy in short_loads:
            copy.start()

    for copy in long_loads:
        copy.start()
    greet_all()
    bufs = list(bufs)
    sums = []
    for i, (grad, total, begun) in enumerate(
        ((gwo_h, gwo_ref, False), (gwu_h, gwu_ref, False), (gwd_h, gwd_ref, False))
    ):
        size = 4 if begun else 5
        mine_bufs, bufs = bufs[:size], bufs[size:]
        sums.append(ShardSum(grad, total, mine_bufs, shard_own.at[i], shard_send.at[i], shard_recv.at[i], begun))
    group_early = GroupSum(bufs[0:4], group_send.at[0], group_recv.at[0])
    group_late = GroupSum(bufs[4:8], group_send.at[1], group_recv.at[1])
    small = SmallSum(bufs[8:13], small_ref, small_send, small_recv)
    rows_sum = RowSum((mine, out, sib, got, fin), (mine_s, out_s, sib_s, fin_s), (r0, r1, r2, r3, r4, r5, r6, r7, r8, r9))
    sum_out, sum_up, sum_down = sums
    sum_up.start()
    short, long = xs_own.shape[1], xl_own.shape[1]
    middles = [
        pltpu.make_async_copy(gmid.at[pl.ds(first + seq * size, size)], dx.at[seq], load_sem.at[14 + 2 * seq + i])
        for seq in range(2)
        for i, (dx, first, size) in enumerate(((dxs_ref, 2 * long, short), (dxl_ref, 0, long)))
    ]
    for copy in middles:
        copy.start()
    gm[...] = jnp.zeros_like(gm)
    dwq[...] = jnp.zeros_like(dwq)
    dtaps[...] = jnp.zeros_like(dtaps)
    dnorms[...] = gnorm[...]
    gain, offset = norms[0:1], norms[1:2]
    causal = causal_mask()
    first_lanes = iota((TILE, LANES), 1) < HEAD_DIM

    def back_head(refs, grad_ref, slot, side, local, block):
        q_ref, k_ref, v_ref, kt_ref, lse, _, g_ref = refs
        head = 2 * slot + side
        own_lanes = first_lanes == (side == 0)
        rows = slice(block * TILE, (block + 1) * TILE)
        query = q_ref[head, rows]
        bare = jnp.where(own_lanes, query.astype(F32), 0.0).astype(BF16)
        grad_out = jnp.where(own_lanes, g_ref[slot, rows].astype(F32), 0.0).astype(BF16)
        stat, less = lse[head, :, rows], delta[local]
        spans = [(block * TILE, TILE, True)]
        if block:
            spans.append((0, block * TILE, False))
        grad_q = None
        for start, size, masked in spans:
            keys = slice(start, start + size)
            scores = dot_nt(k_ref[head, keys], query)
            if masked:
                scores = jnp.where(causal, scores, NEG_FILL)
            probs = jnp.exp(scores - stat)
            grad_probs = dot_nt(v_ref[slot, keys], grad_out)
            grad_ref[keys, 2 * LANES :] += dot_nn(probs.astype(BF16), grad_out)
            grad_scores = (probs * (grad_probs - less)).astype(BF16)
            grad_ref[keys, LANES : 2 * LANES] += dot_nn(grad_scores, bare)
            term = dot_nn(kt_ref[head, :, keys], grad_scores)
            grad_q = term if grad_q is None else grad_q + term
        dqt[local] = (HEAD_DIM**-0.5) * grad_q

    def back_block(refs, x_h, p_h, count, first_slot, first_pair, block):
        o_ref, g_ref = refs[5], refs[6]
        rows = slice(block * TILE, (block + 1) * TILE)
        span = x_h.shape[0] + PAD
        got_x = pltpu.make_async_copy(x_h.at[pl.ds(block * TILE, TILE)], x_tile, tile_sem.at[0])
        got_p = pltpu.make_async_copy(
            p_h.at[pl.ds(first_slot, count), pl.ds(block * TILE, TILE + PAD)], p_tile.at[pl.ds(0, count)], tile_sem.at[1]
        )
        got_x.start()
        got_p.start()
        for local in range(count):
            product = g_ref[first_slot + local, rows].astype(F32) * o_ref[first_slot + local, rows].astype(F32)
            turned = product.T
            delta[2 * local] = jnp.sum(turned[:HEAD_DIM], axis=0, keepdims=True)
            delta[2 * local + 1] = jnp.sum(turned[HEAD_DIM:], axis=0, keepdims=True)

        @pl.loop(0, 2 * count)
        def _(local):
            slot = local // 2
            grad_ref = gm.at[pl.ds(pl.multiple_of(slot * span, PAD), span)]
            back_head(refs, grad_ref, first_slot + slot, local % 2, local, block)

        got_x.wait()
        got_p.wait()
        normal, _ = normalise(x_tile[...].astype(F32))
        low = (normal * gain + offset).astype(BF16)
        for local in range(count):
            grad_ref = gm.at[pl.ds(local * span, span)]
            grad_ref[rows, 0:LANES] = jnp.concatenate([dqt[2 * local], dqt[2 * local + 1]], axis=0).T
            window = grad_ref[pl.ds(block * TILE, TILE + PAD)]
            grad = window[:TILE]
            columns = pl.ds(pl.multiple_of((first_pair + local) * TRIPLE, TRIPLE), TRIPLE)
            kernel = taps[:, columns]
            grad_projected = (
                kernel[0:1] * grad + kernel[1:2] * shifted(window, -1)[:TILE] + kernel[2:3] * shifted(window, -2)[:TILE]
            ).astype(BF16)
            past = p_tile[local].astype(F32)
            dtaps[0:1, columns] += jnp.sum(grad * past[PAD:], axis=0, keepdims=True)
            dtaps[1:2, columns] += jnp.sum(grad * shifted(past, 1)[PAD:], axis=0, keepdims=True)
            dtaps[2:3, columns] += jnp.sum(grad * shifted(past, 2)[PAD:], axis=0, keepdims=True)
            gp[:, local * TRIPLE : (local + 1) * TRIPLE] = grad_projected
        grads = gp[:, : count * TRIPLE]
        columns = pl.ds(pl.multiple_of(first_pair * TRIPLE, TRIPLE), count * TRIPLE)
        grad_normed = dot_nt(grads, wq[:, columns])
        dwq[:, columns] += dot_tn(low, grads)
        dnorms[0:1] += jnp.sum(grad_normed * normal, axis=0, keepdims=True)
        dnorms[1:2] += jnp.sum(grad_normed, axis=0, keepdims=True)
        return grad_normed

    def hook_one():
        sum_up.turn()
        sum_down.start()
        sum_out.start()

    def hook_two():
        sum_up.last()

    def hook_three():
        sum_down.turn()
        sum_out.turn()

    def hook_four():
        sum_down.last()
        sum_out.last()

    def finish_rows(seq, grad, x_ref, dx_ref):
        normal, inverse = normalise(x_ref[seq].astype(F32))
        dx_ref[seq] += norm_back(grad, normal, inverse, gain)

    long_refs = (ql, kl, vl, ktl, lsel, ol, gl)
    short_refs = (qs, ks, vs, kts, lses, os, gs)
    last_long = xl_h.shape[0] // TILE - 1
    last_short = xs_h.shape[0] // TILE - 1

    @pl.when(near == 0)
    def _():
        for copy in long_loads:
            copy.wait()
        for block in range(last_long, -1, -1):
            value = back_block(long_refs, xl_h, pl_h, 1, 0, 0, block)
            early_gn[block * TILE : (block + 1) * TILE] = value.astype(BF16)
            if block == 6:
                hook_one()
            if block == 3:
                hook_two()

    @pl.when(near == 1)
    def _():
        for copy in short_loads:
            copy.wait()
        for block in range(last_short, -1, -1):
            value = back_block(short_refs, xs_h, ps_h, 3, 0, 0, block)
            rows_sum.put_short(block, value.astype(BF16))
            if block == 3:
                hook_one()
            if block == 1:
                hook_two()
        for copy in long_loads:
            copy.wait()

    hook_three()
    group_early.start(dwq, pl.ds(0, 2 * TRIPLE))
    gm[...] = jnp.zeros_like(gm)

    for block in range(last_long, -1, -1):
        value = back_block(long_refs, xl_h, pl_h, 1, 1 - near, 1 + near, block)
        early = early_gn[block * TILE : (block + 1) * TILE].astype(F32)
        rows_sum.put(block, (value + jnp.where(near == 0, early, 0.0)).astype(BF16))
        if block % 2 == 1 and block != last_long:
            rows_sum.add_cores(block // 2 + 1)
        if block > 3:
            rows_sum.add_short(block - 4)
        if block == 7:
            hook_four()
        if block == 6:
            group_early.turn()
        if block == 5:
            group_early.last()
        if block == 2:
            rows_sum.add_chips(3)
    group_late.start(dwq, pl.ds(pl.multiple_of((1 + near) * TRIPLE, TRIPLE), TRIPLE))
    small.start(dtaps[...], dnorms[...])
    rows_sum.add_cores(0)
    rows_sum.add_chips(2)
    small.over()
    group_late.turn()
    rows_sum.add_chips(1)
    small.turn()
    for copy in middles:
        copy.wait()
    rows_sum.shorts()
    finish_rows(half, rows_sum.fin_s[half].astype(F32), xs_own, dxs_ref)
    group_late.last()
    small.last()
    rows_sum.add_chips(0)
    finish_rows(1 - half, rows_sum.fin_s[1 - half].astype(F32), xs_own, dxs_ref)
    finish_rows(half, rows_sum.own_long(), xl_own, dxl_ref)
    for one in sums:
        one.finish()
    group_early.finish()
    small.swap_back()
    group_late.finish()
    join_groups(group_early, group_late, gwq_ref)
    finish_rows(1 - half, rows_sum.other_long(), xl_own, dxl_ref)
    small.finish()
    rows_sum.sends_done()


def third_part(x_short, x_long, gmid, gnorm, wq, taps, norms, kept, grads_in, weight_grads):
    width = x_short.shape[2]
    wide = wq.shape[1]
    count = 8
    short, long = count * x_short.shape[1], count * x_long.shape[1]
    own_short = x_short.shape[1]
    rows = weight_grads[0].shape[3]
    out = jax.ShapeDtypeStruct
    small_wide = wide + width // 2

    def saved(pairs, total):
        return [
            ((2 * pairs, total, LANES), BF16),
            ((2 * pairs, total, LANES), BF16),
            ((pairs, total, LANES), BF16),
            ((2 * pairs, HEAD_DIM, total), BF16),
            ((2 * pairs, 1, total), F32),
            ((pairs, total, LANES), BF16),
            ((pairs, total, LANES), BF16),
        ]

    scratch = (
        saved(2, long)
        + saved(3, short)
        + [
            ((max(long + PAD, 3 * (short + PAD)), TRIPLE), F32),
            ((6, HEAD_DIM, TILE), F32),
            ((6, 1, TILE), F32),
            ((TILE, wide), BF16),
            ((long, width), BF16),
            ((width, wide), F32),
            ((8, wide), F32),
            ((8, width), F32),
            ((TILE, width), BF16),
            ((3, TILE + PAD, TRIPLE), BF16),
        ]
        + [((4, TILE, width), BF16), ((2, TILE, width), BF16)]
        + [((4, TILE, width), BF16)] * 2
        + [((TILE, width), BF16)]
        + [((4, own_short, width), BF16)] * 3
        + [((2, own_short, width), BF16)]
    )
    buffers = []
    for i, g in enumerate(weight_grads):
        buffers += ShardSum.buffers(g)
    buffers += GroupSum.buffers(rows, 2 * TRIPLE) + GroupSum.buffers(rows, TRIPLE) + SmallSum.buffers(wide, width // 2)
    return pl.pallas_call(
        third_kernel,
        out_shape=(
            out(x_short.shape, F32),
            out(x_long.shape, F32),
            out((rows, 2 * wide), F32),
            *[out(g.shape[3:], F32) for g in weight_grads],
            out((2, 8, small_wide), F32),
        ),
        in_specs=[vmem()] * 6 + [hbm()] * (1 + len(kept) + len(grads_in) + len(weight_grads)),
        out_specs=tuple([vmem()] * 7),
        scratch_shapes=[pltpu.VMEM(*one) for one in scratch]
        + [DMA((18,)), DMA((2,))]
        + [DMA((4,))] * 2 + [DMA((4, 2))] * 3 + [DMA((2,))] + [DMA((4,))] * 3 + [DMA((2,))]
        + [DMA((3, 2)), DMA((3, 9)), DMA((3, 9)), DMA((2, 11)), DMA((2, 11)), DMA((7,)), DMA((7,))]
        + buffers,
        compiler_params=params_of(63, collective_id=2, has_side_effects=True),
    )(x_short, x_long, gnorm, wq, taps, norms, gmid, *kept, *grads_in, *weight_grads)


def last_kernel(*refs):
    *arrays, smalls = refs[:9]
    outs, kernel_out, norm_out = refs[9:17], refs[17], refs[18]
    held, sems = refs[19:27], refs[27]
    loads = [pltpu.make_async_copy(a, h, sems.at[0, i]) for i, (a, h) in enumerate(zip(arrays, held))]
    copies = [pltpu.make_async_copy(h, o, sems.at[1, i]) for i, (h, o) in enumerate(zip(held, outs))]
    for copy in loads:
        copy.start()
    number = lax.axis_index("seq") * lax.axis_size("batch") + lax.axis_index("batch")
    (taps, part), (norms, cut) = kernel_out.shape, norm_out.shape
    norm_columns = norm_out.shape[1] * 32 // 2
    wide = smalls.shape[2] - norm_columns
    width = 2 * wide // 3

    def pick(values, source, first):
        chosen = jnp.where(source == first + iota(source.shape, 1), 1.0, 0.0)
        return lax.dot_general(
            values, chosen, (((1,), (0,)), ((), ())), preferred_element_type=F32, precision=lax.Precision.HIGHEST
        )

    row = iota((wide, LANES), 0)
    block = row // LANES
    norm_row = iota((norm_columns, LANES), 0)
    kernel_sum, norm_sum = None, None
    for load, copy in zip(loads, copies):
        load.wait()
        copy.start()
    for side in range(2):
        source = (block % 3) * width + (3 * side + block // 3) * LANES + row % LANES
        term = pick(smalls[side, :, :wide], source, number * part)
        norm_term = pick(smalls[side, :, wide:], norm_row + side * norm_columns, number * cut)
        kernel_sum = term if side == 0 else kernel_sum + term
        norm_sum = norm_term if side == 0 else norm_sum + norm_term
    kernel_out[...] = kernel_sum[:taps, :part]
    norm_out[...] = norm_sum[:norms, :cut]
    for copy in copies:
        copy.wait()


def last_part(arrays, smalls, taps, part, cut):
    out = jax.ShapeDtypeStruct
    return pl.pallas_call(
        last_kernel,
        out_shape=(*[out(a.shape, a.dtype) for a in arrays], out((taps, part), F32), out((4, cut), F32)),
        in_specs=[hbm()] * 8 + [vmem()],
        out_specs=tuple([hbm()] * 8 + [vmem()] * 2),
        scratch_shapes=[pltpu.VMEM(a.shape, a.dtype) for a in arrays] + [DMA((2, 8))],
        compiler_params=params_of(),
    )(*arrays, smalls)


def split_body(
    x_short, x_long, lengths, cot_short, cot_long, w_qkv, w_out, w_up, w_down, conv_kernel, norm_params
):
    count = lax.axis_size("seq")
    width = x_short.shape[2]
    att, full_out, full_up, full_down, xs, xl, wq, taps, norms, *kept = first_part(
        lengths, x_short, x_long, w_qkv, conv_kernel, norm_params, w_out, w_up, w_down, count
    )
    y_short, y_long, gmid, gnorm, gwo, gwu, gwd, gl, gs = second_part(
        x_short, x_long, att, cot_short, cot_long, norms,
        full_out.reshape(width, -1), full_up.reshape(width, -1), full_down.reshape(-1, width), count,
    )
    dx_short, dx_long, sum_qkv, sum_out, sum_up, sum_down, smalls = third_part(
        x_short, x_long, gmid, gnorm, wq, taps, norms, [xs, xl] + kept, [gl, gs], [gwo, gwu, gwd]
    )
    return last_part(
        (y_short, y_long, dx_short, dx_long, sum_qkv, sum_out, sum_up, sum_down), smalls,
        conv_kernel.shape[0], conv_kernel.shape[1], norm_params.shape[1],
    )


GROUP_HEADS = 2


def from_behind(value, axis, by):
    count = lax.axis_size(axis)
    pairs = [(i, i + by) for i in range(count) if 0 <= i + by < count]
    return lax.ppermute(value, axis, pairs)


def layer_norm(values, gain, offset_term):
    average = jnp.mean(values, axis=-1, keepdims=True)
    centred = values - average
    inverse = lax.rsqrt(jnp.mean(centred * centred, axis=-1, keepdims=True) + EPS)
    normal = centred * inverse
    return (normal * gain + offset_term, normal, inverse)


def norm_back_flat(grad, normal, inverse, gain):
    scaled_grad = grad * gain
    first_mean = jnp.mean(scaled_grad, axis=-1, keepdims=True)
    second_mean = jnp.mean(scaled_grad * normal, axis=-1, keepdims=True)
    return inverse * (scaled_grad - first_mean - normal * second_mean)


def front_part(inputs, full_weights):
    w_qkv = full_weights[0]
    kernel = full_weights[4].astype(jnp.float32)
    params = full_weights[5].astype(jnp.float32)
    saved = []
    tails = []
    for part_in in inputs:
        seq_count, block_rows, model_width = part_in.shape
        flat = part_in.reshape(seq_count * block_rows, model_width).astype(jnp.float32)
        normed, normal, inverse = layer_norm(flat, params[0], params[1])
        normed_low = normed.astype(jnp.bfloat16)
        projected = jnp.dot(normed_low, w_qkv, preferred_element_type=jnp.float32).astype(
            jnp.bfloat16
        )
        projected = projected.reshape(seq_count, block_rows, 3 * model_width)
        saved.append((flat, normal, inverse, normed_low, projected))
        tails.append(projected[:, block_rows - 2 :])
    received = from_behind((tails[0], tails[1]), "seq", 1)
    fronts = []
    for index_part in range(2):
        flat, normal, inverse, normed_low, projected = saved[index_part]
        block_rows = projected.shape[1]
        padded = jnp.concatenate([received[index_part], projected], axis=1).astype(jnp.float32)
        mixed = (
            kernel[0] * padded[:, 2:]
            + kernel[1] * padded[:, 1 : block_rows + 1]
            + kernel[2] * padded[:, :block_rows]
        )
        fronts.append((flat, normal, inverse, normed_low, padded, mixed.astype(jnp.bfloat16)))
    return fronts


def attend_block(queries, key_rows, value_rows, usable, grad_heads):
    scaling = queries.shape[-1] ** (-0.5)
    scores = jnp.einsum("sqhd,skhd->shqk", queries, key_rows, preferred_element_type=jnp.float32)
    masked = jnp.where(usable, scaling * scores, NEG_FILL)
    exp_terms = jnp.exp(masked - jnp.max(masked, axis=-1, keepdims=True))
    attn_probs = exp_terms / jnp.sum(exp_terms, axis=-1, keepdims=True)
    probs_low = attn_probs.astype(jnp.bfloat16)
    if grad_heads is None:
        attended = jnp.einsum(
            "shqk,skhd->sqhd", probs_low, value_rows, preferred_element_type=jnp.float32
        )
        return attended.astype(jnp.bfloat16)
    grad_probs = jnp.einsum(
        "sqhd,skhd->shqk", grad_heads, value_rows, preferred_element_type=jnp.float32
    )
    grad_values = jnp.einsum(
        "shqk,sqhd->skhd", probs_low, grad_heads, preferred_element_type=jnp.float32
    )
    row_delta = jnp.sum(attn_probs * grad_probs, axis=-1, keepdims=True)
    grad_scores = (scaling * attn_probs * (grad_probs - row_delta)).astype(jnp.bfloat16)
    grad_queries = jnp.einsum(
        "shqk,skhd->sqhd", grad_scores, key_rows, preferred_element_type=jnp.float32
    )
    grad_keys = jnp.einsum(
        "shqk,sqhd->skhd", grad_scores, queries, preferred_element_type=jnp.float32
    )
    return (grad_queries, grad_keys, grad_values)


def make_usable(query_pos, key_pos, seq_lengths):
    usable = (key_pos[None, None, :] <= query_pos[None, :, None]) & (
        key_pos[None, None, :] < seq_lengths[:, None, None]
    )
    return usable[:, None]


def attention(mixed, kv_full, seq_lengths, offset, grad_attended):
    seq_count, block_rows, three_width = mixed.shape
    model_width = three_width // 3
    full_len = kv_full.shape[1]
    queries = mixed[:, :, :model_width].reshape(seq_count, block_rows, -1, HEAD_DIM)
    key_rows = kv_full[:, :, :model_width].reshape(seq_count, full_len, -1, HEAD_DIM)
    value_rows = kv_full[:, :, model_width:].reshape(seq_count, full_len, -1, HEAD_DIM)
    positions = offset + jnp.arange(block_rows, dtype=jnp.int32)
    key_pos = jnp.arange(full_len, dtype=jnp.int32)
    usable = make_usable(positions, key_pos, seq_lengths)
    heads_total = queries.shape[2]
    grad_heads = None
    if grad_attended is not None:
        grad_heads = grad_attended.reshape(seq_count, block_rows, -1, HEAD_DIM)
    results = []
    for first_head in range(0, heads_total, GROUP_HEADS):
        last_head = first_head + GROUP_HEADS
        grad_part = None if grad_heads is None else grad_heads[:, :, first_head:last_head]
        results.append(
            attend_block(
                queries[:, :, first_head:last_head],
                key_rows[:, :, first_head:last_head],
                value_rows[:, :, first_head:last_head],
                usable,
                grad_part,
            )
        )
    if grad_heads is None:
        return jnp.concatenate(results, axis=2).reshape(seq_count, block_rows, model_width)
    grad_queries = jnp.concatenate([entry_set[0] for entry_set in results], axis=2).reshape(
        seq_count, block_rows, model_width
    )
    grad_keys = jnp.concatenate([entry_set[1] for entry_set in results], axis=2).reshape(
        seq_count, full_len, model_width
    )
    grad_values = jnp.concatenate([entry_set[2] for entry_set in results], axis=2).reshape(
        seq_count, full_len, model_width
    )
    return (grad_queries, grad_keys, grad_values)


def rest_part(front, kv_full, seq_lengths, offset, full_weights, cotangent_in):
    w_out, w_up, w_down = (full_weights[1], full_weights[2], full_weights[3])
    params = full_weights[5].astype(jnp.float32)
    flat, normal_one, inverse_one, normed_low, padded, mixed = front
    seq_count, block_rows, three_width = mixed.shape
    model_width = three_width // 3
    attended = attention(mixed, kv_full, seq_lengths, offset, None).reshape(
        seq_count * block_rows, model_width
    )
    middle = flat + jnp.dot(attended, w_out, preferred_element_type=jnp.float32)
    second, normal_two, inverse_two = layer_norm(middle, params[2], params[3])
    second_low = second.astype(jnp.bfloat16)
    upper = jnp.dot(second_low, w_up, preferred_element_type=jnp.float32)
    hidden = jnp.square(jnp.maximum(upper, 0.0)).astype(jnp.bfloat16)
    if cotangent_in is None:
        result_rows = middle + jnp.dot(hidden, w_down, preferred_element_type=jnp.float32)
        return result_rows.astype(jnp.bfloat16).reshape(seq_count, block_rows, model_width)
    cotangent = cotangent_in.reshape(seq_count * block_rows, model_width)
    grad_down = jnp.dot(hidden.T, cotangent, preferred_element_type=jnp.float32)
    grad_hidden = jnp.dot(cotangent, w_down.T, preferred_element_type=jnp.float32)
    grad_upper = (2.0 * jnp.maximum(upper, 0.0) * grad_hidden).astype(jnp.bfloat16)
    grad_up = jnp.dot(second_low.T, grad_upper, preferred_element_type=jnp.float32)
    grad_second = jnp.dot(grad_upper, w_up.T, preferred_element_type=jnp.float32)
    grad_middle = cotangent.astype(jnp.float32) + norm_back_flat(
        grad_second, normal_two, inverse_two, params[2]
    )
    grad_middle_low = grad_middle.astype(jnp.bfloat16)
    grad_out = jnp.dot(attended.T, grad_middle_low, preferred_element_type=jnp.float32)
    grad_attended = jnp.dot(grad_middle_low, w_out.T, preferred_element_type=jnp.float32).astype(
        jnp.bfloat16
    )
    grad_attended = grad_attended.reshape(seq_count, block_rows, model_width)
    grad_queries, grad_keys, grad_values = attention(
        mixed, kv_full, seq_lengths, offset, grad_attended
    )
    key_term = jnp.concatenate([grad_keys, grad_values], axis=-1)
    norm_two = (jnp.sum(grad_second * normal_two, axis=0), jnp.sum(grad_second, axis=0))
    return (grad_queries, key_term, grad_middle, grad_out, grad_up, grad_down, norm_two)


def general_body(
    x_short,
    x_long,
    lengths,
    cot_short,
    cot_long,
    w_qkv,
    w_out,
    w_up,
    w_down,
    conv_kernel,
    norm_params,
):
    full_weights = (
        lax.all_gather(w_qkv, ("seq", "batch"), axis=0, tiled=True),
        lax.all_gather(w_out, ("seq", "batch"), axis=0, tiled=True),
        lax.all_gather(w_up, ("seq", "batch"), axis=0, tiled=True),
        lax.all_gather(w_down, ("seq", "batch"), axis=0, tiled=True),
        lax.all_gather(conv_kernel, ("seq", "batch"), axis=1, tiled=True),
        lax.all_gather(norm_params, ("seq", "batch"), axis=1, tiled=True),
    )
    inputs = (x_short, x_long)
    cotangents = (cot_short, cot_long)
    model_width = x_short.shape[2]
    offsets = (lax.axis_index("seq") * x_short.shape[1], lax.axis_index("seq") * x_long.shape[1])
    fronts = front_part(inputs, full_weights)
    kv_fwd = (
        lax.all_gather(fronts[0][5][:, :, model_width:], "seq", axis=1, tiled=True),
        lax.all_gather(fronts[1][5][:, :, model_width:], "seq", axis=1, tiled=True),
    )
    outputs = [
        rest_part(
            fronts[index_part],
            kv_fwd[index_part],
            lengths[index_part],
            offsets[index_part],
            full_weights,
            None,
        )
        for index_part in range(2)
    ]
    back_weights = (
        lax.all_gather(w_qkv, ("seq", "batch"), axis=0, tiled=True),
        lax.all_gather(w_out, ("seq", "batch"), axis=0, tiled=True),
        lax.all_gather(w_up, ("seq", "batch"), axis=0, tiled=True),
        lax.all_gather(w_down, ("seq", "batch"), axis=0, tiled=True),
        lax.all_gather(conv_kernel, ("seq", "batch"), axis=1, tiled=True),
        lax.all_gather(norm_params, ("seq", "batch"), axis=1, tiled=True),
    )
    fronts_back = front_part(inputs, back_weights)
    kv_back = (
        lax.all_gather(fronts_back[0][5][:, :, model_width:], "seq", axis=1, tiled=True),
        lax.all_gather(fronts_back[1][5][:, :, model_width:], "seq", axis=1, tiled=True),
    )
    partials = [
        rest_part(
            fronts_back[index_part],
            kv_back[index_part],
            lengths[index_part],
            offsets[index_part],
            back_weights,
            cotangents[index_part],
        )
        for index_part in range(2)
    ]
    kv_grads = (
        lax.psum_scatter(
            partials[0][1].astype(jnp.bfloat16), "seq", scatter_dimension=1, tiled=True
        ).astype(jnp.float32),
        lax.psum_scatter(
            partials[1][1].astype(jnp.bfloat16), "seq", scatter_dimension=1, tiled=True
        ).astype(jnp.float32),
    )
    grad_mixed = [
        jnp.concatenate([partials[index_part][0], kv_grads[index_part]], axis=-1)
        for index_part in range(2)
    ]
    received = (
        from_behind(grad_mixed[0][:, :2].astype(jnp.bfloat16), "seq", -1).astype(jnp.float32),
        from_behind(grad_mixed[1][:, :2].astype(jnp.bfloat16), "seq", -1).astype(jnp.float32),
    )
    kernel = back_weights[4].astype(jnp.float32)
    params = back_weights[5].astype(jnp.float32)
    w_qkv_full = back_weights[0]
    grad_qkv = jnp.zeros(w_qkv_full.shape, jnp.float32)
    grad_kernel = jnp.zeros(kernel.shape, jnp.float32)
    grad_norm = jnp.zeros((4, model_width), jnp.float32)
    grad_out = partials[0][3] + partials[1][3]
    grad_up = partials[0][4] + partials[1][4]
    grad_down = partials[0][5] + partials[1][5]
    input_grads = []
    for index_part in range(2):
        flat, normal_one, inverse_one, normed_low, padded, mixed = fronts_back[index_part]
        seq_count, block_rows, three_width = mixed.shape
        mixed_grad = grad_mixed[index_part]
        extended = jnp.concatenate([mixed_grad, received[index_part]], axis=1)
        grad_projected = (
            kernel[0] * extended[:, :block_rows]
            + kernel[1] * extended[:, 1 : block_rows + 1]
            + kernel[2] * extended[:, 2:]
        ).astype(jnp.bfloat16)
        grad_kernel = grad_kernel + jnp.stack(
            [
                jnp.sum(mixed_grad * padded[:, 2:], axis=(0, 1)),
                jnp.sum(mixed_grad * padded[:, 1 : block_rows + 1], axis=(0, 1)),
                jnp.sum(mixed_grad * padded[:, :block_rows], axis=(0, 1)),
            ]
        )
        grad_flat = grad_projected.reshape(seq_count * block_rows, three_width)
        grad_qkv = grad_qkv + jnp.dot(normed_low.T, grad_flat, preferred_element_type=jnp.float32)
        grad_normed = jnp.dot(grad_flat, w_qkv_full.T, preferred_element_type=jnp.float32)
        grad_input = partials[index_part][2] + norm_back_flat(
            grad_normed, normal_one, inverse_one, params[0]
        )
        input_grads.append(grad_input.reshape(seq_count, block_rows, model_width))
        norm_two = partials[index_part][6]
        grad_norm = grad_norm + jnp.stack(
            [
                jnp.sum(grad_normed * normal_one, axis=0),
                jnp.sum(grad_normed, axis=0),
                norm_two[0],
                norm_two[1],
            ]
        )
    summed = (
        lax.psum_scatter(grad_qkv, ("seq", "batch"), scatter_dimension=0, tiled=True),
        lax.psum_scatter(grad_out, ("seq", "batch"), scatter_dimension=0, tiled=True),
        lax.psum_scatter(grad_up, ("seq", "batch"), scatter_dimension=0, tiled=True),
        lax.psum_scatter(grad_down, ("seq", "batch"), scatter_dimension=0, tiled=True),
        lax.psum_scatter(grad_kernel, ("seq", "batch"), scatter_dimension=1, tiled=True),
        lax.psum_scatter(grad_norm, ("seq", "batch"), scatter_dimension=1, tiled=True),
    )
    return (
        outputs[0],
        outputs[1],
        input_grads[0],
        input_grads[1],
        summed[0],
        summed[1],
        summed[2],
        summed[3],
        summed[4],
        summed[5],
    )


def solution(mesh):
    split = mesh.shape["seq"] == 8
    return jax.shard_map(
        split_body if split else general_body,
        mesh=mesh,
        in_specs=(
            P("batch", "seq", None),
            P("batch", "seq", None),
            P(None, "batch"),
            P("batch", "seq", None),
            P("batch", "seq", None),
            P(("seq", "batch"), None),
            P(("seq", "batch"), None),
            P(("seq", "batch"), None),
            P(("seq", "batch"), None),
            P(None, ("seq", "batch")),
            P(None, ("seq", "batch")),
        ),
        out_specs=(
            P("batch", "seq", None),
            P("batch", "seq", None),
            P("batch", "seq", None),
            P("batch", "seq", None),
            P(("seq", "batch"), None),
            P(("seq", "batch"), None),
            P(("seq", "batch"), None),
            P(("seq", "batch"), None),
            P(None, ("seq", "batch")),
            P(None, ("seq", "batch")),
        ),
        check_vma=False,
    )
```

```python
import functools

import jax
import jax.numpy as jnp
from jax import lax
from jax.experimental import pallas as pl
from jax.experimental.pallas import tpu as pltpu
from jax.sharding import PartitionSpec as P

EPS = 1e-05
NEG_FILL = -1e30
HEAD_DIM = 64
LANES = 128
TRIPLE = 3 * LANES
TILE = 256
PAD = 16
MESH = pl.DeviceIdType.MESH
F32 = jnp.float32
BF16 = jnp.bfloat16
DMA = pltpu.SemaphoreType.DMA


def dot_nn(left, right):
    return lax.dot_general(left, right, (((1,), (0,)), ((), ())), preferred_element_type=F32)


def dot_nt(left, right):
    return lax.dot_general(left, right, (((1,), (1,)), ((), ())), preferred_element_type=F32)


def dot_tn(left, right):
    return lax.dot_general(left, right, (((0,), (0,)), ((), ())), preferred_element_type=F32)


def params_of(limit=60, **more):
    return pltpu.CompilerParams(vmem_limit_bytes=limit * 2**20, **more)


def vmem():
    return pl.BlockSpec(memory_space=pltpu.VMEM)


def smem():
    return pl.BlockSpec(memory_space=pltpu.SMEM)


def hbm():
    return pl.BlockSpec(memory_space=pl.ANY)


def normalise(values):
    average = jnp.mean(values, axis=-1, keepdims=True)
    centred = values - average
    inverse = lax.rsqrt(jnp.mean(centred * centred, axis=-1, keepdims=True) + EPS)
    return centred * inverse, inverse


def norm_back(grad, normal, inverse, gain):
    scaled_grad = grad * gain
    first_mean = jnp.mean(scaled_grad, axis=-1, keepdims=True)
    second_mean = jnp.mean(scaled_grad * normal, axis=-1, keepdims=True)
    return inverse * (scaled_grad - first_mean - normal * second_mean)


def shifted(window, by):
    return pltpu.roll(window, by % window.shape[0], 0)


def iota(shape, axis):
    return lax.broadcasted_iota(jnp.int32, shape, axis)


def times(index, size):
    return pl.ds(pl.multiple_of(index * size, size), size)


def position():
    index, batch = lax.axis_index("seq"), lax.axis_index("batch")
    return index // 2, index % 2, batch // 2, batch % 2


def at(z, core, y, x):
    return (z * 2 + core, y * 2 + x)


def remote(src, dst, send, recv, device):
    return pltpu.make_async_remote_copy(
        src_ref=src, dst_ref=dst, send_sem=send, recv_sem=recv, device_id=device, device_id_type=MESH
    )


def greet(others):
    barrier = pltpu.get_barrier_semaphore()
    for other in others:
        pl.semaphore_signal(barrier, inc=1, device_id=other, device_id_type=MESH)
    pl.semaphore_wait(barrier, len(others))


def whole_line():
    z, core, y, x = position()
    line = [at(lax.rem(z + step, 4), (core + turn) % 2, y, x) for turn in (0, 1) for step in (0, 1, 2, 3)]
    return line[1:]


def greet_all():
    z, core, y, x = position()
    greet(whole_line() + [at(z, core, 1 - y, x), at(z, core, y, 1 - x)])


def roles():
    z = lax.axis_index("seq") // 2
    half = z // 2
    near = jnp.where(half == 0, z, 3 - z)
    partner_z = jnp.where(half == 0, 1 - z, 5 - z)
    return half, near, partner_z, 2 - half


def z_of(half, place):
    return jnp.where(half == 0, place, 3 - place)


def long_source(seq, pair):
    near = 1 if pair % 3 == 2 else 0
    z = near if seq == 0 else 3 - near
    return z * 2 + pair // 3, 0 if near else pair % 3


def short_source(seq, pair):
    return (1 if seq == 0 else 2) * 2 + pair // 3, pair % 3


class Copies:
    def __init__(self, sems):
        self.sems, self.count, self.open = sems, 0, []

    def start(self, src, dst):
        copy = pltpu.make_async_copy(src, dst, self.sems.at[self.count])
        self.count += 1
        copy.start()
        self.open.append(copy)
        return copy

    def finish(self):
        for copy in self.open:
            copy.wait()
        self.open = []


class RowGather:
    def __init__(self, x_ref, o_ref, own_sem, send, recv, sib_send, sib_recv, inner_only):
        self.x_ref, self.o_ref, self.inner_only = x_ref, o_ref, inner_only
        self.own_sem, self.send, self.recv, self.sib_send, self.sib_recv = own_sem, send, recv, sib_send, sib_recv
        self.rows = x_ref.shape[1]
        self.z, self.core, self.y, self.x = position()
        self.half, self.near, self.partner_z, far_z = roles()
        self.sibling = at(self.z, 1 - self.core, self.y, self.x)
        self.partner = at(self.partner_z, self.core, self.y, self.x)
        place = self.block(self.z, self.core)
        mine, other = self.x_ref.at[self.half], self.x_ref.at[1 - self.half]
        self.to_partner = remote(mine, place, send.at[0], recv.at[self.near], self.partner)
        self.to_far = remote(other, place, send.at[1], recv.at[3 - self.near], at(far_z, self.core, self.y, self.x))
        self.to_sibling = remote(mine, place, sib_send.at[0], sib_recv.at[self.near], self.sibling)
        self.own = pltpu.make_async_copy(mine, place, own_sem)

    def block(self, z, core):
        return self.o_ref.at[times(z * 2 + core, self.rows)]

    def at_inner(self, act):
        if self.inner_only:
            pl.when(self.near == 1)(act)
        else:
            act()

    def start(self):
        if self.inner_only:
            pl.when(self.near == 0)(self.to_partner.start)
        else:
            self.to_partner.start()
        pl.when(self.near == 1)(self.to_far.start)

        def inside():
            self.to_sibling.start()
            self.own.start()

        self.at_inner(inside)

    def start_far(self):
        @pl.when(self.near == 0)
        def _():
            self.to_partner.wait_send()
            self.to_far.start()

    def moves(self, slot):
        place = (1 - self.near, 2, 3)[slot]
        block = self.block(z_of(self.half, place), self.core)
        arrival = remote(block, block, self.send.at[0], self.recv.at[place], self.partner)
        onward = remote(block, block, self.send.at[1 + slot], self.recv.at[place], self.partner)
        across = remote(block, block, self.sib_send.at[1 + slot], self.sib_recv.at[place], self.sibling)
        return arrival, onward, across

    def step(self, slot):
        arrival, onward, across = self.moves(slot)

        def inside():
            arrival.wait_recv()
            if slot and not self.inner_only:
                pl.when(self.near == 1)(onward.start)
            across.start()

        self.at_inner(inside)

    def whole(self, place):
        where = (self.near, 1 - self.near, 2, 3)[place]
        block = self.block(z_of(self.half, where), 1 - self.core)

        def inside():
            remote(block, block, self.sib_send.at[0], self.sib_recv.at[where], self.sibling).wait_recv()
            if place == 0:
                self.own.wait()

        self.at_inner(inside)

    def chip_rows(self, place):
        return z_of(self.half, (self.near, 1 - self.near, 2, 3)[place])

    def finish(self):
        if not self.inner_only:
            pl.when(self.near == 1)(self.to_partner.wait_send)
        self.to_far.wait_send()

        def inside():
            self.to_sibling.wait_send()
            for slot in range(3):
                _, onward, across = self.moves(slot)
                across.wait_send()
                if slot and not self.inner_only:
                    pl.when(self.near == 1)(onward.wait_send)

        self.at_inner(inside)


class ShardGather:
    def __init__(self, shard, full, own_sem, send, recv, halves=False):
        self.shard, self.full, self.own_sem, self.send_sem, self.recv_sem = shard, full, own_sem, send, recv
        self.z, self.core, self.y, self.x = position()
        self.halves = halves
        self.sent = []

    def go(self, src, dst, slot, device):
        copy = remote(src, dst, self.send_sem.at[slot], self.recv_sem.at[slot], device)
        copy.start()
        self.sent.append(copy)

    def arrived(self, dst, slot):
        remote(dst, dst, self.send_sem.at[0], self.recv_sem.at[slot], at(self.z, self.core, self.y, self.x)).wait_recv()

    def start(self):
        z, core, y, x = self.z, self.core, self.y, self.x
        mine = self.full.at[z, core, y, x]
        for step in (1, 2, 3):
            target = lax.rem(z + step, 4)
            self.go(self.shard, mine, step, at(target, core, y, x))
        self.own = pltpu.make_async_copy(self.shard, mine, self.own_sem)
        self.own.start()

    def part(self, core, zs, ys, xs, reader):
        ref = self.full.at[zs, core, ys, xs]
        return self.full.at[zs, core, ys, xs, reader] if self.halves else ref

    def across(self, zs, ys, xs, slot):
        ref = self.part(self.core, zs, ys, xs, 1 - self.core)
        self.go(ref, ref, slot, at(self.z, 1 - self.core, self.y, self.x))

    def over(self):
        z, core, y, x = self.z, self.core, self.y, self.x
        for step in (1, 2, 3):
            self.arrived(self.full.at[lax.rem(z + 4 - step, 4), core, y, x], step)
        self.own.wait()
        first, second = pl.ds(0, 2), pl.ds(2, 2)
        ref = self.full.at[first, core, y, x]
        self.go(ref, ref, 4, at(z, core, y, 1 - x))
        ref = self.full.at[second, core, y, x]
        self.go(ref, ref, 5, at(z, core, 1 - y, x))
        self.across(pl.ds(0, 4), y, x, 8)

    def turn(self):
        z, core, y, x = self.z, self.core, self.y, self.x
        first, second = pl.ds(0, 2), pl.ds(2, 2)
        self.arrived(self.full.at[first, core, y, 1 - x], 4)
        ref = self.full.at[first, core, y]
        self.go(ref, ref, 6, at(z, core, 1 - y, x))
        self.across(first, y, 1 - x, 9)
        self.arrived(self.full.at[second, core, 1 - y, x], 5)
        ref = self.full.at[second, core, :, x]
        self.go(ref, ref, 7, at(z, core, y, 1 - x))
        self.across(second, 1 - y, x, 10)

    def last(self):
        core, y, x = self.core, self.y, self.x
        first, second = pl.ds(0, 2), pl.ds(2, 2)
        self.arrived(self.full.at[first, core, 1 - y], 6)
        self.across(first, 1 - y, pl.ds(0, 2), 11)
        self.arrived(self.full.at[second, core, :, 1 - x], 7)
        self.across(second, pl.ds(0, 2), 1 - x, 12)

    def finish(self):
        y, x, core, other = self.y, self.x, self.core, 1 - self.core
        first, second, both = pl.ds(0, 2), pl.ds(2, 2), pl.ds(0, 2)
        parts = (
            (pl.ds(0, 4), y, x), (first, y, 1 - x), (second, 1 - y, x), (first, 1 - y, both), (second, both, 1 - x),
        )
        for slot, (zs, ys, xs) in enumerate(parts):
            self.arrived(self.part(other, zs, ys, xs, core), 8 + slot)

    def sends_done(self):
        for copy in self.sent:
            copy.wait_send()


def add_into(total, part):
    total[...] = (total[...].astype(F32) + part[...].astype(F32)).astype(total.dtype)


class CoreSum:
    def __init__(self, grad, sib, out, send, recv, save, hop=None):
        self.grad, self.sib, self.out, self.save = grad, sib, out, save
        self.z, self.core, self.y, self.x = position()
        z, core, y, x = position()
        self.copy = remote(grad.at[:, 1 - core], sib, send.at[0], recv.at[0], at(z, 1 - core, y, x))
        self.hop = hop
        first, second = pl.ds(0, 2), pl.ds(2, 2)
        if hop is not None:
            self.hops = (
                remote(sib.at[first, :, 1 - x], hop.at[0], send.at[1], recv.at[1], at(z, core, y, 1 - x)),
                remote(sib.at[second, 1 - y], hop.at[1], send.at[2], recv.at[2], at(z, core, 1 - y, x)),
            )

    def start(self):
        self.copy.start()

    def keep(self, *moves):
        self.kept = [pltpu.make_async_copy(src, dst, self.save.at[i]) for i, (src, dst) in enumerate(moves)]
        for copy in self.kept:
            copy.start()

    def add(self):
        self.copy.wait_recv()

        @pl.loop(0, 4)
        def _(zz):
            for ys in range(2):
                for xs in range(2):
                    add_into(self.sib.at[zz, ys, xs], self.grad.at[zz, self.core, ys, xs])

        if self.hop is None:
            self.keep((self.sib, self.out))
        else:
            for copy in self.hops:
                copy.start()

    def add_hop(self):
        x, y = self.x, self.y
        self.hops[0].wait_recv()
        for zz in range(2):
            for ys in range(2):
                add_into(self.sib.at[zz, ys, x], self.hop.at[0, zz, ys])
        self.hops[1].wait_recv()
        for zz in range(2):
            for xs in range(2):
                add_into(self.sib.at[2 + zz, y, xs], self.hop.at[1, zz, xs])
        self.keep(
            (self.sib.at[pl.ds(0, 2), :, x], self.out.at[0]),
            (self.sib.at[pl.ds(2, 2), y], self.out.at[1]),
        )

    def finish(self):
        self.copy.wait_send()
        for copy in self.kept:
            copy.wait()
        if self.hop is not None:
            for copy in self.hops:
                copy.wait_send()


class ShardSum:
    def __init__(self, grad, out, bufs, own_sem, send, recv, begun=False):
        self.grad, self.out, self.begun = grad, out, begun
        self.near_x, self.near_y, self.two, self.line = bufs[:4]
        self.one = None if begun else bufs[4]
        self.own_sem, self.send_sem, self.recv_sem = own_sem, send, recv
        self.z, self.core, self.y, self.x = position()
        self.sent = []
        first, second = pl.ds(0, 2), pl.ds(2, 2)
        self.loads = (
            pltpu.make_async_copy(grad.at[0] if begun else grad.at[first, :, self.x], self.near_x, own_sem.at[0]),
            pltpu.make_async_copy(grad.at[1] if begun else grad.at[second, self.y], self.near_y, own_sem.at[1]),
        )

    def copy(self, src, dst, slot, device):
        return remote(src, dst, self.send_sem.at[slot], self.recv_sem.at[slot], device)

    def go(self, src, dst, slot, device):
        copy = self.copy(src, dst, slot, device)
        copy.start()
        self.sent.append(copy)

    def arrived(self, dst, slot):
        remote(dst, dst, self.send_sem.at[0], self.recv_sem.at[slot], at(self.z, self.core, self.y, self.x)).wait_recv()

    def moves(self):
        z, core, y, x = self.z, self.core, self.y, self.x
        first, second = pl.ds(0, 2), pl.ds(2, 2)
        return ([] if self.begun else [
            self.copy(self.grad.at[first, :, 1 - x], self.one.at[0], 2, at(z, core, y, 1 - x)),
            self.copy(self.grad.at[second, 1 - y], self.one.at[1], 3, at(z, core, 1 - y, x)),
        ]) + [
            self.copy(self.near_x.at[:, 1 - y], self.two.at[0], 4, at(z, core, 1 - y, x)),
            self.copy(self.near_y.at[:, 1 - x], self.two.at[1], 5, at(z, core, y, 1 - x)),
        ]

    def to_line(self, step):
        z, core, y, x = self.z, self.core, self.y, self.x
        target = lax.rem(z + step, 4)
        device = at(target, core, y, x)
        low = self.copy(self.near_x.at[lax.rem(target, 2), y], self.line.at[step - 1], 5 + step, device)
        high = self.copy(self.near_y.at[lax.rem(target, 2), x], self.line.at[step - 1], 5 + step, device)
        return target, low, high

    def start(self):
        for copy in self.moves()[:-2]:
            copy.start()
        for copy in self.loads:
            copy.start()

    def turn(self):
        moves = self.moves()
        for side, near in enumerate((self.near_x, self.near_y)):
            self.loads[side].wait()
            if not self.begun:
                self.arrived(self.one.at[side], 2 + side)
                for zz in range(2):
                    for other in range(2):
                        add_into(near.at[zz, other], self.one.at[side, zz, other])
            moves[side - 2].start()

    def last(self):
        y, x = self.y, self.x
        self.arrived(self.two.at[0], 4)
        for zz in range(2):
            add_into(self.near_x.at[zz, y], self.two.at[0, zz])
        self.arrived(self.two.at[1], 5)
        for zz in range(2):
            add_into(self.near_y.at[zz, x], self.two.at[1, zz])
        for step in (1, 2, 3):
            target, low, high = self.to_line(step)
            pl.when(target < 2)(low.start)
            pl.when(target >= 2)(high.start)

    def finish(self):
        z, y, x = self.z, self.y, self.x
        low = self.near_x[lax.rem(z, 2), y].astype(F32)
        high = self.near_y[lax.rem(z, 2), x].astype(F32)
        total = jnp.where(z < 2, low, high)
        for step in (1, 2, 3):
            self.arrived(self.line.at[step - 1], 5 + step)
            total = total + self.line[step - 1].astype(F32)
        self.out[...] = total
        for copy in self.moves():
            copy.wait_send()
        for step in (1, 2, 3):
            target, low, high = self.to_line(step)
            pl.when(target < 2)(low.wait_send)
            pl.when(target >= 2)(high.wait_send)

    @staticmethod
    def buffers(grad, begun=False):
        tail, kind = grad.shape[3:], grad.dtype
        shapes = [(2, 2), (2, 2), (2, 2), (3,)] + ([] if begun else [(2, 2, 2)])
        return [pltpu.VMEM(shape + tail, kind) for shape in shapes]


class GroupSum:
    def __init__(self, bufs, send, recv):
        self.tot, self.one, self.two, self.line = bufs
        self.send_sem, self.recv_sem = send, recv
        self.z, self.core, self.y, self.x = position()
        self.sent = []

    copy = ShardSum.copy
    go = ShardSum.go
    arrived = ShardSum.arrived

    def start(self, total, columns):
        z, core, y, x = self.z, self.core, self.y, self.x
        rows = self.tot.shape[4]

        @pl.loop(0, 4)
        def _(zz):
            for cc in range(2):
                for yy in range(2):
                    for xx in range(2):
                        first = pl.multiple_of(zz * 8 * rows, 8) + ((cc * 2 + yy) * 2 + xx) * rows
                        part = total[pl.ds(pl.multiple_of(first, 8), rows), columns]
                        self.tot[zz, cc, yy, xx] = part.astype(BF16)

        self.go(self.tot.at[pl.ds(0, 2), :, :, 1 - x], self.one.at[0], 0, at(z, core, y, 1 - x))
        self.go(self.tot.at[pl.ds(2, 2), :, 1 - y], self.one.at[1], 1, at(z, core, 1 - y, x))

    def turn(self):
        z, core, y, x = self.z, self.core, self.y, self.x
        self.arrived(self.one.at[0], 0)

        @pl.loop(0, 2)
        def _(zz):
            for cc in range(2):
                for ys in range(2):
                    add_into(self.tot.at[zz, cc, ys, x], self.one.at[0, zz, cc, ys])

        self.go(self.tot.at[pl.ds(0, 2), :, 1 - y, x], self.two.at[0], 2, at(z, core, 1 - y, x))
        self.arrived(self.one.at[1], 1)

        @pl.loop(0, 2)
        def _(zz):
            for cc in range(2):
                for xs in range(2):
                    add_into(self.tot.at[2 + zz, cc, y, xs], self.one.at[1, zz, cc, xs])

        self.go(self.tot.at[pl.ds(2, 2), :, y, 1 - x], self.two.at[1], 3, at(z, core, y, 1 - x))

    def last(self):
        z, core, y, x = self.z, self.core, self.y, self.x
        for side in (0, 1):
            self.arrived(self.two.at[side], 2 + side)

            @pl.loop(0, 2)
            def _(zz, side=side):
                for cc in range(2):
                    add_into(self.tot.at[2 * side + zz, cc, y, x], self.two.at[side, zz, cc])

        mine = z * 2 + core
        for step in range(1, 8):
            target = lax.rem(mine + step, 8)
            tz, tc = target // 2, target % 2
            self.go(self.tot.at[tz, tc, y, x], self.line.at[step - 1], 3 + step, at(tz, tc, y, x))

    def finish(self):
        for step in range(1, 8):
            self.arrived(self.line.at[step - 1], 3 + step)
        for copy in self.sent:
            copy.wait_send()

    def term(self, source):
        z, core, y, x = self.z, self.core, self.y, self.x
        back = lax.rem(z * 2 + core - source + 8 + 7, 8)
        own = self.tot[z, core, y, x].astype(F32)
        return jnp.where(back == 7, own, self.line[jnp.minimum(back, 6)].astype(F32))

    @staticmethod
    def buffers(rows, columns):
        return [
            pltpu.VMEM((4, 2, 2, 2, rows, columns), BF16),
            pltpu.VMEM((2, 2, 2, 2, rows, columns), BF16),
            pltpu.VMEM((2, 2, 2, rows, columns), BF16),
            pltpu.VMEM((7, rows, columns), BF16),
        ]


def join_groups(first, second, out):
    width = out.shape[1] // 3
    for side in range(2):
        early = None
        for z in range(4):
            term = first.term(z * 2 + side)
            early = term if early is None else early + term
        outer = second.term(side) + second.term(6 + side)
        inner = second.term(2 + side) + second.term(4 + side)
        pairs = (early[:, :TRIPLE], early[:, TRIPLE:] + outer, inner)
        for j, pair in enumerate(pairs):
            for kind in range(3):
                target = kind * width + (3 * side + j) * LANES
                out[:, target : target + LANES] = pair[:, kind * LANES : (kind + 1) * LANES]


class SmallSum:
    def __init__(self, bufs, out, send, recv):
        self.norms, self.swap, self.acc, self.got, self.line = bufs
        self.out, self.send_sem, self.recv_sem = out, send, recv
        self.z, self.core, self.y, self.x = position()
        self.sent = []
        self.cut = self.norms.shape[2]

    copy = ShardSum.copy
    go = ShardSum.go
    arrived = ShardSum.arrived

    def start(self, kernel_grad, norm_grad):
        z, core, y, x = self.z, self.core, self.y, self.x
        cut = self.cut
        self.norms[0] = norm_grad[:, :cut]
        self.norms[1] = norm_grad[:, cut:]
        self.acc[0, :, : kernel_grad.shape[1]] = kernel_grad
        self.go(self.norms.at[1 - core], self.swap, 0, at(z, 1 - core, y, x))

    def over(self):
        z, core, y, x = self.z, self.core, self.y, self.x
        self.arrived(self.swap, 0)
        self.acc[0, :, self.acc.shape[2] - self.cut :] = self.norms[core] + self.swap[...]
        self.go(self.acc.at[0], self.got.at[0], 1, at(z, core, y, 1 - x))

    def turn(self):
        z, core, y, x = self.z, self.core, self.y, self.x
        self.arrived(self.got.at[0], 1)
        self.acc[1] = self.acc[0] + self.got[0]
        self.go(self.acc.at[1], self.got.at[1], 2, at(z, core, 1 - y, x))

    def last(self):
        z, core, y, x = self.z, self.core, self.y, self.x
        self.arrived(self.got.at[1], 2)
        self.acc[2] = self.acc[1] + self.got[1]
        for step in (1, 2, 3):
            self.go(self.acc.at[2], self.line.at[step - 1], 2 + step, at(lax.rem(z + step, 4), core, y, x))

    def swap_back(self):
        z, core, y, x = self.z, self.core, self.y, self.x
        for step in (1, 2, 3):
            self.arrived(self.line.at[step - 1], 2 + step)
        total = None
        for source in range(4):
            back = lax.rem(z - source + 4, 4)
            term = jnp.where(back == 0, self.acc[2], self.line[jnp.maximum(back - 1, 0)])
            total = term if total is None else total + term
        self.out[core] = total
        self.go(self.out.at[core], self.out.at[core], 6, at(z, 1 - core, y, x))

    def finish(self):
        self.arrived(self.out.at[1 - self.core], 6)
        for copy in self.sent:
            copy.wait_send()

    @staticmethod
    def buffers(columns, norm_columns):
        wide = columns + norm_columns
        return [
            pltpu.VMEM((2, 8, norm_columns), F32),
            pltpu.VMEM((8, norm_columns), F32),
            pltpu.VMEM((3, 8, wide), F32),
            pltpu.VMEM((2, 8, wide), F32),
            pltpu.VMEM((3, 8, wide), F32),
        ]


def causal_mask():
    return iota((TILE, TILE), 0) <= iota((TILE, TILE), 1)


def place_small(smalls, kernel_out, norm_out, core, part, cut):
    wide, width = kernel_out.shape[1], norm_out.shape[1]
    column = iota((LANES, wide), 1)
    block, lane = column // LANES, column % LANES
    source = (block % 3) * width + (core * 3 + block // 3) * LANES + lane - iota((LANES, wide), 0)
    norm_source = iota((LANES, width), 1) - iota((LANES, width), 0)
    kernel_out[...] = jnp.zeros_like(kernel_out)
    norm_out[...] = jnp.zeros_like(norm_out)

    @pl.loop(0, smalls.shape[0])
    def _(device):
        low = smalls[device].astype(BF16)
        kernel_out[...] += dot_nn(low, jnp.where(source == device * part, 1.0, 0.0).astype(BF16))
        norm_out[...] += dot_nn(low, jnp.where(norm_source == device * cut, 1.0, 0.0).astype(BF16))

    norm_out[0:4] = norm_out[3:7]


def attend(query_ref, key_ref, value_t, lse, out_t, head, block):
    rows, past = slice(block * TILE, (block + 1) * TILE), slice(0, block * TILE)
    query = query_ref[head, rows]
    diagonal = jnp.where(causal_mask(), dot_nt(key_ref[head, rows], query), NEG_FILL)
    top = jnp.max(diagonal, axis=0, keepdims=True)
    if block:
        before = dot_nt(key_ref[head, past], query)
        top = jnp.maximum(top, jnp.max(before, axis=0, keepdims=True))
        exp_before = jnp.exp(before - top)
    exp_diagonal = jnp.exp(diagonal - top)
    norm = jnp.sum(exp_diagonal, axis=0, keepdims=True)
    if block:
        norm = norm + jnp.sum(exp_before, axis=0, keepdims=True)
    lse[head, :, rows] = top + jnp.log(norm)
    inverse = 1.0 / norm
    result = dot_nn(value_t[head, :, rows], (exp_diagonal * inverse).astype(BF16))
    if block:
        result = result + dot_nn(value_t[head, :, past], (exp_before * inverse).astype(BF16))
    out_t[head, :, rows] = result


def convolve(proj, taps, slot, local, start, length, query_ref, key_ref, value_ref, key_t, value_t):
    window = proj[slot, pl.ds(pl.multiple_of(start, PAD), TILE + PAD)].astype(F32)
    columns = times(local, TRIPLE)
    mixed = (
        taps[0:1, columns] * window[PAD:]
        + taps[1:2, columns] * shifted(window, 1)[PAD:]
        + taps[2:3, columns] * shifted(window, 2)[PAD:]
    ).astype(BF16).astype(F32)
    query, key, value = mixed[:, 0:LANES] * (HEAD_DIM**-0.5), mixed[:, LANES : 2 * LANES], mixed[:, 2 * LANES :]
    rows = pl.ds(pl.multiple_of(start, TILE), TILE)
    lanes = iota((TILE, LANES), 1)
    low_half = lanes < HEAD_DIM
    bias = jnp.where(start + iota((TILE, LANES), 0) < length, 0.0, NEG_FILL)
    at_zero, at_half = lanes == 0, lanes == HEAD_DIM
    query_ref[2 * slot, rows] = jnp.where(low_half, query, jnp.where(at_half, 1.0, 0.0)).astype(BF16)
    query_ref[2 * slot + 1, rows] = jnp.where(low_half, jnp.where(at_zero, 1.0, 0.0), query).astype(BF16)
    key_ref[2 * slot, rows] = jnp.where(low_half, key, jnp.where(at_half, bias, 0.0)).astype(BF16)
    key_ref[2 * slot + 1, rows] = jnp.where(low_half, jnp.where(at_zero, bias, 0.0), key).astype(BF16)
    value_ref[slot, rows] = value.astype(BF16)
    turned_key, turned_value = key.T.astype(BF16), value.T.astype(BF16)
    for head in range(2):
        part = slice(head * HEAD_DIM, (head + 1) * HEAD_DIM)
        key_t[2 * slot + head, :, rows] = turned_key[part]
        value_t[2 * slot + head, :, rows] = turned_value[part]


def first_kernel(
    lens, xs_ref, xl_ref, qkv_ref, conv_ref, norm_ref, out_s, up_s, down_s,
    att, full_out, full_up, full_down, xs_o, xl_o, wq_o, taps_o, norms_o,
    ql_o, kl_o, vl_o, ktl_o, lsel_o, pl_o, ol_o, qs_o, ks_o, vs_o, kts_o, lses_o, ps_o, os_o,
    xs, xl, small, smalls, shard, wq_parts, wq, taps, norms,
    ql, kl, vl, ktl, lsel, proj_l, ol, qs, ks, vs, kts, lses, proj_s, os,
    vtl, vts, otl, ots,
    own_sem, send, recv, sib_send, sib_recv, shard_own, shard_send, shard_recv,
    att_send_l, att_recv_l, att_send_s, att_recv_s, att_own_l, att_own_s, save_sem,
):
    z, core, y, x = position()
    half, near, _, _ = roles()
    index = z * 2 + core
    pairs_long = 2 - near
    own_short, own_long = xs_ref.shape[1], xl_ref.shape[1]
    long_rows, short_rows = xl.shape[0], xs.shape[0]
    part, cut = conv_ref.shape[1], norm_ref.shape[1]
    length_short = jnp.where(half == 0, lens[0, 0], lens[0, 1])
    length_long = jnp.where(half == 0, lens[1, 0], lens[1, 1])

    small[...] = jnp.zeros_like(small)
    small[0:3, 0:part] = conv_ref[...].astype(F32)
    small[3:7, 0:cut] = norm_ref[...].astype(F32)
    width = wq.shape[0]
    for side in range(2):
        for j in range(3):
            for kind in range(3):
                source = kind * width + (3 * side + j) * LANES
                target = (3 * j + kind) * LANES
                shard[side, :, target : target + LANES] = qkv_ref[:, source : source + LANES]
    greet_all()
    rows_short = RowGather(
        xs_ref, xs, own_sem.at[0], send.at[0], recv.at[0], sib_send.at[0], sib_recv.at[0], True
    )
    rows_long = RowGather(
        xl_ref, xl, own_sem.at[1], send.at[1], recv.at[1], sib_send.at[1], sib_recv.at[1], False
    )
    weights = [
        ShardGather(a, f, shard_own.at[i], shard_send.at[i], shard_recv.at[i], halves=i == 1)
        for i, (a, f) in enumerate(
            ((small, smalls), (shard, wq_parts), (out_s, full_out), (up_s, full_up), (down_s, full_down))
        )
    ]
    small_w, qkv_w, out_w, up_w, down_w = weights

    def place():
        place_small(smalls.reshape(32, 8, LANES), taps, norms, core, part, cut)

    def join_weights():
        pieces = wq_parts.shape[5]
        for zz in range(4):
            for cc in range(2):
                for yy in range(2):
                    first = ((zz * 2 + cc) * 2 + yy) * 2 * pieces
                    both = jnp.concatenate([wq_parts[zz, cc, yy, xx, core].astype(F32) for xx in range(2)], axis=0)
                    wq[first : first + 2 * pieces] = both.astype(BF16)

    def project(x_ref, proj, start, size, slots, first_pair):
        normal, _ = normalise(x_ref[pl.ds(pl.multiple_of(start, size), size)].astype(F32))
        low = (normal * norms[0:1] + norms[1:2]).astype(BF16)

        @pl.loop(0, slots)
        def _(slot):
            result = dot_nn(low, wq[:, times(slot + first_pair, TRIPLE)])
            proj[slot, pl.ds(pl.multiple_of(PAD + start, PAD), size)] = result.astype(BF16)

    def project_long(place):
        @pl.loop(0, 2)
        def _(side):
            project(xl, proj_l, rows_long.chip_rows(place) * 2 * own_long + side * TILE, TILE, pairs_long, 2 * near)

    def project_short(place):
        @pl.when(near == 1)
        def _():
            project(xs, proj_s, rows_short.chip_rows(place) * 2 * own_short, TILE, 3, 0)

    def conv_short():
        @pl.when(near == 1)
        def _():
            @pl.loop(0, 3)
            def _(slot):
                @pl.loop(0, short_rows // TILE)
                def _(step):
                    convolve(proj_s, taps, slot, slot, step * TILE, length_short, qs, ks, vs, kts, vts)

    def conv_long():
        @pl.loop(0, pairs_long)
        def _(slot):
            @pl.loop(0, long_rows // TILE)
            def _(step):
                convolve(proj_l, taps, slot, slot + 2 * near, step * TILE, length_long, ql, kl, vl, ktl, vtl)

    saves = Copies(save_sem)

    def save(*moves):
        for source, target in moves:
            saves.start(source, target)

    def save_long():
        save((xl, xl_o), (wq, wq_o), (taps, taps_o), (norms, norms_o))
        save((ql, ql_o), (kl, kl_o), (vl, vl_o), (ktl, ktl_o), (proj_l, pl_o))

    def save_short():
        save((xs, xs_o), (qs, qs_o), (ks, ks_o), (vs, vs_o))
        save((kts, kts_o), (proj_s, ps_o), (lses, lses_o), (os, os_o))

    def save_last():
        save((lsel, lsel_o), (ol, ol_o))

    def to_owner(o_ref, slot, first, rows, owner, row_in_owner, pair, send_sem, recv_sem, own_sem):
        source = o_ref.at[slot, pl.ds(first, rows)]
        target = att.at[
            pl.ds(pl.multiple_of(row_in_owner, LANES), rows), times(pair, LANES)
        ]
        far = remote(source, target, send_sem, recv_sem, (owner, y * 2 + x))
        close = pltpu.make_async_copy(source, target, own_sem)
        return far, close

    def short_moves(slot, owner):
        return to_owner(
            os, slot, owner * own_short, own_short, owner, 2 * own_long + half * own_short, 3 * core + slot,
            att_send_s.at[slot, owner], att_recv_s.at[half, 3 * core + slot], att_own_s.at[slot],
        )

    def long_moves(slot, owner):
        pair = 3 * core + slot + 2 * near
        return to_owner(
            ol, slot, owner * own_long, own_long, owner, half * own_long, pair,
            att_send_l.at[slot, owner], att_recv_l.at[half, pair], att_own_l.at[slot],
        )

    def send_block(o_ref, o_t, slot, block, moves, owners):
        rows = slice(block * TILE, (block + 1) * TILE)
        both = jnp.concatenate([o_t[2 * slot, :, rows], o_t[2 * slot + 1, :, rows]], axis=0)
        o_ref[slot, rows] = both.T.astype(BF16)
        for owner in owners:
            far, close = moves(slot, owner)
            pl.when(index != owner)(far.start)
            pl.when(index == owner)(close.start)

    def attend_short(block):
        @pl.when(near == 1)
        def _():
            @pl.loop(0, 6)
            def _(head):
                attend(qs, ks, vts, lses, ots, head, block)

    def send_short(block):
        @pl.when(near == 1)
        def _():
            @pl.loop(0, 3)
            def _(slot):
                send_block(os, ots, slot, block, short_moves, (2 * block, 2 * block + 1))

    def attend_long(block):
        @pl.loop(0, 2 * pairs_long)
        def _(head):
            attend(ql, kl, vtl, lsel, otl, head, block)

    def send_long(block):
        @pl.loop(0, pairs_long)
        def _(slot):
            send_block(ol, otl, slot, block, long_moves, (block,))

    zeros = jnp.zeros((PAD, TRIPLE), BF16)
    for slot in range(2):
        proj_l[slot, 0:PAD] = zeros
    for slot in range(3):
        proj_s[slot, 0:PAD] = zeros
    small_w.start()
    qkv_w.start()
    rows_long.start()
    rows_long.start_far()
    rows_short.start()
    small_w.over()
    small_w.turn()
    small_w.last()
    small_w.finish()
    place()
    qkv_w.over()
    rows_long.step(0)
    qkv_w.turn()
    rows_short.start_far()
    up_w.start()
    out_w.start()
    rows_long.step(1)
    qkv_w.last()
    rows_long.step(2)
    down_w.start()
    qkv_w.finish()
    join_weights()
    rows_long.whole(0)
    project_long(0)
    rows_long.whole(1)
    project_long(1)
    up_w.over()
    rows_long.whole(2)
    project_long(2)
    rows_short.step(0)
    rows_short.step(1)
    rows_short.step(2)
    rows_short.whole(0)
    project_short(0)
    rows_short.whole(1)
    project_short(1)
    rows_short.whole(2)
    project_short(2)
    rows_short.whole(3)
    project_short(3)
    rows_long.whole(3)
    project_long(3)
    out_w.over()
    up_w.turn()
    conv_short()
    attend_short(0)
    send_short(0)
    attend_short(2)
    send_short(2)
    attend_short(1)
    send_short(1)
    attend_short(3)
    send_short(3)
    save_short()
    conv_long()
    save_long()
    attend_long(0)
    send_long(0)
    attend_long(4)
    send_long(4)
    out_w.turn()
    down_w.over()
    attend_long(1)
    send_long(1)
    attend_long(5)
    send_long(5)
    up_w.last()
    out_w.last()
    attend_long(2)
    send_long(2)
    attend_long(6)
    send_long(6)
    down_w.turn()
    attend_long(3)
    send_long(3)
    attend_long(7)
    send_long(7)
    save_last()
    down_w.last()
    out_w.finish()
    up_w.finish()
    down_w.finish()
    for one in weights:
        one.sends_done()

    def own_or_wait(source, moves, slot, arrival):
        @pl.when(index == source)
        def _():
            moves(slot, index)[1].wait()

        @pl.when(index != source)
        def _():
            arrival.wait_recv()

    me = (index, y * 2 + x)
    for seq in range(2):
        for pair in range(6):
            columns = pl.ds(pair * LANES, LANES)
            block = att.at[pl.ds(seq * own_long, own_long), columns]
            source, slot = long_source(seq, pair)
            own_or_wait(
                source, long_moves, slot,
                remote(block, block, att_send_l.at[0, 0], att_recv_l.at[seq, pair], me),
            )
            block = att.at[pl.ds(2 * own_long + seq * own_short, own_short), columns]
            source, slot = short_source(seq, pair)
            own_or_wait(
                source, short_moves, slot,
                remote(block, block, att_send_s.at[0, 0], att_recv_s.at[seq, pair], me),
            )

    def sends_done(moves, slot):
        for owner in range(8):
            far, _ = moves(slot, owner)
            pl.when(index != owner)(far.wait_send)

    sends_done(long_moves, 0)
    pl.when(near == 0)(lambda: sends_done(long_moves, 1))

    @pl.when(near == 1)
    def _():
        for slot in range(3):
            sends_done(short_moves, slot)

    rows_long.finish()
    rows_short.finish()
    saves.finish()


def first_part(lengths, x_short, x_long, w_qkv, conv_kernel, norm_params, w_out, w_up, w_down, count):
    width = x_short.shape[2]
    short, long = count * x_short.shape[1], count * x_long.shape[1]
    owned = x_short.shape[1] + x_long.shape[1]
    wide = w_qkv.shape[1] // 2
    rows = w_qkv.shape[0]
    out = jax.ShapeDtypeStruct

    def saved(pairs, total):
        return [
            ((2 * pairs, total, LANES), BF16),
            ((2 * pairs, total, LANES), BF16),
            ((pairs, total, LANES), BF16),
            ((2 * pairs, HEAD_DIM, total), BF16),
            ((2 * pairs, 1, total), F32),
            ((pairs, PAD + total, TRIPLE), BF16),
            ((pairs, total, LANES), BF16),
        ]

    kept = saved(2, long) + saved(3, short)
    basic = [((short, width), BF16), ((long, width), BF16)]
    consts = [((width, wide), BF16), ((8, wide), F32), ((8, width), F32)]
    full = [((4, 2, 2, 2) + w.shape, BF16) for w in (w_out, w_up, w_down)]
    outs = [((2 * owned, width), BF16)] + full + basic + consts + kept
    scratch = (
        basic
        + [((8, LANES), F32), ((4, 2, 2, 2, 8, LANES), F32), ((2, rows, wide), BF16)]
        + [((4, 2, 2, 2, 2, rows, wide), BF16)]
        + consts
        + kept
        + [((4, HEAD_DIM, long), BF16), ((6, HEAD_DIM, short), BF16)]
        + [((4, HEAD_DIM, long), F32), ((6, HEAD_DIM, short), F32)]
    )
    return pl.pallas_call(
        first_kernel,
        out_shape=tuple(out(*one) for one in outs),
        in_specs=[smem(), hbm(), hbm(), vmem(), vmem(), vmem(), hbm(), hbm(), hbm()],
        out_specs=tuple([hbm()] * len(outs)),
        scratch_shapes=[pltpu.VMEM(*one) for one in scratch]
        + [DMA((2,))] + [DMA((2, 4))] * 4
        + [DMA((5,)), DMA((5, 13)), DMA((5, 13))]
        + [DMA((2, 8)), DMA((2, 6)), DMA((3, 8)), DMA((2, 6)), DMA((2,)), DMA((3,))]
        + [DMA((24,))],
        compiler_params=params_of(collective_id=0, has_side_effects=True),
    )(lengths, x_short, x_long, w_qkv, conv_kernel, norm_params, w_out, w_up, w_down)


def second_kernel(
    xs_ref, xl_ref, att, cs_ref, cl_ref, np_ref, wo_ref, wu_ref, wd_ref,
    ys_ref, yl_ref, gmid, gnorm, gwo_o, gwu_o, gwd_o, gl_o, gs_o,
    wo, wu, wd, middle, normal_two, inverse_two, second, second_t, cot, y_acc, gsec, gml, hid, gup,
    gwo, gwu, gwd, sib_out, sib_up, sib_down,
    load_sem, save_sem, send_l, recv_l, send_s, recv_s, core_send, core_recv,
):
    z, core, y, x = position()
    half, near, _, _ = roles()
    index = z * 2 + core
    pairs_long = 2 - near
    loads = Copies(load_sem)
    got_out = loads.start(wo_ref, wo)
    got_up = loads.start(wu_ref, wu)
    got_down = loads.start(wd_ref, wd)
    greet_all()
    short, long = xs_ref.shape[1], xl_ref.shape[1]
    first_short = 2 * long
    for seq in range(2):
        rows = slice(seq * long, (seq + 1) * long)
        cot[rows] = cl_ref[seq]
        middle[rows] = xl_ref[seq].astype(F32)
        rows = slice(first_short + seq * short, first_short + (seq + 1) * short)
        cot[rows] = cs_ref[seq]
        middle[rows] = xs_ref[seq].astype(F32)
    gnorm[...] = jnp.zeros_like(gnorm)
    inner = 512

    def through(part, size):
        @pl.loop(0, size // TILE)
        def _(step):
            rows = pl.ds(pl.multiple_of(part + step * TILE, TILE), TILE)
            values = middle[rows] + dot_nn(att[rows], wo[...])
            normal, inverse = normalise(values)
            normal_two[rows] = normal
            inverse_two[rows] = inverse
            second[rows] = (normal * np_ref[2:3] + np_ref[3:4]).astype(BF16)
            y_acc[rows] = values
            gsec[rows] = jnp.zeros_like(values)

        all_rows = slice(part, part + size)
        second_t[:, all_rows] = second[all_rows].T
        if part == 0:
            got_up.wait()
            got_down.wait()

        @pl.loop(0, wu.shape[1] // inner)
        def _(step):
            columns = times(step, inner)
            upper = jnp.maximum(dot_nn(second[all_rows], wu[:, columns]), 0.0)
            hidden = (upper * upper).astype(BF16)
            grad_hidden = dot_nt(cot[all_rows], wd[columns])
            grad_upper = (2.0 * upper * grad_hidden).astype(BF16)
            hid[all_rows, columns] = hidden
            gup[all_rows, columns] = grad_upper
            y_acc[all_rows] += dot_nn(hidden, wd[columns])
            gsec[all_rows] += dot_nt(grad_upper, wu[:, columns])

        @pl.loop(0, size // TILE)
        def _(step):
            rows = pl.ds(pl.multiple_of(part + step * TILE, TILE), TILE)
            grad = gsec[rows]
            normal = normal_two[rows]
            gnorm[2:3] += jnp.sum(grad * normal, axis=0, keepdims=True)
            gnorm[3:4] += jnp.sum(grad, axis=0, keepdims=True)
            total = cot[rows].astype(F32) + norm_back(grad, normal, inverse_two[rows], np_ref[2:3])
            gmid[rows] = total
            gml[rows] = total.astype(BF16)
            second[rows] = dot_nt(gml[rows], wo[...]).astype(BF16)

    def moves(seq, pair, is_long):
        target, slot = (long_source if is_long else short_source)(seq, pair)
        rows = long if is_long else short
        out, send, recv = (gl_o, send_l, recv_l) if is_long else (gs_o, send_s, recv_s)
        first = seq * long if is_long else first_short + seq * short
        source = second.at[pl.ds(first, rows), pl.ds(pair * LANES, LANES)]
        place = out.at[slot, times(index, rows)]
        far = remote(source, place, send.at[seq, pair], recv.at[slot, index], (target, y * 2 + x))
        close = pltpu.make_async_copy(source, place, recv.at[slot, index])
        return target, far, close

    kinds = [(seq, pair, is_long) for is_long in (True, False) for pair in range(6) for seq in range(2)]

    def send_part(is_long):
        for kind in kinds:
            if kind[2] == is_long:
                target, far, close = moves(*kind)
                pl.when(index != target)(far.start)
                pl.when(index == target)(close.start)

    got_out.wait()
    through(0, first_short)
    send_part(True)
    through(first_short, 2 * short)
    send_part(False)

    sums = [
        CoreSum(grad, sib, total, core_send.at[i], core_recv.at[i], save_sem.at[i], hop)
        for i, (grad, sib, total, hop) in enumerate(
            ((gwu, sib_up, gwu_o, None), (gwd, sib_down, gwd_o, None), (gwo, sib_out, gwo_o, None))
        )
    ]

    def cut(value, grad):
        return value.reshape(grad.shape[:5] + value.shape[1:]).astype(BF16)

    @pl.loop(0, wu.shape[1] // inner)
    def _(step):
        columns = times(step, inner)
        gwu[:, :, :, :, :, columns] = cut(dot_nn(second_t[...], gup[:, columns]), gwu)

    sums[0].start()
    per = gwd.shape[4]
    slabs = gwd.shape[2] * gwd.shape[3]

    @pl.loop(0, gwd.shape[0])
    def _(zz):
        for cc in range(2):
            columns = times(zz * 2 + cc, slabs * per)
            value = dot_tn(hid[:, columns], cot[...])
            gwd[zz, cc] = value.reshape(gwd.shape[2:]).astype(BF16)

    sums[1].start()
    sums[0].add()
    gwo[...] = cut(dot_tn(att[...], gml[...]), gwo)
    sums[2].start()
    for seq in range(2):
        ys_ref[seq] = y_acc[first_short + seq * short : first_short + (seq + 1) * short].astype(BF16)
        yl_ref[seq] = y_acc[seq * long : (seq + 1) * long].astype(BF16)

    sums[1].add()
    sums[2].add()
    me = (index, y * 2 + x)

    def arrivals(out, recv, slot, rows):
        for source in range(8):
            block = out.at[slot, pl.ds(source * rows, rows)]

            @pl.when(index != source)
            def _(block=block, source=source):
                remote(block, block, send_l.at[0, 0], recv.at[slot, source], me).wait_recv()

    arrivals(gl_o, recv_l, 0, long)
    pl.when(near == 0)(lambda: arrivals(gl_o, recv_l, 1, long))

    @pl.when(near == 1)
    def _():
        for slot in range(3):
            arrivals(gs_o, recv_s, slot, short)

    for kind in kinds:
        target, far, close = moves(*kind)
        pl.when(index != target)(far.wait_send)
        pl.when(index == target)(close.wait)
    for one in sums:
        one.finish()


def second_part(x_short, x_long, att, cot_short, cot_long, norms, w_out, w_up, w_down, count):
    width = x_short.shape[2]
    rows = att.shape[0]
    short, long = count * x_short.shape[1], count * x_long.shape[1]
    hidden = w_up.shape[1]
    out = jax.ShapeDtypeStruct
    devices = 4 * count

    def shards(w):
        return (4, 2, 2, 2, w.shape[0] // devices, w.shape[1])

    def halves(w):
        return (4, 2, 2, w.shape[0] // devices, w.shape[1])

    return pl.pallas_call(
        second_kernel,
        out_shape=(
            out(x_short.shape, BF16),
            out(x_long.shape, BF16),
            out((rows, width), F32),
            out((8, width), F32),
            out(halves(w_out), BF16),
            out(halves(w_up), BF16),
            out(halves(w_down), BF16),
            out((2, long, LANES), BF16),
            out((3, short, LANES), BF16),
        ),
        in_specs=[vmem()] * 6 + [hbm()] * 3,
        out_specs=tuple([vmem()] * 4 + [hbm()] * 5),
        scratch_shapes=[
            pltpu.VMEM(w_out.shape, BF16),
            pltpu.VMEM(w_up.shape, BF16),
            pltpu.VMEM(w_down.shape, BF16),
            pltpu.VMEM((rows, width), F32),
            pltpu.VMEM((rows, width), F32),
            pltpu.VMEM((rows, 1), F32),
            pltpu.VMEM((rows, width), BF16),
            pltpu.VMEM((width, rows), BF16),
            pltpu.VMEM((rows, width), BF16),
            pltpu.VMEM((rows, width), F32),
            pltpu.VMEM((rows, width), F32),
            pltpu.VMEM((rows, width), BF16),
            pltpu.VMEM((rows, hidden), BF16),
            pltpu.VMEM((rows, hidden), BF16),
            *[pltpu.VMEM(shards(w), BF16) for w in (w_out, w_up, w_down)],
            *[pltpu.VMEM(halves(w), BF16) for w in (w_out, w_up, w_down)],
            DMA((3,)), DMA((3, 2)), DMA((2, 6)), DMA((2, 8)), DMA((2, 6)), DMA((3, 8)), DMA((3, 3)), DMA((3, 3)),
        ],
        compiler_params=params_of(collective_id=1, has_side_effects=True),
    )(x_short, x_long, att, cot_short, cot_long, norms, w_out, w_up, w_down)


class RowSum:
    def __init__(self, long_bufs, short_bufs, sems):
        self.mine, self.out, self.sib, self.got, self.fin = long_bufs
        self.mine_s, self.out_s, self.sib_s, self.fin_s = short_bufs
        (
            self.sib_send, self.sib_recv, self.send, self.recv, self.on_send, self.fin_recv,
            self.sib_send_s, self.sib_recv_s, self.send_s, self.fin_recv_s,
        ) = sems
        self.z, self.core, self.y, self.x = position()
        self.half, self.near, partner_z, far_z = roles()
        self.partner = at(partner_z, self.core, self.y, self.x)
        self.sibling = at(self.z, 1 - self.core, self.y, self.x)
        self.far = at(far_z, self.core, self.y, self.x)

    def across(self, zz):
        return remote(self.out.at[zz % 2], self.sib.at[zz], self.sib_send.at[zz], self.sib_recv.at[zz], self.sibling)

    def put(self, block, value):
        zz, parity = block // 2, block % 2

        @pl.when(self.core == parity)
        def _():
            self.mine[zz] = value

        @pl.when(self.core != parity)
        def _():
            if zz < 2:
                self.across(zz + 2).wait_send()
            self.out[zz % 2] = value
            self.across(zz).start()

    def place(self, zz):
        return jnp.where(self.half == 0, zz, 3 - zz)

    def part(self, side):
        rows = self.fin.shape[0] // 2
        return pl.ds(side * rows, rows)

    def to_partner(self, zz, side):
        rows = self.part(side)
        return remote(
            self.mine.at[zz, rows], self.got.at[zz, rows], self.send.at[zz, side], self.recv.at[zz, side], self.partner
        )

    def to_owner(self, zz, side):
        rows = self.part(side)
        return remote(
            self.mine.at[zz, rows], self.fin.at[rows], self.on_send.at[zz, side], self.fin_recv.at[side],
            at(zz, self.core, self.y, self.x),
        )

    def sends_to_partner(self, zz):
        place = self.place(zz)
        return jnp.where(self.near == 0, place != 0, place == 0)

    def add_cores(self, zz):
        self.across(zz).wait_recv()
        for side in range(2):
            rows = self.part(side)
            add_into(self.mine.at[zz, rows], self.sib.at[zz, rows])
            pl.when(self.sends_to_partner(zz))(self.to_partner(zz, side).start)

    def sends_on(self, zz):
        return jnp.logical_and(self.near == 1, self.place(zz) >= 2)

    def add_chips(self, zz):
        @pl.when(self.sends_on(zz))
        def _():
            for side in range(2):
                rows = self.part(side)
                self.to_partner(zz, side).wait_recv()
                add_into(self.mine.at[zz, rows], self.got.at[zz, rows])
                self.to_owner(zz, side).start()

    def across_s(self, zz):
        return remote(
            self.out_s.at[zz], self.sib_s.at[zz], self.sib_send_s.at[zz], self.sib_recv_s.at[zz], self.sibling
        )

    def put_short(self, zz, value):
        rows = value.shape[0] // 2
        first, second = value[:rows], value[rows:]

        @pl.when(self.core == 0)
        def _():
            self.mine_s[zz] = first
            self.out_s[zz] = second

        @pl.when(self.core == 1)
        def _():
            self.mine_s[zz] = second
            self.out_s[zz] = first

        self.across_s(zz).start()

    def to_owner_s(self, zz):
        return remote(
            self.mine_s.at[zz], self.fin_s.at[self.half], self.send_s.at[zz], self.fin_recv_s.at[self.half],
            at(zz, self.core, self.y, self.x),
        )

    def add_short(self, zz):
        @pl.when(self.near == 1)
        def _():
            self.across_s(zz).wait_recv()
            add_into(self.mine_s.at[zz], self.sib_s.at[zz])
            pl.when(self.z != zz)(self.to_owner_s(zz).start)

    def own_long(self):
        for side in range(2):
            self.to_partner(self.z, side).wait_recv()
        return self.mine[self.z].astype(F32) + self.got[self.z].astype(F32)

    def other_long(self):
        for side in range(2):
            block = self.fin.at[self.part(side)]
            remote(block, block, self.on_send.at[0, 0], self.fin_recv.at[side], self.far).wait_recv()
        return self.fin[...].astype(F32)

    def shorts(self):
        def arrival(seq):
            block = self.fin_s.at[seq]
            remote(block, block, self.send_s.at[0], self.fin_recv_s.at[seq], self.far).wait_recv()

        arrival(1 - self.half)
        pl.when(self.near == 0)(lambda: arrival(self.half))

        @pl.when(self.near == 1)
        def _():
            self.fin_s[self.half] = self.mine_s[self.z]

    def sends_done(self):
        for zz in range(4):
            if zz < 2:
                self.across(zz).wait_send()
            for side in range(2):
                pl.when(self.sends_to_partner(zz))(self.to_partner(zz, side).wait_send)
                pl.when(self.sends_on(zz))(self.to_owner(zz, side).wait_send)

        @pl.when(self.near == 1)
        def _():
            for zz in range(4):
                self.across_s(zz).wait_send()
                pl.when(self.z != zz)(self.to_owner_s(zz).wait_send)


def third_kernel(
    xs_own, xl_own, gnorm, wq, taps, norms, gmid,
    xs_h, xl_h, ql_h, kl_h, vl_h, ktl_h, lsel_h, pl_h, ol_h, qs_h, ks_h, vs_h, kts_h, lses_h, ps_h, os_h,
    gl_h, gs_h, gwo_h, gwu_h, gwd_h,
    dxs_ref, dxl_ref, gwq_ref, gwo_ref, gwu_ref, gwd_ref, small_ref,
    ql, kl, vl, ktl, lsel, ol, gl, qs, ks, vs, kts, lses, os, gs,
    gm, dqt, delta, gp, early_gn, dwq, dtaps, dnorms, x_tile, p_tile,
    mine, out, sib, got, fin, mine_s, out_s, sib_s, fin_s,
    load_sem, tile_sem,
    r0, r1, r2, r3, r4, r5, r6, r7, r8, r9,
    shard_own, shard_send, shard_recv, group_send, group_recv, small_send, small_recv,
    *bufs,
):
    z, core, y, x = position()
    half, near, _, _ = roles()
    long_moves = (
        (ql_h, ql), (kl_h, kl), (vl_h, vl), (ktl_h, ktl), (lsel_h, lsel), (ol_h, ol), (gl_h, gl),
    )
    short_moves = (
        (qs_h, qs), (ks_h, ks), (vs_h, vs), (kts_h, kts), (lses_h, lses), (os_h, os), (gs_h, gs),
    )
    loads = [
        pltpu.make_async_copy(source, target, load_sem.at[i])
        for i, (source, target) in enumerate(long_moves + short_moves)
    ]
    long_loads, short_loads = loads[:7], loads[7:]

    @pl.when(near == 1)
    def _():
        for copy in short_loads:
            copy.start()

    for copy in long_loads:
        copy.start()
    greet_all()
    bufs = list(bufs)
    sums = []
    for i, (grad, total, begun) in enumerate(
        ((gwo_h, gwo_ref, False), (gwu_h, gwu_ref, False), (gwd_h, gwd_ref, False))
    ):
        size = 4 if begun else 5
        mine_bufs, bufs = bufs[:size], bufs[size:]
        sums.append(ShardSum(grad, total, mine_bufs, shard_own.at[i], shard_send.at[i], shard_recv.at[i], begun))
    group_early = GroupSum(bufs[0:4], group_send.at[0], group_recv.at[0])
    group_late = GroupSum(bufs[4:8], group_send.at[1], group_recv.at[1])
    small = SmallSum(bufs[8:13], small_ref, small_send, small_recv)
    rows_sum = RowSum((mine, out, sib, got, fin), (mine_s, out_s, sib_s, fin_s), (r0, r1, r2, r3, r4, r5, r6, r7, r8, r9))
    sum_out, sum_up, sum_down = sums
    sum_up.start()
    short, long = xs_own.shape[1], xl_own.shape[1]
    middles = [
        pltpu.make_async_copy(gmid.at[pl.ds(first + seq * size, size)], dx.at[seq], load_sem.at[14 + 2 * seq + i])
        for seq in range(2)
        for i, (dx, first, size) in enumerate(((dxs_ref, 2 * long, short), (dxl_ref, 0, long)))
    ]
    for copy in middles:
        copy.start()
    gm[...] = jnp.zeros_like(gm)
    dwq[...] = jnp.zeros_like(dwq)
    dtaps[...] = jnp.zeros_like(dtaps)
    dnorms[...] = gnorm[...]
    gain, offset = norms[0:1], norms[1:2]
    causal = causal_mask()
    first_lanes = iota((TILE, LANES), 1) < HEAD_DIM

    def back_head(refs, grad_ref, slot, side, local, block):
        q_ref, k_ref, v_ref, kt_ref, lse, _, g_ref = refs
        head = 2 * slot + side
        own_lanes = first_lanes == (side == 0)
        rows = slice(block * TILE, (block + 1) * TILE)
        query = q_ref[head, rows]
        bare = jnp.where(own_lanes, query.astype(F32), 0.0).astype(BF16)
        grad_out = jnp.where(own_lanes, g_ref[slot, rows].astype(F32), 0.0).astype(BF16)
        stat, less = lse[head, :, rows], delta[local]
        spans = [(block * TILE, TILE, True)]
        if block:
            spans.append((0, block * TILE, False))
        grad_q = None
        for start, size, masked in spans:
            keys = slice(start, start + size)
            scores = dot_nt(k_ref[head, keys], query)
            if masked:
                scores = jnp.where(causal, scores, NEG_FILL)
            probs = jnp.exp(scores - stat)
            grad_probs = dot_nt(v_ref[slot, keys], grad_out)
            grad_ref[keys, 2 * LANES :] += dot_nn(probs.astype(BF16), grad_out)
            grad_scores = (probs * (grad_probs - less)).astype(BF16)
            grad_ref[keys, LANES : 2 * LANES] += dot_nn(grad_scores, bare)
            term = dot_nn(kt_ref[head, :, keys], grad_scores)
            grad_q = term if grad_q is None else grad_q + term
        dqt[local] = (HEAD_DIM**-0.5) * grad_q

    def back_block(refs, x_h, p_h, count, first_slot, first_pair, block):
        o_ref, g_ref = refs[5], refs[6]
        rows = slice(block * TILE, (block + 1) * TILE)
        span = x_h.shape[0] + PAD
        got_x = pltpu.make_async_copy(x_h.at[pl.ds(block * TILE, TILE)], x_tile, tile_sem.at[0])
        got_p = pltpu.make_async_copy(
            p_h.at[pl.ds(first_slot, count), pl.ds(block * TILE, TILE + PAD)], p_tile.at[pl.ds(0, count)], tile_sem.at[1]
        )
        got_x.start()
        got_p.start()
        for local in range(count):
            product = g_ref[first_slot + local, rows].astype(F32) * o_ref[first_slot + local, rows].astype(F32)
            turned = product.T
            delta[2 * local] = jnp.sum(turned[:HEAD_DIM], axis=0, keepdims=True)
            delta[2 * local + 1] = jnp.sum(turned[HEAD_DIM:], axis=0, keepdims=True)

        @pl.loop(0, 2 * count)
        def _(local):
            slot = local // 2
            grad_ref = gm.at[pl.ds(pl.multiple_of(slot * span, PAD), span)]
            back_head(refs, grad_ref, first_slot + slot, local % 2, local, block)

        got_x.wait()
        got_p.wait()
        normal, _ = normalise(x_tile[...].astype(F32))
        low = (normal * gain + offset).astype(BF16)
        for local in range(count):
            grad_ref = gm.at[pl.ds(local * span, span)]
            grad_ref[rows, 0:LANES] = jnp.concatenate([dqt[2 * local], dqt[2 * local + 1]], axis=0).T
            window = grad_ref[pl.ds(block * TILE, TILE + PAD)]
            grad = window[:TILE]
            columns = pl.ds(pl.multiple_of((first_pair + local) * TRIPLE, TRIPLE), TRIPLE)
            kernel = taps[:, columns]
            grad_projected = (
                kernel[0:1] * grad + kernel[1:2] * shifted(window, -1)[:TILE] + kernel[2:3] * shifted(window, -2)[:TILE]
            ).astype(BF16)
            past = p_tile[local].astype(F32)
            dtaps[0:1, columns] += jnp.sum(grad * past[PAD:], axis=0, keepdims=True)
            dtaps[1:2, columns] += jnp.sum(grad * shifted(past, 1)[PAD:], axis=0, keepdims=True)
            dtaps[2:3, columns] += jnp.sum(grad * shifted(past, 2)[PAD:], axis=0, keepdims=True)
            gp[:, local * TRIPLE : (local + 1) * TRIPLE] = grad_projected
        grads = gp[:, : count * TRIPLE]
        columns = pl.ds(pl.multiple_of(first_pair * TRIPLE, TRIPLE), count * TRIPLE)
        grad_normed = dot_nt(grads, wq[:, columns])
        dwq[:, columns] += dot_tn(low, grads)
        dnorms[0:1] += jnp.sum(grad_normed * normal, axis=0, keepdims=True)
        dnorms[1:2] += jnp.sum(grad_normed, axis=0, keepdims=True)
        return grad_normed

    def hook_one():
        sum_up.turn()
        sum_down.start()
        sum_out.start()

    def hook_two():
        sum_up.last()

    def hook_three():
        sum_down.turn()
        sum_out.turn()

    def hook_four():
        sum_down.last()
        sum_out.last()

    def finish_rows(seq, grad, x_ref, dx_ref):
        normal, inverse = normalise(x_ref[seq].astype(F32))
        dx_ref[seq] += norm_back(grad, normal, inverse, gain)

    long_refs = (ql, kl, vl, ktl, lsel, ol, gl)
    short_refs = (qs, ks, vs, kts, lses, os, gs)
    last_long = xl_h.shape[0] // TILE - 1
    last_short = xs_h.shape[0] // TILE - 1

    @pl.when(near == 0)
    def _():
        for copy in long_loads:
            copy.wait()
        for block in range(last_long, -1, -1):
            value = back_block(long_refs, xl_h, pl_h, 1, 0, 0, block)
            early_gn[block * TILE : (block + 1) * TILE] = value.astype(BF16)
            if block == 6:
                hook_one()
            if block == 3:
                hook_two()

    @pl.when(near == 1)
    def _():
        for copy in short_loads:
            copy.wait()
        for block in range(last_short, -1, -1):
            value = back_block(short_refs, xs_h, ps_h, 3, 0, 0, block)
            rows_sum.put_short(block, value.astype(BF16))
            if block == 3:
                hook_one()
            if block == 1:
                hook_two()
        for copy in long_loads:
            copy.wait()

    hook_three()
    group_early.start(dwq, pl.ds(0, 2 * TRIPLE))
    gm[...] = jnp.zeros_like(gm)

    for block in range(last_long, -1, -1):
        value = back_block(long_refs, xl_h, pl_h, 1, 1 - near, 1 + near, block)
        early = early_gn[block * TILE : (block + 1) * TILE].astype(F32)
        rows_sum.put(block, (value + jnp.where(near == 0, early, 0.0)).astype(BF16))
        if block % 2 == 1 and block != last_long:
            rows_sum.add_cores(block // 2 + 1)
        if block > 3:
            rows_sum.add_short(block - 4)
        if block == 7:
            hook_four()
        if block == 6:
            group_early.turn()
        if block == 5:
            group_early.last()
        if block == 2:
            rows_sum.add_chips(3)
    group_late.start(dwq, pl.ds(pl.multiple_of((1 + near) * TRIPLE, TRIPLE), TRIPLE))
    small.start(dtaps[...], dnorms[...])
    rows_sum.add_cores(0)
    rows_sum.add_chips(2)
    small.over()
    group_late.turn()
    rows_sum.add_chips(1)
    small.turn()
    for copy in middles:
        copy.wait()
    rows_sum.shorts()
    finish_rows(half, rows_sum.fin_s[half].astype(F32), xs_own, dxs_ref)
    group_late.last()
    small.last()
    rows_sum.add_chips(0)
    finish_rows(1 - half, rows_sum.fin_s[1 - half].astype(F32), xs_own, dxs_ref)
    finish_rows(half, rows_sum.own_long(), xl_own, dxl_ref)
    for one in sums:
        one.finish()
    group_early.finish()
    small.swap_back()
    group_late.finish()
    join_groups(group_early, group_late, gwq_ref)
    finish_rows(1 - half, rows_sum.other_long(), xl_own, dxl_ref)
    small.finish()
    rows_sum.sends_done()


def third_part(x_short, x_long, gmid, gnorm, wq, taps, norms, kept, grads_in, weight_grads):
    width = x_short.shape[2]
    wide = wq.shape[1]
    count = 8
    short, long = count * x_short.shape[1], count * x_long.shape[1]
    own_short = x_short.shape[1]
    rows = weight_grads[0].shape[3]
    out = jax.ShapeDtypeStruct
    small_wide = wide + width // 2

    def saved(pairs, total):
        return [
            ((2 * pairs, total, LANES), BF16),
            ((2 * pairs, total, LANES), BF16),
            ((pairs, total, LANES), BF16),
            ((2 * pairs, HEAD_DIM, total), BF16),
            ((2 * pairs, 1, total), F32),
            ((pairs, total, LANES), BF16),
            ((pairs, total, LANES), BF16),
        ]

    scratch = (
        saved(2, long)
        + saved(3, short)
        + [
            ((max(long + PAD, 3 * (short + PAD)), TRIPLE), F32),
            ((6, HEAD_DIM, TILE), F32),
            ((6, 1, TILE), F32),
            ((TILE, wide), BF16),
            ((long, width), BF16),
            ((width, wide), F32),
            ((8, wide), F32),
            ((8, width), F32),
            ((TILE, width), BF16),
            ((3, TILE + PAD, TRIPLE), BF16),
        ]
        + [((4, TILE, width), BF16), ((2, TILE, width), BF16)]
        + [((4, TILE, width), BF16)] * 2
        + [((TILE, width), BF16)]
        + [((4, own_short, width), BF16)] * 3
        + [((2, own_short, width), BF16)]
    )
    buffers = []
    for i, g in enumerate(weight_grads):
        buffers += ShardSum.buffers(g)
    buffers += GroupSum.buffers(rows, 2 * TRIPLE) + GroupSum.buffers(rows, TRIPLE) + SmallSum.buffers(wide, width // 2)
    return pl.pallas_call(
        third_kernel,
        out_shape=(
            out(x_short.shape, F32),
            out(x_long.shape, F32),
            out((rows, 2 * wide), F32),
            *[out(g.shape[3:], F32) for g in weight_grads],
            out((2, 8, small_wide), F32),
        ),
        in_specs=[vmem()] * 6 + [hbm()] * (1 + len(kept) + len(grads_in) + len(weight_grads)),
        out_specs=tuple([vmem()] * 7),
        scratch_shapes=[pltpu.VMEM(*one) for one in scratch]
        + [DMA((18,)), DMA((2,))]
        + [DMA((4,))] * 2 + [DMA((4, 2))] * 3 + [DMA((2,))] + [DMA((4,))] * 3 + [DMA((2,))]
        + [DMA((3, 2)), DMA((3, 9)), DMA((3, 9)), DMA((2, 11)), DMA((2, 11)), DMA((7,)), DMA((7,))]
        + buffers,
        compiler_params=params_of(63, collective_id=2, has_side_effects=True),
    )(x_short, x_long, gnorm, wq, taps, norms, gmid, *kept, *grads_in, *weight_grads)


def last_kernel(*refs):
    *arrays, smalls = refs[:9]
    outs, kernel_out, norm_out = refs[9:17], refs[17], refs[18]
    held, sems = refs[19:27], refs[27]
    loads = [pltpu.make_async_copy(a, h, sems.at[0, i]) for i, (a, h) in enumerate(zip(arrays, held))]
    copies = [pltpu.make_async_copy(h, o, sems.at[1, i]) for i, (h, o) in enumerate(zip(held, outs))]
    for copy in loads:
        copy.start()
    number = lax.axis_index("seq") * lax.axis_size("batch") + lax.axis_index("batch")
    (taps, part), (norms, cut) = kernel_out.shape, norm_out.shape
    norm_columns = norm_out.shape[1] * 32 // 2
    wide = smalls.shape[2] - norm_columns
    width = 2 * wide // 3

    def pick(values, source, first):
        chosen = jnp.where(source == first + iota(source.shape, 1), 1.0, 0.0)
        return lax.dot_general(
            values, chosen, (((1,), (0,)), ((), ())), preferred_element_type=F32, precision=lax.Precision.HIGHEST
        )

    row = iota((wide, LANES), 0)
    block = row // LANES
    norm_row = iota((norm_columns, LANES), 0)
    kernel_sum, norm_sum = None, None
    for load, copy in zip(loads, copies):
        load.wait()
        copy.start()
    for side in range(2):
        source = (block % 3) * width + (3 * side + block // 3) * LANES + row % LANES
        term = pick(smalls[side, :, :wide], source, number * part)
        norm_term = pick(smalls[side, :, wide:], norm_row + side * norm_columns, number * cut)
        kernel_sum = term if side == 0 else kernel_sum + term
        norm_sum = norm_term if side == 0 else norm_sum + norm_term
    kernel_out[...] = kernel_sum[:taps, :part]
    norm_out[...] = norm_sum[:norms, :cut]
    for copy in copies:
        copy.wait()


def last_part(arrays, smalls, taps, part, cut):
    out = jax.ShapeDtypeStruct
    return pl.pallas_call(
        last_kernel,
        out_shape=(*[out(a.shape, a.dtype) for a in arrays], out((taps, part), F32), out((4, cut), F32)),
        in_specs=[hbm()] * 8 + [vmem()],
        out_specs=tuple([hbm()] * 8 + [vmem()] * 2),
        scratch_shapes=[pltpu.VMEM(a.shape, a.dtype) for a in arrays] + [DMA((2, 8))],
        compiler_params=params_of(),
    )(*arrays, smalls)


def split_body(
    x_short, x_long, lengths, cot_short, cot_long, w_qkv, w_out, w_up, w_down, conv_kernel, norm_params
):
    count = lax.axis_size("seq")
    width = x_short.shape[2]
    att, full_out, full_up, full_down, xs, xl, wq, taps, norms, *kept = first_part(
        lengths, x_short, x_long, w_qkv, conv_kernel, norm_params, w_out, w_up, w_down, count
    )
    y_short, y_long, gmid, gnorm, gwo, gwu, gwd, gl, gs = second_part(
        x_short, x_long, att, cot_short, cot_long, norms,
        full_out.reshape(width, -1), full_up.reshape(width, -1), full_down.reshape(-1, width), count,
    )
    dx_short, dx_long, sum_qkv, sum_out, sum_up, sum_down, smalls = third_part(
        x_short, x_long, gmid, gnorm, wq, taps, norms, [xs, xl] + kept, [gl, gs], [gwo, gwu, gwd]
    )
    return last_part(
        (y_short, y_long, dx_short, dx_long, sum_qkv, sum_out, sum_up, sum_down), smalls,
        conv_kernel.shape[0], conv_kernel.shape[1], norm_params.shape[1],
    )


GROUP_HEADS = 2


def from_behind(value, axis, by):
    count = lax.axis_size(axis)
    pairs = [(i, i + by) for i in range(count) if 0 <= i + by < count]
    return lax.ppermute(value, axis, pairs)


def layer_norm(values, gain, offset_term):
    average = jnp.mean(values, axis=-1, keepdims=True)
    centred = values - average
    inverse = lax.rsqrt(jnp.mean(centred * centred, axis=-1, keepdims=True) + EPS)
    normal = centred * inverse
    return (normal * gain + offset_term, normal, inverse)


def norm_back_flat(grad, normal, inverse, gain):
    scaled_grad = grad * gain
    first_mean = jnp.mean(scaled_grad, axis=-1, keepdims=True)
    second_mean = jnp.mean(scaled_grad * normal, axis=-1, keepdims=True)
    return inverse * (scaled_grad - first_mean - normal * second_mean)


def front_part(inputs, full_weights):
    w_qkv = full_weights[0]
    kernel = full_weights[4].astype(jnp.float32)
    params = full_weights[5].astype(jnp.float32)
    saved = []
    tails = []
    for part_in in inputs:
        seq_count, block_rows, model_width = part_in.shape
        flat = part_in.reshape(seq_count * block_rows, model_width).astype(jnp.float32)
        normed, normal, inverse = layer_norm(flat, params[0], params[1])
        normed_low = normed.astype(jnp.bfloat16)
        projected = jnp.dot(normed_low, w_qkv, preferred_element_type=jnp.float32).astype(
            jnp.bfloat16
        )
        projected = projected.reshape(seq_count, block_rows, 3 * model_width)
        saved.append((flat, normal, inverse, normed_low, projected))
        tails.append(projected[:, block_rows - 2 :])
    received = from_behind((tails[0], tails[1]), "seq", 1)
    fronts = []
    for index_part in range(2):
        flat, normal, inverse, normed_low, projected = saved[index_part]
        block_rows = projected.shape[1]
        padded = jnp.concatenate([received[index_part], projected], axis=1).astype(jnp.float32)
        mixed = (
            kernel[0] * padded[:, 2:]
            + kernel[1] * padded[:, 1 : block_rows + 1]
            + kernel[2] * padded[:, :block_rows]
        )
        fronts.append((flat, normal, inverse, normed_low, padded, mixed.astype(jnp.bfloat16)))
    return fronts


def attend_block(queries, key_rows, value_rows, usable, grad_heads):
    scaling = queries.shape[-1] ** (-0.5)
    scores = jnp.einsum("sqhd,skhd->shqk", queries, key_rows, preferred_element_type=jnp.float32)
    masked = jnp.where(usable, scaling * scores, NEG_FILL)
    exp_terms = jnp.exp(masked - jnp.max(masked, axis=-1, keepdims=True))
    attn_probs = exp_terms / jnp.sum(exp_terms, axis=-1, keepdims=True)
    probs_low = attn_probs.astype(jnp.bfloat16)
    if grad_heads is None:
        attended = jnp.einsum(
            "shqk,skhd->sqhd", probs_low, value_rows, preferred_element_type=jnp.float32
        )
        return attended.astype(jnp.bfloat16)
    grad_probs = jnp.einsum(
        "sqhd,skhd->shqk", grad_heads, value_rows, preferred_element_type=jnp.float32
    )
    grad_values = jnp.einsum(
        "shqk,sqhd->skhd", probs_low, grad_heads, preferred_element_type=jnp.float32
    )
    row_delta = jnp.sum(attn_probs * grad_probs, axis=-1, keepdims=True)
    grad_scores = (scaling * attn_probs * (grad_probs - row_delta)).astype(jnp.bfloat16)
    grad_queries = jnp.einsum(
        "shqk,skhd->sqhd", grad_scores, key_rows, preferred_element_type=jnp.float32
    )
    grad_keys = jnp.einsum(
        "shqk,sqhd->skhd", grad_scores, queries, preferred_element_type=jnp.float32
    )
    return (grad_queries, grad_keys, grad_values)


def make_usable(query_pos, key_pos, seq_lengths):
    usable = (key_pos[None, None, :] <= query_pos[None, :, None]) & (
        key_pos[None, None, :] < seq_lengths[:, None, None]
    )
    return usable[:, None]


def attention(mixed, kv_full, seq_lengths, offset, grad_attended):
    seq_count, block_rows, three_width = mixed.shape
    model_width = three_width // 3
    full_len = kv_full.shape[1]
    queries = mixed[:, :, :model_width].reshape(seq_count, block_rows, -1, HEAD_DIM)
    key_rows = kv_full[:, :, :model_width].reshape(seq_count, full_len, -1, HEAD_DIM)
    value_rows = kv_full[:, :, model_width:].reshape(seq_count, full_len, -1, HEAD_DIM)
    positions = offset + jnp.arange(block_rows, dtype=jnp.int32)
    key_pos = jnp.arange(full_len, dtype=jnp.int32)
    usable = make_usable(positions, key_pos, seq_lengths)
    heads_total = queries.shape[2]
    grad_heads = None
    if grad_attended is not None:
        grad_heads = grad_attended.reshape(seq_count, block_rows, -1, HEAD_DIM)
    results = []
    for first_head in range(0, heads_total, GROUP_HEADS):
        last_head = first_head + GROUP_HEADS
        grad_part = None if grad_heads is None else grad_heads[:, :, first_head:last_head]
        results.append(
            attend_block(
                queries[:, :, first_head:last_head],
                key_rows[:, :, first_head:last_head],
                value_rows[:, :, first_head:last_head],
                usable,
                grad_part,
            )
        )
    if grad_heads is None:
        return jnp.concatenate(results, axis=2).reshape(seq_count, block_rows, model_width)
    grad_queries = jnp.concatenate([entry_set[0] for entry_set in results], axis=2).reshape(
        seq_count, block_rows, model_width
    )
    grad_keys = jnp.concatenate([entry_set[1] for entry_set in results], axis=2).reshape(
        seq_count, full_len, model_width
    )
    grad_values = jnp.concatenate([entry_set[2] for entry_set in results], axis=2).reshape(
        seq_count, full_len, model_width
    )
    return (grad_queries, grad_keys, grad_values)


def rest_part(front, kv_full, seq_lengths, offset, full_weights, cotangent_in):
    w_out, w_up, w_down = (full_weights[1], full_weights[2], full_weights[3])
    params = full_weights[5].astype(jnp.float32)
    flat, normal_one, inverse_one, normed_low, padded, mixed = front
    seq_count, block_rows, three_width = mixed.shape
    model_width = three_width // 3
    attended = attention(mixed, kv_full, seq_lengths, offset, None).reshape(
        seq_count * block_rows, model_width
    )
    middle = flat + jnp.dot(attended, w_out, preferred_element_type=jnp.float32)
    second, normal_two, inverse_two = layer_norm(middle, params[2], params[3])
    second_low = second.astype(jnp.bfloat16)
    upper = jnp.dot(second_low, w_up, preferred_element_type=jnp.float32)
    hidden = jnp.square(jnp.maximum(upper, 0.0)).astype(jnp.bfloat16)
    if cotangent_in is None:
        result_rows = middle + jnp.dot(hidden, w_down, preferred_element_type=jnp.float32)
        return result_rows.astype(jnp.bfloat16).reshape(seq_count, block_rows, model_width)
    cotangent = cotangent_in.reshape(seq_count * block_rows, model_width)
    grad_down = jnp.dot(hidden.T, cotangent, preferred_element_type=jnp.float32)
    grad_hidden = jnp.dot(cotangent, w_down.T, preferred_element_type=jnp.float32)
    grad_upper = (2.0 * jnp.maximum(upper, 0.0) * grad_hidden).astype(jnp.bfloat16)
    grad_up = jnp.dot(second_low.T, grad_upper, preferred_element_type=jnp.float32)
    grad_second = jnp.dot(grad_upper, w_up.T, preferred_element_type=jnp.float32)
    grad_middle = cotangent.astype(jnp.float32) + norm_back_flat(
        grad_second, normal_two, inverse_two, params[2]
    )
    grad_middle_low = grad_middle.astype(jnp.bfloat16)
    grad_out = jnp.dot(attended.T, grad_middle_low, preferred_element_type=jnp.float32)
    grad_attended = jnp.dot(grad_middle_low, w_out.T, preferred_element_type=jnp.float32).astype(
        jnp.bfloat16
    )
    grad_attended = grad_attended.reshape(seq_count, block_rows, model_width)
    grad_queries, grad_keys, grad_values = attention(
        mixed, kv_full, seq_lengths, offset, grad_attended
    )
    key_term = jnp.concatenate([grad_keys, grad_values], axis=-1)
    norm_two = (jnp.sum(grad_second * normal_two, axis=0), jnp.sum(grad_second, axis=0))
    return (grad_queries, key_term, grad_middle, grad_out, grad_up, grad_down, norm_two)


def general_body(
    x_short,
    x_long,
    lengths,
    cot_short,
    cot_long,
    w_qkv,
    w_out,
    w_up,
    w_down,
    conv_kernel,
    norm_params,
):
    full_weights = (
        lax.all_gather(w_qkv, ("seq", "batch"), axis=0, tiled=True),
        lax.all_gather(w_out, ("seq", "batch"), axis=0, tiled=True),
        lax.all_gather(w_up, ("seq", "batch"), axis=0, tiled=True),
        lax.all_gather(w_down, ("seq", "batch"), axis=0, tiled=True),
        lax.all_gather(conv_kernel, ("seq", "batch"), axis=1, tiled=True),
        lax.all_gather(norm_params, ("seq", "batch"), axis=1, tiled=True),
    )
    inputs = (x_short, x_long)
    cotangents = (cot_short, cot_long)
    model_width = x_short.shape[2]
    offsets = (lax.axis_index("seq") * x_short.shape[1], lax.axis_index("seq") * x_long.shape[1])
    fronts = front_part(inputs, full_weights)
    kv_fwd = (
        lax.all_gather(fronts[0][5][:, :, model_width:], "seq", axis=1, tiled=True),
        lax.all_gather(fronts[1][5][:, :, model_width:], "seq", axis=1, tiled=True),
    )
    outputs = [
        rest_part(
            fronts[index_part],
            kv_fwd[index_part],
            lengths[index_part],
            offsets[index_part],
            full_weights,
            None,
        )
        for index_part in range(2)
    ]
    back_weights = (
        lax.all_gather(w_qkv, ("seq", "batch"), axis=0, tiled=True),
        lax.all_gather(w_out, ("seq", "batch"), axis=0, tiled=True),
        lax.all_gather(w_up, ("seq", "batch"), axis=0, tiled=True),
        lax.all_gather(w_down, ("seq", "batch"), axis=0, tiled=True),
        lax.all_gather(conv_kernel, ("seq", "batch"), axis=1, tiled=True),
        lax.all_gather(norm_params, ("seq", "batch"), axis=1, tiled=True),
    )
    fronts_back = front_part(inputs, back_weights)
    kv_back = (
        lax.all_gather(fronts_back[0][5][:, :, model_width:], "seq", axis=1, tiled=True),
        lax.all_gather(fronts_back[1][5][:, :, model_width:], "seq", axis=1, tiled=True),
    )
    partials = [
        rest_part(
            fronts_back[index_part],
            kv_back[index_part],
            lengths[index_part],
            offsets[index_part],
            back_weights,
            cotangents[index_part],
        )
        for index_part in range(2)
    ]
    kv_grads = (
        lax.psum_scatter(
            partials[0][1].astype(jnp.bfloat16), "seq", scatter_dimension=1, tiled=True
        ).astype(jnp.float32),
        lax.psum_scatter(
            partials[1][1].astype(jnp.bfloat16), "seq", scatter_dimension=1, tiled=True
        ).astype(jnp.float32),
    )
    grad_mixed = [
        jnp.concatenate([partials[index_part][0], kv_grads[index_part]], axis=-1)
        for index_part in range(2)
    ]
    received = (
        from_behind(grad_mixed[0][:, :2].astype(jnp.bfloat16), "seq", -1).astype(jnp.float32),
        from_behind(grad_mixed[1][:, :2].astype(jnp.bfloat16), "seq", -1).astype(jnp.float32),
    )
    kernel = back_weights[4].astype(jnp.float32)
    params = back_weights[5].astype(jnp.float32)
    w_qkv_full = back_weights[0]
    grad_qkv = jnp.zeros(w_qkv_full.shape, jnp.float32)
    grad_kernel = jnp.zeros(kernel.shape, jnp.float32)
    grad_norm = jnp.zeros((4, model_width), jnp.float32)
    grad_out = partials[0][3] + partials[1][3]
    grad_up = partials[0][4] + partials[1][4]
    grad_down = partials[0][5] + partials[1][5]
    input_grads = []
    for index_part in range(2):
        flat, normal_one, inverse_one, normed_low, padded, mixed = fronts_back[index_part]
        seq_count, block_rows, three_width = mixed.shape
        mixed_grad = grad_mixed[index_part]
        extended = jnp.concatenate([mixed_grad, received[index_part]], axis=1)
        grad_projected = (
            kernel[0] * extended[:, :block_rows]
            + kernel[1] * extended[:, 1 : block_rows + 1]
            + kernel[2] * extended[:, 2:]
        ).astype(jnp.bfloat16)
        grad_kernel = grad_kernel + jnp.stack(
            [
                jnp.sum(mixed_grad * padded[:, 2:], axis=(0, 1)),
                jnp.sum(mixed_grad * padded[:, 1 : block_rows + 1], axis=(0, 1)),
                jnp.sum(mixed_grad * padded[:, :block_rows], axis=(0, 1)),
            ]
        )
        grad_flat = grad_projected.reshape(seq_count * block_rows, three_width)
        grad_qkv = grad_qkv + jnp.dot(normed_low.T, grad_flat, preferred_element_type=jnp.float32)
        grad_normed = jnp.dot(grad_flat, w_qkv_full.T, preferred_element_type=jnp.float32)
        grad_input = partials[index_part][2] + norm_back_flat(
            grad_normed, normal_one, inverse_one, params[0]
        )
        input_grads.append(grad_input.reshape(seq_count, block_rows, model_width))
        norm_two = partials[index_part][6]
        grad_norm = grad_norm + jnp.stack(
            [
                jnp.sum(grad_normed * normal_one, axis=0),
                jnp.sum(grad_normed, axis=0),
                norm_two[0],
                norm_two[1],
            ]
        )
    summed = (
        lax.psum_scatter(grad_qkv, ("seq", "batch"), scatter_dimension=0, tiled=True),
        lax.psum_scatter(grad_out, ("seq", "batch"), scatter_dimension=0, tiled=True),
        lax.psum_scatter(grad_up, ("seq", "batch"), scatter_dimension=0, tiled=True),
        lax.psum_scatter(grad_down, ("seq", "batch"), scatter_dimension=0, tiled=True),
        lax.psum_scatter(grad_kernel, ("seq", "batch"), scatter_dimension=1, tiled=True),
        lax.psum_scatter(grad_norm, ("seq", "batch"), scatter_dimension=1, tiled=True),
    )
    return (
        outputs[0],
        outputs[1],
        input_grads[0],
        input_grads[1],
        summed[0],
        summed[1],
        summed[2],
        summed[3],
        summed[4],
        summed[5],
    )


def solution(mesh):
    split = mesh.shape["seq"] == 8
    return jax.shard_map(
        split_body if split else general_body,
        mesh=mesh,
        in_specs=(
            P("batch", "seq", None),
            P("batch", "seq", None),
            P(None, "batch"),
            P("batch", "seq", None),
            P("batch", "seq", None),
            P(("seq", "batch"), None),
            P(("seq", "batch"), None),
            P(("seq", "batch"), None),
            P(("seq", "batch"), None),
            P(None, ("seq", "batch")),
            P(None, ("seq", "batch")),
        ),
        out_specs=(
            P("batch", "seq", None),
            P("batch", "seq", None),
            P("batch", "seq", None),
            P("batch", "seq", None),
            P(("seq", "batch"), None),
            P(("seq", "batch"), None),
            P(("seq", "batch"), None),
            P(("seq", "batch"), None),
            P(None, ("seq", "batch")),
            P(None, ("seq", "batch")),
        ),
        check_vma=False,
    )
```
